32 devices in a mesh: ctx: 2 (over core), exp: 4 (over y, x), dp: 4 (over z).
Axes of the slice: x: 2, y: 2, z: 4, core: 2. Of those that a mesh axis runs over, the one named last changes fastest.
Arguments:
- queries: bfloat16 [16, 256, 2048], P(('exp', 'dp'), 'ctx'), may hold values from -8 to 8
- keys: bfloat16 [16, 256, 256], P(('exp', 'dp'), 'ctx'), may hold values from -8 to 8
- values: bfloat16 [16, 256, 256], P(('exp', 'dp'), 'ctx'), may hold values from -6 to 6
- resid: bfloat16 [16, 256, 2048], P(('exp', 'dp'), 'ctx'), may hold values from -6 to 6
- block_order: int32 [16], replicated, may hold values from 0 to 15, each once
- norm_gain: float32 [2048], replicated, may hold values from 0.1 to 1.9
- w_gate: bfloat16 [8, 2048, 384], P('exp'), may hold values from -0.125 to 0.125
- w_down: bfloat16 [8, 384, 2048], P('exp'), may hold values from -0.3125 to 0.3125
- routes: int32 [16, 256, 1], P(('exp', 'dp'), 'ctx'), may hold values from 0 to 7; in each aligned block of 128 rows (0 to 127, 128 to 255, ..., all dimensions but the last counted through in order) at most 24 rows name the same one
- route_weight: float32 [16, 256], P(('exp', 'dp'), 'ctx'), may hold values from 0.2 to 1
- d_out: bfloat16 [16, 256, 2048], P(('exp', 'dp'), 'ctx'), may hold values from -6 to 6
Outputs:
- layer_out: bfloat16 [16, 256, 2048], P(('exp', 'dp'), 'ctx')
- d_resid: bfloat16 [16, 256, 2048], P(('exp', 'dp'), 'ctx')
- d_queries: bfloat16 [16, 256, 2048], P(('exp', 'dp'), 'ctx')
- d_keys: bfloat16 [16, 256, 256], P(('exp', 'dp'), 'ctx')
- d_values: bfloat16 [16, 256, 256], P(('exp', 'dp'), 'ctx')
- d_weight: float32 [16, 256], P(('exp', 'dp'), 'ctx')
- d_gain: float32 [2048], replicated
The draws below stay inside these ranges and needn't reach their ends.
Inputs may be any that keep to these rules, and one draw needn't show every extreme that they name: `routes`: within the rows of one device (aligned blocks of 128 rows) no expert is named more than 24 times, and in every draw some expert is named exactly 24 times in some block.
All inputs are finite; a program needn't handle non-finite values.
Results may differ from the reference program's by a relative error of at most 0.028.
Values may be sent and summed in bfloat16 or wider, within the bound.
No kernel may reach another device: no remote copies, remote signals or barrier semaphores. Data moves between devices by JAX's collectives and lax.ppermute only.
A program may use at most 64 MiB of HBM per device.

```python
import math
import jax
import jax.numpy as jnp
import numpy as np
from jax import lax

D = 2048
HEAD_SIZE = 128
QUERY_HEADS = 16
KEY_VALUE_HEADS = 2
FFE = 384
TOK = 128
EXPERTS = 8
CAP = 24
SEQUENCE_LENGTH = 256
SEQUENCE_COUNT = 16
N_CTX = 2


def draw_queries(key, part):
    drawn_result = jnp.clip(jax.random.normal(jax.random.fold_in(key, 11), (SEQUENCE_COUNT, SEQUENCE_LENGTH, QUERY_HEADS * HEAD_SIZE), jnp.float32), -6.0, 6.0)
    return drawn_result.astype(jnp.bfloat16)


def draw_keys(key, part):
    drawn_result = jnp.clip(jax.random.normal(jax.random.fold_in(key, 13), (SEQUENCE_COUNT, SEQUENCE_LENGTH, KEY_VALUE_HEADS * HEAD_SIZE), jnp.float32), -6.0, 6.0)
    return drawn_result.astype(jnp.bfloat16)


def steps_of(own_key, extent, cuts, low, top_value):
    loudness = 1.0
    for dim, parts in cuts:
        draws = jax.random.uniform(jax.random.fold_in(jax.random.fold_in(own_key, 6), dim), (parts,), jnp.float32, low / len(cuts), top_value / len(cuts))
        loudness = loudness * jnp.repeat(jnp.exp(draws), extent[dim] // parts).reshape((-1,) + (1,) * (len(extent) - 1 - dim))
    return loudness


def routed_block(rng, own, number, rows, count, top, limit, lean):
    order = jax.random.permutation(rng, count)
    crowded, ordinary = load_shares(count, rows * top, limit, lean, True), load_shares(count, rows * top, limit, lean, False)
    places = jnp.arange(count)

    def named(tallies, turn):
        used = int((tallies > 0).sum())
        fixed = max(1, used // 4)
        shifted = fixed + (places - fixed + turn * (used - fixed)) % max(1, count - fixed)
        return jnp.zeros((count,), jnp.int32).at[order[jnp.where(places < fixed, places, shifted)]].set(jnp.asarray(tallies, jnp.int32))

    tallies = jnp.where(number % 4 == 0, named(crowded, number // 4), named(ordinary, number - number // 4 - 1))
    mixed = jax.random.permutation(jax.random.fold_in(own, 3), count)
    source_of, taker = mixed[0:count // 2 * 2:2], mixed[1:count // 2 * 2:2]
    margin = jnp.minimum(tallies[source_of] - 1, limit - tallies[taker]) // 2
    margin = jnp.where((source_of == order[0]) | (taker == order[0]) | (tallies[taker] == 0), 0, jnp.maximum(margin, 0))
    shifted = jax.random.randint(jax.random.fold_in(own, 4), (count // 2,), 0, 1 << 20) % (margin + 1)
    tallies = tallies.at[source_of].add(-shifted).at[taker].add(shifted)
    labels = jnp.searchsorted(jnp.cumsum(tallies), jnp.arange(rows * top), side="right").astype(jnp.int32)
    table = labels.reshape(top, rows).T
    table = table[jax.random.permutation(jax.random.fold_in(own, 1), rows)]
    turn = jax.random.randint(jax.random.fold_in(own, 2), (rows, 1), 0, top)
    return jnp.take_along_axis(table, (jnp.arange(top)[None, :] + turn) % top, axis=1)


def load_shares(amount, total, limit, lean, full):
    weights = [(1 << 20) // math.isqrt(rank ** lean) + 1 for rank in range(1, amount + 1)]
    largest = limit if full else min(limit, max(-(-total // amount), total * weights[0] // sum(weights)))
    least = 1 if total - largest >= amount - 1 else 0
    given, surplus = [largest] + [least] * (amount - 1), total - largest - least * (amount - 1)
    while surplus > 0:
        candidates = [i for i in range(1, amount) if given[i] < largest] or [i for i in range(1, amount) if given[i] < limit]
        pool, remaining = sum([weights[i] for i in candidates]), surplus
        for i in candidates:
            extra = min(limit - given[i], max(1, remaining * weights[i] // pool), surplus)
            given[i] = given[i] + extra
            surplus = surplus - extra
    return np.array(given)


def centred(key, extent, spread, reach, cuts=(), kind=jnp.bfloat16):
    loudness = steps_of(key, extent, cuts, -0.22, 0.18) if cuts else 1.0
    values = jax.random.normal(key, extent, jnp.float32) * spread * loudness
    return jnp.minimum(jnp.maximum(values, -reach), reach).astype(kind)


def setup_inputs(seed: int = 0) -> dict:
    key_of = jax.random.split(jax.random.key(seed), 12)
    queries = draw_queries(jax.random.fold_in(key_of[11], 71), 0)
    keys = draw_keys(jax.random.fold_in(key_of[11], 71), 0)
    values = centred(key_of[2], (SEQUENCE_COUNT, SEQUENCE_LENGTH, KEY_VALUE_HEADS * HEAD_SIZE), 1.0, 6.0, ((0, 16), (1, 2)))
    resid = centred(key_of[3], (SEQUENCE_COUNT, SEQUENCE_LENGTH, D), 1.0, 6.0, ((0, 16), (1, 2)))
    block_order = jax.random.permutation(key_of[4], 8 * N_CTX).astype(jnp.int32)
    norm_gain = jnp.clip(1.0 + 0.18 * jax.random.normal(key_of[5], (D,), jnp.float32), 0.1, 1.9)
    w_gate = centred(key_of[6], (EXPERTS, D, FFE), D ** -0.5, 0.125, ((0, 4),))
    w_down = centred(key_of[7], (EXPERTS, FFE, D), FFE ** -0.5, 0.3125, ((0, 4),))
    routes_keys = jax.random.split(jax.random.fold_in(key_of[8], 1), SEQUENCE_COUNT * SEQUENCE_LENGTH // TOK)
    routes_turns = jax.random.permutation(jax.random.fold_in(key_of[8], 3), SEQUENCE_COUNT * SEQUENCE_LENGTH // TOK)
    routes = jax.vmap(lambda own, number: routed_block(jax.random.fold_in(key_of[8], 2), own, number, TOK, EXPERTS, 1, CAP, 2))(routes_keys, routes_turns).reshape((SEQUENCE_COUNT, SEQUENCE_LENGTH, 1))
    route_weight = jnp.clip(0.2 + 0.8 * jax.random.uniform(key_of[9], (SEQUENCE_COUNT, SEQUENCE_LENGTH), jnp.float32) ** steps_of(key_of[9], (SEQUENCE_COUNT, SEQUENCE_LENGTH), ((0, 16), (1, 2)), -0.2, 0.2), 0.2, 1.0)
    d_out = centred(key_of[10], (SEQUENCE_COUNT, SEQUENCE_LENGTH, D), 1.0, 6.0, ((0, 16), (1, 2)))
    return dict(queries=queries, keys=keys, values=values, resid=resid, block_order=block_order, norm_gain=norm_gain, w_gate=w_gate, w_down=w_down, routes=routes, route_weight=route_weight, d_out=d_out)


def rounded(value):
    return lax.optimization_barrier(value.astype(jnp.bfloat16))

def group_scores(q_group, k_head, allowed):
    scores = jnp.einsum('tgd,kd->gtk', q_group.astype(jnp.float32), k_head.astype(jnp.float32)) * HEAD_SIZE ** (-0.5)
    scores = jnp.where(allowed[None], scores, -1e+30)
    peak_score = lax.optimization_barrier(jnp.max(scores, axis=2, keepdims=True))
    exponent = jnp.exp(scores - peak_score)
    return exponent / lax.optimization_barrier(jnp.sum(exponent, axis=2, keepdims=True))

def attention_forward(query_rows, key_rows, value_rows, allowed):
    group_count = QUERY_HEADS // KEY_VALUE_HEADS
    length = query_rows.shape[0]
    pieces = []
    for query_group in range(KEY_VALUE_HEADS):
        q_group = query_rows[:, query_group * group_count * HEAD_SIZE:(query_group + 1) * group_count * HEAD_SIZE].reshape(length, group_count, HEAD_SIZE)
        k_head = key_rows[:, query_group * HEAD_SIZE:(query_group + 1) * HEAD_SIZE]
        v_head = value_rows[:, query_group * HEAD_SIZE:(query_group + 1) * HEAD_SIZE]
        probability = group_scores(q_group, k_head, allowed)
        prob_low = rounded(probability).astype(jnp.float32)
        pieces.append(jnp.einsum('gtk,kd->tgd', prob_low, v_head.astype(jnp.float32)).reshape(length, group_count * HEAD_SIZE))
    return jnp.concatenate(pieces, axis=1)

def attention_backward(query_rows, key_rows, value_rows, allowed, d_hidden):
    group_count = QUERY_HEADS // KEY_VALUE_HEADS
    length = query_rows.shape[0]
    dq_parts = []
    dk_parts = []
    dv_parts = []
    for query_group in range(KEY_VALUE_HEADS):
        q_group = query_rows[:, query_group * group_count * HEAD_SIZE:(query_group + 1) * group_count * HEAD_SIZE].reshape(length, group_count, HEAD_SIZE)
        k_head = key_rows[:, query_group * HEAD_SIZE:(query_group + 1) * HEAD_SIZE]
        v_head = value_rows[:, query_group * HEAD_SIZE:(query_group + 1) * HEAD_SIZE]
        probability = group_scores(q_group, k_head, allowed)
        prob_low = rounded(probability).astype(jnp.float32)
        attn_group = jnp.einsum('gtk,kd->tgd', prob_low, v_head.astype(jnp.float32))
        grad_group = d_hidden[:, query_group * group_count * HEAD_SIZE:(query_group + 1) * group_count * HEAD_SIZE].reshape(length, group_count, HEAD_SIZE).astype(jnp.float32)
        d_prob = jnp.einsum('tgd,kd->gtk', grad_group, v_head.astype(jnp.float32))
        row_dot = jnp.transpose(lax.optimization_barrier(jnp.sum(grad_group * attn_group, axis=2)))[:, :, None]
        d_score = rounded(probability * (d_prob - row_dot)).astype(jnp.float32)
        dq_group = jnp.einsum('gtk,kd->tgd', d_score, k_head.astype(jnp.float32)) * HEAD_SIZE ** (-0.5)
        dq_parts.append(dq_group.reshape(length, group_count * HEAD_SIZE).astype(jnp.bfloat16))
        dk_parts.append(jnp.einsum('gtk,tgd->kd', d_score, q_group.astype(jnp.float32)) * HEAD_SIZE ** (-0.5))
        dv_parts.append(jnp.einsum('gtk,tgd->kd', prob_low, grad_group))
    return (jnp.concatenate(dq_parts, axis=1), jnp.concatenate(dk_parts, axis=1), jnp.concatenate(dv_parts, axis=1))

def expert_forward(rows_x, gate_mat, down_mat):
    pre_act = jnp.dot(rows_x, gate_mat, preferred_element_type=jnp.float32)
    activity = jax.nn.silu(pre_act).astype(jnp.bfloat16)
    return (pre_act, jnp.dot(activity, down_mat, preferred_element_type=jnp.float32).astype(jnp.bfloat16))

def expert_backward(pre_act, rows_grad, gate_mat, down_mat):
    d_act = lax.dot_general(rows_grad, down_mat, (((1,), (1,)), ((), ())), preferred_element_type=jnp.float32)
    sigmoid_pre = jax.nn.sigmoid(pre_act)
    d_pre = (d_act * sigmoid_pre * (1.0 + pre_act * (1.0 - sigmoid_pre))).astype(jnp.bfloat16)
    return lax.dot_general(d_pre, gate_mat, (((1,), (1,)), ((), ())), preferred_element_type=jnp.float32).astype(jnp.bfloat16)

def pick_rows(block_rows, row_ids):
    return block_rows[row_ids]

def reference(queries, keys, values, resid, block_order, norm_gain, w_gate, w_down, routes, route_weight, d_out):
    seqs = queries.shape[0]
    length = queries.shape[1]
    span_rows = TOK // 8
    row_index = jnp.arange(length, dtype=jnp.int32)
    position = block_order[row_index // span_rows] * span_rows + row_index % span_rows
    allowed = position[None, :] <= position[:, None]

    def forward_one(items):
        query_rows, key_rows, value_rows, resid_rows, grad_rows, weight_rows = items
        attended = attention_forward(query_rows, key_rows, value_rows, allowed)
        hidden = rounded(resid_rows.astype(jnp.float32) + attended)
        hidden_wide = hidden.astype(jnp.float32)
        inv_rms = lax.rsqrt(lax.optimization_barrier(jnp.mean(hidden_wide * hidden_wide, axis=1, keepdims=True)) + 1e-06)
        normed = rounded(hidden_wide * inv_rms * norm_gain[None, :])
        scaled_grad = rounded(weight_rows[:, None] * grad_rows.astype(jnp.float32))
        return (hidden, normed, scaled_grad)
    hidden, normed, scaled_grad = lax.map(forward_one, (queries, keys, values, resid, d_out, route_weight))
    blocks = seqs * N_CTX
    normed_blocks = normed.reshape(blocks, TOK, D)
    grad_blocks = scaled_grad.reshape(blocks, TOK, D)
    chosen = routes.reshape(blocks, TOK)
    hits = (chosen[:, :, None] == jnp.arange(EXPERTS, dtype=jnp.int32)[None, None, :]).astype(jnp.int32)
    slot_rank = lax.optimization_barrier(jnp.sum(hits * (jnp.cumsum(hits, axis=1) - hits), axis=2))
    slot_of = chosen * CAP + slot_rank
    token_ids = jnp.arange(TOK, dtype=jnp.int32)

    def one_expert(expert):
        wanted = expert * CAP + jnp.arange(CAP, dtype=jnp.int32)
        match = slot_of[:, None, :] == wanted[None, :, None]
        source = lax.optimization_barrier(jnp.sum(jnp.where(match, token_ids[None, None, :], 0), axis=2)).astype(jnp.int32)
        live = jnp.any(match, axis=2)[:, :, None]
        rows_x = jnp.where(live, jax.vmap(pick_rows)(normed_blocks, source), jnp.zeros((), jnp.bfloat16))
        rows_grad = jnp.where(live, jax.vmap(pick_rows)(grad_blocks, source), jnp.zeros((), jnp.bfloat16))
        pre_act, result = expert_forward(rows_x.reshape(-1, D), w_gate[expert], w_down[expert])
        back = expert_backward(pre_act, rows_grad.reshape(-1, D), w_gate[expert], w_down[expert])
        return (result.reshape(blocks, CAP, D), back.reshape(blocks, CAP, D))
    y_all, dn_all = lax.map(one_expert, jnp.arange(EXPERTS, dtype=jnp.int32))
    block_index = jnp.arange(blocks, dtype=jnp.int32)[:, None]
    y_tok = y_all[chosen, block_index, slot_rank].reshape(seqs, length, D)
    dn_tok = dn_all[chosen, block_index, slot_rank].reshape(seqs, length, D)

    def backward_one(items):
        query_rows, key_rows, value_rows, hidden_rows, y_rows, dn_rows, grad_rows, weight_rows = items
        hidden_wide = hidden_rows.astype(jnp.float32)
        inv_rms = lax.rsqrt(lax.optimization_barrier(jnp.mean(hidden_wide * hidden_wide, axis=1, keepdims=True)) + 1e-06)
        y_wide = y_rows.astype(jnp.float32)
        dn_wide = dn_rows.astype(jnp.float32)
        grad_wide = grad_rows.astype(jnp.float32)
        layer_out = (hidden_wide + weight_rows[:, None] * y_wide).astype(jnp.bfloat16)
        d_weight = lax.optimization_barrier(jnp.sum(y_wide * grad_wide, axis=1))
        gained = norm_gain[None, :] * dn_wide
        mixing = lax.optimization_barrier(jnp.mean(gained * hidden_wide, axis=1, keepdims=True))
        d_hidden = rounded(grad_wide + inv_rms * gained - hidden_wide * inv_rms ** 3 * mixing)
        gain_part = lax.optimization_barrier(jnp.sum(dn_wide * hidden_wide * inv_rms, axis=0))
        d_queries, key_grad, value_grad = attention_backward(query_rows, key_rows, value_rows, allowed, d_hidden)
        return (layer_out, d_hidden, d_queries, key_grad.astype(jnp.bfloat16), value_grad.astype(jnp.bfloat16), d_weight, gain_part)
    results = lax.map(backward_one, (queries, keys, values, hidden, y_tok, dn_tok, d_out, route_weight))
    d_gain = lax.optimization_barrier(jnp.sum(results[6], axis=0)) / (seqs * length)
    return (results[0], results[1], results[2], results[3], results[4], results[5], d_gain)
```

```python
import functools

import jax
import jax.numpy as jnp
from jax import lax
from jax.experimental import pallas as pl
from jax.experimental.pallas import tpu as pltpu
from jax.sharding import PartitionSpec as P

D = 2048
HEAD_SIZE = 128
QUERY_HEADS = 16
KEY_VALUE_HEADS = 2
GROUP = QUERY_HEADS // KEY_VALUE_HEADS
FFE = 384
EXP_DEV = 2
COLS = 256
SCALE = HEAD_SIZE ** (-0.5)
EXP2_SCALE = SCALE * 1.4426950408889634
F32 = jnp.float32
BF16 = jnp.bfloat16
NN = (((1,), (0,)), ((), ()))
NT = (((1,), (1,)), ((), ()))
MIB = 1 << 20


def mm(a, b, dims=NN):
    return lax.dot_general(a, b, dims, preferred_element_type=F32)


def iota(shape, dim):
    return lax.broadcasted_iota(jnp.int32, shape, dim)


def row_to_col(row):
    n = row.shape[1]
    eye = iota((n, n), 0) == iota((n, n), 1)
    return jnp.sum(jnp.where(eye, row, jnp.zeros((), row.dtype)), axis=1, keepdims=True)


def col_to_row(col):
    n = col.shape[0]
    eye = iota((n, n), 0) == iota((n, n), 1)
    return jnp.sum(jnp.where(eye, col, jnp.zeros((), col.dtype)), axis=0, keepdims=True)


def block_positions(order_ref, ctx_index, shape, dim):
    span = shape[dim] // 8
    index = iota(shape, dim)
    which = index // span
    start = jnp.zeros(shape, jnp.int32)
    for b in range(8):
        start = jnp.where(which == b, order_ref[ctx_index * 8 + b], start)
    return start * span + index % span


def stacked(refs, cols=slice(None)):
    parts = [r[:, cols] for r in refs]
    return parts[0] if len(parts) == 1 else jnp.concatenate(parts, axis=0)


def column_blocks(width=D, step=COLS):
    return [slice(c, c + step) for c in range(0, width, step)]


def store_pieces(refs, cols, rows_value):
    at = 0
    for r in refs:
        n = r.shape[0]
        r[:, cols] = rows_value[at : at + n]
        at += n


def placement_rows(slot_row, slots):
    tokens = slot_row.shape[1]
    return jnp.where(iota((slots, tokens), 0) == slot_row, 1.0, 0.0).astype(BF16)


def placement_cols(slot_row, slots):
    tokens = slot_row.shape[1]
    slot_col = row_to_col(slot_row)
    return jnp.where(iota((tokens, slots), 1) == slot_col, 1.0, 0.0).astype(BF16)


def dispatch_kernel(experts, capacity, routes_ref, weight_ref, grad_ref, slot_ref, *send_refs):
    tokens = routes_ref.shape[1]
    chosen = routes_ref[...]
    lanes = max(experts, 16)
    hits = jnp.where(iota((lanes, tokens), 0) == chosen, 1.0, 0.0)
    before = jnp.where(iota((tokens, tokens), 0) < iota((tokens, tokens), 1), 1.0, 0.0)
    earlier = mm(hits.astype(BF16), before.astype(BF16))
    rank = jnp.sum(hits * earlier, axis=0, keepdims=True).astype(jnp.int32)
    target = (chosen // EXP_DEV) ^ lax.axis_index("exp")
    slot = (target * EXP_DEV + chosen % EXP_DEV) * capacity + rank
    slot_ref[...] = slot
    place = placement_rows(slot, experts * capacity)
    weight = row_to_col(weight_ref[...])
    for cols in column_blocks():
        scaled = (weight * grad_ref[:, cols].astype(F32)).astype(BF16)
        store_pieces(send_refs, cols, mm(place, scaled).astype(BF16))


def attention_kernel(count, pieces, order_ref, slot_ref, gain_ref, query_ref, resid_ref, *refs):
    kv_refs = refs[:count]
    hidden_ref = refs[count]
    send_refs = refs[count + 1 : count + 1 + pieces]
    tokens = query_ref.shape[0]
    me = lax.axis_index("ctx")
    query_pos = block_positions(order_ref, me, (tokens, 1), 0)
    bias = jnp.concatenate(
        [
            jnp.where(block_positions(order_ref, me ^ s, (1, tokens), 1) <= query_pos, 0.0, -1e30)
            for s in range(count)
        ],
        axis=1,
    )
    length = count * tokens
    ones = jnp.ones((length, HEAD_SIZE), BF16)
    total = jnp.zeros((tokens, HEAD_SIZE), F32)
    for g in range(KEY_VALUE_HEADS):
        k_cols = slice(g * HEAD_SIZE, (g + 1) * HEAD_SIZE)
        v_cols = slice((KEY_VALUE_HEADS + g) * HEAD_SIZE, (KEY_VALUE_HEADS + g + 1) * HEAD_SIZE)
        keys = stacked(kv_refs, k_cols)
        values = jnp.concatenate([stacked(kv_refs, v_cols), ones], axis=1)
        for h in range(g * GROUP, (g + 1) * GROUP):
            cols = slice(h * HEAD_SIZE, (h + 1) * HEAD_SIZE)
            scores = mm(query_ref[:, cols], keys, NT) + bias
            peak = jnp.max(scores, axis=1, keepdims=True)
            weights = jnp.exp2((scores - peak) * EXP2_SCALE).astype(BF16)
            mixed = mm(weights, values)
            attended = mixed[:, :HEAD_SIZE] / mixed[:, HEAD_SIZE:]
            hidden = (resid_ref[:, cols].astype(F32) + attended).astype(BF16)
            hidden_ref[:, cols] = hidden
            wide = hidden.astype(F32)
            total = total + wide * wide
    inv_rms = lax.rsqrt(jnp.sum(total, axis=1, keepdims=True) * (1.0 / D) + 1e-06)
    slots = sum(r.shape[0] for r in send_refs)
    place = placement_rows(slot_ref[...], slots)
    for cols in column_blocks():
        normed = (hidden_ref[:, cols].astype(F32) * inv_rms * gain_ref[:, cols]).astype(BF16)
        store_pieces(send_refs, cols, mm(place, normed).astype(BF16))


def first_expert_rows(slots, capacity):
    return iota((slots, 1), 0) % (EXP_DEV * capacity) < capacity


def expert_grad_kernel(capacity, pieces, down_ref, *refs):
    grads = stacked(refs[:pieces])
    out_ref = refs[pieces]
    first = first_expert_rows(grads.shape[0], capacity)
    out_ref[...] = jnp.where(first, mm(grads, down_ref[0], NT), mm(grads, down_ref[1], NT))


def expert_back_kernel(capacity, pieces, gate_ref, d_act_ref, *refs):
    rows = stacked(refs[:pieces])
    act_ref = refs[pieces]
    out_refs = refs[pieces + 1 :]
    first = first_expert_rows(rows.shape[0], capacity)
    pre = jnp.where(first, mm(rows, gate_ref[0]), mm(rows, gate_ref[1]))
    gate = 1.0 / (1.0 + jnp.exp(-pre))
    act = pre * gate
    act_ref[:, :FFE] = jnp.where(first, act, 0.0).astype(BF16)
    act_ref[:, FFE:] = jnp.where(first, 0.0, act).astype(BF16)
    d_pre = d_act_ref[...] * gate * (1.0 + pre * (1.0 - gate))
    d_first = jnp.where(first, d_pre, 0.0).astype(BF16)
    d_second = jnp.where(first, 0.0, d_pre).astype(BF16)
    for cols in column_blocks():
        back = mm(d_first, gate_ref[0, cols, :], NT) + mm(d_second, gate_ref[1, cols, :], NT)
        store_pieces(out_refs, cols, back.astype(BF16))


def expert_out_kernel(down_ref, act_ref, *out_refs):
    act = act_ref[...]
    for cols in column_blocks():
        y = mm(act[:, :FFE], down_ref[0, :, cols]) + mm(act[:, FFE:], down_ref[1, :, cols])
        store_pieces(out_refs, cols, y.astype(BF16))


def residual_kernel(pieces, slot_ref, gain_ref, hidden_ref, grad_ref, *refs):
    dn_refs = refs[:pieces]
    resid_ref, gain_out_ref, dn_scratch = refs[pieces:]
    tokens = hidden_ref.shape[0]
    slots = sum(r.shape[0] for r in dn_refs)
    place = placement_cols(slot_ref[...], slots)
    square = jnp.zeros((tokens, COLS), F32)
    mixing = jnp.zeros((tokens, COLS), F32)
    for cols in column_blocks():
        dn = mm(place, stacked(dn_refs, cols))
        dn_scratch[:, cols] = dn
        hidden = hidden_ref[:, cols].astype(F32)
        square = square + hidden * hidden
        mixing = mixing + dn * gain_ref[:, cols] * hidden
    inv_rms = lax.rsqrt(jnp.sum(square, axis=1, keepdims=True) * (1.0 / D) + 1e-06)
    mean_mix = jnp.sum(mixing, axis=1, keepdims=True) * (1.0 / D)
    factor = inv_rms * inv_rms * inv_rms * mean_mix
    for cols in column_blocks():
        dn = dn_scratch[:, cols] * inv_rms
        hidden = hidden_ref[:, cols].astype(F32)
        resid_ref[:, cols] = (
            grad_ref[:, cols].astype(F32) + dn * gain_ref[:, cols] - hidden * factor
        ).astype(BF16)
        gain_out_ref[:, cols] = jnp.sum(dn * hidden, axis=0, keepdims=True)


def attention_back_kernel(count, order_ref, query_ref, d_resid_ref, *refs):
    kv_refs = refs[:count]
    dq_ref, own_ref = refs[count : count + 2]
    other_refs = refs[count + 2 :]
    tokens = query_ref.shape[0]
    me = lax.axis_index("ctx")
    query_pos = block_positions(order_ref, me, (1, tokens), 1)
    bias = jnp.concatenate(
        [
            jnp.where(block_positions(order_ref, me ^ s, (tokens, 1), 0) <= query_pos, 0.0, -1e30)
            for s in range(count)
        ],
        axis=0,
    )
    pair_bias = jnp.concatenate([bias, bias], axis=1)
    length = count * tokens
    for g in range(KEY_VALUE_HEADS):
        k_cols = slice(g * HEAD_SIZE, (g + 1) * HEAD_SIZE)
        v_cols = slice((KEY_VALUE_HEADS + g) * HEAD_SIZE, (KEY_VALUE_HEADS + g + 1) * HEAD_SIZE)
        keys = stacked(kv_refs, k_cols)
        values = stacked(kv_refs, v_cols)
        keys_t = jnp.transpose(keys.astype(F32)).astype(BF16)
        d_keys = jnp.zeros((length, HEAD_SIZE), F32)
        d_values = jnp.zeros((length, HEAD_SIZE), F32)
        for h in range(g * GROUP, (g + 1) * GROUP, 2):
            cols_a = slice(h * HEAD_SIZE, (h + 1) * HEAD_SIZE)
            cols_b = slice((h + 1) * HEAD_SIZE, (h + 2) * HEAD_SIZE)
            queries = jnp.concatenate([query_ref[:, cols_a], query_ref[:, cols_b]], axis=0)
            d_out = jnp.concatenate([d_resid_ref[:, cols_a], d_resid_ref[:, cols_b]], axis=0)
            scores = mm(keys, queries, NT) + pair_bias
            peak = jnp.max(scores, axis=0, keepdims=True)
            weights = jnp.exp2((scores - peak) * EXP2_SCALE)
            probs = weights * (1.0 / jnp.sum(weights, axis=0, keepdims=True))
            probs_low = probs.astype(BF16)
            d_probs = mm(values, d_out, NT)
            row_dot = jnp.sum(probs * d_probs, axis=0, keepdims=True)
            d_scores = (probs * (d_probs - row_dot)).astype(BF16)
            d_keys = d_keys + mm(d_scores, queries)
            d_values = d_values + mm(probs_low, d_out)
            d_query_t = mm(keys_t, d_scores) * SCALE
            dq_ref[:, cols_a] = jnp.transpose(d_query_t[:, :tokens]).astype(BF16)
            dq_ref[:, cols_b] = jnp.transpose(d_query_t[:, tokens:]).astype(BF16)
        d_keys = d_keys * SCALE
        own_ref[:, k_cols] = d_keys[:tokens]
        own_ref[:, v_cols] = d_values[:tokens]
        for s, ref in enumerate(other_refs, 1):
            ref[:, k_cols] = d_keys[s * tokens : (s + 1) * tokens].astype(BF16)
            ref[:, v_cols] = d_values[s * tokens : (s + 1) * tokens].astype(BF16)


def output_kernel(pieces, slot_ref, weight_ref, hidden_ref, grad_ref, *refs):
    y_refs = refs[:pieces]
    out_ref, d_weight_ref = refs[pieces:]
    tokens = hidden_ref.shape[0]
    slots = sum(r.shape[0] for r in y_refs)
    place = placement_cols(slot_ref[...], slots)
    weight = row_to_col(weight_ref[...])
    total = jnp.zeros((tokens, COLS), F32)
    for cols in column_blocks():
        y = mm(place, stacked(y_refs, cols))
        out_ref[:, cols] = (hidden_ref[:, cols].astype(F32) + weight * y).astype(BF16)
        total = total + y * grad_ref[:, cols].astype(F32)
    d_weight_ref[...] = col_to_row(jnp.sum(total, axis=1, keepdims=True))


def run(kernel, name, inputs, outputs, flops, smem=0, scratch=(), limit=20 * MIB):
    nbytes = sum(x.size * x.dtype.itemsize for x in inputs) + sum(
        x.size * x.dtype.itemsize for x in outputs
    )
    vmem = pl.BlockSpec(memory_space=pltpu.VMEM)
    scalar = pl.BlockSpec(memory_space=pltpu.SMEM)
    return pl.pallas_call(
        kernel,
        out_shape=list(outputs),
        in_specs=[scalar] * smem + [vmem] * (len(inputs) - smem),
        out_specs=[vmem] * len(outputs),
        scratch_shapes=list(scratch),
        compiler_params=pltpu.CompilerParams(vmem_limit_bytes=limit),
        cost_estimate=pl.CostEstimate(flops=flops, bytes_accessed=nbytes, transcendentals=0),
        name=name,
    )(*inputs)


def pairwise(value, axis, step):
    count = lax.axis_size(axis)
    return lax.ppermute(value, axis, [(i, i ^ step) for i in range(count)])


def exchange(pieces, capacity):
    count = lax.axis_size("exp")
    rows = EXP_DEV * capacity
    if len(pieces) == count:
        return [pieces[0]] + [pairwise(pieces[s], "exp", s) for s in range(1, count)]
    flat = pieces[0]
    blocks = [flat[s * rows : (s + 1) * rows] for s in range(count)]
    moved = [blocks[0]] + [pairwise(blocks[s], "exp", s) for s in range(1, count)]
    return [jnp.concatenate(moved, axis=0)]


def sum_over(value, axis):
    parts = [value] + [pairwise(value, axis, s) for s in range(1, lax.axis_size(axis))]
    while len(parts) > 1:
        parts = [parts[i] + parts[i + 1] for i in range(0, len(parts), 2)]
    return parts[0]


def shaped(shape, dtype):
    return jax.ShapeDtypeStruct(shape, dtype)


def per_device(
    queries,
    keys,
    values,
    resid,
    block_order,
    norm_gain,
    w_gate,
    w_down,
    routes,
    route_weight,
    d_out,
):
    query_rows = queries[0]
    resid_rows = resid[0]
    grad_rows = d_out[0]
    tokens = query_rows.shape[0]
    chosen = routes.reshape(1, tokens)
    gain = norm_gain.reshape(1, D)
    ctx_count = lax.axis_size("ctx")
    exp_count = lax.axis_size("exp")
    experts = EXP_DEV * exp_count
    capacity = 3 * tokens // (2 * experts)
    slots = experts * capacity
    rows = EXP_DEV * capacity
    piece_count = exp_count if rows % 16 == 0 else 1
    piece_shapes = [shaped((slots // piece_count, D), BF16)] * piece_count
    token_shape = shaped((tokens, D), BF16)
    kv_width = 2 * KEY_VALUE_HEADS * HEAD_SIZE
    attn_flops = 4 * tokens * ctx_count * tokens * QUERY_HEADS * HEAD_SIZE
    place_flops = 2 * slots * tokens * D
    expert_flops = 2 * slots * D * FFE * EXP_DEV

    own_kv = jnp.concatenate([keys[0], values[0]], axis=1)
    kv = [own_kv] + [pairwise(own_kv, "ctx", s) for s in range(1, ctx_count)]

    slot, *send_grad = run(
        functools.partial(dispatch_kernel, experts, capacity),
        "dispatch_grads",
        [chosen, route_weight, grad_rows],
        [shaped((1, tokens), jnp.int32)] + piece_shapes,
        place_flops,
    )
    arrived_grad = exchange(send_grad, capacity)

    hidden, *send_x = run(
        functools.partial(attention_kernel, ctx_count, piece_count),
        "attention_forward",
        [block_order, slot, gain, query_rows, resid_rows] + kv,
        [token_shape] + piece_shapes,
        attn_flops + place_flops,
        smem=1,
    )
    arrived_x = exchange(send_x, capacity)

    (d_act,) = run(
        functools.partial(expert_grad_kernel, capacity, piece_count),
        "expert_act_grad",
        [w_down] + arrived_grad,
        [shaped((slots, FFE), F32)],
        expert_flops,
    )
    act, *send_dn = run(
        functools.partial(expert_back_kernel, capacity, piece_count),
        "expert_backward",
        [w_gate, d_act] + arrived_x,
        [shaped((slots, EXP_DEV * FFE), BF16)] + piece_shapes,
        2 * expert_flops,
    )
    dn = exchange(send_dn, capacity)
    send_y = run(
        expert_out_kernel, "expert_output", [w_down, act], piece_shapes, expert_flops
    )
    returned = exchange(send_y, capacity)

    d_hidden, gain_local = run(
        functools.partial(residual_kernel, piece_count),
        "residual_grad",
        [slot, gain, hidden, grad_rows] + dn,
        [token_shape, shaped((1, D), F32)],
        place_flops,
        scratch=[pltpu.VMEM((tokens, D), F32)],
    )
    gain_total = gain_local
    for axis in ("dp", "exp", "ctx"):
        gain_total = sum_over(gain_total, axis)
    total_tokens = tokens * ctx_count * exp_count * lax.axis_size("dp")
    d_gain = gain_total[0] / total_tokens

    d_queries, kv_own, *kv_send = run(
        functools.partial(attention_back_kernel, ctx_count),
        "attention_backward",
        [block_order, query_rows, d_hidden] + kv,
        [token_shape, shaped((tokens, kv_width), F32)]
        + [shaped((tokens, kv_width), BF16)] * (ctx_count - 1),
        5 * attn_flops // 2,
        smem=1,
    )
    kv_grad = kv_own
    for s, part in enumerate(kv_send, 1):
        kv_grad = kv_grad + pairwise(part, "ctx", s).astype(F32)
    kv_grad = kv_grad.astype(BF16)

    layer_out, d_weight = run(
        functools.partial(output_kernel, piece_count),
        "layer_output",
        [slot, route_weight, hidden, grad_rows] + returned,
        [token_shape, shaped((1, tokens), F32)],
        place_flops,
    )
    split = KEY_VALUE_HEADS * HEAD_SIZE
    return (
        layer_out[None],
        d_hidden[None],
        d_queries[None],
        kv_grad[:, :split][None],
        kv_grad[:, split:][None],
        d_weight,
        d_gain,
    )


def solution(mesh):
    in_specs = (
        P(("exp", "dp"), "ctx", None),
        P(("exp", "dp"), "ctx", None),
        P(("exp", "dp"), "ctx", None),
        P(("exp", "dp"), "ctx", None),
        P(),
        P(),
        P("exp", None, None),
        P("exp", None, None),
        P(("exp", "dp"), "ctx", None),
        P(("exp", "dp"), "ctx"),
        P(("exp", "dp"), "ctx", None),
    )
    out_specs = (
        P(("exp", "dp"), "ctx", None),
        P(("exp", "dp"), "ctx", None),
        P(("exp", "dp"), "ctx", None),
        P(("exp", "dp"), "ctx", None),
        P(("exp", "dp"), "ctx", None),
        P(("exp", "dp"), "ctx"),
        P(),
    )
    return jax.shard_map(
        per_device, mesh=mesh, in_specs=in_specs, out_specs=out_specs, check_vma=False
    )
```

```python
import functools

import jax
import jax.numpy as jnp
from jax import lax
from jax.experimental import pallas as pl
from jax.experimental.pallas import tpu as pltpu
from jax.sharding import PartitionSpec as P

D = 2048
HEAD_SIZE = 128
QUERY_HEADS = 16
KEY_VALUE_HEADS = 2
GROUP = QUERY_HEADS // KEY_VALUE_HEADS
FFE = 384
EXP_DEV = 2
COLS = 256
SCALE = HEAD_SIZE ** (-0.5)
EXP2_SCALE = SCALE * 1.4426950408889634
F32 = jnp.float32
BF16 = jnp.bfloat16
NN = (((1,), (0,)), ((), ()))
NT = (((1,), (1,)), ((), ()))
MIB = 1 << 20
VMEM, HBM = pltpu.VMEM, pltpu.HBM


def mm(a, b, dims=NN):
    return lax.dot_general(a, b, dims, preferred_element_type=F32)


def iota(shape, dim):
    return lax.broadcasted_iota(jnp.int32, shape, dim)


def row_to_col(row):
    n = row.shape[1]
    eye = iota((n, n), 0) == iota((n, n), 1)
    return jnp.sum(jnp.where(eye, row, jnp.zeros((), row.dtype)), axis=1, keepdims=True)


def col_to_row(col):
    n = col.shape[0]
    eye = iota((n, n), 0) == iota((n, n), 1)
    return jnp.sum(jnp.where(eye, col, jnp.zeros((), col.dtype)), axis=0, keepdims=True)


def block_positions(order_ref, ctx_index, tokens):
    span = tokens // 8
    index = iota((1, tokens), 1)
    which = index // span
    start = jnp.zeros((1, tokens), jnp.int32)
    for b in range(8):
        start = jnp.where(which == b, order_ref[ctx_index * 8 + b], start)
    return start * span + index % span


def stacked(refs, cols=slice(None)):
    parts = [r[:, cols] for r in refs]
    return parts[0] if len(parts) == 1 else jnp.concatenate(parts, axis=0)


def column_blocks(width=D, step=COLS):
    return [slice(c, c + step) for c in range(0, width, step)]


def store_pieces(refs, cols, rows_value):
    at = 0
    for r in refs:
        n = r.shape[0]
        r[:, cols] = rows_value[at : at + n]
        at += n


def pair_cols(pair):
    start = 2 * pair * HEAD_SIZE
    return slice(start, start + HEAD_SIZE), slice(start + HEAD_SIZE, start + 2 * HEAD_SIZE)


def head_pair(ref, pair):
    first, second = pair_cols(pair)
    return jnp.concatenate([ref[:, first], ref[:, second]], axis=0)


def placement_rows(slot_row, slots):
    tokens = slot_row.shape[1]
    return jnp.where(iota((slots, tokens), 0) == slot_row, 1.0, 0.0).astype(BF16)


def placement_cols(slot_row, slots):
    tokens = slot_row.shape[1]
    slot_col = row_to_col(slot_row)
    return jnp.where(iota((tokens, slots), 1) == slot_col, 1.0, 0.0).astype(BF16)


def dispatch_kernel(count, experts, capacity, *refs):
    sources, refs = refs[:9], refs[9:]
    targets, refs = refs[:6], refs[6:]
    grad_ref = targets[0]
    slot_ref, pos_ref, weight_ref = refs[:3]
    send_refs = refs[3:-3]
    order_ref, routes_ref, sems = refs[-3:]
    targets = targets + (weight_ref, routes_ref, order_ref)
    copies = [
        pltpu.make_async_copy(source, target, sems.at[i])
        for i, (source, target) in enumerate(zip(sources, targets))
    ]
    for copy in copies[::-1]:
        copy.start()
    for copy in copies[:5:-1]:
        copy.wait()
    tokens = routes_ref.shape[1]
    chosen = routes_ref[...]
    lanes = max(experts, 16)
    hits = jnp.where(iota((lanes, tokens), 0) == chosen, 1.0, 0.0)
    before = jnp.where(iota((tokens, tokens), 0) < iota((tokens, tokens), 1), 1.0, 0.0)
    earlier = mm(hits.astype(BF16), before.astype(BF16))
    rank = jnp.sum(hits * earlier, axis=0, keepdims=True).astype(jnp.int32)
    target = (chosen // EXP_DEV) ^ lax.axis_index("exp")
    slot = (target * EXP_DEV + chosen % EXP_DEV) * capacity + rank
    slot_ref[...] = slot
    me = lax.axis_index("ctx")
    for s in range(count):
        pos_ref[s : s + 1, :] = block_positions(order_ref, me ^ s, tokens)
    place = placement_rows(slot, experts * capacity)
    weight = row_to_col(weight_ref[...])
    copies[0].wait()
    for cols in column_blocks():
        scaled = (weight * grad_ref[:, cols].astype(F32)).astype(BF16)
        store_pieces(send_refs, cols, mm(place, scaled).astype(BF16))
    for copy in copies[1:6]:
        copy.wait()


def kv_stacks(key_refs, value_refs, g):
    cols = slice(g * HEAD_SIZE, (g + 1) * HEAD_SIZE)
    return stacked(key_refs, cols), stacked(value_refs, cols)


def attention_kernel(
    count, pieces, pos_ref, slot_ref, gain_ref, query_ref, resid_ref, down_hbm, *refs
):
    key_refs, value_refs = refs[:count], refs[count : 2 * count]
    hidden_ref, down_ref = refs[2 * count : 2 * count + 2]
    send_refs = refs[2 * count + 2 : -1]
    down_copy = pltpu.make_async_copy(down_hbm, down_ref, refs[-1])
    down_copy.start()
    tokens = query_ref.shape[0]
    query_pos = row_to_col(pos_ref[:1, :])
    bias = jnp.concatenate(
        [jnp.where(pos_ref[s : s + 1, :] <= query_pos, 0.0, -1e30) for s in range(count)],
        axis=1,
    )
    length = count * tokens
    ones = jnp.ones((length, HEAD_SIZE), BF16)
    total = jnp.zeros((tokens, HEAD_SIZE), F32)
    for g in range(KEY_VALUE_HEADS):
        keys, values = kv_stacks(key_refs, value_refs, g)
        values = jnp.concatenate([values, ones], axis=1)
        for h in range(g * GROUP, (g + 1) * GROUP):
            cols = slice(h * HEAD_SIZE, (h + 1) * HEAD_SIZE)
            scores = mm(query_ref[:, cols], keys, NT) + bias
            peak = jnp.max(scores, axis=1, keepdims=True)
            weights = jnp.exp2((scores - peak) * EXP2_SCALE).astype(BF16)
            mixed = mm(weights, values)
            attended = mixed[:, :HEAD_SIZE] / mixed[:, HEAD_SIZE:]
            hidden = (resid_ref[:, cols].astype(F32) + attended).astype(BF16)
            hidden_ref[:, cols] = hidden
            wide = hidden.astype(F32)
            total = total + wide * wide
    inv_rms = lax.rsqrt(jnp.sum(total, axis=1, keepdims=True) * (1.0 / D) + 1e-06)
    slots = sum(r.shape[0] for r in send_refs)
    place = placement_rows(slot_ref[...], slots)
    for cols in column_blocks():
        normed = (hidden_ref[:, cols].astype(F32) * inv_rms * gain_ref[:, cols]).astype(BF16)
        store_pieces(send_refs, cols, mm(place, normed).astype(BF16))
    down_copy.wait()


def first_expert_rows(slots, capacity):
    return iota((slots, 1), 0) % (EXP_DEV * capacity) < capacity


def probs_kernel(count, capacity, pieces, pos_ref, down_ref, gate_hbm, query_ref, *refs):
    key_refs = refs[:count]
    grad_refs = refs[count : count + pieces]
    d_act_ref, probs_ref, gate_ref, sem = refs[count + pieces :]
    gate_copy = pltpu.make_async_copy(gate_hbm, gate_ref, sem)
    gate_copy.start()
    grads = stacked(grad_refs)
    first = first_expert_rows(grads.shape[0], capacity)
    d_act_ref[...] = jnp.where(first, mm(grads, down_ref[0], NT), mm(grads, down_ref[1], NT))
    query_pos = pos_ref[:1, :]
    bias = jnp.concatenate(
        [
            jnp.where(row_to_col(pos_ref[s : s + 1, :]) <= query_pos, 0.0, -1e30)
            for s in range(count)
        ],
        axis=0,
    )
    bias = jnp.concatenate([bias, bias], axis=1)
    for g in range(KEY_VALUE_HEADS):
        keys = stacked(key_refs, slice(g * HEAD_SIZE, (g + 1) * HEAD_SIZE))
        for pair in range(g * GROUP // 2, (g + 1) * GROUP // 2):
            scores = mm(keys, head_pair(query_ref, pair), NT) + bias
            peak = jnp.max(scores, axis=0, keepdims=True)
            weights = jnp.exp2((scores - peak) * EXP2_SCALE)
            probs_ref[pair] = weights * (1.0 / jnp.sum(weights, axis=0, keepdims=True))
    gate_copy.wait()


def expert_back_kernel(capacity, pieces, gate_ref, d_act_ref, *refs):
    rows = stacked(refs[:pieces])
    act_ref = refs[pieces]
    out_refs = refs[pieces + 1 :]
    first = first_expert_rows(rows.shape[0], capacity)
    pre = jnp.where(first, mm(rows, gate_ref[0]), mm(rows, gate_ref[1]))
    gate = 1.0 / (1.0 + jnp.exp(-pre))
    act = pre * gate
    act_ref[:, :FFE] = jnp.where(first, act, 0.0).astype(BF16)
    act_ref[:, FFE:] = jnp.where(first, 0.0, act).astype(BF16)
    d_pre = d_act_ref[...] * gate * (1.0 + pre * (1.0 - gate))
    d_first = jnp.where(first, d_pre, 0.0).astype(BF16)
    d_second = jnp.where(first, 0.0, d_pre).astype(BF16)
    for cols in column_blocks():
        back = mm(d_first, gate_ref[0, cols, :], NT) + mm(d_second, gate_ref[1, cols, :], NT)
        store_pieces(out_refs, cols, back.astype(BF16))


def expert_out_kernel(pieces, down_ref, act_ref, gain_ref, *refs):
    row_refs, dn_refs = refs[:pieces], refs[pieces : 2 * pieces]
    gain_out_ref = refs[2 * pieces]
    out_refs = refs[2 * pieces + 1 :]
    act = act_ref[...]
    for cols in column_blocks():
        y = mm(act[:, :FFE], down_ref[0, :, cols]) + mm(act[:, FFE:], down_ref[1, :, cols])
        store_pieces(out_refs, cols, y.astype(BF16))
        terms = stacked(row_refs, cols).astype(F32) * stacked(dn_refs, cols).astype(F32)
        gain_out_ref[:, cols] = jnp.sum(terms, axis=0, keepdims=True) / gain_ref[:, cols]


def backward_kernel(count, pieces, slot_ref, gain_ref, hidden_ref, grad_ref, query_ref, probs_ref, *refs):
    dn_refs = refs[:pieces]
    key_refs = refs[pieces : pieces + count]
    value_refs = refs[pieces + count : pieces + 2 * count]
    resid_hbm, dq_hbm, own_ref = refs[pieces + 2 * count : pieces + 2 * count + 3]
    other_refs = refs[pieces + 2 * count + 3 : -4]
    resid_ref, dq_ref, dn_scratch, sems = refs[-4:]
    tokens = hidden_ref.shape[0]
    slots = sum(r.shape[0] for r in dn_refs)
    place = placement_cols(slot_ref[...], slots)
    square = jnp.zeros((tokens, COLS), F32)
    mixing = jnp.zeros((tokens, COLS), F32)
    for cols in column_blocks():
        dn = mm(place, stacked(dn_refs, cols)) * gain_ref[:, cols]
        dn_scratch[:, cols] = dn
        hidden = hidden_ref[:, cols].astype(F32)
        square = square + hidden * hidden
        mixing = mixing + dn * hidden
    inv_rms = lax.rsqrt(jnp.sum(square, axis=1, keepdims=True) * (1.0 / D) + 1e-06)
    mean_mix = jnp.sum(mixing, axis=1, keepdims=True) * (1.0 / D)
    factor = inv_rms * inv_rms * inv_rms * mean_mix
    for cols in column_blocks():
        resid_ref[:, cols] = (
            grad_ref[:, cols].astype(F32)
            + dn_scratch[:, cols] * inv_rms
            - hidden_ref[:, cols].astype(F32) * factor
        ).astype(BF16)
    copies = [pltpu.make_async_copy(resid_ref, resid_hbm, sems.at[0])]
    copies[0].start()
    length = count * tokens
    group_width = GROUP * HEAD_SIZE
    for g in range(KEY_VALUE_HEADS):
        keys, values = kv_stacks(key_refs, value_refs, g)
        keys_t = jnp.transpose(keys.astype(F32)).astype(BF16)
        d_keys = jnp.zeros((length, HEAD_SIZE), F32)
        d_values = jnp.zeros((length, HEAD_SIZE), F32)
        for pair in range(g * GROUP // 2, (g + 1) * GROUP // 2):
            cols_a, cols_b = pair_cols(pair)
            d_out = head_pair(resid_ref, pair)
            probs = probs_ref[pair]
            d_probs = mm(values, d_out, NT)
            row_dot = jnp.sum(probs * d_probs, axis=0, keepdims=True)
            d_scores = (probs * (d_probs - row_dot)).astype(BF16)
            d_keys = d_keys + mm(d_scores, head_pair(query_ref, pair))
            d_values = d_values + mm(probs.astype(BF16), d_out)
            d_query_t = mm(keys_t, d_scores) * SCALE
            dq_ref[:, cols_a] = jnp.transpose(d_query_t[:, :tokens]).astype(BF16)
            dq_ref[:, cols_b] = jnp.transpose(d_query_t[:, tokens:]).astype(BF16)
        cols = slice(g * group_width, (g + 1) * group_width)
        copy = pltpu.make_async_copy(dq_ref.at[:, cols], dq_hbm.at[:, cols], sems.at[1 + g])
        copy.start()
        copies.append(copy)
        k_cols = slice(g * HEAD_SIZE, (g + 1) * HEAD_SIZE)
        v_cols = slice((KEY_VALUE_HEADS + g) * HEAD_SIZE, (KEY_VALUE_HEADS + g + 1) * HEAD_SIZE)
        d_keys = d_keys * SCALE
        own_ref[:, k_cols] = d_keys[:tokens]
        own_ref[:, v_cols] = d_values[:tokens]
        for s, ref in enumerate(other_refs, 1):
            ref[:, k_cols] = d_keys[s * tokens : (s + 1) * tokens].astype(BF16)
            ref[:, v_cols] = d_values[s * tokens : (s + 1) * tokens].astype(BF16)
    for copy in copies:
        copy.wait()


def output_kernel(
    count,
    pieces,
    tokens_in_all,
    slot_ref,
    weight_ref,
    gain_ref,
    hidden_ref,
    grad_ref,
    own_ref,
    *refs,
):
    arrived_refs = refs[: count - 1]
    y_refs = refs[count - 1 : count - 1 + pieces]
    out_hbm, dk_hbm, dv_hbm, d_weight_hbm, d_gain_hbm = refs[count - 1 + pieces : -6]
    out_ref, dk_ref, dv_ref, d_weight_ref, d_gain_ref, sems = refs[-6:]
    split = KEY_VALUE_HEADS * HEAD_SIZE
    d_kv = own_ref[...]
    for ref in arrived_refs:
        d_kv = d_kv + ref[...].astype(F32)
    dk_ref[...] = d_kv[:, :split].astype(BF16)
    dv_ref[...] = d_kv[:, split:].astype(BF16)
    d_gain_ref[...] = gain_ref[...] * (1.0 / tokens_in_all)
    copies = []

    def send(source, target):
        copy = pltpu.make_async_copy(source, target, sems.at[len(copies)])
        copy.start()
        copies.append(copy)

    send(dk_ref, dk_hbm)
    send(dv_ref, dv_hbm)
    send(d_gain_ref, d_gain_hbm)
    tokens = hidden_ref.shape[0]
    slots = sum(r.shape[0] for r in y_refs)
    place = placement_cols(slot_ref[...], slots)
    weight = row_to_col(weight_ref[...])
    total = jnp.zeros((tokens, COLS), F32)
    for cols in column_blocks():
        y = mm(place, stacked(y_refs, cols))
        out_ref[:, cols] = (hidden_ref[:, cols].astype(F32) + weight * y).astype(BF16)
        send(out_ref.at[:, cols], out_hbm.at[:, cols])
        total = total + y * grad_ref[:, cols].astype(F32)
    d_weight_ref[...] = col_to_row(jnp.sum(total, axis=1, keepdims=True))
    send(d_weight_ref, d_weight_hbm)
    for copy in copies:
        copy.wait()


def run(kernel, name, inputs, outputs, flops, scratch=(), limit=20 * MIB):
    nbytes = sum(x.size * x.dtype.itemsize for _, x in inputs) + sum(
        x.size * x.dtype.itemsize for _, x in outputs
    )
    spec = {space: pl.BlockSpec(memory_space=space) for space in (VMEM, HBM)}
    return pl.pallas_call(
        kernel,
        out_shape=[x for _, x in outputs],
        in_specs=[spec[space] for space, _ in inputs],
        out_specs=[spec[space] for space, _ in outputs],
        scratch_shapes=list(scratch),
        compiler_params=pltpu.CompilerParams(vmem_limit_bytes=limit),
        cost_estimate=pl.CostEstimate(flops=flops, bytes_accessed=nbytes, transcendentals=0),
        name=name,
    )(*[pltpu.with_memory_space_constraint(x, HBM) if space is HBM else x for space, x in inputs])


def placed(space, arrays):
    return [(space, x) for x in arrays]


def pairwise(value, axis, step):
    count = lax.axis_size(axis)
    return lax.ppermute(value, axis, [(i, i ^ step) for i in range(count)])


def exchange(pieces, capacity):
    count = lax.axis_size("exp")
    rows = EXP_DEV * capacity
    if len(pieces) == count:
        return [pieces[0]] + [pairwise(pieces[s], "exp", s) for s in range(1, count)]
    flat = pieces[0]
    blocks = [flat[s * rows : (s + 1) * rows] for s in range(count)]
    moved = [blocks[0]] + [pairwise(blocks[s], "exp", s) for s in range(1, count)]
    return [jnp.concatenate(moved, axis=0)]


def sum_over(value, axis):
    step = 1
    while step < lax.axis_size(axis):
        value = value + pairwise(value, axis, step)
        step *= 2
    return value


def shaped(shape, dtype):
    return jax.ShapeDtypeStruct(shape, dtype)


def per_device(
    queries,
    keys,
    values,
    resid,
    block_order,
    norm_gain,
    w_gate,
    w_down,
    routes,
    route_weight,
    d_out,
):
    query_rows = queries[0]
    resid_rows = resid[0]
    grad_rows = d_out[0]
    tokens = query_rows.shape[0]
    chosen = routes.reshape(1, tokens)
    gain = norm_gain.reshape(1, D)
    ctx_count = lax.axis_size("ctx")
    exp_count = lax.axis_size("exp")
    experts = EXP_DEV * exp_count
    capacity = 3 * tokens // (2 * experts)
    slots = experts * capacity
    rows = EXP_DEV * capacity
    piece_count = exp_count if rows % 16 == 0 else 1
    piece_shapes = [shaped((slots // piece_count, D), BF16)] * piece_count
    token_shape = shaped((tokens, D), BF16)
    kv_width = 2 * KEY_VALUE_HEADS * HEAD_SIZE
    attn_flops = 4 * tokens * ctx_count * tokens * QUERY_HEADS * HEAD_SIZE
    place_flops = 2 * slots * tokens * D
    expert_flops = 2 * slots * D * FFE * EXP_DEV

    own_keys, own_values = keys[0], values[0]
    all_keys = [own_keys] + [pairwise(own_keys, "ctx", s) for s in range(1, ctx_count)]
    all_values = [own_values] + [pairwise(own_values, "ctx", s) for s in range(1, ctx_count)]

    near = [grad_rows, query_rows, resid_rows, own_keys, own_values, gain]
    grad_rows, query_rows, resid_rows, own_keys, own_values, gain, slot, pos, weight, *send_grad = run(
        functools.partial(dispatch_kernel, ctx_count, experts, capacity),
        "dispatch_grads",
        placed(HBM, near + [route_weight, chosen, block_order]),
        placed(
            VMEM,
            [shaped(x.shape, x.dtype) for x in near]
            + [
                shaped((1, tokens), jnp.int32),
                shaped((ctx_count, tokens), jnp.int32),
                shaped((1, tokens), F32),
            ]
            + piece_shapes,
        ),
        place_flops,
        scratch=[
            pltpu.SMEM(block_order.shape, jnp.int32),
            pltpu.VMEM((1, tokens), jnp.int32),
            pltpu.SemaphoreType.DMA((9,)),
        ],
    )
    all_keys[0], all_values[0] = own_keys, own_values
    arrived_grad = exchange(send_grad, capacity)

    hidden, down_near, *send_x = run(
        functools.partial(attention_kernel, ctx_count, piece_count),
        "attention_forward",
        placed(VMEM, [pos, slot, gain, query_rows, resid_rows])
        + placed(HBM, [w_down])
        + placed(VMEM, all_keys + all_values),
        placed(VMEM, [token_shape, shaped(w_down.shape, BF16)] + piece_shapes),
        attn_flops + place_flops,
        scratch=[pltpu.SemaphoreType.DMA(())],
    )
    arrived_x = exchange(send_x, capacity)

    d_act, probs, gate_near = run(
        functools.partial(probs_kernel, ctx_count, capacity, piece_count),
        "act_grads_and_probs",
        placed(VMEM, [pos, down_near])
        + placed(HBM, [w_gate])
        + placed(VMEM, [query_rows] + all_keys + arrived_grad),
        placed(
            VMEM,
            [
                shaped((slots, FFE), F32),
                shaped((QUERY_HEADS // 2, ctx_count * tokens, 2 * tokens), F32),
                shaped(w_gate.shape, BF16),
            ],
        ),
        expert_flops + attn_flops // 2,
        scratch=[pltpu.SemaphoreType.DMA(())],
    )
    act, *send_dn = run(
        functools.partial(expert_back_kernel, capacity, piece_count),
        "expert_backward",
        placed(VMEM, [gate_near, d_act] + arrived_x),
        placed(VMEM, [shaped((slots, EXP_DEV * FFE), BF16)] + piece_shapes),
        2 * expert_flops,
    )
    dn = exchange(send_dn, capacity)
    gain_part, *send_y = run(
        functools.partial(expert_out_kernel, piece_count),
        "expert_output",
        placed(VMEM, [down_near, act, gain] + arrived_x + send_dn),
        placed(VMEM, [shaped((1, D), F32)] + piece_shapes),
        expert_flops,
    )
    returned = exchange(send_y, capacity)
    gain_part, slot = lax.optimization_barrier((sum_over(gain_part, "dp"), slot))
    for axis in ("exp", "ctx"):
        gain_part = sum_over(gain_part, axis)

    d_hidden, d_queries, kv_own, *kv_send = run(
        functools.partial(backward_kernel, ctx_count, piece_count),
        "residual_attention_backward",
        placed(VMEM, [slot, gain, hidden, grad_rows, query_rows, probs] + dn + all_keys + all_values),
        placed(HBM, [token_shape] * 2)
        + placed(
            VMEM,
            [shaped((tokens, kv_width), F32)]
            + [shaped((tokens, kv_width), BF16)] * (ctx_count - 1),
        ),
        2 * attn_flops + place_flops,
        scratch=[
            pltpu.VMEM((tokens, D), BF16),
            pltpu.VMEM((tokens, D), BF16),
            pltpu.VMEM((tokens, D), F32),
            pltpu.SemaphoreType.DMA((1 + KEY_VALUE_HEADS,)),
        ],
    )
    kv_arrived = [pairwise(part, "ctx", s) for s, part in enumerate(kv_send, 1)]

    kv_shape = shaped((tokens, kv_width // 2), BF16)
    final_shapes = [token_shape, kv_shape, kv_shape, shaped((1, tokens), F32), shaped((1, D), F32)]
    total_tokens = tokens * ctx_count * exp_count * lax.axis_size("dp")
    layer_out, d_keys, d_values, d_weight, d_gain = run(
        functools.partial(output_kernel, ctx_count, piece_count, total_tokens),
        "layer_output",
        placed(
            VMEM,
            [slot, weight, gain_part, hidden, grad_rows, kv_own] + kv_arrived + returned,
        ),
        placed(HBM, final_shapes),
        place_flops,
        scratch=[pltpu.VMEM(x.shape, x.dtype) for x in final_shapes]
        + [pltpu.SemaphoreType.DMA((4 + D // COLS,))],
    )
    return (
        layer_out[None],
        d_hidden[None],
        d_queries[None],
        d_keys[None],
        d_values[None],
        d_weight,
        d_gain[0],
    )


def solution(mesh):
    in_specs = (
        P(("exp", "dp"), "ctx", None),
        P(("exp", "dp"), "ctx", None),
        P(("exp", "dp"), "ctx", None),
        P(("exp", "dp"), "ctx", None),
        P(),
        P(),
        P("exp", None, None),
        P("exp", None, None),
        P(("exp", "dp"), "ctx", None),
        P(("exp", "dp"), "ctx"),
        P(("exp", "dp"), "ctx", None),
    )
    out_specs = (
        P(("exp", "dp"), "ctx", None),
        P(("exp", "dp"), "ctx", None),
        P(("exp", "dp"), "ctx", None),
        P(("exp", "dp"), "ctx", None),
        P(("exp", "dp"), "ctx", None),
        P(("exp", "dp"), "ctx"),
        P(),
    )
    return jax.shard_map(
        per_device, mesh=mesh, in_specs=in_specs, out_specs=out_specs, check_vma=False
    )
```

```python
import functools

import jax
import jax.numpy as jnp
from jax import lax
from jax.experimental import pallas as pl
from jax.experimental.pallas import tpu as pltpu
from jax.sharding import PartitionSpec as P

D = 2048
HEAD_SIZE = 128
QUERY_HEADS = 16
KEY_VALUE_HEADS = 2
GROUP = QUERY_HEADS // KEY_VALUE_HEADS
FFE = 384
EXP_DEV = 2
COLS = 256
LANES = 128
GAIN_LINES = D // LANES
SCALE = HEAD_SIZE ** (-0.5)
EXP2_SCALE = SCALE * 1.4426950408889634
F32 = jnp.float32
BF16 = jnp.bfloat16
NN = (((1,), (0,)), ((), ()))
NT = (((1,), (1,)), ((), ()))
MIB = 1 << 20
VMEM, HBM = pltpu.VMEM, pltpu.HBM


def mm(a, b, dims=NN):
    return lax.dot_general(a, b, dims, preferred_element_type=F32)


def iota(shape, dim):
    return lax.broadcasted_iota(jnp.int32, shape, dim)


def row_to_col(row):
    n = row.shape[1]
    eye = iota((n, n), 0) == iota((n, n), 1)
    return jnp.sum(jnp.where(eye, row, jnp.zeros((), row.dtype)), axis=1, keepdims=True)


def col_to_row(col):
    n = col.shape[0]
    eye = iota((n, n), 0) == iota((n, n), 1)
    return jnp.sum(jnp.where(eye, col, jnp.zeros((), col.dtype)), axis=0, keepdims=True)


def block_positions(order_ref, ctx_index, tokens):
    span = tokens // 8
    index = iota((1, tokens), 1)
    which = index // span
    start = jnp.zeros((1, tokens), jnp.int32)
    for b in range(8):
        start = jnp.where(which == b, order_ref[ctx_index * 8 + b], start)
    return start * span + index % span


def stacked(refs, cols=slice(None)):
    parts = [r[:, cols] for r in refs]
    return parts[0] if len(parts) == 1 else jnp.concatenate(parts, axis=0)


def column_blocks(width=D, step=COLS):
    return [slice(c, c + step) for c in range(0, width, step)]


def store_pieces(refs, cols, rows_value):
    at = 0
    for r in refs:
        n = r.shape[0]
        r[:, cols] = rows_value[at : at + n]
        at += n


def pair_cols(pair):
    start = 2 * pair * HEAD_SIZE
    return slice(start, start + HEAD_SIZE), slice(start + HEAD_SIZE, start + 2 * HEAD_SIZE)


def head_pair(ref, pair):
    first, second = pair_cols(pair)
    return jnp.concatenate([ref[:, first], ref[:, second]], axis=0)


def placement_rows(slot_row, slots):
    tokens = slot_row.shape[1]
    return jnp.where(iota((slots, tokens), 0) == slot_row, 1.0, 0.0).astype(BF16)


def placement_cols(slot_row, slots):
    tokens = slot_row.shape[1]
    slot_col = row_to_col(slot_row)
    return jnp.where(iota((tokens, slots), 1) == slot_col, 1.0, 0.0).astype(BF16)


def dispatch_kernel(count, experts, capacity, *refs):
    sources, refs = refs[:9], refs[9:]
    targets, refs = refs[:6], refs[6:]
    grad_ref = targets[0]
    slot_ref, pos_ref, weight_ref = refs[:3]
    send_refs = refs[3:-3]
    order_ref, routes_ref, sems = refs[-3:]
    targets = targets + (weight_ref, routes_ref, order_ref)
    copies = [
        pltpu.make_async_copy(source, target, sems.at[i])
        for i, (source, target) in enumerate(zip(sources, targets))
    ]
    for copy in copies[6:] + copies[:6]:
        copy.start()
    for copy in copies[6:]:
        copy.wait()
    tokens = routes_ref.shape[1]
    chosen = routes_ref[...]
    lanes = max(experts, 16)
    hits = jnp.where(iota((lanes, tokens), 0) == chosen, 1.0, 0.0)
    before = jnp.where(iota((tokens, tokens), 0) < iota((tokens, tokens), 1), 1.0, 0.0)
    earlier = mm(hits.astype(BF16), before.astype(BF16))
    rank = jnp.sum(hits * earlier, axis=0, keepdims=True).astype(jnp.int32)
    target = (chosen // EXP_DEV) ^ lax.axis_index("exp")
    slot = (target * EXP_DEV + chosen % EXP_DEV) * capacity + rank
    slot_ref[...] = slot
    me = lax.axis_index("ctx")
    for s in range(count):
        pos_ref[s : s + 1, :] = block_positions(order_ref, me ^ s, tokens)
    place = placement_rows(slot, experts * capacity)
    weight = row_to_col(weight_ref[...])
    copies[0].wait()
    for cols in column_blocks():
        scaled = (weight * grad_ref[:, cols].astype(F32)).astype(BF16)
        store_pieces(send_refs, cols, mm(place, scaled).astype(BF16))
    for copy in copies[1:6]:
        copy.wait()


def kv_stacks(key_refs, value_refs, g):
    cols = slice(g * HEAD_SIZE, (g + 1) * HEAD_SIZE)
    return stacked(key_refs, cols), stacked(value_refs, cols)


def attention_kernel(
    count, pieces, pos_ref, slot_ref, gain_ref, query_ref, resid_ref, down_hbm, *refs
):
    key_refs, value_refs = refs[:count], refs[count : 2 * count]
    hidden_ref, down_ref = refs[2 * count : 2 * count + 2]
    send_refs = refs[2 * count + 2 : -1]
    down_copy = pltpu.make_async_copy(down_hbm, down_ref, refs[-1])
    down_copy.start()
    tokens = query_ref.shape[0]
    query_pos = row_to_col(pos_ref[:1, :])
    bias = jnp.concatenate(
        [jnp.where(pos_ref[s : s + 1, :] <= query_pos, 0.0, -1e30) for s in range(count)],
        axis=1,
    )
    length = count * tokens
    ones = jnp.ones((length, HEAD_SIZE), BF16)
    total = jnp.zeros((tokens, HEAD_SIZE), F32)
    for g in range(KEY_VALUE_HEADS):
        keys, values = kv_stacks(key_refs, value_refs, g)
        values = jnp.concatenate([values, ones], axis=1)
        for h in range(g * GROUP, (g + 1) * GROUP):
            cols = slice(h * HEAD_SIZE, (h + 1) * HEAD_SIZE)
            scores = mm(query_ref[:, cols], keys, NT) + bias
            peak = jnp.max(scores, axis=1, keepdims=True)
            weights = jnp.exp2((scores - peak) * EXP2_SCALE).astype(BF16)
            mixed = mm(weights, values)
            attended = mixed[:, :HEAD_SIZE] / mixed[:, HEAD_SIZE:]
            hidden = (resid_ref[:, cols].astype(F32) + attended).astype(BF16)
            hidden_ref[:, cols] = hidden
            wide = hidden.astype(F32)
            total = total + wide * wide
    inv_rms = lax.rsqrt(jnp.sum(total, axis=1, keepdims=True) * (1.0 / D) + 1e-06)
    slots = sum(r.shape[0] for r in send_refs)
    place = placement_rows(slot_ref[...], slots)
    for cols in column_blocks():
        normed = (hidden_ref[:, cols].astype(F32) * inv_rms * gain_ref[:, cols]).astype(BF16)
        store_pieces(send_refs, cols, mm(place, normed).astype(BF16))
    down_copy.wait()


def first_expert_rows(slots, capacity):
    return iota((slots, 1), 0) % (EXP_DEV * capacity) < capacity


def probs_kernel(
    count, capacity, pieces, pos_ref, slot_ref, weight_ref, down_ref, gate_hbm, query_ref, *refs
):
    key_refs = refs[:count]
    grad_refs = refs[count : count + pieces]
    d_act_ref, probs_ref, gate_ref, place_ref, wide_ref, sem = refs[count + pieces :]
    gate_copy = pltpu.make_async_copy(gate_hbm, gate_ref, sem)
    gate_copy.start()
    place_ref[...] = placement_cols(slot_ref[...], place_ref.shape[1])
    wide_ref[...] = jnp.broadcast_to(row_to_col(weight_ref[...]), wide_ref.shape)
    grads = stacked(grad_refs)
    first = first_expert_rows(grads.shape[0], capacity)
    d_act_ref[...] = jnp.where(first, mm(grads, down_ref[0], NT), mm(grads, down_ref[1], NT))
    query_pos = pos_ref[:1, :]
    bias = jnp.concatenate(
        [
            jnp.where(row_to_col(pos_ref[s : s + 1, :]) <= query_pos, 0.0, -1e30)
            for s in range(count)
        ],
        axis=0,
    )
    bias = jnp.concatenate([bias, bias], axis=1)
    for g in range(KEY_VALUE_HEADS):
        keys = stacked(key_refs, slice(g * HEAD_SIZE, (g + 1) * HEAD_SIZE))
        for pair in range(g * GROUP // 2, (g + 1) * GROUP // 2):
            scores = mm(keys, head_pair(query_ref, pair), NT) + bias
            peak = jnp.max(scores, axis=0, keepdims=True)
            weights = jnp.exp2((scores - peak) * EXP2_SCALE)
            probs_ref[pair] = weights * (1.0 / jnp.sum(weights, axis=0, keepdims=True))
    gate_copy.wait()


def expert_back_kernel(capacity, pieces, gate_ref, d_act_ref, gain_ref, *refs):
    rows = stacked(refs[:pieces])
    act_ref = refs[pieces]
    out_refs = refs[pieces + 1 : -1]
    terms_ref = refs[-1]
    first = first_expert_rows(rows.shape[0], capacity)
    pre = jnp.where(first, mm(rows, gate_ref[0]), mm(rows, gate_ref[1]))
    gate = 1.0 / (1.0 + jnp.exp(-pre))
    act = pre * gate
    act_ref[:, :FFE] = jnp.where(first, act, 0.0).astype(BF16)
    act_ref[:, FFE:] = jnp.where(first, 0.0, act).astype(BF16)
    d_pre = d_act_ref[...] * gate * (1.0 + pre * (1.0 - gate))
    d_first = jnp.where(first, d_pre, 0.0).astype(BF16)
    d_second = jnp.where(first, 0.0, d_pre).astype(BF16)
    for cols in column_blocks():
        back = mm(d_first, gate_ref[0, cols, :], NT) + mm(d_second, gate_ref[1, cols, :], NT)
        back = back.astype(BF16)
        store_pieces(out_refs, cols, back)
        products = rows[:, cols].astype(F32) * back.astype(F32)
        terms = jnp.sum(products, axis=0, keepdims=True) / gain_ref[:, cols]
        for at in range(0, COLS, LANES):
            line = (cols.start + at) // LANES
            terms_ref[line : line + 1, :] = terms[:, at : at + LANES]
    if pieces > 1:
        total = terms_ref[...]
        high = total.astype(BF16)
        low = (total - high.astype(F32)).astype(BF16)
        for ref in out_refs:
            ref[:GAIN_LINES, D:] = high
            ref[GAIN_LINES : 2 * GAIN_LINES, D:] = low
            ref[2 * GAIN_LINES :, D:] = jnp.zeros((ref.shape[0] - 2 * GAIN_LINES, LANES), BF16)


def expert_out_kernel(down_ref, act_ref, *out_refs):
    act = act_ref[...]
    for cols in column_blocks():
        y = mm(act[:, :FFE], down_ref[0, :, cols]) + mm(act[:, FFE:], down_ref[1, :, cols])
        store_pieces(out_refs, cols, y.astype(BF16))


def backward_kernel(
    count, pieces, place_ref, gain_ref, hidden_ref, grad_ref, query_ref, probs_ref, *refs
):
    dn_refs = refs[:pieces]
    key_refs = refs[pieces : pieces + count]
    value_refs = refs[pieces + count : pieces + 2 * count]
    resid_hbm, dq_hbm, own_ref = refs[pieces + 2 * count : pieces + 2 * count + 3]
    other_refs = refs[pieces + 2 * count + 3 : -4]
    resid_ref, dq_ref, dn_scratch, sems = refs[-4:]
    tokens = hidden_ref.shape[0]
    place = place_ref[...]
    square = jnp.zeros((tokens, COLS), F32)
    mixing = jnp.zeros((tokens, COLS), F32)
    for cols in column_blocks():
        dn = mm(place, stacked(dn_refs, cols)) * gain_ref[:, cols]
        dn_scratch[:, cols] = dn
        hidden = hidden_ref[:, cols].astype(F32)
        square = square + hidden * hidden
        mixing = mixing + dn * hidden
    inv_rms = lax.rsqrt(jnp.sum(square, axis=1, keepdims=True) * (1.0 / D) + 1e-06)
    mean_mix = jnp.sum(mixing, axis=1, keepdims=True) * (1.0 / D)
    factor = inv_rms * inv_rms * inv_rms * mean_mix
    for cols in column_blocks():
        resid_ref[:, cols] = (
            grad_ref[:, cols].astype(F32)
            + dn_scratch[:, cols] * inv_rms
            - hidden_ref[:, cols].astype(F32) * factor
        ).astype(BF16)
    copies = [pltpu.make_async_copy(resid_ref, resid_hbm, sems.at[0])]
    copies[0].start()
    length = count * tokens
    group_width = GROUP * HEAD_SIZE
    for g in range(KEY_VALUE_HEADS):
        keys, values = kv_stacks(key_refs, value_refs, g)
        keys_t = jnp.transpose(keys.astype(F32)).astype(BF16)
        d_keys = jnp.zeros((length, HEAD_SIZE), F32)
        d_values = jnp.zeros((length, HEAD_SIZE), F32)
        for pair in range(g * GROUP // 2, (g + 1) * GROUP // 2):
            cols_a, cols_b = pair_cols(pair)
            d_out = head_pair(resid_ref, pair)
            probs = probs_ref[pair]
            d_probs = mm(values, d_out, NT)
            row_dot = jnp.sum(probs * d_probs, axis=0, keepdims=True)
            d_scores = (probs * (d_probs - row_dot)).astype(BF16)
            d_keys = d_keys + mm(d_scores, head_pair(query_ref, pair))
            d_values = d_values + mm(probs.astype(BF16), d_out)
            d_query_t = mm(keys_t, d_scores) * SCALE
            dq_ref[:, cols_a] = jnp.transpose(d_query_t[:, :tokens]).astype(BF16)
            dq_ref[:, cols_b] = jnp.transpose(d_query_t[:, tokens:]).astype(BF16)
        cols = slice(g * group_width, (g + 1) * group_width)
        copy = pltpu.make_async_copy(dq_ref.at[:, cols], dq_hbm.at[:, cols], sems.at[1 + g])
        copy.start()
        copies.append(copy)
        k_cols = slice(g * HEAD_SIZE, (g + 1) * HEAD_SIZE)
        v_cols = slice((KEY_VALUE_HEADS + g) * HEAD_SIZE, (KEY_VALUE_HEADS + g + 1) * HEAD_SIZE)
        d_keys = d_keys * SCALE
        own_ref[:, k_cols] = d_keys[:tokens]
        own_ref[:, v_cols] = d_values[:tokens]
        for s, ref in enumerate(other_refs, 1):
            ref[:, k_cols] = d_keys[s * tokens : (s + 1) * tokens].astype(BF16)
            ref[:, v_cols] = d_values[s * tokens : (s + 1) * tokens].astype(BF16)
    for copy in copies:
        copy.wait()


def tree_sum(parts):
    while len(parts) > 1:
        parts = [parts[i] + parts[i + 1] for i in range(0, len(parts), 2)]
    return parts[0]


def output_kernel(
    count,
    pieces,
    gain_parts,
    tokens_in_all,
    place_ref,
    weight_ref,
    hidden_ref,
    grad_ref,
    own_ref,
    *refs,
):
    gain_refs, refs = refs[:gain_parts], refs[gain_parts:]
    arrived_refs = refs[: count - 1]
    y_refs = refs[count - 1 : count - 1 + pieces]
    out_hbm, dk_hbm, dv_hbm, d_weight_hbm, d_gain_hbm = refs[count - 1 + pieces : -6]
    out_ref, dk_ref, dv_ref, d_weight_ref, d_gain_ref, sems = refs[-6:]
    split = KEY_VALUE_HEADS * HEAD_SIZE
    d_kv = own_ref[...]
    for ref in arrived_refs:
        d_kv = d_kv + ref[...].astype(F32)
    dk_ref[...] = d_kv[:, :split].astype(BF16)
    dv_ref[...] = d_kv[:, split:].astype(BF16)
    d_gain_ref[...] = tree_sum([ref[...] for ref in gain_refs]) * (1.0 / tokens_in_all)
    copies = []

    def send(source, target):
        copy = pltpu.make_async_copy(source, target, sems.at[len(copies)])
        copy.start()
        copies.append(copy)

    send(dk_ref, dk_hbm)
    send(dv_ref, dv_hbm)
    send(d_gain_ref, d_gain_hbm)
    tokens = hidden_ref.shape[0]
    place = place_ref[...]
    weight = weight_ref[...]
    total = jnp.zeros((tokens, COLS), F32)
    for cols in column_blocks():
        y = mm(place, stacked(y_refs, cols))
        out_ref[:, cols] = (hidden_ref[:, cols].astype(F32) + weight * y).astype(BF16)
        send(out_ref.at[:, cols], out_hbm.at[:, cols])
        total = total + y * grad_ref[:, cols].astype(F32)
    d_weight_ref[...] = col_to_row(jnp.sum(total, axis=1, keepdims=True))
    send(d_weight_ref, d_weight_hbm)
    for copy in copies:
        copy.wait()


def run(kernel, name, inputs, outputs, flops, scratch=(), limit=20 * MIB):
    nbytes = sum(x.size * x.dtype.itemsize for _, x in inputs) + sum(
        x.size * x.dtype.itemsize for _, x in outputs
    )
    spec = {space: pl.BlockSpec(memory_space=space) for space in (VMEM, HBM)}
    return pl.pallas_call(
        kernel,
        out_shape=[x for _, x in outputs],
        in_specs=[spec[space] for space, _ in inputs],
        out_specs=[spec[space] for space, _ in outputs],
        scratch_shapes=list(scratch),
        compiler_params=pltpu.CompilerParams(vmem_limit_bytes=limit),
        cost_estimate=pl.CostEstimate(flops=flops, bytes_accessed=nbytes, transcendentals=0),
        name=name,
    )(*[pltpu.with_memory_space_constraint(x, HBM) if space is HBM else x for space, x in inputs])


def placed(space, arrays):
    return [(space, x) for x in arrays]


def pairwise(value, axis, step):
    count = lax.axis_size(axis)
    return lax.ppermute(value, axis, [(i, i ^ step) for i in range(count)])


def exchange(pieces, capacity):
    count = lax.axis_size("exp")
    rows = EXP_DEV * capacity
    if len(pieces) == count:
        return [pieces[0]] + [pairwise(pieces[s], "exp", s) for s in range(1, count)]
    flat = pieces[0]
    blocks = [flat[s * rows : (s + 1) * rows] for s in range(count)]
    moved = [blocks[0]] + [pairwise(blocks[s], "exp", s) for s in range(1, count)]
    return [jnp.concatenate(moved, axis=0)]


def with_partners(value, axis):
    return [value] + [pairwise(value, axis, s) for s in range(1, lax.axis_size(axis))]


def in_turns(value, axis, ahead):
    parts = [value]
    for s in range(1, lax.axis_size(axis)):
        parts.append(pairwise(value, axis, s))
        value, _ = lax.optimization_barrier((value, ahead))
        ahead = parts[-1]
    return parts


def shaped(shape, dtype):
    return jax.ShapeDtypeStruct(shape, dtype)


def per_device(
    queries,
    keys,
    values,
    resid,
    block_order,
    norm_gain,
    w_gate,
    w_down,
    routes,
    route_weight,
    d_out,
):
    query_rows = queries[0]
    resid_rows = resid[0]
    grad_rows = d_out[0]
    tokens = query_rows.shape[0]
    chosen = routes.reshape(1, tokens)
    gain = norm_gain.reshape(1, D)
    ctx_count = lax.axis_size("ctx")
    exp_count = lax.axis_size("exp")
    experts = EXP_DEV * exp_count
    capacity = 3 * tokens // (2 * experts)
    slots = experts * capacity
    rows = EXP_DEV * capacity
    piece_count = exp_count if rows % 16 == 0 else 1
    piece_shapes = [shaped((slots // piece_count, D), BF16)] * piece_count
    token_shape = shaped((tokens, D), BF16)
    kv_width = 2 * KEY_VALUE_HEADS * HEAD_SIZE
    attn_flops = 4 * tokens * ctx_count * tokens * QUERY_HEADS * HEAD_SIZE
    place_flops = 2 * slots * tokens * D
    expert_flops = 2 * slots * D * FFE * EXP_DEV

    own_keys, own_values = keys[0], values[0]
    all_keys = [own_keys] + [pairwise(own_keys, "ctx", s) for s in range(1, ctx_count)]
    all_values = [own_values] + [pairwise(own_values, "ctx", s) for s in range(1, ctx_count)]

    near = [grad_rows, own_keys, own_values, gain, query_rows, resid_rows]
    grad_rows, own_keys, own_values, gain, query_rows, resid_rows, slot, pos, weight, *send_grad = run(
        functools.partial(dispatch_kernel, ctx_count, experts, capacity),
        "dispatch_grads",
        placed(HBM, near + [route_weight, chosen, block_order]),
        placed(
            VMEM,
            [shaped(x.shape, x.dtype) for x in near]
            + [
                shaped((1, tokens), jnp.int32),
                shaped((ctx_count, tokens), jnp.int32),
                shaped((1, tokens), F32),
            ]
            + piece_shapes,
        ),
        place_flops,
        scratch=[
            pltpu.SMEM(block_order.shape, jnp.int32),
            pltpu.VMEM((1, tokens), jnp.int32),
            pltpu.SemaphoreType.DMA((9,)),
        ],
    )
    all_keys[0], all_values[0] = own_keys, own_values
    arrived_grad = exchange(send_grad, capacity)

    hidden, down_near, *send_x = run(
        functools.partial(attention_kernel, ctx_count, piece_count),
        "attention_forward",
        placed(VMEM, [pos, slot, gain, query_rows, resid_rows])
        + placed(HBM, [w_down])
        + placed(VMEM, all_keys + all_values),
        placed(VMEM, [token_shape, shaped(w_down.shape, BF16)] + piece_shapes),
        attn_flops + place_flops,
        scratch=[pltpu.SemaphoreType.DMA(())],
    )
    arrived_x = exchange(send_x, capacity)

    d_act, probs, gate_near, place, weight_wide = run(
        functools.partial(probs_kernel, ctx_count, capacity, piece_count),
        "act_grads_and_probs",
        placed(VMEM, [pos, slot, weight, down_near])
        + placed(HBM, [w_gate])
        + placed(VMEM, [query_rows] + all_keys + arrived_grad),
        placed(
            VMEM,
            [
                shaped((slots, FFE), F32),
                shaped((QUERY_HEADS // 2, ctx_count * tokens, 2 * tokens), F32),
                shaped(w_gate.shape, BF16),
                shaped((tokens, slots), BF16),
                shaped((tokens, COLS), F32),
            ],
        ),
        expert_flops + attn_flops // 2,
        scratch=[pltpu.SemaphoreType.DMA(())],
    )
    carried = piece_count > 1
    terms_shape = shaped((GAIN_LINES, LANES), F32)
    dn_shapes = [shaped((x.shape[0], D + LANES * carried), BF16) for x in piece_shapes]
    act, *send_dn, terms = run(
        functools.partial(expert_back_kernel, capacity, piece_count),
        "expert_backward",
        placed(VMEM, [gate_near, d_act, gain] + arrived_x),
        placed(VMEM, [shaped((slots, EXP_DEV * FFE), BF16)] + dn_shapes + [terms_shape]),
        2 * expert_flops,
    )
    dn = exchange(send_dn, capacity)
    if carried:
        terms = tree_sum(
            [
                x[:GAIN_LINES, D:].astype(F32) + x[GAIN_LINES : 2 * GAIN_LINES, D:].astype(F32)
                for x in dn
            ]
        )
    else:
        terms = tree_sum(with_partners(terms, "exp"))
    terms, place_back = lax.optimization_barrier((terms, place))
    terms = tree_sum(with_partners(terms, "ctx"))
    send_y = run(
        expert_out_kernel,
        "expert_output",
        placed(VMEM, [down_near, act]),
        placed(VMEM, piece_shapes),
        expert_flops,
    )
    returned = exchange(send_y, capacity)

    d_hidden, d_queries, kv_own, *kv_send = run(
        functools.partial(backward_kernel, ctx_count, piece_count),
        "residual_attention_backward",
        placed(VMEM, [place_back, gain, hidden, grad_rows, query_rows, probs] + dn + all_keys + all_values),
        placed(HBM, [token_shape] * 2)
        + placed(
            VMEM,
            [shaped((tokens, kv_width), F32)]
            + [shaped((tokens, kv_width), BF16)] * (ctx_count - 1),
        ),
        2 * attn_flops + place_flops,
        scratch=[
            pltpu.VMEM((tokens, D), BF16),
            pltpu.VMEM((tokens, D), BF16),
            pltpu.VMEM((tokens, D), F32),
            pltpu.SemaphoreType.DMA((1 + KEY_VALUE_HEADS,)),
        ],
    )
    kv_arrived = [pairwise(part, "ctx", s) for s, part in enumerate(kv_send, 1)]
    terms, kv_own = lax.optimization_barrier((terms, kv_own))
    gain_parts = in_turns(terms, "dp", kv_arrived[0])

    kv_shape = shaped((tokens, kv_width // 2), BF16)
    final_shapes = [token_shape, kv_shape, kv_shape, shaped((1, tokens), F32), terms_shape]
    total_tokens = tokens * ctx_count * exp_count * lax.axis_size("dp")
    layer_out, d_keys, d_values, d_weight, d_gain = run(
        functools.partial(
            output_kernel, ctx_count, piece_count, len(gain_parts), total_tokens
        ),
        "layer_output",
        placed(
            VMEM,
            [place, weight_wide, hidden, grad_rows, kv_own] + gain_parts + kv_arrived + returned,
        ),
        placed(HBM, final_shapes),
        place_flops,
        scratch=[pltpu.VMEM(x.shape, x.dtype) for x in final_shapes]
        + [pltpu.SemaphoreType.DMA((4 + D // COLS,))],
    )
    return (
        layer_out[None],
        d_hidden[None],
        d_queries[None],
        d_keys[None],
        d_values[None],
        d_weight,
        d_gain.reshape(D),
    )


def solution(mesh):
    in_specs = (
        P(("exp", "dp"), "ctx", None),
        P(("exp", "dp"), "ctx", None),
        P(("exp", "dp"), "ctx", None),
        P(("exp", "dp"), "ctx", None),
        P(),
        P(),
        P("exp", None, None),
        P("exp", None, None),
        P(("exp", "dp"), "ctx", None),
        P(("exp", "dp"), "ctx"),
        P(("exp", "dp"), "ctx", None),
    )
    out_specs = (
        P(("exp", "dp"), "ctx", None),
        P(("exp", "dp"), "ctx", None),
        P(("exp", "dp"), "ctx", None),
        P(("exp", "dp"), "ctx", None),
        P(("exp", "dp"), "ctx", None),
        P(("exp", "dp"), "ctx"),
        P(),
    )
    return jax.shard_map(
        per_device, mesh=mesh, in_specs=in_specs, out_specs=out_specs, check_vma=False
    )
```

```python
import functools

import jax
import jax.numpy as jnp
from jax import lax
from jax.experimental import pallas as pl
from jax.experimental.pallas import tpu as pltpu
from jax.sharding import PartitionSpec as P

D = 2048
HEAD_SIZE = 128
QUERY_HEADS = 16
KEY_VALUE_HEADS = 2
GROUP = QUERY_HEADS // KEY_VALUE_HEADS
FFE = 384
EXP_DEV = 2
COLS = 256
LANES = 128
GAIN_LINES = D // LANES
WIDE_LINES = 128
SCALE = HEAD_SIZE ** (-0.5)
EXP2_SCALE = SCALE * 1.4426950408889634
F32 = jnp.float32
BF16 = jnp.bfloat16
NN = (((1,), (0,)), ((), ()))
NT = (((1,), (1,)), ((), ()))
MIB = 1 << 20
VMEM, HBM = pltpu.VMEM, pltpu.HBM


def mm(a, b, dims=NN):
    return lax.dot_general(a, b, dims, preferred_element_type=F32)


def iota(shape, dim):
    return lax.broadcasted_iota(jnp.int32, shape, dim)


def row_to_col(row):
    n = row.shape[1]
    eye = iota((n, n), 0) == iota((n, n), 1)
    return jnp.sum(jnp.where(eye, row.astype(F32), 0.0), axis=1, keepdims=True)


def col_to_row(col):
    n = col.shape[0]
    eye = iota((n, n), 0) == iota((n, n), 1)
    return jnp.sum(jnp.where(eye, col, 0.0), axis=0, keepdims=True)


def block_positions(order_ref, ctx_index, tokens):
    span = tokens // 8
    index = iota((1, tokens), 1)
    which = index // span
    start = jnp.zeros((1, tokens), jnp.int32)
    for b in range(8):
        start = jnp.where(which == b, order_ref[ctx_index * 8 + b], start)
    return start * span + index % span


def stacked(refs, cols=slice(None)):
    parts = [r[:, cols] for r in refs]
    return parts[0] if len(parts) == 1 else jnp.concatenate(parts, axis=0)


def column_blocks(width=D, step=COLS):
    return [slice(c, c + step) for c in range(0, width, step)]


def store_pieces(refs, cols, rows_value):
    at = 0
    for r in refs:
        n = r.shape[0]
        r[:, cols] = rows_value[at : at + n]
        at += n


def pair_cols(pair):
    start = 2 * pair * HEAD_SIZE
    return slice(start, start + HEAD_SIZE), slice(start + HEAD_SIZE, start + 2 * HEAD_SIZE)


def head_pair(ref, pair):
    first, second = pair_cols(pair)
    return jnp.concatenate([ref[:, first], ref[:, second]], axis=0)


def placement_rows(slot_row, slots):
    tokens = slot_row.shape[1]
    return jnp.where(iota((slots, tokens), 0) == slot_row, 1.0, 0.0).astype(BF16)


def placement_cols(slot_row, slots):
    tokens = slot_row.shape[1]
    slot_col = row_to_col(slot_row)
    return jnp.where(iota((tokens, slots), 1).astype(F32) == slot_col, 1.0, 0.0).astype(BF16)


def dispatch_kernel(count, experts, capacity, *refs):
    sources, refs = refs[:9], refs[9:]
    targets, refs = refs[:6], refs[6:]
    grad_ref = targets[0]
    slot_ref, pos_ref, weight_ref = refs[:3]
    send_refs = refs[3:-3]
    order_ref, routes_ref, sems = refs[-3:]
    targets = targets + (weight_ref, routes_ref, order_ref)
    copies = [
        pltpu.make_async_copy(source, target, sems.at[i])
        for i, (source, target) in enumerate(zip(sources, targets))
    ]
    for copy in copies[6:] + copies[:6]:
        copy.start()
    for copy in copies[6:]:
        copy.wait()
    tokens = routes_ref.shape[1]
    chosen = routes_ref[...]
    lanes = max(experts, 16)
    hits = jnp.where(iota((lanes, tokens), 0) == chosen, 1.0, 0.0)
    before = jnp.where(iota((tokens, tokens), 0) < iota((tokens, tokens), 1), 1.0, 0.0)
    earlier = mm(hits.astype(BF16), before.astype(BF16))
    rank = jnp.sum(hits * earlier, axis=0, keepdims=True).astype(jnp.int32)
    target = (chosen // EXP_DEV) ^ lax.axis_index("exp")
    slot = (target * EXP_DEV + chosen % EXP_DEV) * capacity + rank
    slot_ref[...] = slot
    me = lax.axis_index("ctx")
    for s in range(count):
        pos_ref[s : s + 1, :] = block_positions(order_ref, me ^ s, tokens)
    place = placement_rows(slot, experts * capacity)
    weight = row_to_col(weight_ref[...])
    copies[0].wait()
    for cols in column_blocks():
        scaled = (weight * grad_ref[:, cols].astype(F32)).astype(BF16)
        store_pieces(send_refs, cols, mm(place, scaled).astype(BF16))
    for copy in copies[1:6]:
        copy.wait()


def kv_stacks(key_refs, value_refs, g):
    cols = slice(g * HEAD_SIZE, (g + 1) * HEAD_SIZE)
    return stacked(key_refs, cols), stacked(value_refs, cols)


def attention_kernel(
    count, pos_ref, slot_ref, gain_ref, query_ref, resid_ref, *refs
):
    key_refs, value_refs = refs[:count], refs[count : 2 * count]
    hidden_ref, send_refs = refs[2 * count], refs[2 * count + 1 :]
    tokens = query_ref.shape[0]
    query_pos = row_to_col(pos_ref[:1, :])
    bias = jnp.concatenate(
        [
            jnp.where(pos_ref[s : s + 1, :].astype(F32) <= query_pos, 0.0, -1e30)
            for s in range(count)
        ],
        axis=1,
    )
    length = count * tokens
    ones = jnp.ones((length, HEAD_SIZE), BF16)
    total = jnp.zeros((tokens, HEAD_SIZE), F32)
    for g in range(KEY_VALUE_HEADS):
        keys, values = kv_stacks(key_refs, value_refs, g)
        values = jnp.concatenate([values, ones], axis=1)
        for h in range(g * GROUP, (g + 1) * GROUP):
            cols = slice(h * HEAD_SIZE, (h + 1) * HEAD_SIZE)
            scores = mm(query_ref[:, cols], keys, NT) + bias
            peak = jnp.max(scores, axis=1, keepdims=True)
            weights = jnp.exp2((scores - peak) * EXP2_SCALE).astype(BF16)
            mixed = mm(weights, values)
            attended = mixed[:, :HEAD_SIZE] / mixed[:, HEAD_SIZE:]
            hidden = (resid_ref[:, cols].astype(F32) + attended).astype(BF16)
            hidden_ref[:, cols] = hidden
            wide = hidden.astype(F32)
            total = total + wide * wide
    inv_rms = lax.rsqrt(jnp.sum(total, axis=1, keepdims=True) * (1.0 / D) + 1e-06)
    slots = sum(r.shape[0] for r in send_refs)
    place = placement_rows(slot_ref[...], slots)
    for cols in column_blocks():
        normed = (hidden_ref[:, cols].astype(F32) * inv_rms * gain_ref[:, cols]).astype(BF16)
        store_pieces(send_refs, cols, mm(place, normed).astype(BF16))


def first_expert_rows(slots, capacity):
    return iota((slots, 1), 0) % (EXP_DEV * capacity) < capacity


def probs_kernel(
    count,
    capacity,
    pieces,
    pos_ref,
    slot_ref,
    weight_ref,
    down_hbm,
    gate_hbm,
    query_ref,
    *refs,
):
    key_refs = refs[:count]
    grad_refs = refs[count : count + pieces]
    d_act_ref, probs_ref, down_ref, gate_ref, place_ref, wide_ref, sems = refs[count + pieces :]
    down_copy = pltpu.make_async_copy(down_hbm, down_ref, sems.at[0])
    gate_copy = pltpu.make_async_copy(gate_hbm, gate_ref, sems.at[1])
    down_copy.start()
    gate_copy.start()
    place_ref[...] = placement_cols(slot_ref[...], place_ref.shape[1])
    wide_ref[...] = jnp.broadcast_to(row_to_col(weight_ref[...]), wide_ref.shape)
    query_pos = pos_ref[:1, :].astype(F32)
    bias = jnp.concatenate(
        [
            jnp.where(row_to_col(pos_ref[s : s + 1, :]) <= query_pos, 0.0, -1e30)
            for s in range(count)
        ],
        axis=0,
    )
    bias = jnp.concatenate([bias, bias], axis=1)
    for g in range(KEY_VALUE_HEADS):
        keys = stacked(key_refs, slice(g * HEAD_SIZE, (g + 1) * HEAD_SIZE))
        for pair in range(g * GROUP // 2, (g + 1) * GROUP // 2):
            scores = mm(keys, head_pair(query_ref, pair), NT) + bias
            peak = jnp.max(scores, axis=0, keepdims=True)
            weights = jnp.exp2((scores - peak) * EXP2_SCALE)
            probs_ref[pair] = weights * (1.0 / jnp.sum(weights, axis=0, keepdims=True))
    grads = stacked(grad_refs)
    first = first_expert_rows(grads.shape[0], capacity)
    down_copy.wait()
    d_act_ref[...] = jnp.where(first, mm(grads, down_ref[0], NT), mm(grads, down_ref[1], NT))
    gate_copy.wait()


def part_views(refs, rows, part):
    return [r if r.shape[0] != 2 * rows else r.at[part * rows : (part + 1) * rows] for r in refs]


def joined(step, pieces):
    return pieces > 1 and step > 0 and step & (step - 1) == 0


def split_parts(refs, pieces):
    back, out = [], []
    at = 0
    for s in range(pieces):
        back.append(refs[at])
        at += not joined(s, pieces)
        out.append(refs[at])
        at += 1
    return back, out


def expert_kernel(capacity, pieces, gate_ref, down_ref, d_act_ref, *refs):
    rows = stacked(refs[:pieces])
    back_refs, out_refs = split_parts(refs[pieces:], pieces)
    back_refs = part_views(back_refs, EXP_DEV * capacity, 0)
    out_refs = part_views(out_refs, EXP_DEV * capacity, 1)
    first = first_expert_rows(rows.shape[0], capacity)
    pre = jnp.where(first, mm(rows, gate_ref[0]), mm(rows, gate_ref[1]))
    gate = 1.0 / (1.0 + jnp.exp(-pre))
    act = pre * gate
    act_first = jnp.where(first, act, 0.0).astype(BF16)
    act_second = jnp.where(first, 0.0, act).astype(BF16)
    d_pre = d_act_ref[...] * gate * (1.0 + pre * (1.0 - gate))
    d_first = jnp.where(first, d_pre, 0.0).astype(BF16)
    d_second = jnp.where(first, 0.0, d_pre).astype(BF16)
    for cols in column_blocks():
        back = mm(d_first, gate_ref[0, cols, :], NT) + mm(d_second, gate_ref[1, cols, :], NT)
        store_pieces(back_refs, cols, back.astype(BF16))
        y = mm(act_first, down_ref[0, :, cols]) + mm(act_second, down_ref[1, :, cols])
        store_pieces(out_refs, cols, y.astype(BF16))


def gain_kernel(pieces, rows, gain_ref, *refs):
    row_refs = refs[:pieces]
    back_refs = part_views(refs[pieces:-1], rows, 0)
    terms_ref = refs[-1]
    for cols in column_blocks():
        products = stacked(row_refs, cols).astype(F32) * stacked(back_refs, cols).astype(F32)
        terms = jnp.sum(products, axis=0, keepdims=True) / gain_ref[:, cols]
        for at in range(0, COLS, LANES):
            line = (cols.start + at) // LANES
            terms_ref[line : line + 1, :] = terms[:, at : at + LANES]


def backward_kernel(
    count, pieces, rows, place_ref, gain_ref, hidden_ref, grad_ref, query_ref, probs_ref, *refs
):
    dn_refs = part_views(refs[:pieces], rows, 0)
    key_refs = refs[pieces : pieces + count]
    value_refs = refs[pieces + count : pieces + 2 * count]
    resid_hbm, dq_hbm, own_ref = refs[pieces + 2 * count : pieces + 2 * count + 3]
    other_refs = refs[pieces + 2 * count + 3 : -4]
    resid_ref, dq_ref, dn_scratch, sems = refs[-4:]
    tokens = hidden_ref.shape[0]
    place = place_ref[...]
    square = jnp.zeros((tokens, COLS), F32)
    mixing = jnp.zeros((tokens, COLS), F32)
    for cols in column_blocks():
        dn = mm(place, stacked(dn_refs, cols)) * gain_ref[:, cols]
        dn_scratch[:, cols] = dn
        hidden = hidden_ref[:, cols].astype(F32)
        square = square + hidden * hidden
        mixing = mixing + dn * hidden
    inv_rms = lax.rsqrt(jnp.sum(square, axis=1, keepdims=True) * (1.0 / D) + 1e-06)
    mean_mix = jnp.sum(mixing, axis=1, keepdims=True) * (1.0 / D)
    factor = inv_rms * inv_rms * inv_rms * mean_mix
    for cols in column_blocks():
        resid_ref[:, cols] = (
            grad_ref[:, cols].astype(F32)
            + dn_scratch[:, cols] * inv_rms
            - hidden_ref[:, cols].astype(F32) * factor
        ).astype(BF16)
    copies = [pltpu.make_async_copy(resid_ref, resid_hbm, sems.at[0])]
    copies[0].start()
    length = count * tokens
    group_width = GROUP * HEAD_SIZE
    for g in range(KEY_VALUE_HEADS):
        keys, values = kv_stacks(key_refs, value_refs, g)
        keys_t = jnp.transpose(keys.astype(F32)).astype(BF16)
        d_keys = jnp.zeros((length, HEAD_SIZE), F32)
        d_values = jnp.zeros((length, HEAD_SIZE), F32)
        for pair in range(g * GROUP // 2, (g + 1) * GROUP // 2):
            cols_a, cols_b = pair_cols(pair)
            d_out = head_pair(resid_ref, pair)
            probs = probs_ref[pair]
            d_probs = mm(values, d_out, NT)
            row_dot = jnp.sum(probs * d_probs, axis=0, keepdims=True)
            d_scores = (probs * (d_probs - row_dot)).astype(BF16)
            d_keys = d_keys + mm(d_scores, head_pair(query_ref, pair))
            d_values = d_values + mm(probs.astype(BF16), d_out)
            d_query_t = mm(keys_t, d_scores) * SCALE
            dq_ref[:, cols_a] = jnp.transpose(d_query_t[:, :tokens]).astype(BF16)
            dq_ref[:, cols_b] = jnp.transpose(d_query_t[:, tokens:]).astype(BF16)
        cols = slice(g * group_width, (g + 1) * group_width)
        copy = pltpu.make_async_copy(dq_ref.at[:, cols], dq_hbm.at[:, cols], sems.at[1 + g])
        copy.start()
        copies.append(copy)
        k_cols = slice(g * HEAD_SIZE, (g + 1) * HEAD_SIZE)
        v_cols = slice((KEY_VALUE_HEADS + g) * HEAD_SIZE, (KEY_VALUE_HEADS + g + 1) * HEAD_SIZE)
        d_keys = d_keys * SCALE
        own_ref[:, k_cols] = d_keys[:tokens]
        own_ref[:, v_cols] = d_values[:tokens]
        for s, ref in enumerate(other_refs, 1):
            ref[:, k_cols] = d_keys[s * tokens : (s + 1) * tokens].astype(BF16)
            ref[:, v_cols] = d_values[s * tokens : (s + 1) * tokens].astype(BF16)
    for copy in copies:
        copy.wait()


def output_kernel(
    count, pieces, rows, tokens_in_all, place_ref, weight_ref, gain_ref, hidden_ref, grad_ref, *refs
):
    own_ref, refs = refs[0], refs[1:]
    arrived_refs = refs[: count - 1]
    y_refs = part_views(refs[count - 1 : count - 1 + pieces], rows, 1)
    out_hbm, dk_hbm, dv_hbm, d_weight_hbm, d_gain_hbm = refs[count - 1 + pieces : -6]
    out_ref, dk_ref, dv_ref, d_weight_ref, d_gain_ref, sems = refs[-6:]
    split = KEY_VALUE_HEADS * HEAD_SIZE
    d_kv = own_ref[...]
    for ref in arrived_refs:
        d_kv = d_kv + ref[...].astype(F32)
    dk_ref[...] = d_kv[:, :split].astype(BF16)
    dv_ref[...] = d_kv[:, split:].astype(BF16)
    d_gain_ref[...] = gain_ref[...] * (1.0 / tokens_in_all)
    copies = []

    def send(source, target):
        copy = pltpu.make_async_copy(source, target, sems.at[len(copies)])
        copy.start()
        copies.append(copy)

    send(dk_ref, dk_hbm)
    send(dv_ref, dv_hbm)
    send(d_gain_ref, d_gain_hbm)
    tokens = hidden_ref.shape[0]
    place = place_ref[...]
    weight = weight_ref[...]
    total = jnp.zeros((tokens, COLS), F32)
    for cols in column_blocks():
        y = mm(place, stacked(y_refs, cols))
        out_ref[:, cols] = (hidden_ref[:, cols].astype(F32) + weight * y).astype(BF16)
        send(out_ref.at[:, cols], out_hbm.at[:, cols])
        total = total + y * grad_ref[:, cols].astype(F32)
    d_weight_ref[...] = col_to_row(jnp.sum(total, axis=1, keepdims=True))
    send(d_weight_ref, d_weight_hbm)
    for copy in copies:
        copy.wait()


def run(kernel, name, inputs, outputs, flops, scratch=(), limit=20 * MIB):
    nbytes = sum(x.size * x.dtype.itemsize for _, x in inputs) + sum(
        x.size * x.dtype.itemsize for _, x in outputs
    )
    spec = {space: pl.BlockSpec(memory_space=space) for space in (VMEM, HBM)}
    results = pl.pallas_call(
        kernel,
        out_shape=[x for _, x in outputs],
        in_specs=[spec[space] for space, _ in inputs],
        out_specs=[spec[space] for space, _ in outputs],
        scratch_shapes=list(scratch),
        compiler_params=pltpu.CompilerParams(vmem_limit_bytes=limit),
        cost_estimate=pl.CostEstimate(flops=flops, bytes_accessed=nbytes, transcendentals=0),
        name=name,
    )(*[pltpu.with_memory_space_constraint(x, HBM) if space is HBM else x for space, x in inputs])
    return list(results)


def placed(space, arrays):
    return [(space, x) for x in arrays]


def pairwise(value, axis, step):
    count = lax.axis_size(axis)
    return lax.ppermute(value, axis, [(i, i ^ step) for i in range(count)])


def exchange(pieces, capacity):
    count = lax.axis_size("exp")
    rows = EXP_DEV * capacity
    if len(pieces) == count:
        return [pieces[0]] + [pairwise(pieces[s], "exp", s) for s in range(1, count)]
    flat = pieces[0]
    blocks = [flat[s * rows : (s + 1) * rows] for s in range(count)]
    moved = [blocks[0]] + [pairwise(blocks[s], "exp", s) for s in range(1, count)]
    return [jnp.concatenate(moved, axis=0)]


def exchange_apart(pieces, capacity):
    if len(pieces) == 1:
        return exchange(pieces, capacity)
    return [
        piece if s == 0 or joined(s, len(pieces)) else pairwise(piece, "exp", s)
        for s, piece in enumerate(pieces)
    ]


def sum_over(value, axis, first=1, last=None):
    step = first
    while step < lax.axis_size(axis) and (last is None or step <= last):
        value = value + pairwise(value, axis, step)
        step *= 2
    return value


def shaped(shape, dtype):
    return jax.ShapeDtypeStruct(shape, dtype)


def per_device(
    queries,
    keys,
    values,
    resid,
    block_order,
    norm_gain,
    w_gate,
    w_down,
    routes,
    route_weight,
    d_out,
):
    query_rows = queries[0]
    resid_rows = resid[0]
    grad_rows = d_out[0]
    tokens = query_rows.shape[0]
    chosen = routes.reshape(1, tokens)
    gain = norm_gain.reshape(1, D)
    ctx_count = lax.axis_size("ctx")
    exp_count = lax.axis_size("exp")
    experts = EXP_DEV * exp_count
    capacity = 3 * tokens // (2 * experts)
    slots = experts * capacity
    rows = EXP_DEV * capacity
    piece_count = exp_count if rows % 16 == 0 else 1
    piece_shapes = [shaped((slots // piece_count, D), BF16)] * piece_count
    token_shape = shaped((tokens, D), BF16)
    kv_width = 2 * KEY_VALUE_HEADS * HEAD_SIZE
    attn_flops = 4 * tokens * ctx_count * tokens * QUERY_HEADS * HEAD_SIZE
    place_flops = 2 * slots * tokens * D
    expert_flops = 2 * slots * D * FFE * EXP_DEV

    own_keys, own_values = keys[0], values[0]
    all_keys = [own_keys] + [pairwise(own_keys, "ctx", s) for s in range(1, ctx_count)]
    all_values = [own_values] + [pairwise(own_values, "ctx", s) for s in range(1, ctx_count)]

    near = [grad_rows, own_keys, own_values, gain, query_rows, resid_rows]
    grad_rows, own_keys, own_values, gain, query_rows, resid_rows, slot, pos, weight, *send_grad = run(
        functools.partial(dispatch_kernel, ctx_count, experts, capacity),
        "dispatch_grads",
        placed(HBM, near + [route_weight, chosen, block_order]),
        placed(
            VMEM,
            [shaped(x.shape, x.dtype) for x in near]
            + [
                shaped((1, tokens), jnp.int32),
                shaped((ctx_count, tokens), jnp.int32),
                shaped((1, tokens), F32),
            ]
            + piece_shapes,
        ),
        place_flops,
        scratch=[
            pltpu.SMEM(block_order.shape, jnp.int32),
            pltpu.VMEM((1, tokens), jnp.int32),
            pltpu.SemaphoreType.DMA((9,)),
        ],
    )
    all_keys[0], all_values[0] = own_keys, own_values
    arrived_grad = exchange(send_grad, capacity)

    hidden, *send_x = run(
        functools.partial(attention_kernel, ctx_count),
        "attention_forward",
        placed(VMEM, [pos, slot, gain, query_rows, resid_rows] + all_keys + all_values),
        placed(VMEM, [token_shape] + piece_shapes),
        attn_flops + place_flops,
    )
    arrived_x = exchange(send_x, capacity)

    d_act, probs, down_near, gate_near, place, weight_wide = run(
        functools.partial(probs_kernel, ctx_count, capacity, piece_count),
        "act_grads_and_probs",
        placed(VMEM, [pos, slot, weight])
        + placed(HBM, [w_down, w_gate])
        + placed(VMEM, [query_rows] + all_keys + arrived_grad),
        placed(
            VMEM,
            [
                shaped((slots, FFE), F32),
                shaped((QUERY_HEADS // 2, ctx_count * tokens, 2 * tokens), F32),
                shaped(w_down.shape, BF16),
                shaped(w_gate.shape, BF16),
                shaped((tokens, slots), BF16),
                shaped((tokens, COLS), F32),
            ],
        ),
        expert_flops + attn_flops // 2,
        scratch=[pltpu.SemaphoreType.DMA((2,))],
    )

    return_shapes = []
    for s in range(piece_count):
        if joined(s, piece_count):
            return_shapes.append(shaped((2 * rows, D), BF16))
        else:
            return_shapes.extend([piece_shapes[0]] * 2)
    sent = run(
        functools.partial(expert_kernel, capacity, piece_count),
        "experts",
        placed(VMEM, [gate_near, down_near, d_act] + arrived_x),
        placed(VMEM, return_shapes),
        3 * expert_flops,
    )
    send_dn, send_y = split_parts(sent, piece_count)
    dn = exchange(send_dn, capacity)
    y = [
        dn[s] if joined(s, piece_count) else moved
        for s, moved in enumerate(exchange_apart(send_y, capacity))
    ]
    (terms,) = run(
        functools.partial(gain_kernel, piece_count, rows),
        "gain_terms",
        placed(VMEM, [gain] + arrived_x + send_dn),
        placed(VMEM, [shaped((GAIN_LINES, LANES), F32)]),
        2 * slots * D,
    )
    terms, place_back = lax.optimization_barrier((sum_over(terms, "dp"), place))
    terms = sum_over(terms, "exp", last=1)

    terms = jnp.pad(terms, ((0, WIDE_LINES - GAIN_LINES), (0, 0)))
    terms = sum_over(terms, "exp", first=2)[:GAIN_LINES]

    d_hidden, d_queries, kv_own, *kv_send = run(
        functools.partial(backward_kernel, ctx_count, piece_count, rows),
        "residual_attention_backward",
        placed(VMEM, [place_back, gain, hidden, grad_rows, query_rows, probs])
        + placed(VMEM, dn + all_keys + all_values),
        placed(HBM, [token_shape] * 2)
        + placed(
            VMEM,
            [shaped((tokens, kv_width), F32)]
            + [shaped((tokens, kv_width), BF16)] * (ctx_count - 1),
        ),
        attn_flops + place_flops,
        scratch=[
            pltpu.VMEM((tokens, D), BF16),
            pltpu.VMEM((tokens, D), BF16),
            pltpu.VMEM((tokens, D), F32),
            pltpu.SemaphoreType.DMA((1 + KEY_VALUE_HEADS,)),
        ],
    )
    terms, kv_own = lax.optimization_barrier((terms, kv_own))
    terms = sum_over(terms, "ctx")
    kv_arrived = [pairwise(part, "ctx", s) for s, part in enumerate(kv_send, 1)]

    kv_shape = shaped((tokens, kv_width // 2), BF16)
    final_shapes = [token_shape, kv_shape, kv_shape]
    final_shapes += [shaped((1, tokens), F32), shaped((GAIN_LINES, LANES), F32)]
    total_tokens = tokens * ctx_count * exp_count * lax.axis_size("dp")
    layer_out, d_keys, d_values, d_weight, d_gain = run(
        functools.partial(output_kernel, ctx_count, piece_count, rows, total_tokens),
        "layer_output",
        placed(
            VMEM,
            [place, weight_wide, terms, hidden, grad_rows, kv_own]
            + kv_arrived
            + y,
        ),
        placed(HBM, final_shapes),
        place_flops,
        scratch=[pltpu.VMEM(x.shape, x.dtype) for x in final_shapes]
        + [pltpu.SemaphoreType.DMA((4 + D // COLS,))],
    )
    return (
        layer_out[None],
        d_hidden[None],
        d_queries[None],
        d_keys[None],
        d_values[None],
        d_weight,
        d_gain.reshape(D),
    )


def solution(mesh):
    in_specs = (
        P(("exp", "dp"), "ctx", None),
        P(("exp", "dp"), "ctx", None),
        P(("exp", "dp"), "ctx", None),
        P(("exp", "dp"), "ctx", None),
        P(),
        P(),
        P("exp", None, None),
        P("exp", None, None),
        P(("exp", "dp"), "ctx", None),
        P(("exp", "dp"), "ctx"),
        P(("exp", "dp"), "ctx", None),
    )
    out_specs = (
        P(("exp", "dp"), "ctx", None),
        P(("exp", "dp"), "ctx", None),
        P(("exp", "dp"), "ctx", None),
        P(("exp", "dp"), "ctx", None),
        P(("exp", "dp"), "ctx", None),
        P(("exp", "dp"), "ctx"),
        P(),
    )
    return jax.shard_map(
        per_device, mesh=mesh, in_specs=in_specs, out_specs=out_specs, check_vma=False
    )
```

```python
import functools

import jax
import jax.numpy as jnp
from jax import lax
from jax.experimental import pallas as pl
from jax.experimental.pallas import tpu as pltpu
from jax.sharding import PartitionSpec as P

D = 2048
HEAD_SIZE = 128
QUERY_HEADS = 16
KEY_VALUE_HEADS = 2
GROUP = QUERY_HEADS // KEY_VALUE_HEADS
FFE = 384
EXP_DEV = 2
COLS = 256
LANES = 128
GAIN_LINES = D // LANES
SCALE = HEAD_SIZE ** (-0.5)
EXP2_SCALE = SCALE * 1.4426950408889634
F32 = jnp.float32
BF16 = jnp.bfloat16
NN = (((1,), (0,)), ((), ()))
NT = (((1,), (1,)), ((), ()))
MIB = 1 << 20
VMEM, HBM = pltpu.VMEM, pltpu.HBM


def mm(a, b, dims=NN):
    return lax.dot_general(a, b, dims, preferred_element_type=F32)


def iota(shape, dim):
    return lax.broadcasted_iota(jnp.int32, shape, dim)


def row_to_col(row):
    n = row.shape[1]
    eye = iota((n, n), 0) == iota((n, n), 1)
    return jnp.sum(jnp.where(eye, row.astype(F32), 0.0), axis=1, keepdims=True)


def col_to_row(col):
    n = col.shape[0]
    eye = iota((n, n), 0) == iota((n, n), 1)
    return jnp.sum(jnp.where(eye, col, 0.0), axis=0, keepdims=True)


def block_positions(order_ref, ctx_index, tokens):
    span = tokens // 8
    index = iota((1, tokens), 1)
    which = index // span
    start = jnp.zeros((1, tokens), jnp.int32)
    for b in range(8):
        start = jnp.where(which == b, order_ref[ctx_index * 8 + b], start)
    return start * span + index % span


def stacked(refs, cols=slice(None)):
    parts = [r[:, cols] for r in refs]
    return parts[0] if len(parts) == 1 else jnp.concatenate(parts, axis=0)


def column_blocks(width=D, step=COLS):
    return [slice(c, c + step) for c in range(0, width, step)]


def store_pieces(refs, cols, rows_value):
    at = 0
    for r in refs:
        n = r.shape[0]
        r[:, cols] = rows_value[at : at + n]
        at += n


def pair_cols(pair):
    start = 2 * pair * HEAD_SIZE
    return slice(start, start + HEAD_SIZE), slice(start + HEAD_SIZE, start + 2 * HEAD_SIZE)


def head_pair(ref, pair):
    first, second = pair_cols(pair)
    return jnp.concatenate([ref[:, first], ref[:, second]], axis=0)


def placement_rows(slot_row, slots):
    tokens = slot_row.shape[1]
    return jnp.where(iota((slots, tokens), 0) == slot_row, 1.0, 0.0).astype(BF16)


def placement_cols(slot_row, slots):
    tokens = slot_row.shape[1]
    slot_col = row_to_col(slot_row)
    return jnp.where(iota((tokens, slots), 1).astype(F32) == slot_col, 1.0, 0.0).astype(BF16)


def dispatch_kernel(count, experts, capacity, *refs):
    sources, refs = refs[:9], refs[9:]
    targets, refs = refs[:6], refs[6:]
    grad_ref = targets[0]
    slot_ref, pos_ref, weight_ref = refs[:3]
    send_refs = refs[3:-3]
    order_ref, routes_ref, sems = refs[-3:]
    targets = targets + (weight_ref, routes_ref, order_ref)
    copies = [
        pltpu.make_async_copy(source, target, sems.at[i])
        for i, (source, target) in enumerate(zip(sources, targets))
    ]
    for copy in copies[6:] + copies[:6]:
        copy.start()
    for copy in copies[6:]:
        copy.wait()
    tokens = routes_ref.shape[1]
    chosen = routes_ref[...]
    lanes = max(experts, 16)
    hits = jnp.where(iota((lanes, tokens), 0) == chosen, 1.0, 0.0)
    before = jnp.where(iota((tokens, tokens), 0) < iota((tokens, tokens), 1), 1.0, 0.0)
    earlier = mm(hits.astype(BF16), before.astype(BF16))
    rank = jnp.sum(hits * earlier, axis=0, keepdims=True).astype(jnp.int32)
    target = (chosen // EXP_DEV) ^ lax.axis_index("exp")
    slot = (target * EXP_DEV + chosen % EXP_DEV) * capacity + rank
    slot_ref[...] = slot
    me = lax.axis_index("ctx")
    for s in range(count):
        pos_ref[s : s + 1, :] = block_positions(order_ref, me ^ s, tokens)
    place = placement_rows(slot, experts * capacity)
    weight = row_to_col(weight_ref[...])
    copies[0].wait()
    for cols in column_blocks():
        scaled = (weight * grad_ref[:, cols].astype(F32)).astype(BF16)
        store_pieces(send_refs, cols, mm(place, scaled).astype(BF16))
    for copy in copies[1:6]:
        copy.wait()


def kv_stacks(key_refs, value_refs, g):
    cols = slice(g * HEAD_SIZE, (g + 1) * HEAD_SIZE)
    return stacked(key_refs, cols), stacked(value_refs, cols)


def attention_kernel(
    count, pos_ref, slot_ref, gain_ref, query_ref, resid_ref, *refs
):
    key_refs, value_refs = refs[:count], refs[count : 2 * count]
    hidden_ref, send_refs = refs[2 * count], refs[2 * count + 1 :]
    tokens = query_ref.shape[0]
    query_pos = row_to_col(pos_ref[:1, :])
    bias = jnp.concatenate(
        [
            jnp.where(pos_ref[s : s + 1, :].astype(F32) <= query_pos, 0.0, -1e30)
            for s in range(count)
        ],
        axis=1,
    )
    length = count * tokens
    ones = jnp.ones((length, HEAD_SIZE), BF16)
    total = jnp.zeros((tokens, HEAD_SIZE), F32)
    for g in range(KEY_VALUE_HEADS):
        keys, values = kv_stacks(key_refs, value_refs, g)
        values = jnp.concatenate([values, ones], axis=1)
        for h in range(g * GROUP, (g + 1) * GROUP):
            cols = slice(h * HEAD_SIZE, (h + 1) * HEAD_SIZE)
            scores = mm(query_ref[:, cols], keys, NT) + bias
            peak = jnp.max(scores, axis=1, keepdims=True)
            weights = jnp.exp2((scores - peak) * EXP2_SCALE).astype(BF16)
            mixed = mm(weights, values)
            attended = mixed[:, :HEAD_SIZE] / mixed[:, HEAD_SIZE:]
            hidden = (resid_ref[:, cols].astype(F32) + attended).astype(BF16)
            hidden_ref[:, cols] = hidden
            wide = hidden.astype(F32)
            total = total + wide * wide
    inv_rms = lax.rsqrt(jnp.sum(total, axis=1, keepdims=True) * (1.0 / D) + 1e-06)
    slots = sum(r.shape[0] for r in send_refs)
    place = placement_rows(slot_ref[...], slots)
    for cols in column_blocks():
        normed = (hidden_ref[:, cols].astype(F32) * inv_rms * gain_ref[:, cols]).astype(BF16)
        store_pieces(send_refs, cols, mm(place, normed).astype(BF16))


def first_expert_rows(slots, capacity):
    return iota((slots, 1), 0) % (EXP_DEV * capacity) < capacity


def probs_kernel(
    count,
    capacity,
    pieces,
    pos_ref,
    slot_ref,
    weight_ref,
    down_hbm,
    gate_hbm,
    query_ref,
    *refs,
):
    key_refs = refs[:count]
    grad_refs = refs[count : count + pieces]
    d_act_ref, probs_ref, down_ref, gate_ref, place_ref, wide_ref, sems = refs[count + pieces :]
    spans = [slice(e * FFE, (e + 1) * FFE) for e in range(EXP_DEV)]
    down_copies = [
        pltpu.make_async_copy(down_hbm.at[e], down_ref.at[span, :], sems.at[e])
        for e, span in enumerate(spans)
    ]
    gate_copies = [
        pltpu.make_async_copy(gate_hbm.at[e], gate_ref.at[:, span], sems.at[EXP_DEV + e])
        for e, span in enumerate(spans)
    ]
    for copy in down_copies + gate_copies:
        copy.start()
    place_ref[...] = placement_cols(slot_ref[...], place_ref.shape[1])
    wide_ref[...] = jnp.broadcast_to(row_to_col(weight_ref[...]), wide_ref.shape)
    query_pos = pos_ref[:1, :].astype(F32)
    bias = jnp.concatenate(
        [
            jnp.where(row_to_col(pos_ref[s : s + 1, :]) <= query_pos, 0.0, -1e30)
            for s in range(count)
        ],
        axis=0,
    )
    bias = jnp.concatenate([bias, bias], axis=1)
    for g in range(KEY_VALUE_HEADS):
        keys = stacked(key_refs, slice(g * HEAD_SIZE, (g + 1) * HEAD_SIZE))
        for pair in range(g * GROUP // 2, (g + 1) * GROUP // 2):
            scores = mm(keys, head_pair(query_ref, pair), NT) + bias
            peak = jnp.max(scores, axis=0, keepdims=True)
            weights = jnp.exp2((scores - peak) * EXP2_SCALE)
            probs_ref[pair] = weights * (1.0 / jnp.sum(weights, axis=0, keepdims=True))
    grads = stacked(grad_refs)
    first = first_expert_rows(grads.shape[0], capacity)
    for copy in down_copies:
        copy.wait()
    d_act = mm(grads, down_ref[...], NT)
    d_act_ref[...] = jnp.where(first, d_act[:, :FFE], d_act[:, FFE:])
    for copy in gate_copies:
        copy.wait()


def part_views(refs, rows, part):
    return [r if r.shape[0] != 2 * rows else r.at[part * rows : (part + 1) * rows] for r in refs]


def joined(step, pieces):
    return pieces > 1 and step > 0 and step & (step - 1) == 0


def split_parts(refs, pieces):
    back, out = [], []
    at = 0
    for s in range(pieces):
        back.append(refs[at])
        at += not joined(s, pieces)
        out.append(refs[at])
        at += 1
    return back, out


def expert_kernel(capacity, pieces, gate_ref, down_ref, d_act_ref, *refs):
    rows = stacked(refs[:pieces])
    back_refs, out_refs = split_parts(refs[pieces:], pieces)
    back_refs = part_views(back_refs, EXP_DEV * capacity, 0)
    out_refs = part_views(out_refs, EXP_DEV * capacity, 1)
    first = first_expert_rows(rows.shape[0], capacity)
    both = mm(rows, gate_ref[...])
    pre = jnp.where(first, both[:, :FFE], both[:, FFE:])
    gate = 1.0 / (1.0 + jnp.exp(-pre))
    act = pre * gate
    d_pre = d_act_ref[...] * gate * (1.0 + pre * (1.0 - gate))
    act, d_pre = [
        jnp.concatenate([jnp.where(first, x, 0.0), jnp.where(first, 0.0, x)], axis=1).astype(BF16)
        for x in (act, d_pre)
    ]
    for cols in column_blocks():
        store_pieces(back_refs, cols, mm(d_pre, gate_ref[cols, :], NT).astype(BF16))
        store_pieces(out_refs, cols, mm(act, down_ref[:, cols]).astype(BF16))


def gain_kernel(pieces, rows, gain_ref, *refs):
    row_refs = refs[:pieces]
    back_refs = part_views(refs[pieces:-1], rows, 0)
    terms_ref = refs[-1]
    for cols in column_blocks():
        products = stacked(row_refs, cols).astype(F32) * stacked(back_refs, cols).astype(F32)
        terms = jnp.sum(products, axis=0, keepdims=True) / gain_ref[:, cols]
        for at in range(0, COLS, LANES):
            line = (cols.start + at) // LANES
            terms_ref[line : line + 1, :] = terms[:, at : at + LANES]


def backward_kernel(
    count, pieces, rows, place_ref, gain_ref, hidden_ref, grad_ref, query_ref, probs_ref, *refs
):
    dn_refs = part_views(refs[:pieces], rows, 0)
    key_refs = refs[pieces : pieces + count]
    value_refs = refs[pieces + count : pieces + 2 * count]
    resid_hbm, dq_hbm, own_ref = refs[pieces + 2 * count : pieces + 2 * count + 3]
    other_refs = refs[pieces + 2 * count + 3 : -4]
    resid_ref, dq_ref, dn_scratch, sems = refs[-4:]
    tokens = hidden_ref.shape[0]
    place = place_ref[...]
    square = jnp.zeros((tokens, COLS), F32)
    mixing = jnp.zeros((tokens, COLS), F32)
    for cols in column_blocks():
        dn = mm(place, stacked(dn_refs, cols)) * gain_ref[:, cols]
        dn_scratch[:, cols] = dn
        hidden = hidden_ref[:, cols].astype(F32)
        square = square + hidden * hidden
        mixing = mixing + dn * hidden
    inv_rms = lax.rsqrt(jnp.sum(square, axis=1, keepdims=True) * (1.0 / D) + 1e-06)
    mean_mix = jnp.sum(mixing, axis=1, keepdims=True) * (1.0 / D)
    factor = inv_rms * inv_rms * inv_rms * mean_mix
    for cols in column_blocks():
        resid_ref[:, cols] = (
            grad_ref[:, cols].astype(F32)
            + dn_scratch[:, cols] * inv_rms
            - hidden_ref[:, cols].astype(F32) * factor
        ).astype(BF16)
    copies = [pltpu.make_async_copy(resid_ref, resid_hbm, sems.at[0])]
    copies[0].start()
    length = count * tokens
    group_width = GROUP * HEAD_SIZE
    for g in range(KEY_VALUE_HEADS):
        keys, values = kv_stacks(key_refs, value_refs, g)
        keys_t = jnp.transpose(keys.astype(F32)).astype(BF16)
        d_keys = jnp.zeros((length, HEAD_SIZE), F32)
        d_values = jnp.zeros((length, HEAD_SIZE), F32)
        for pair in range(g * GROUP // 2, (g + 1) * GROUP // 2):
            cols_a, cols_b = pair_cols(pair)
            d_out = head_pair(resid_ref, pair)
            probs = probs_ref[pair]
            d_probs = mm(values, d_out, NT)
            row_dot = jnp.sum(probs * d_probs, axis=0, keepdims=True)
            d_scores = (probs * (d_probs - row_dot)).astype(BF16)
            d_keys = d_keys + mm(d_scores, head_pair(query_ref, pair))
            d_values = d_values + mm(probs.astype(BF16), d_out)
            d_query_t = mm(keys_t, d_scores) * SCALE
            dq_ref[:, cols_a] = jnp.transpose(d_query_t[:, :tokens]).astype(BF16)
            dq_ref[:, cols_b] = jnp.transpose(d_query_t[:, tokens:]).astype(BF16)
        cols = slice(g * group_width, (g + 1) * group_width)
        copy = pltpu.make_async_copy(dq_ref.at[:, cols], dq_hbm.at[:, cols], sems.at[1 + g])
        copy.start()
        copies.append(copy)
        k_cols = slice(g * HEAD_SIZE, (g + 1) * HEAD_SIZE)
        v_cols = slice((KEY_VALUE_HEADS + g) * HEAD_SIZE, (KEY_VALUE_HEADS + g + 1) * HEAD_SIZE)
        d_keys = d_keys * SCALE
        own_ref[:, k_cols] = d_keys[:tokens]
        own_ref[:, v_cols] = d_values[:tokens]
        for s, ref in enumerate(other_refs, 1):
            ref[:, k_cols] = d_keys[s * tokens : (s + 1) * tokens].astype(BF16)
            ref[:, v_cols] = d_values[s * tokens : (s + 1) * tokens].astype(BF16)
    for copy in copies:
        copy.wait()


def output_kernel(
    count, pieces, rows, tokens_in_all, place_ref, weight_ref, gain_ref, hidden_ref, grad_ref, *refs
):
    own_ref, refs = refs[0], refs[1:]
    arrived_refs = refs[: count - 1]
    y_refs = part_views(refs[count - 1 : count - 1 + pieces], rows, 1)
    out_hbm, dk_hbm, dv_hbm, d_weight_hbm, d_gain_hbm = refs[count - 1 + pieces : -6]
    out_ref, dk_ref, dv_ref, d_weight_ref, d_gain_ref, sems = refs[-6:]
    split = KEY_VALUE_HEADS * HEAD_SIZE
    d_kv = own_ref[...]
    for ref in arrived_refs:
        d_kv = d_kv + ref[...].astype(F32)
    dk_ref[...] = d_kv[:, :split].astype(BF16)
    dv_ref[...] = d_kv[:, split:].astype(BF16)
    d_gain_ref[...] = gain_ref[...] * (1.0 / tokens_in_all)
    copies = []

    def send(source, target):
        copy = pltpu.make_async_copy(source, target, sems.at[len(copies)])
        copy.start()
        copies.append(copy)

    send(dk_ref, dk_hbm)
    send(dv_ref, dv_hbm)
    send(d_gain_ref, d_gain_hbm)
    tokens = hidden_ref.shape[0]
    place = place_ref[...]
    weight = weight_ref[...]
    total = jnp.zeros((tokens, COLS), F32)
    for cols in column_blocks():
        y = mm(place, stacked(y_refs, cols))
        out_ref[:, cols] = (hidden_ref[:, cols].astype(F32) + weight * y).astype(BF16)
        send(out_ref.at[:, cols], out_hbm.at[:, cols])
        total = total + y * grad_ref[:, cols].astype(F32)
    d_weight_ref[...] = col_to_row(jnp.sum(total, axis=1, keepdims=True))
    send(d_weight_ref, d_weight_hbm)
    for copy in copies:
        copy.wait()


def run(kernel, name, inputs, outputs, flops, scratch=(), limit=20 * MIB):
    nbytes = sum(x.size * x.dtype.itemsize for _, x in inputs) + sum(
        x.size * x.dtype.itemsize for _, x in outputs
    )
    spec = {space: pl.BlockSpec(memory_space=space) for space in (VMEM, HBM)}
    results = pl.pallas_call(
        kernel,
        out_shape=[x for _, x in outputs],
        in_specs=[spec[space] for space, _ in inputs],
        out_specs=[spec[space] for space, _ in outputs],
        scratch_shapes=list(scratch),
        compiler_params=pltpu.CompilerParams(vmem_limit_bytes=limit),
        cost_estimate=pl.CostEstimate(flops=flops, bytes_accessed=nbytes, transcendentals=0),
        name=name,
    )(*[pltpu.with_memory_space_constraint(x, HBM) if space is HBM else x for space, x in inputs])
    return list(results)


def placed(space, arrays):
    return [(space, x) for x in arrays]


def pairwise(value, axis, step):
    count = lax.axis_size(axis)
    return lax.ppermute(value, axis, [(i, i ^ step) for i in range(count)])


def exchange(pieces, capacity):
    count = lax.axis_size("exp")
    rows = EXP_DEV * capacity
    if len(pieces) == count:
        return [pieces[0]] + [pairwise(pieces[s], "exp", s) for s in range(count - 1, 0, -1)][::-1]
    flat = pieces[0]
    blocks = [flat[s * rows : (s + 1) * rows] for s in range(count)]
    moved = [blocks[0]] + [pairwise(blocks[s], "exp", s) for s in range(1, count)]
    return [jnp.concatenate(moved, axis=0)]


def exchange_apart(pieces, capacity):
    if len(pieces) == 1:
        return exchange(pieces, capacity)
    return [
        piece if s == 0 or joined(s, len(pieces)) else pairwise(piece, "exp", s)
        for s, piece in enumerate(pieces)
    ]


def sum_over(value, axis):
    step = 1
    while step < lax.axis_size(axis):
        value = value + pairwise(value, axis, step)
        step *= 2
    return value


def tree_sum(parts):
    while len(parts) > 1:
        parts = [parts[i] + parts[i + 1] for i in range(0, len(parts), 2)]
    return parts[0]


def shaped(shape, dtype):
    return jax.ShapeDtypeStruct(shape, dtype)


def per_device(
    queries,
    keys,
    values,
    resid,
    block_order,
    norm_gain,
    w_gate,
    w_down,
    routes,
    route_weight,
    d_out,
):
    query_rows = queries[0]
    resid_rows = resid[0]
    grad_rows = d_out[0]
    tokens = query_rows.shape[0]
    chosen = routes.reshape(1, tokens)
    gain = norm_gain.reshape(1, D)
    ctx_count = lax.axis_size("ctx")
    exp_count = lax.axis_size("exp")
    experts = EXP_DEV * exp_count
    capacity = 3 * tokens // (2 * experts)
    slots = experts * capacity
    rows = EXP_DEV * capacity
    piece_count = exp_count if rows % 16 == 0 else 1
    piece_shapes = [shaped((slots // piece_count, D), BF16)] * piece_count
    token_shape = shaped((tokens, D), BF16)
    kv_width = 2 * KEY_VALUE_HEADS * HEAD_SIZE
    attn_flops = 4 * tokens * ctx_count * tokens * QUERY_HEADS * HEAD_SIZE
    place_flops = 2 * slots * tokens * D
    expert_flops = 2 * slots * D * FFE * EXP_DEV

    own_keys, own_values = keys[0], values[0]
    all_keys = [own_keys] + [pairwise(own_keys, "ctx", s) for s in range(1, ctx_count)]
    all_values = [own_values] + [pairwise(own_values, "ctx", s) for s in range(1, ctx_count)]

    near = [grad_rows, own_keys, own_values, gain, query_rows, resid_rows]
    grad_rows, own_keys, own_values, gain, query_rows, resid_rows, slot, pos, weight, *send_grad = run(
        functools.partial(dispatch_kernel, ctx_count, experts, capacity),
        "dispatch_grads",
        placed(HBM, near + [route_weight, chosen, block_order]),
        placed(
            VMEM,
            [shaped(x.shape, x.dtype) for x in near]
            + [
                shaped((1, tokens), jnp.int32),
                shaped((ctx_count, tokens), jnp.int32),
                shaped((1, tokens), F32),
            ]
            + piece_shapes,
        ),
        place_flops,
        scratch=[
            pltpu.SMEM(block_order.shape, jnp.int32),
            pltpu.VMEM((1, tokens), jnp.int32),
            pltpu.SemaphoreType.DMA((9,)),
        ],
    )
    all_keys[0], all_values[0] = own_keys, own_values
    apart = [s for s in range(1, piece_count) if not joined(s, piece_count)]
    near = [s for s in range(1, piece_count) if joined(s, piece_count)]
    arrived_grad = exchange(send_grad, capacity) if piece_count == 1 else list(send_grad)
    for s in apart:
        arrived_grad[s] = pairwise(send_grad[s], "exp", s)

    hidden, *send_x = run(
        functools.partial(attention_kernel, ctx_count),
        "attention_forward",
        placed(VMEM, [pos, slot, gain, query_rows, resid_rows] + all_keys + all_values),
        placed(VMEM, [token_shape] + piece_shapes),
        attn_flops + place_flops,
    )
    arrived_x = exchange(send_x, capacity) if piece_count == 1 else list(send_x)
    for s in apart:
        arrived_x[s] = pairwise(send_x[s], "exp", s)
    if near:
        after, _ = lax.optimization_barrier(([send_grad[s] for s in near], send_x[0]))
        for s, piece in zip(near, after):
            arrived_grad[s] = pairwise(piece, "exp", s)
        for s in near:
            arrived_x[s] = pairwise(send_x[s], "exp", s)

    d_act, probs, down_near, gate_near, place, weight_wide = run(
        functools.partial(probs_kernel, ctx_count, capacity, piece_count),
        "act_grads_and_probs",
        placed(VMEM, [pos, slot, weight])
        + placed(HBM, [w_down, w_gate])
        + placed(VMEM, [query_rows] + all_keys + arrived_grad),
        placed(
            VMEM,
            [
                shaped((slots, FFE), F32),
                shaped((QUERY_HEADS // 2, ctx_count * tokens, 2 * tokens), F32),
                shaped((EXP_DEV * FFE, D), BF16),
                shaped((D, EXP_DEV * FFE), BF16),
                shaped((tokens, slots), BF16),
                shaped((tokens, COLS), F32),
            ],
        ),
        expert_flops + attn_flops // 2,
        scratch=[pltpu.SemaphoreType.DMA((2 * EXP_DEV,))],
    )

    return_shapes = []
    for s in range(piece_count):
        if joined(s, piece_count):
            return_shapes.append(shaped((2 * rows, D), BF16))
        else:
            return_shapes.extend([piece_shapes[0]] * 2)
    sent = run(
        functools.partial(expert_kernel, capacity, piece_count),
        "experts",
        placed(VMEM, [gate_near, down_near, d_act] + arrived_x),
        placed(VMEM, return_shapes),
        3 * expert_flops,
    )
    send_dn, send_y = split_parts(sent, piece_count)
    dn = exchange(send_dn, capacity)
    y = [
        dn[s] if joined(s, piece_count) else moved
        for s, moved in enumerate(exchange_apart(send_y, capacity))
    ]
    (terms,) = run(
        functools.partial(gain_kernel, piece_count, rows),
        "gain_terms",
        placed(VMEM, [gain] + arrived_x + send_dn),
        placed(VMEM, [shaped((GAIN_LINES, LANES), F32)]),
        2 * slots * D,
    )
    terms, place_back = lax.optimization_barrier((sum_over(terms, "dp"), place))

    if piece_count == 1:
        terms = sum_over(terms, "exp")
    else:
        terms = tree_sum([terms] + [pairwise(terms, "exp", s) for s in range(1, exp_count)])

    d_hidden, d_queries, kv_own, *kv_send = run(
        functools.partial(backward_kernel, ctx_count, piece_count, rows),
        "residual_attention_backward",
        placed(VMEM, [place_back, gain, hidden, grad_rows, query_rows, probs])
        + placed(VMEM, dn + all_keys + all_values),
        placed(HBM, [token_shape] * 2)
        + placed(
            VMEM,
            [shaped((tokens, kv_width), F32)]
            + [shaped((tokens, kv_width), BF16)] * (ctx_count - 1),
        ),
        attn_flops + place_flops,
        scratch=[
            pltpu.VMEM((tokens, D), BF16),
            pltpu.VMEM((tokens, D), BF16),
            pltpu.VMEM((tokens, D), F32),
            pltpu.SemaphoreType.DMA((1 + KEY_VALUE_HEADS,)),
        ],
    )
    terms, kv_own = lax.optimization_barrier((terms, kv_own))
    terms = sum_over(terms, "ctx")
    kv_arrived = [pairwise(part, "ctx", s) for s, part in enumerate(kv_send, 1)]

    kv_shape = shaped((tokens, kv_width // 2), BF16)
    final_shapes = [token_shape, kv_shape, kv_shape]
    final_shapes += [shaped((1, tokens), F32), shaped((GAIN_LINES, LANES), F32)]
    total_tokens = tokens * ctx_count * exp_count * lax.axis_size("dp")
    layer_out, d_keys, d_values, d_weight, d_gain = run(
        functools.partial(output_kernel, ctx_count, piece_count, rows, total_tokens),
        "layer_output",
        placed(
            VMEM,
            [place, weight_wide, terms, hidden, grad_rows, kv_own]
            + kv_arrived
            + y,
        ),
        placed(HBM, final_shapes),
        place_flops,
        scratch=[pltpu.VMEM(x.shape, x.dtype) for x in final_shapes]
        + [pltpu.SemaphoreType.DMA((4 + D // COLS,))],
    )
    return (
        layer_out[None],
        d_hidden[None],
        d_queries[None],
        d_keys[None],
        d_values[None],
        d_weight,
        d_gain.reshape(D),
    )


def solution(mesh):
    in_specs = (
        P(("exp", "dp"), "ctx", None),
        P(("exp", "dp"), "ctx", None),
        P(("exp", "dp"), "ctx", None),
        P(("exp", "dp"), "ctx", None),
        P(),
        P(),
        P("exp", None, None),
        P("exp", None, None),
        P(("exp", "dp"), "ctx", None),
        P(("exp", "dp"), "ctx"),
        P(("exp", "dp"), "ctx", None),
    )
    out_specs = (
        P(("exp", "dp"), "ctx", None),
        P(("exp", "dp"), "ctx", None),
        P(("exp", "dp"), "ctx", None),
        P(("exp", "dp"), "ctx", None),
        P(("exp", "dp"), "ctx", None),
        P(("exp", "dp"), "ctx"),
        P(),
    )
    return jax.shard_map(
        per_device, mesh=mesh, in_specs=in_specs, out_specs=out_specs, check_vma=False
    )
```

```python
import functools

import jax
import jax.numpy as jnp
from jax import lax
from jax.experimental import pallas as pl
from jax.experimental.pallas import tpu as pltpu
from jax.sharding import PartitionSpec as P

D = 2048
HEAD_SIZE = 128
QUERY_HEADS = 16
KEY_VALUE_HEADS = 2
GROUP = QUERY_HEADS // KEY_VALUE_HEADS
FFE = 384
EXP_DEV = 2
COLS = 256
LANES = 128
GAIN_LINES = D // LANES
WIDE_LINES = 128
SCALE = HEAD_SIZE ** (-0.5)
EXP2_SCALE = SCALE * 1.4426950408889634
F32 = jnp.float32
BF16 = jnp.bfloat16
NN = (((1,), (0,)), ((), ()))
NT = (((1,), (1,)), ((), ()))
MIB = 1 << 20
VMEM, HBM = pltpu.VMEM, pltpu.HBM


def mm(a, b, dims=NN):
    return lax.dot_general(a, b, dims, preferred_element_type=F32)


def iota(shape, dim):
    return lax.broadcasted_iota(jnp.int32, shape, dim)


def row_to_col(row):
    n = row.shape[1]
    eye = iota((n, n), 0) == iota((n, n), 1)
    return jnp.sum(jnp.where(eye, row.astype(F32), 0.0), axis=1, keepdims=True)


def col_to_row(col):
    n = col.shape[0]
    eye = iota((n, n), 0) == iota((n, n), 1)
    return jnp.sum(jnp.where(eye, col, 0.0), axis=0, keepdims=True)


def block_positions(order_ref, ctx_index, tokens):
    span = tokens // 8
    index = iota((1, tokens), 1)
    which = index // span
    start = jnp.zeros((1, tokens), jnp.int32)
    for b in range(8):
        start = jnp.where(which == b, order_ref[ctx_index * 8 + b], start)
    return start * span + index % span


def stacked(refs, cols=slice(None)):
    parts = [r[:, cols] for r in refs]
    return parts[0] if len(parts) == 1 else jnp.concatenate(parts, axis=0)


def column_blocks(width=D, step=COLS):
    return [slice(c, c + step) for c in range(0, width, step)]


def store_pieces(refs, cols, rows_value):
    at = 0
    for r in refs:
        n = r.shape[0]
        r[:, cols] = rows_value[at : at + n]
        at += n


def pair_cols(pair):
    start = 2 * pair * HEAD_SIZE
    return slice(start, start + HEAD_SIZE), slice(start + HEAD_SIZE, start + 2 * HEAD_SIZE)


def head_pair(ref, pair):
    first, second = pair_cols(pair)
    return jnp.concatenate([ref[:, first], ref[:, second]], axis=0)


def placement_rows(slot_row, slots):
    tokens = slot_row.shape[1]
    return jnp.where(iota((slots, tokens), 0) == slot_row, 1.0, 0.0).astype(BF16)


def placement_cols(slot_row, slots):
    tokens = slot_row.shape[1]
    slot_col = row_to_col(slot_row)
    return jnp.where(iota((tokens, slots), 1).astype(F32) == slot_col, 1.0, 0.0).astype(BF16)


def dispatch_kernel(count, experts, capacity, *refs):
    sources, refs = refs[:9], refs[9:]
    targets, refs = refs[:6], refs[6:]
    grad_ref = targets[0]
    slot_ref, pos_ref, weight_ref = refs[:3]
    send_refs = refs[3:-3]
    order_ref, routes_ref, sems = refs[-3:]
    targets = targets + (weight_ref, routes_ref, order_ref)
    copies = [
        pltpu.make_async_copy(source, target, sems.at[i])
        for i, (source, target) in enumerate(zip(sources, targets))
    ]
    for copy in copies[6:] + copies[:6]:
        copy.start()
    for copy in copies[6:]:
        copy.wait()
    tokens = routes_ref.shape[1]
    chosen = routes_ref[...]
    lanes = max(experts, 16)
    hits = jnp.where(iota((lanes, tokens), 0) == chosen, 1.0, 0.0)
    before = jnp.where(iota((tokens, tokens), 0) < iota((tokens, tokens), 1), 1.0, 0.0)
    earlier = mm(hits.astype(BF16), before.astype(BF16))
    rank = jnp.sum(hits * earlier, axis=0, keepdims=True).astype(jnp.int32)
    target = (chosen // EXP_DEV) ^ lax.axis_index("exp")
    slot = (target * EXP_DEV + chosen % EXP_DEV) * capacity + rank
    slot_ref[...] = slot
    me = lax.axis_index("ctx")
    for s in range(count):
        pos_ref[s : s + 1, :] = block_positions(order_ref, me ^ s, tokens)
    place = placement_rows(slot, experts * capacity)
    weight = row_to_col(weight_ref[...])
    copies[0].wait()
    for cols in column_blocks():
        scaled = (weight * grad_ref[:, cols].astype(F32)).astype(BF16)
        store_pieces(send_refs, cols, mm(place, scaled).astype(BF16))
    for copy in copies[1:6]:
        copy.wait()


def kv_stacks(key_refs, value_refs, g):
    cols = slice(g * HEAD_SIZE, (g + 1) * HEAD_SIZE)
    return stacked(key_refs, cols), stacked(value_refs, cols)


def attention_kernel(
    count, pos_ref, slot_ref, gain_ref, query_ref, resid_ref, *refs
):
    key_refs, value_refs = refs[:count], refs[count : 2 * count]
    hidden_ref, send_refs = refs[2 * count], refs[2 * count + 1 :]
    tokens = query_ref.shape[0]
    query_pos = row_to_col(pos_ref[:1, :])
    bias = jnp.concatenate(
        [
            jnp.where(pos_ref[s : s + 1, :].astype(F32) <= query_pos, 0.0, -1e30)
            for s in range(count)
        ],
        axis=1,
    )
    length = count * tokens
    ones = jnp.ones((length, HEAD_SIZE), BF16)
    total = jnp.zeros((tokens, HEAD_SIZE), F32)
    for g in range(KEY_VALUE_HEADS):
        keys, values = kv_stacks(key_refs, value_refs, g)
        values = jnp.concatenate([values, ones], axis=1)
        for h in range(g * GROUP, (g + 1) * GROUP):
            cols = slice(h * HEAD_SIZE, (h + 1) * HEAD_SIZE)
            scores = mm(query_ref[:, cols], keys, NT) + bias
            peak = jnp.max(scores, axis=1, keepdims=True)
            weights = jnp.exp2((scores - peak) * EXP2_SCALE).astype(BF16)
            mixed = mm(weights, values)
            attended = mixed[:, :HEAD_SIZE] / mixed[:, HEAD_SIZE:]
            hidden = (resid_ref[:, cols].astype(F32) + attended).astype(BF16)
            hidden_ref[:, cols] = hidden
            wide = hidden.astype(F32)
            total = total + wide * wide
    inv_rms = lax.rsqrt(jnp.sum(total, axis=1, keepdims=True) * (1.0 / D) + 1e-06)
    slots = sum(r.shape[0] for r in send_refs)
    place = placement_rows(slot_ref[...], slots)
    for cols in column_blocks():
        normed = (hidden_ref[:, cols].astype(F32) * inv_rms * gain_ref[:, cols]).astype(BF16)
        store_pieces(send_refs, cols, mm(place, normed).astype(BF16))


def first_expert_rows(slots, capacity):
    return iota((slots, 1), 0) % (EXP_DEV * capacity) < capacity


def probs_kernel(
    count,
    capacity,
    pieces,
    pos_ref,
    slot_ref,
    weight_ref,
    down_hbm,
    gate_hbm,
    query_ref,
    *refs,
):
    key_refs = refs[:count]
    grad_refs = refs[count : count + pieces]
    d_act_ref, probs_ref, down_ref, gate_ref, place_ref, wide_ref, sems = refs[count + pieces :]
    spans = [slice(e * FFE, (e + 1) * FFE) for e in range(EXP_DEV)]
    down_copies = [
        pltpu.make_async_copy(down_hbm.at[e], down_ref.at[span, :], sems.at[e])
        for e, span in enumerate(spans)
    ]
    gate_copies = [
        pltpu.make_async_copy(gate_hbm.at[e], gate_ref.at[:, span], sems.at[EXP_DEV + e])
        for e, span in enumerate(spans)
    ]
    for copy in down_copies + gate_copies:
        copy.start()
    place_ref[...] = placement_cols(slot_ref[...], place_ref.shape[1])
    wide_ref[...] = jnp.broadcast_to(row_to_col(weight_ref[...]), wide_ref.shape)
    query_pos = pos_ref[:1, :].astype(F32)
    bias = jnp.concatenate(
        [
            jnp.where(row_to_col(pos_ref[s : s + 1, :]) <= query_pos, 0.0, -1e30)
            for s in range(count)
        ],
        axis=0,
    )
    bias = jnp.concatenate([bias, bias], axis=1)
    for g in range(KEY_VALUE_HEADS):
        keys = stacked(key_refs, slice(g * HEAD_SIZE, (g + 1) * HEAD_SIZE))
        for pair in range(g * GROUP // 2, (g + 1) * GROUP // 2):
            scores = mm(keys, head_pair(query_ref, pair), NT) + bias
            peak = jnp.max(scores, axis=0, keepdims=True)
            weights = jnp.exp2((scores - peak) * EXP2_SCALE)
            probs_ref[pair] = weights * (1.0 / jnp.sum(weights, axis=0, keepdims=True))
    grads = stacked(grad_refs)
    first = first_expert_rows(grads.shape[0], capacity)
    for copy in down_copies:
        copy.wait()
    d_act = mm(grads, down_ref[...], NT)
    d_act_ref[...] = jnp.where(first, d_act[:, :FFE], d_act[:, FFE:])
    for copy in gate_copies:
        copy.wait()


def expert_back_kernel(capacity, pieces, start, gate_ref, d_act_ref, *refs):
    rows = stacked(refs[:pieces])
    act_ref, back_refs = refs[pieces], refs[pieces + 1 :]
    count = rows.shape[0]
    first = first_expert_rows(count, capacity)
    both = mm(rows, gate_ref[...])
    pre = jnp.where(first, both[:, :FFE], both[:, FFE:])
    gate = 1.0 / (1.0 + jnp.exp(-pre))
    act = pre * gate
    d_pre = d_act_ref[start : start + count, :] * gate * (1.0 + pre * (1.0 - gate))
    act, d_pre = [
        jnp.concatenate([jnp.where(first, x, 0.0), jnp.where(first, 0.0, x)], axis=1).astype(BF16)
        for x in (act, d_pre)
    ]
    act_ref[...] = act
    for cols in column_blocks():
        store_pieces(back_refs, cols, mm(d_pre, gate_ref[cols, :], NT).astype(BF16))


def expert_out_kernel(pieces, acts, down_ref, gain_ref, *refs):
    act = stacked(refs[:acts])
    refs = refs[acts:]
    row_refs, back_refs = refs[:pieces], refs[pieces : 2 * pieces]
    terms_ref, out_refs = refs[2 * pieces], refs[2 * pieces + 1 :]
    for cols in column_blocks():
        store_pieces(out_refs, cols, mm(act, down_ref[:, cols]).astype(BF16))
        products = stacked(row_refs, cols).astype(F32) * stacked(back_refs, cols).astype(F32)
        terms = jnp.sum(products, axis=0, keepdims=True) / gain_ref[:, cols]
        for at in range(0, COLS, LANES):
            line = (cols.start + at) // LANES
            terms_ref[line : line + 1, :] = terms[:, at : at + LANES]


def backward_kernel(
    count, pieces, place_ref, gain_ref, hidden_ref, grad_ref, query_ref, probs_ref, *refs
):
    dn_refs = refs[:pieces]
    key_refs = refs[pieces : pieces + count]
    value_refs = refs[pieces + count : pieces + 2 * count]
    resid_hbm, dq_hbm, own_ref = refs[pieces + 2 * count : pieces + 2 * count + 3]
    other_refs = refs[pieces + 2 * count + 3 : -4]
    resid_ref, dq_ref, dn_scratch, sems = refs[-4:]
    tokens = hidden_ref.shape[0]
    place = place_ref[...]
    square = jnp.zeros((tokens, COLS), F32)
    mixing = jnp.zeros((tokens, COLS), F32)
    for cols in column_blocks():
        dn = mm(place, stacked(dn_refs, cols)) * gain_ref[:, cols]
        dn_scratch[:, cols] = dn
        hidden = hidden_ref[:, cols].astype(F32)
        square = square + hidden * hidden
        mixing = mixing + dn * hidden
    inv_rms = lax.rsqrt(jnp.sum(square, axis=1, keepdims=True) * (1.0 / D) + 1e-06)
    mean_mix = jnp.sum(mixing, axis=1, keepdims=True) * (1.0 / D)
    factor = inv_rms * inv_rms * inv_rms * mean_mix
    for cols in column_blocks():
        resid_ref[:, cols] = (
            grad_ref[:, cols].astype(F32)
            + dn_scratch[:, cols] * inv_rms
            - hidden_ref[:, cols].astype(F32) * factor
        ).astype(BF16)
    copies = [pltpu.make_async_copy(resid_ref, resid_hbm, sems.at[0])]
    copies[0].start()
    length = count * tokens
    group_width = GROUP * HEAD_SIZE
    for g in range(KEY_VALUE_HEADS):
        keys, values = kv_stacks(key_refs, value_refs, g)
        keys_t = jnp.transpose(keys.astype(F32)).astype(BF16)
        d_keys = jnp.zeros((length, HEAD_SIZE), F32)
        d_values = jnp.zeros((length, HEAD_SIZE), F32)
        for pair in range(g * GROUP // 2, (g + 1) * GROUP // 2):
            cols_a, cols_b = pair_cols(pair)
            d_out = head_pair(resid_ref, pair)
            probs = probs_ref[pair]
            d_probs = mm(values, d_out, NT)
            row_dot = jnp.sum(probs * d_probs, axis=0, keepdims=True)
            d_scores = (probs * (d_probs - row_dot)).astype(BF16)
            d_keys = d_keys + mm(d_scores, head_pair(query_ref, pair))
            d_values = d_values + mm(probs.astype(BF16), d_out)
            d_query_t = mm(keys_t, d_scores) * SCALE
            dq_ref[:, cols_a] = jnp.transpose(d_query_t[:, :tokens]).astype(BF16)
            dq_ref[:, cols_b] = jnp.transpose(d_query_t[:, tokens:]).astype(BF16)
        cols = slice(g * group_width, (g + 1) * group_width)
        copy = pltpu.make_async_copy(dq_ref.at[:, cols], dq_hbm.at[:, cols], sems.at[1 + g])
        copy.start()
        copies.append(copy)
        k_cols = slice(g * HEAD_SIZE, (g + 1) * HEAD_SIZE)
        v_cols = slice((KEY_VALUE_HEADS + g) * HEAD_SIZE, (KEY_VALUE_HEADS + g + 1) * HEAD_SIZE)
        d_keys = d_keys * SCALE
        own_ref[:, k_cols] = d_keys[:tokens]
        own_ref[:, v_cols] = d_values[:tokens]
        for s, ref in enumerate(other_refs, 1):
            ref[:, k_cols] = d_keys[s * tokens : (s + 1) * tokens].astype(BF16)
            ref[:, v_cols] = d_values[s * tokens : (s + 1) * tokens].astype(BF16)
    for copy in copies:
        copy.wait()


def output_kernel(
    count, pieces, tokens_in_all, place_ref, weight_ref, gain_ref, hidden_ref, grad_ref, *refs
):
    own_ref, refs = refs[0], refs[1:]
    arrived_refs = refs[: count - 1]
    y_refs = refs[count - 1 : count - 1 + pieces]
    out_hbm, dk_hbm, dv_hbm, d_weight_hbm, d_gain_hbm = refs[count - 1 + pieces : -6]
    out_ref, dk_ref, dv_ref, d_weight_ref, d_gain_ref, sems = refs[-6:]
    split = KEY_VALUE_HEADS * HEAD_SIZE
    d_kv = own_ref[...]
    for ref in arrived_refs:
        d_kv = d_kv + ref[...].astype(F32)
    dk_ref[...] = d_kv[:, :split].astype(BF16)
    dv_ref[...] = d_kv[:, split:].astype(BF16)
    d_gain_ref[...] = gain_ref[...] * (1.0 / tokens_in_all)
    copies = []

    def send(source, target):
        copy = pltpu.make_async_copy(source, target, sems.at[len(copies)])
        copy.start()
        copies.append(copy)

    send(dk_ref, dk_hbm)
    send(dv_ref, dv_hbm)
    send(d_gain_ref, d_gain_hbm)
    tokens = hidden_ref.shape[0]
    place = place_ref[...]
    weight = weight_ref[...]
    total = jnp.zeros((tokens, COLS), F32)
    for cols in column_blocks():
        y = mm(place, stacked(y_refs, cols))
        out_ref[:, cols] = (hidden_ref[:, cols].astype(F32) + weight * y).astype(BF16)
        send(out_ref.at[:, cols], out_hbm.at[:, cols])
        total = total + y * grad_ref[:, cols].astype(F32)
    d_weight_ref[...] = col_to_row(jnp.sum(total, axis=1, keepdims=True))
    send(d_weight_ref, d_weight_hbm)
    for copy in copies:
        copy.wait()


def run(kernel, name, inputs, outputs, flops, scratch=(), limit=20 * MIB):
    nbytes = sum(x.size * x.dtype.itemsize for _, x in inputs) + sum(
        x.size * x.dtype.itemsize for _, x in outputs
    )
    spec = {space: pl.BlockSpec(memory_space=space) for space in (VMEM, HBM)}
    results = pl.pallas_call(
        kernel,
        out_shape=[x for _, x in outputs],
        in_specs=[spec[space] for space, _ in inputs],
        out_specs=[spec[space] for space, _ in outputs],
        scratch_shapes=list(scratch),
        compiler_params=pltpu.CompilerParams(vmem_limit_bytes=limit),
        cost_estimate=pl.CostEstimate(flops=flops, bytes_accessed=nbytes, transcendentals=0),
        name=name,
    )(*[pltpu.with_memory_space_constraint(x, HBM) if space is HBM else x for space, x in inputs])
    return list(results)


def placed(space, arrays):
    return [(space, x) for x in arrays]


def pairwise(value, axis, step):
    count = lax.axis_size(axis)
    return lax.ppermute(value, axis, [(i, i ^ step) for i in range(count)])


def exchange_flat(flat, capacity):
    count = lax.axis_size("exp")
    rows = EXP_DEV * capacity
    blocks = [flat[s * rows : (s + 1) * rows] for s in range(count)]
    moved = [blocks[0]] + [pairwise(blocks[s], "exp", s) for s in range(1, count)]
    return jnp.concatenate(moved, axis=0)


def exchange(pieces, capacity, steps):
    if lax.axis_size("exp") != len(pieces):
        return [exchange_flat(pieces[0], capacity)]
    return [
        pairwise(piece, "exp", s) if s in steps and s > 0 else piece for s, piece in enumerate(pieces)
    ]


def sum_over(value, axis, first=1, last=None):
    step = first
    while step < lax.axis_size(axis) and (last is None or step <= last):
        value = value + pairwise(value, axis, step)
        step *= 2
    return value


def shaped(shape, dtype):
    return jax.ShapeDtypeStruct(shape, dtype)


def per_device(
    queries,
    keys,
    values,
    resid,
    block_order,
    norm_gain,
    w_gate,
    w_down,
    routes,
    route_weight,
    d_out,
):
    query_rows = queries[0]
    resid_rows = resid[0]
    grad_rows = d_out[0]
    tokens = query_rows.shape[0]
    chosen = routes.reshape(1, tokens)
    gain = norm_gain.reshape(1, D)
    ctx_count = lax.axis_size("ctx")
    exp_count = lax.axis_size("exp")
    experts = EXP_DEV * exp_count
    capacity = 3 * tokens // (2 * experts)
    slots = experts * capacity
    rows = EXP_DEV * capacity
    piece_count = exp_count if rows % 16 == 0 else 1
    piece_shapes = [shaped((slots // piece_count, D), BF16)] * piece_count
    token_shape = shaped((tokens, D), BF16)
    kv_width = 2 * KEY_VALUE_HEADS * HEAD_SIZE
    attn_flops = 4 * tokens * ctx_count * tokens * QUERY_HEADS * HEAD_SIZE
    place_flops = 2 * slots * tokens * D
    expert_flops = 2 * slots * D * FFE * EXP_DEV

    own_keys, own_values = keys[0], values[0]
    all_keys = [own_keys] + [pairwise(own_keys, "ctx", s) for s in range(1, ctx_count)]
    all_values = [own_values] + [pairwise(own_values, "ctx", s) for s in range(1, ctx_count)]

    near = [grad_rows, own_keys, own_values, gain, query_rows, resid_rows]
    grad_rows, own_keys, own_values, gain, query_rows, resid_rows, slot, pos, weight, *send_grad = run(
        functools.partial(dispatch_kernel, ctx_count, experts, capacity),
        "dispatch_grads",
        placed(HBM, near + [route_weight, chosen, block_order]),
        placed(
            VMEM,
            [shaped(x.shape, x.dtype) for x in near]
            + [
                shaped((1, tokens), jnp.int32),
                shaped((ctx_count, tokens), jnp.int32),
                shaped((1, tokens), F32),
            ]
            + piece_shapes,
        ),
        place_flops,
        scratch=[
            pltpu.SMEM(block_order.shape, jnp.int32),
            pltpu.VMEM((1, tokens), jnp.int32),
            pltpu.SemaphoreType.DMA((9,)),
        ],
    )
    all_keys[0], all_values[0] = own_keys, own_values
    steps = range(piece_count)
    groups = [[s for s in steps if s & (s - 1) == 0], [s for s in steps if s & (s - 1) != 0]]
    groups = [group for group in groups if group]
    arrived_grad = exchange(send_grad, capacity, steps)

    hidden, *send_x = run(
        functools.partial(attention_kernel, ctx_count),
        "attention_forward",
        placed(VMEM, [pos, slot, gain, query_rows, resid_rows] + all_keys + all_values),
        placed(VMEM, [token_shape] + piece_shapes),
        attn_flops + place_flops,
    )
    arrived_x = exchange(send_x, capacity, steps)

    d_act, probs, down_near, gate_near, place, weight_wide = run(
        functools.partial(probs_kernel, ctx_count, capacity, piece_count),
        "act_grads_and_probs",
        placed(VMEM, [pos, slot, weight])
        + placed(HBM, [w_down, w_gate])
        + placed(VMEM, [query_rows] + all_keys + arrived_grad),
        placed(
            VMEM,
            [
                shaped((slots, FFE), F32),
                shaped((QUERY_HEADS // 2, ctx_count * tokens, 2 * tokens), F32),
                shaped((EXP_DEV * FFE, D), BF16),
                shaped((D, EXP_DEV * FFE), BF16),
                shaped((tokens, slots), BF16),
                shaped((tokens, COLS), F32),
            ],
        ),
        expert_flops + attn_flops // 2,
        scratch=[pltpu.SemaphoreType.DMA((2 * EXP_DEV,))],
    )

    ordered = [s for group in groups for s in group]
    dn = [None] * piece_count
    send_dn = [None] * piece_count
    acts = []
    done = 0
    for group in groups:
        group_rows = sum(piece_shapes[s].shape[0] for s in group)
        act, *parts = run(
            functools.partial(expert_back_kernel, capacity, len(group), done),
            "expert_backward",
            placed(VMEM, [gate_near, d_act] + [arrived_x[s] for s in group]),
            placed(
                VMEM,
                [shaped((group_rows, EXP_DEV * FFE), BF16)] + [piece_shapes[s] for s in group],
            ),
            2 * expert_flops * group_rows // slots,
        )
        acts.append(act)
        done += group_rows
        for s, part in zip(group, parts):
            send_dn[s] = part
    dn = exchange(send_dn, capacity, steps)
    terms, *outs = run(
        functools.partial(expert_out_kernel, piece_count, len(acts)),
        "expert_output",
        placed(VMEM, [down_near, gain] + acts)
        + placed(VMEM, [arrived_x[s] for s in ordered] + [send_dn[s] for s in ordered]),
        placed(VMEM, [shaped((GAIN_LINES, LANES), F32)] + piece_shapes),
        expert_flops,
    )
    terms = sum_over(sum_over(terms, "ctx"), "dp", last=1)
    send_y = [outs[ordered.index(s)] for s in steps]
    terms, send_y, dn = lax.optimization_barrier((terms, send_y, dn))
    y = exchange(send_y, capacity, steps)
    terms = jnp.pad(terms, ((0, WIDE_LINES - GAIN_LINES), (0, 0)))
    terms = sum_over(terms, "dp", first=2)[:GAIN_LINES]
    terms, place_back = lax.optimization_barrier((terms, place))
    terms = sum_over(terms, "exp", last=1)

    d_hidden, d_queries, kv_own, *kv_send = run(
        functools.partial(backward_kernel, ctx_count, piece_count),
        "residual_attention_backward",
        placed(VMEM, [place_back, gain, hidden, grad_rows, query_rows, probs])
        + placed(VMEM, dn + all_keys + all_values),
        placed(HBM, [token_shape] * 2)
        + placed(
            VMEM,
            [shaped((tokens, kv_width), F32)]
            + [shaped((tokens, kv_width), BF16)] * (ctx_count - 1),
        ),
        attn_flops + place_flops,
        scratch=[
            pltpu.VMEM((tokens, D), BF16),
            pltpu.VMEM((tokens, D), BF16),
            pltpu.VMEM((tokens, D), F32),
            pltpu.SemaphoreType.DMA((1 + KEY_VALUE_HEADS,)),
        ],
    )
    terms, kv_send = lax.optimization_barrier((terms, kv_send))
    terms = sum_over(terms, "exp", first=2)
    kv_arrived = [pairwise(part, "ctx", s) for s, part in enumerate(kv_send, 1)]

    kv_shape = shaped((tokens, kv_width // 2), BF16)
    final_shapes = [token_shape, kv_shape, kv_shape]
    final_shapes += [shaped((1, tokens), F32), shaped((GAIN_LINES, LANES), F32)]
    total_tokens = tokens * ctx_count * exp_count * lax.axis_size("dp")
    layer_out, d_keys, d_values, d_weight, d_gain = run(
        functools.partial(output_kernel, ctx_count, piece_count, total_tokens),
        "layer_output",
        placed(
            VMEM,
            [place, weight_wide, terms, hidden, grad_rows, kv_own]
            + kv_arrived
            + y,
        ),
        placed(HBM, final_shapes),
        place_flops,
        scratch=[pltpu.VMEM(x.shape, x.dtype) for x in final_shapes]
        + [pltpu.SemaphoreType.DMA((4 + D // COLS,))],
    )
    return (
        layer_out[None],
        d_hidden[None],
        d_queries[None],
        d_keys[None],
        d_values[None],
        d_weight,
        d_gain.reshape(D),
    )


def solution(mesh):
    in_specs = (
        P(("exp", "dp"), "ctx", None),
        P(("exp", "dp"), "ctx", None),
        P(("exp", "dp"), "ctx", None),
        P(("exp", "dp"), "ctx", None),
        P(),
        P(),
        P("exp", None, None),
        P("exp", None, None),
        P(("exp", "dp"), "ctx", None),
        P(("exp", "dp"), "ctx"),
        P(("exp", "dp"), "ctx", None),
    )
    out_specs = (
        P(("exp", "dp"), "ctx", None),
        P(("exp", "dp"), "ctx", None),
        P(("exp", "dp"), "ctx", None),
        P(("exp", "dp"), "ctx", None),
        P(("exp", "dp"), "ctx", None),
        P(("exp", "dp"), "ctx"),
        P(),
    )
    return jax.shard_map(
        per_device, mesh=mesh, in_specs=in_specs, out_specs=out_specs, check_vma=False
    )
```

```python
import functools

import jax
import jax.numpy as jnp
from jax import lax
from jax.experimental import pallas as pl
from jax.experimental.pallas import tpu as pltpu
from jax.sharding import PartitionSpec as P

D = 2048
HEAD_SIZE = 128
QUERY_HEADS = 16
KEY_VALUE_HEADS = 2
GROUP = QUERY_HEADS // KEY_VALUE_HEADS
FFE = 384
EXP_DEV = 2
COLS = 256
LANES = 128
GAIN_LINES = D // LANES
WIDE_LINES = 32
SCALE = HEAD_SIZE ** (-0.5)
EXP2_SCALE = SCALE * 1.4426950408889634
F32 = jnp.float32
BF16 = jnp.bfloat16
NN = (((1,), (0,)), ((), ()))
NT = (((1,), (1,)), ((), ()))
MIB = 1 << 20
VMEM, HBM = pltpu.VMEM, pltpu.HBM


def mm(a, b, dims=NN):
    return lax.dot_general(a, b, dims, preferred_element_type=F32)


def iota(shape, dim):
    return lax.broadcasted_iota(jnp.int32, shape, dim)


def row_to_col(row):
    n = row.shape[1]
    eye = iota((n, n), 0) == iota((n, n), 1)
    return jnp.sum(jnp.where(eye, row.astype(F32), 0.0), axis=1, keepdims=True)


def col_to_row(col):
    n = col.shape[0]
    eye = iota((n, n), 0) == iota((n, n), 1)
    return jnp.sum(jnp.where(eye, col, 0.0), axis=0, keepdims=True)


def block_positions(order_ref, ctx_index, tokens):
    span = tokens // 8
    index = iota((1, tokens), 1)
    which = index // span
    start = jnp.zeros((1, tokens), jnp.int32)
    for b in range(8):
        start = jnp.where(which == b, order_ref[ctx_index * 8 + b], start)
    return start * span + index % span


def stacked(refs, cols=slice(None)):
    parts = [r[:, cols] for r in refs]
    return parts[0] if len(parts) == 1 else jnp.concatenate(parts, axis=0)


def column_blocks(width=D, step=COLS):
    return [slice(c, c + step) for c in range(0, width, step)]


def store_pieces(refs, cols, rows_value):
    at = 0
    for r in refs:
        n = r.shape[0]
        r[:, cols] = rows_value[at : at + n]
        at += n


def pair_cols(pair):
    start = 2 * pair * HEAD_SIZE
    return slice(start, start + HEAD_SIZE), slice(start + HEAD_SIZE, start + 2 * HEAD_SIZE)


def head_pair(ref, pair):
    first, second = pair_cols(pair)
    return jnp.concatenate([ref[:, first], ref[:, second]], axis=0)


def placement_rows(slot_row, slots):
    tokens = slot_row.shape[1]
    return jnp.where(iota((slots, tokens), 0) == slot_row, 1.0, 0.0).astype(BF16)


def placement_cols(slot_row, slots):
    tokens = slot_row.shape[1]
    slot_col = row_to_col(slot_row)
    return jnp.where(iota((tokens, slots), 1).astype(F32) == slot_col, 1.0, 0.0).astype(BF16)


def dispatch_kernel(count, experts, capacity, *refs):
    sources, refs = refs[:9], refs[9:]
    targets, refs = refs[:6], refs[6:]
    grad_ref = targets[0]
    slot_ref, pos_ref, weight_ref = refs[:3]
    send_refs = refs[3:-3]
    order_ref, routes_ref, sems = refs[-3:]
    targets = targets + (weight_ref, routes_ref, order_ref)
    copies = [
        pltpu.make_async_copy(source, target, sems.at[i])
        for i, (source, target) in enumerate(zip(sources, targets))
    ]
    for copy in copies[6:] + copies[:6]:
        copy.start()
    for copy in copies[6:]:
        copy.wait()
    tokens = routes_ref.shape[1]
    chosen = routes_ref[...]
    lanes = max(experts, 16)
    hits = jnp.where(iota((lanes, tokens), 0) == chosen, 1.0, 0.0)
    before = jnp.where(iota((tokens, tokens), 0) < iota((tokens, tokens), 1), 1.0, 0.0)
    earlier = mm(hits.astype(BF16), before.astype(BF16))
    rank = jnp.sum(hits * earlier, axis=0, keepdims=True).astype(jnp.int32)
    target = (chosen // EXP_DEV) ^ lax.axis_index("exp")
    slot = (target * EXP_DEV + chosen % EXP_DEV) * capacity + rank
    slot_ref[...] = slot
    me = lax.axis_index("ctx")
    for s in range(count):
        pos_ref[s : s + 1, :] = block_positions(order_ref, me ^ s, tokens)
    place = placement_rows(slot, experts * capacity)
    weight = row_to_col(weight_ref[...])
    copies[0].wait()
    for cols in column_blocks():
        scaled = (weight * grad_ref[:, cols].astype(F32)).astype(BF16)
        store_pieces(send_refs, cols, mm(place, scaled).astype(BF16))
    for copy in copies[1:6]:
        copy.wait()


def kv_stacks(key_refs, value_refs, g):
    cols = slice(g * HEAD_SIZE, (g + 1) * HEAD_SIZE)
    return stacked(key_refs, cols), stacked(value_refs, cols)


def attention_kernel(
    count, pos_ref, slot_ref, gain_ref, query_ref, resid_ref, *refs
):
    key_refs, value_refs = refs[:count], refs[count : 2 * count]
    hidden_ref, send_refs = refs[2 * count], refs[2 * count + 1 :]
    tokens = query_ref.shape[0]
    query_pos = row_to_col(pos_ref[:1, :])
    bias = jnp.concatenate(
        [
            jnp.where(pos_ref[s : s + 1, :].astype(F32) <= query_pos, 0.0, -1e30)
            for s in range(count)
        ],
        axis=1,
    )
    length = count * tokens
    ones = jnp.ones((length, HEAD_SIZE), BF16)
    total = jnp.zeros((tokens, HEAD_SIZE), F32)
    for g in range(KEY_VALUE_HEADS):
        keys, values = kv_stacks(key_refs, value_refs, g)
        values = jnp.concatenate([values, ones], axis=1)
        for h in range(g * GROUP, (g + 1) * GROUP):
            cols = slice(h * HEAD_SIZE, (h + 1) * HEAD_SIZE)
            scores = mm(query_ref[:, cols], keys, NT) + bias
            peak = jnp.max(scores, axis=1, keepdims=True)
            weights = jnp.exp2((scores - peak) * EXP2_SCALE).astype(BF16)
            mixed = mm(weights, values)
            attended = mixed[:, :HEAD_SIZE] / mixed[:, HEAD_SIZE:]
            hidden = (resid_ref[:, cols].astype(F32) + attended).astype(BF16)
            hidden_ref[:, cols] = hidden
            wide = hidden.astype(F32)
            total = total + wide * wide
    inv_rms = lax.rsqrt(jnp.sum(total, axis=1, keepdims=True) * (1.0 / D) + 1e-06)
    slots = sum(r.shape[0] for r in send_refs)
    place = placement_rows(slot_ref[...], slots)
    for cols in column_blocks():
        normed = (hidden_ref[:, cols].astype(F32) * inv_rms * gain_ref[:, cols]).astype(BF16)
        store_pieces(send_refs, cols, mm(place, normed).astype(BF16))


def first_expert_rows(slots, capacity):
    return iota((slots, 1), 0) % (EXP_DEV * capacity) < capacity


def probs_kernel(count, pos_ref, slot_ref, weight_ref, down_hbm, gate_hbm, query_ref, *refs):
    key_refs = refs[:count]
    probs_ref, down_ref, gate_ref, place_ref, wide_ref, sems = refs[count:]
    spans = [slice(e * FFE, (e + 1) * FFE) for e in range(EXP_DEV)]
    down_copies = [
        pltpu.make_async_copy(down_hbm.at[e], down_ref.at[span, :], sems.at[e])
        for e, span in enumerate(spans)
    ]
    gate_copies = [
        pltpu.make_async_copy(gate_hbm.at[e], gate_ref.at[:, span], sems.at[EXP_DEV + e])
        for e, span in enumerate(spans)
    ]
    for copy in down_copies + gate_copies:
        copy.start()
    place_ref[...] = placement_cols(slot_ref[...], place_ref.shape[1])
    wide_ref[...] = jnp.broadcast_to(row_to_col(weight_ref[...]), wide_ref.shape)
    query_pos = pos_ref[:1, :].astype(F32)
    bias = jnp.concatenate(
        [
            jnp.where(row_to_col(pos_ref[s : s + 1, :]) <= query_pos, 0.0, -1e30)
            for s in range(count)
        ],
        axis=0,
    )
    bias = jnp.concatenate([bias, bias], axis=1)
    for g in range(KEY_VALUE_HEADS):
        keys = stacked(key_refs, slice(g * HEAD_SIZE, (g + 1) * HEAD_SIZE))
        for pair in range(g * GROUP // 2, (g + 1) * GROUP // 2):
            scores = mm(keys, head_pair(query_ref, pair), NT) + bias
            peak = jnp.max(scores, axis=0, keepdims=True)
            weights = jnp.exp2((scores - peak) * EXP2_SCALE)
            probs_ref[pair] = weights * (1.0 / jnp.sum(weights, axis=0, keepdims=True))
    for copy in down_copies + gate_copies:
        copy.wait()


def expert_grad_kernel(capacity, down_ref, *refs):
    grads = stacked(refs[:-1])
    first = first_expert_rows(grads.shape[0], capacity)
    both = mm(grads, down_ref[...], NT)
    refs[-1][...] = jnp.where(first, both[:, :FFE], both[:, FFE:])


def expert_back_kernel(capacity, pieces, gate_ref, d_act_ref, *refs):
    rows = stacked(refs[:pieces])
    act_ref, back_refs = refs[pieces], refs[pieces + 1 :]
    first = first_expert_rows(rows.shape[0], capacity)
    both = mm(rows, gate_ref[...])
    pre = jnp.where(first, both[:, :FFE], both[:, FFE:])
    gate = 1.0 / (1.0 + jnp.exp(-pre))
    act = pre * gate
    d_pre = d_act_ref[...] * gate * (1.0 + pre * (1.0 - gate))
    act, d_pre = [
        jnp.concatenate([jnp.where(first, x, 0.0), jnp.where(first, 0.0, x)], axis=1).astype(BF16)
        for x in (act, d_pre)
    ]
    act_ref[...] = act
    for cols in column_blocks():
        store_pieces(back_refs, cols, mm(d_pre, gate_ref[cols, :], NT).astype(BF16))


def expert_out_kernel(pieces, down_ref, gain_ref, act_ref, *refs):
    act = act_ref[...]
    row_refs, back_refs = refs[:pieces], refs[pieces : 2 * pieces]
    terms_ref, out_refs = refs[2 * pieces], refs[2 * pieces + 1 :]
    for cols in column_blocks():
        store_pieces(out_refs, cols, mm(act, down_ref[:, cols]).astype(BF16))
        products = stacked(row_refs, cols).astype(F32) * stacked(back_refs, cols).astype(F32)
        terms = jnp.sum(products, axis=0, keepdims=True) / gain_ref[:, cols]
        for at in range(0, COLS, LANES):
            line = (cols.start + at) // LANES
            terms_ref[line : line + 1, :] = terms[:, at : at + LANES]


def backward_kernel(
    count, pieces, place_ref, gain_ref, hidden_ref, grad_ref, query_ref, probs_ref, *refs
):
    dn_refs = refs[:pieces]
    key_refs = refs[pieces : pieces + count]
    value_refs = refs[pieces + count : pieces + 2 * count]
    resid_hbm, dq_hbm, own_ref = refs[pieces + 2 * count : pieces + 2 * count + 3]
    other_refs = refs[pieces + 2 * count + 3 : -4]
    resid_ref, dq_ref, dn_scratch, sems = refs[-4:]
    tokens = hidden_ref.shape[0]
    place = place_ref[...]
    square = jnp.zeros((tokens, COLS), F32)
    mixing = jnp.zeros((tokens, COLS), F32)
    for cols in column_blocks():
        dn = mm(place, stacked(dn_refs, cols)) * gain_ref[:, cols]
        dn_scratch[:, cols] = dn
        hidden = hidden_ref[:, cols].astype(F32)
        square = square + hidden * hidden
        mixing = mixing + dn * hidden
    inv_rms = lax.rsqrt(jnp.sum(square, axis=1, keepdims=True) * (1.0 / D) + 1e-06)
    mean_mix = jnp.sum(mixing, axis=1, keepdims=True) * (1.0 / D)
    factor = inv_rms * inv_rms * inv_rms * mean_mix
    for cols in column_blocks():
        resid_ref[:, cols] = (
            grad_ref[:, cols].astype(F32)
            + dn_scratch[:, cols] * inv_rms
            - hidden_ref[:, cols].astype(F32) * factor
        ).astype(BF16)
    copies = [pltpu.make_async_copy(resid_ref, resid_hbm, sems.at[0])]
    copies[0].start()
    length = count * tokens
    group_width = GROUP * HEAD_SIZE
    for g in range(KEY_VALUE_HEADS):
        keys, values = kv_stacks(key_refs, value_refs, g)
        keys_t = jnp.transpose(keys.astype(F32)).astype(BF16)
        d_keys = jnp.zeros((length, HEAD_SIZE), F32)
        d_values = jnp.zeros((length, HEAD_SIZE), F32)
        for pair in range(g * GROUP // 2, (g + 1) * GROUP // 2):
            cols_a, cols_b = pair_cols(pair)
            d_out = head_pair(resid_ref, pair)
            probs = probs_ref[pair]
            d_probs = mm(values, d_out, NT)
            row_dot = jnp.sum(probs * d_probs, axis=0, keepdims=True)
            d_scores = (probs * (d_probs - row_dot)).astype(BF16)
            d_keys = d_keys + mm(d_scores, head_pair(query_ref, pair))
            d_values = d_values + mm(probs.astype(BF16), d_out)
            d_query_t = mm(keys_t, d_scores) * SCALE
            dq_ref[:, cols_a] = jnp.transpose(d_query_t[:, :tokens]).astype(BF16)
            dq_ref[:, cols_b] = jnp.transpose(d_query_t[:, tokens:]).astype(BF16)
        cols = slice(g * group_width, (g + 1) * group_width)
        copy = pltpu.make_async_copy(dq_ref.at[:, cols], dq_hbm.at[:, cols], sems.at[1 + g])
        copy.start()
        copies.append(copy)
        k_cols = slice(g * HEAD_SIZE, (g + 1) * HEAD_SIZE)
        v_cols = slice((KEY_VALUE_HEADS + g) * HEAD_SIZE, (KEY_VALUE_HEADS + g + 1) * HEAD_SIZE)
        d_keys = d_keys * SCALE
        own_ref[:, k_cols] = d_keys[:tokens]
        own_ref[:, v_cols] = d_values[:tokens]
        for s, ref in enumerate(other_refs, 1):
            ref[:, k_cols] = d_keys[s * tokens : (s + 1) * tokens].astype(BF16)
            ref[:, v_cols] = d_values[s * tokens : (s + 1) * tokens].astype(BF16)
    for copy in copies:
        copy.wait()


def output_kernel(
    count, pieces, tokens_in_all, place_ref, weight_ref, gain_ref, hidden_ref, grad_ref, *refs
):
    own_ref, refs = refs[0], refs[1:]
    arrived_refs = refs[: count - 1]
    y_refs = refs[count - 1 : count - 1 + pieces]
    out_hbm, dk_hbm, dv_hbm, d_weight_hbm, d_gain_hbm = refs[count - 1 + pieces : -6]
    out_ref, dk_ref, dv_ref, d_weight_ref, d_gain_ref, sems = refs[-6:]
    split = KEY_VALUE_HEADS * HEAD_SIZE
    d_kv = own_ref[...]
    for ref in arrived_refs:
        d_kv = d_kv + ref[...].astype(F32)
    dk_ref[...] = d_kv[:, :split].astype(BF16)
    dv_ref[...] = d_kv[:, split:].astype(BF16)
    d_gain_ref[...] = gain_ref[...] * (1.0 / tokens_in_all)
    copies = []

    def send(source, target):
        copy = pltpu.make_async_copy(source, target, sems.at[len(copies)])
        copy.start()
        copies.append(copy)

    send(dk_ref, dk_hbm)
    send(dv_ref, dv_hbm)
    send(d_gain_ref, d_gain_hbm)
    tokens = hidden_ref.shape[0]
    place = place_ref[...]
    weight = weight_ref[...]
    total = jnp.zeros((tokens, COLS), F32)
    for cols in column_blocks():
        y = mm(place, stacked(y_refs, cols))
        out_ref[:, cols] = (hidden_ref[:, cols].astype(F32) + weight * y).astype(BF16)
        send(out_ref.at[:, cols], out_hbm.at[:, cols])
        total = total + y * grad_ref[:, cols].astype(F32)
    d_weight_ref[...] = col_to_row(jnp.sum(total, axis=1, keepdims=True))
    send(d_weight_ref, d_weight_hbm)
    for copy in copies:
        copy.wait()


def run(kernel, name, inputs, outputs, flops, scratch=(), limit=20 * MIB):
    nbytes = sum(x.size * x.dtype.itemsize for _, x in inputs) + sum(
        x.size * x.dtype.itemsize for _, x in outputs
    )
    spec = {space: pl.BlockSpec(memory_space=space) for space in (VMEM, HBM)}
    results = pl.pallas_call(
        kernel,
        out_shape=[x for _, x in outputs],
        in_specs=[spec[space] for space, _ in inputs],
        out_specs=[spec[space] for space, _ in outputs],
        scratch_shapes=list(scratch),
        compiler_params=pltpu.CompilerParams(vmem_limit_bytes=limit),
        cost_estimate=pl.CostEstimate(flops=flops, bytes_accessed=nbytes, transcendentals=0),
        name=name,
    )(*[pltpu.with_memory_space_constraint(x, HBM) if space is HBM else x for space, x in inputs])
    return list(results)


def placed(space, arrays):
    return [(space, x) for x in arrays]


def pairwise(value, axis, step):
    count = lax.axis_size(axis)
    return lax.ppermute(value, axis, [(i, i ^ step) for i in range(count)])


def exchange_flat(flat, capacity):
    count = lax.axis_size("exp")
    rows = EXP_DEV * capacity
    blocks = [flat[s * rows : (s + 1) * rows] for s in range(count)]
    moved = [blocks[0]] + [pairwise(blocks[s], "exp", s) for s in range(1, count)]
    return jnp.concatenate(moved, axis=0)


def exchange(pieces, capacity):
    if lax.axis_size("exp") != len(pieces):
        return [exchange_flat(pieces[0], capacity)]
    return [pairwise(piece, "exp", s) if s > 0 else piece for s, piece in enumerate(pieces)]


def doubled(value, axis, step):
    return value + pairwise(value, axis, step)


def sum_over(value, axis, first=1):
    step = first
    while step < lax.axis_size(axis):
        value = doubled(value, axis, step)
        step *= 2
    return value


def widened(act, value, axis, step):
    rows = value.shape[0]
    wide = jnp.pad(value, ((0, WIDE_LINES - rows), (0, 0)))
    return act(wide, axis, step)[:rows]


def shaped(shape, dtype):
    return jax.ShapeDtypeStruct(shape, dtype)


def per_device(
    queries,
    keys,
    values,
    resid,
    block_order,
    norm_gain,
    w_gate,
    w_down,
    routes,
    route_weight,
    d_out,
):
    query_rows = queries[0]
    resid_rows = resid[0]
    grad_rows = d_out[0]
    tokens = query_rows.shape[0]
    chosen = routes.reshape(1, tokens)
    gain = norm_gain.reshape(1, D)
    ctx_count = lax.axis_size("ctx")
    exp_count = lax.axis_size("exp")
    experts = EXP_DEV * exp_count
    capacity = 3 * tokens // (2 * experts)
    slots = experts * capacity
    rows = EXP_DEV * capacity
    piece_count = exp_count if rows % 16 == 0 else 1
    piece_shapes = [shaped((slots // piece_count, D), BF16)] * piece_count
    token_shape = shaped((tokens, D), BF16)
    kv_width = 2 * KEY_VALUE_HEADS * HEAD_SIZE
    attn_flops = 4 * tokens * ctx_count * tokens * QUERY_HEADS * HEAD_SIZE
    place_flops = 2 * slots * tokens * D
    expert_flops = 2 * slots * D * FFE * EXP_DEV

    own_keys, own_values = keys[0], values[0]
    all_keys = [own_keys] + [pairwise(own_keys, "ctx", s) for s in range(1, ctx_count)]
    all_values = [own_values] + [pairwise(own_values, "ctx", s) for s in range(1, ctx_count)]

    near = [grad_rows, own_keys, own_values, gain, query_rows, resid_rows]
    grad_rows, own_keys, own_values, gain, query_rows, resid_rows, slot, pos, weight, *send_grad = run(
        functools.partial(dispatch_kernel, ctx_count, experts, capacity),
        "dispatch_grads",
        placed(HBM, near + [route_weight, chosen, block_order]),
        placed(
            VMEM,
            [shaped(x.shape, x.dtype) for x in near]
            + [
                shaped((1, tokens), jnp.int32),
                shaped((ctx_count, tokens), jnp.int32),
                shaped((1, tokens), F32),
            ]
            + piece_shapes,
        ),
        place_flops,
        scratch=[
            pltpu.SMEM(block_order.shape, jnp.int32),
            pltpu.VMEM((1, tokens), jnp.int32),
            pltpu.SemaphoreType.DMA((9,)),
        ],
    )
    all_keys[0], all_values[0] = own_keys, own_values
    arrived_grad = exchange(send_grad, capacity)

    hidden, *send_x = run(
        functools.partial(attention_kernel, ctx_count),
        "attention_forward",
        placed(VMEM, [pos, slot, gain, query_rows, resid_rows] + all_keys + all_values),
        placed(VMEM, [token_shape] + piece_shapes),
        attn_flops + place_flops,
    )
    arrived_x = exchange(send_x, capacity)

    probs, down_near, gate_near, place, weight_wide = run(
        functools.partial(probs_kernel, ctx_count),
        "probs_and_weights",
        placed(VMEM, [pos, slot, weight])
        + placed(HBM, [w_down, w_gate])
        + placed(VMEM, [query_rows] + all_keys),
        placed(
            VMEM,
            [
                shaped((QUERY_HEADS // 2, ctx_count * tokens, 2 * tokens), F32),
                shaped((EXP_DEV * FFE, D), BF16),
                shaped((D, EXP_DEV * FFE), BF16),
                shaped((tokens, slots), BF16),
                shaped((tokens, COLS), F32),
            ],
        ),
        attn_flops // 2,
        scratch=[pltpu.SemaphoreType.DMA((2 * EXP_DEV,))],
    )

    (d_act,) = run(
        functools.partial(expert_grad_kernel, capacity),
        "act_grads",
        placed(VMEM, [down_near] + arrived_grad),
        placed(VMEM, [shaped((slots, FFE), F32)]),
        expert_flops,
    )
    act, *send_dn = run(
        functools.partial(expert_back_kernel, capacity, piece_count),
        "expert_backward",
        placed(VMEM, [gate_near, d_act] + arrived_x),
        placed(VMEM, [shaped((slots, EXP_DEV * FFE), BF16)] + piece_shapes),
        2 * expert_flops,
    )
    dn = exchange(send_dn, capacity)
    terms, *send_y = run(
        functools.partial(expert_out_kernel, piece_count),
        "expert_output",
        placed(VMEM, [down_near, gain, act] + arrived_x + send_dn),
        placed(VMEM, [shaped((GAIN_LINES, LANES), F32)] + piece_shapes),
        expert_flops,
    )
    terms = doubled(sum_over(terms, "ctx"), "exp", 2)
    terms, send_y, dn = lax.optimization_barrier((terms, send_y, dn))
    y = exchange(send_y, capacity)
    terms = widened(doubled, terms, "dp", 2)
    terms, place_back = lax.optimization_barrier((terms, place))
    terms = doubled(terms, "exp", 1)

    d_hidden, d_queries, kv_own, *kv_send = run(
        functools.partial(backward_kernel, ctx_count, piece_count),
        "residual_attention_backward",
        placed(VMEM, [place_back, gain, hidden, grad_rows, query_rows, probs])
        + placed(VMEM, dn + all_keys + all_values),
        placed(HBM, [token_shape] * 2)
        + placed(
            VMEM,
            [shaped((tokens, kv_width), F32)]
            + [shaped((tokens, kv_width), BF16)] * (ctx_count - 1),
        ),
        attn_flops + place_flops,
        scratch=[
            pltpu.VMEM((tokens, D), BF16),
            pltpu.VMEM((tokens, D), BF16),
            pltpu.VMEM((tokens, D), F32),
            pltpu.SemaphoreType.DMA((1 + KEY_VALUE_HEADS,)),
        ],
    )
    terms, kv_send = lax.optimization_barrier((terms, kv_send))
    terms = sum_over(sum_over(terms, "exp", first=4), "dp", first=4)
    terms = doubled(terms, "dp", 1)
    kv_arrived = [pairwise(part, "ctx", s) for s, part in enumerate(kv_send, 1)]

    kv_shape = shaped((tokens, kv_width // 2), BF16)
    final_shapes = [token_shape, kv_shape, kv_shape]
    final_shapes += [shaped((1, tokens), F32), shaped((GAIN_LINES, LANES), F32)]
    total_tokens = tokens * ctx_count * exp_count * lax.axis_size("dp")
    layer_out, d_keys, d_values, d_weight, d_gain = run(
        functools.partial(output_kernel, ctx_count, piece_count, total_tokens),
        "layer_output",
        placed(
            VMEM,
            [place, weight_wide, terms, hidden, grad_rows, kv_own]
            + kv_arrived
            + y,
        ),
        placed(HBM, final_shapes),
        place_flops,
        scratch=[pltpu.VMEM(x.shape, x.dtype) for x in final_shapes]
        + [pltpu.SemaphoreType.DMA((4 + D // COLS,))],
    )
    return (
        layer_out[None],
        d_hidden[None],
        d_queries[None],
        d_keys[None],
        d_values[None],
        d_weight,
        d_gain.reshape(D),
    )


def solution(mesh):
    in_specs = (
        P(("exp", "dp"), "ctx", None),
        P(("exp", "dp"), "ctx", None),
        P(("exp", "dp"), "ctx", None),
        P(("exp", "dp"), "ctx", None),
        P(),
        P(),
        P("exp", None, None),
        P("exp", None, None),
        P(("exp", "dp"), "ctx", None),
        P(("exp", "dp"), "ctx"),
        P(("exp", "dp"), "ctx", None),
    )
    out_specs = (
        P(("exp", "dp"), "ctx", None),
        P(("exp", "dp"), "ctx", None),
        P(("exp", "dp"), "ctx", None),
        P(("exp", "dp"), "ctx", None),
        P(("exp", "dp"), "ctx", None),
        P(("exp", "dp"), "ctx"),
        P(),
    )
    return jax.shard_map(
        per_device, mesh=mesh, in_specs=in_specs, out_specs=out_specs, check_vma=False
    )
```

```python
import functools

import jax
import jax.numpy as jnp
from jax import lax
from jax.experimental import pallas as pl
from jax.experimental.pallas import tpu as pltpu
from jax.sharding import PartitionSpec as P

D = 2048
HEAD_SIZE = 128
QUERY_HEADS = 16
KEY_VALUE_HEADS = 2
GROUP = QUERY_HEADS // KEY_VALUE_HEADS
FFE = 384
EXP_DEV = 2
COLS = 256
LANES = 128
GAIN_LINES = D // LANES
WIDE_LINES = 32
SCALE = HEAD_SIZE ** (-0.5)
EXP2_SCALE = SCALE * 1.4426950408889634
F32 = jnp.float32
BF16 = jnp.bfloat16
NN = (((1,), (0,)), ((), ()))
NT = (((1,), (1,)), ((), ()))
MIB = 1 << 20
VMEM, HBM = pltpu.VMEM, pltpu.HBM


def mm(a, b, dims=NN):
    return lax.dot_general(a, b, dims, preferred_element_type=F32)


def iota(shape, dim):
    return lax.broadcasted_iota(jnp.int32, shape, dim)


def row_to_col(row):
    n = row.shape[1]
    eye = iota((n, n), 0) == iota((n, n), 1)
    return jnp.sum(jnp.where(eye, row.astype(F32), 0.0), axis=1, keepdims=True)


def col_to_row(col):
    n = col.shape[0]
    eye = iota((n, n), 0) == iota((n, n), 1)
    return jnp.sum(jnp.where(eye, col, 0.0), axis=0, keepdims=True)


def block_positions(order_ref, ctx_index, tokens):
    span = tokens // 8
    index = iota((1, tokens), 1)
    which = index // span
    start = jnp.zeros((1, tokens), jnp.int32)
    for b in range(8):
        start = jnp.where(which == b, order_ref[ctx_index * 8 + b], start)
    return start * span + index % span


def stacked(refs, cols=slice(None)):
    parts = [r[:, cols] for r in refs]
    return parts[0] if len(parts) == 1 else jnp.concatenate(parts, axis=0)


def column_blocks(width=D, step=COLS):
    return [slice(c, c + step) for c in range(0, width, step)]


def store_pieces(refs, cols, rows_value):
    at = 0
    for r in refs:
        n = r.shape[0]
        r[:, cols] = rows_value[at : at + n]
        at += n


def pair_cols(pair):
    start = 2 * pair * HEAD_SIZE
    return slice(start, start + HEAD_SIZE), slice(start + HEAD_SIZE, start + 2 * HEAD_SIZE)


def head_pair(ref, pair):
    first, second = pair_cols(pair)
    return jnp.concatenate([ref[:, first], ref[:, second]], axis=0)


def placement_rows(slot_row, slots):
    tokens = slot_row.shape[1]
    return jnp.where(iota((slots, tokens), 0) == slot_row, 1.0, 0.0).astype(BF16)


def placement_cols(slot_row, slots):
    tokens = slot_row.shape[1]
    slot_col = row_to_col(slot_row)
    return jnp.where(iota((tokens, slots), 1).astype(F32) == slot_col, 1.0, 0.0).astype(BF16)


def dispatch_kernel(count, experts, capacity, *refs):
    sources, refs = refs[:9], refs[9:]
    targets, refs = refs[:6], refs[6:]
    grad_ref = targets[0]
    slot_ref, pos_ref, weight_ref = refs[:3]
    send_refs = refs[3:-3]
    order_ref, routes_ref, sems = refs[-3:]
    targets = targets + (weight_ref, routes_ref, order_ref)
    copies = [
        pltpu.make_async_copy(source, target, sems.at[i])
        for i, (source, target) in enumerate(zip(sources, targets))
    ]
    for copy in copies[6:] + copies[:6]:
        copy.start()
    for copy in copies[6:]:
        copy.wait()
    tokens = routes_ref.shape[1]
    chosen = routes_ref[...]
    lanes = max(experts, 16)
    hits = jnp.where(iota((lanes, tokens), 0) == chosen, 1.0, 0.0)
    before = jnp.where(iota((tokens, tokens), 0) < iota((tokens, tokens), 1), 1.0, 0.0)
    earlier = mm(hits.astype(BF16), before.astype(BF16))
    rank = jnp.sum(hits * earlier, axis=0, keepdims=True).astype(jnp.int32)
    target = (chosen // EXP_DEV) ^ lax.axis_index("exp")
    slot = (target * EXP_DEV + chosen % EXP_DEV) * capacity + rank
    slot_ref[...] = slot
    me = lax.axis_index("ctx")
    for s in range(count):
        pos_ref[s : s + 1, :] = block_positions(order_ref, me ^ s, tokens)
    place = placement_rows(slot, experts * capacity)
    weight = row_to_col(weight_ref[...])
    copies[0].wait()
    for cols in column_blocks():
        scaled = (weight * grad_ref[:, cols].astype(F32)).astype(BF16)
        store_pieces(send_refs, cols, mm(place, scaled).astype(BF16))
    for copy in copies[1:6]:
        copy.wait()


def kv_stacks(key_refs, value_refs, g):
    cols = slice(g * HEAD_SIZE, (g + 1) * HEAD_SIZE)
    return stacked(key_refs, cols), stacked(value_refs, cols)


def attention_kernel(
    count, pos_ref, slot_ref, gain_ref, query_ref, resid_ref, *refs
):
    key_refs, value_refs = refs[:count], refs[count : 2 * count]
    hidden_ref, send_refs = refs[2 * count], refs[2 * count + 1 :]
    tokens = query_ref.shape[0]
    query_pos = row_to_col(pos_ref[:1, :])
    bias = jnp.concatenate(
        [
            jnp.where(pos_ref[s : s + 1, :].astype(F32) <= query_pos, 0.0, -1e30)
            for s in range(count)
        ],
        axis=1,
    )
    length = count * tokens
    ones = jnp.ones((length, HEAD_SIZE), BF16)
    total = jnp.zeros((tokens, HEAD_SIZE), F32)
    for g in range(KEY_VALUE_HEADS):
        keys, values = kv_stacks(key_refs, value_refs, g)
        values = jnp.concatenate([values, ones], axis=1)
        for h in range(g * GROUP, (g + 1) * GROUP):
            cols = slice(h * HEAD_SIZE, (h + 1) * HEAD_SIZE)
            scores = mm(query_ref[:, cols], keys, NT) + bias
            peak = jnp.max(scores, axis=1, keepdims=True)
            weights = jnp.exp2((scores - peak) * EXP2_SCALE).astype(BF16)
            mixed = mm(weights, values)
            attended = mixed[:, :HEAD_SIZE] / mixed[:, HEAD_SIZE:]
            hidden = (resid_ref[:, cols].astype(F32) + attended).astype(BF16)
            hidden_ref[:, cols] = hidden
            wide = hidden.astype(F32)
            total = total + wide * wide
    inv_rms = lax.rsqrt(jnp.sum(total, axis=1, keepdims=True) * (1.0 / D) + 1e-06)
    slots = sum(r.shape[0] for r in send_refs)
    place = placement_rows(slot_ref[...], slots)
    for cols in column_blocks():
        normed = (hidden_ref[:, cols].astype(F32) * inv_rms * gain_ref[:, cols]).astype(BF16)
        store_pieces(send_refs, cols, mm(place, normed).astype(BF16))


def first_expert_rows(slots, capacity):
    return iota((slots, 1), 0) % (EXP_DEV * capacity) < capacity


def probs_kernel(count, pos_ref, slot_ref, weight_ref, down_hbm, gate_hbm, query_ref, *refs):
    key_refs = refs[:count]
    probs_ref, down_ref, gate_ref, place_ref, wide_ref, sems = refs[count:]
    spans = [slice(e * FFE, (e + 1) * FFE) for e in range(EXP_DEV)]
    down_copies = [
        pltpu.make_async_copy(down_hbm.at[e], down_ref.at[span, :], sems.at[e])
        for e, span in enumerate(spans)
    ]
    gate_copies = [
        pltpu.make_async_copy(gate_hbm.at[e], gate_ref.at[:, span], sems.at[EXP_DEV + e])
        for e, span in enumerate(spans)
    ]
    for copy in down_copies + gate_copies:
        copy.start()
    place_ref[...] = placement_cols(slot_ref[...], place_ref.shape[1])
    wide_ref[...] = jnp.broadcast_to(row_to_col(weight_ref[...]), wide_ref.shape)
    query_pos = pos_ref[:1, :].astype(F32)
    bias = jnp.concatenate(
        [
            jnp.where(row_to_col(pos_ref[s : s + 1, :]) <= query_pos, 0.0, -1e30)
            for s in range(count)
        ],
        axis=0,
    )
    bias = jnp.concatenate([bias, bias], axis=1)
    for g in range(KEY_VALUE_HEADS):
        keys = stacked(key_refs, slice(g * HEAD_SIZE, (g + 1) * HEAD_SIZE))
        for pair in range(g * GROUP // 2, (g + 1) * GROUP // 2):
            scores = mm(keys, head_pair(query_ref, pair), NT) + bias
            peak = jnp.max(scores, axis=0, keepdims=True)
            weights = jnp.exp2((scores - peak) * EXP2_SCALE)
            probs_ref[pair] = weights * (1.0 / jnp.sum(weights, axis=0, keepdims=True))
    for copy in down_copies + gate_copies:
        copy.wait()


def expert_grad_kernel(capacity, down_ref, *refs):
    grads = stacked(refs[:-1])
    first = first_expert_rows(grads.shape[0], capacity)
    both = mm(grads, down_ref[...], NT)
    refs[-1][...] = jnp.where(first, both[:, :FFE], both[:, FFE:])


def expert_back_kernel(capacity, pieces, start, gate_ref, d_act_ref, *refs):
    rows = stacked(refs[:pieces])
    act_ref, back_refs = refs[pieces], refs[pieces + 1 :]
    count = rows.shape[0]
    first = first_expert_rows(count, capacity)
    both = mm(rows, gate_ref[...])
    pre = jnp.where(first, both[:, :FFE], both[:, FFE:])
    gate = 1.0 / (1.0 + jnp.exp(-pre))
    act = pre * gate
    d_pre = d_act_ref[start : start + count, :] * gate * (1.0 + pre * (1.0 - gate))
    act, d_pre = [
        jnp.concatenate([jnp.where(first, x, 0.0), jnp.where(first, 0.0, x)], axis=1).astype(BF16)
        for x in (act, d_pre)
    ]
    act_ref[...] = act
    for cols in column_blocks():
        store_pieces(back_refs, cols, mm(d_pre, gate_ref[cols, :], NT).astype(BF16))


def expert_out_kernel(pieces, acts, down_ref, gain_ref, *refs):
    act = stacked(refs[:acts])
    refs = refs[acts:]
    row_refs, back_refs = refs[:pieces], refs[pieces : 2 * pieces]
    terms_ref, out_refs = refs[2 * pieces], refs[2 * pieces + 1 :]
    for cols in column_blocks():
        store_pieces(out_refs, cols, mm(act, down_ref[:, cols]).astype(BF16))
        products = stacked(row_refs, cols).astype(F32) * stacked(back_refs, cols).astype(F32)
        terms = jnp.sum(products, axis=0, keepdims=True) / gain_ref[:, cols]
        for at in range(0, COLS, LANES):
            line = (cols.start + at) // LANES
            terms_ref[line : line + 1, :] = terms[:, at : at + LANES]


def backward_kernel(
    count, pieces, place_ref, gain_ref, hidden_ref, grad_ref, query_ref, probs_ref, *refs
):
    dn_refs = refs[:pieces]
    key_refs = refs[pieces : pieces + count]
    value_refs = refs[pieces + count : pieces + 2 * count]
    resid_hbm, dq_hbm, own_ref = refs[pieces + 2 * count : pieces + 2 * count + 3]
    other_refs = refs[pieces + 2 * count + 3 : -4]
    resid_ref, dq_ref, dn_scratch, sems = refs[-4:]
    tokens = hidden_ref.shape[0]
    place = place_ref[...]
    square = jnp.zeros((tokens, COLS), F32)
    mixing = jnp.zeros((tokens, COLS), F32)
    for cols in column_blocks():
        dn = mm(place, stacked(dn_refs, cols)) * gain_ref[:, cols]
        dn_scratch[:, cols] = dn
        hidden = hidden_ref[:, cols].astype(F32)
        square = square + hidden * hidden
        mixing = mixing + dn * hidden
    inv_rms = lax.rsqrt(jnp.sum(square, axis=1, keepdims=True) * (1.0 / D) + 1e-06)
    mean_mix = jnp.sum(mixing, axis=1, keepdims=True) * (1.0 / D)
    factor = inv_rms * inv_rms * inv_rms * mean_mix
    for cols in column_blocks():
        resid_ref[:, cols] = (
            grad_ref[:, cols].astype(F32)
            + dn_scratch[:, cols] * inv_rms
            - hidden_ref[:, cols].astype(F32) * factor
        ).astype(BF16)
    copies = [pltpu.make_async_copy(resid_ref, resid_hbm, sems.at[0])]
    copies[0].start()
    length = count * tokens
    group_width = GROUP * HEAD_SIZE
    for g in range(KEY_VALUE_HEADS):
        keys, values = kv_stacks(key_refs, value_refs, g)
        keys_t = jnp.transpose(keys.astype(F32)).astype(BF16)
        d_keys = jnp.zeros((length, HEAD_SIZE), F32)
        d_values = jnp.zeros((length, HEAD_SIZE), F32)
        for pair in range(g * GROUP // 2, (g + 1) * GROUP // 2):
            cols_a, cols_b = pair_cols(pair)
            d_out = head_pair(resid_ref, pair)
            probs = probs_ref[pair]
            d_probs = mm(values, d_out, NT)
            row_dot = jnp.sum(probs * d_probs, axis=0, keepdims=True)
            d_scores = (probs * (d_probs - row_dot)).astype(BF16)
            d_keys = d_keys + mm(d_scores, head_pair(query_ref, pair))
            d_values = d_values + mm(probs.astype(BF16), d_out)
            d_query_t = mm(keys_t, d_scores) * SCALE
            dq_ref[:, cols_a] = jnp.transpose(d_query_t[:, :tokens]).astype(BF16)
            dq_ref[:, cols_b] = jnp.transpose(d_query_t[:, tokens:]).astype(BF16)
        cols = slice(g * group_width, (g + 1) * group_width)
        copy = pltpu.make_async_copy(dq_ref.at[:, cols], dq_hbm.at[:, cols], sems.at[1 + g])
        copy.start()
        copies.append(copy)
        k_cols = slice(g * HEAD_SIZE, (g + 1) * HEAD_SIZE)
        v_cols = slice((KEY_VALUE_HEADS + g) * HEAD_SIZE, (KEY_VALUE_HEADS + g + 1) * HEAD_SIZE)
        d_keys = d_keys * SCALE
        own_ref[:, k_cols] = d_keys[:tokens]
        own_ref[:, v_cols] = d_values[:tokens]
        for s, ref in enumerate(other_refs, 1):
            ref[:, k_cols] = d_keys[s * tokens : (s + 1) * tokens].astype(BF16)
            ref[:, v_cols] = d_values[s * tokens : (s + 1) * tokens].astype(BF16)
    for copy in copies:
        copy.wait()


def output_kernel(
    count, pieces, tokens_in_all, place_ref, weight_ref, gain_ref, hidden_ref, grad_ref, *refs
):
    own_ref, refs = refs[0], refs[1:]
    arrived_refs = refs[: count - 1]
    y_refs = refs[count - 1 : count - 1 + pieces]
    out_hbm, dk_hbm, dv_hbm, d_weight_hbm, d_gain_hbm = refs[count - 1 + pieces : -6]
    out_ref, dk_ref, dv_ref, d_weight_ref, d_gain_ref, sems = refs[-6:]
    split = KEY_VALUE_HEADS * HEAD_SIZE
    d_kv = own_ref[...]
    for ref in arrived_refs:
        d_kv = d_kv + ref[...].astype(F32)
    dk_ref[...] = d_kv[:, :split].astype(BF16)
    dv_ref[...] = d_kv[:, split:].astype(BF16)
    d_gain_ref[...] = gain_ref[...] * (1.0 / tokens_in_all)
    copies = []

    def send(source, target):
        copy = pltpu.make_async_copy(source, target, sems.at[len(copies)])
        copy.start()
        copies.append(copy)

    send(dk_ref, dk_hbm)
    send(dv_ref, dv_hbm)
    send(d_gain_ref, d_gain_hbm)
    tokens = hidden_ref.shape[0]
    place = place_ref[...]
    weight = weight_ref[...]
    total = jnp.zeros((tokens, COLS), F32)
    for cols in column_blocks():
        y = mm(place, stacked(y_refs, cols))
        out_ref[:, cols] = (hidden_ref[:, cols].astype(F32) + weight * y).astype(BF16)
        send(out_ref.at[:, cols], out_hbm.at[:, cols])
        total = total + y * grad_ref[:, cols].astype(F32)
    d_weight_ref[...] = col_to_row(jnp.sum(total, axis=1, keepdims=True))
    send(d_weight_ref, d_weight_hbm)
    for copy in copies:
        copy.wait()


def run(kernel, name, inputs, outputs, flops, scratch=(), limit=20 * MIB):
    nbytes = sum(x.size * x.dtype.itemsize for _, x in inputs) + sum(
        x.size * x.dtype.itemsize for _, x in outputs
    )
    spec = {space: pl.BlockSpec(memory_space=space) for space in (VMEM, HBM)}
    results = pl.pallas_call(
        kernel,
        out_shape=[x for _, x in outputs],
        in_specs=[spec[space] for space, _ in inputs],
        out_specs=[spec[space] for space, _ in outputs],
        scratch_shapes=list(scratch),
        compiler_params=pltpu.CompilerParams(vmem_limit_bytes=limit),
        cost_estimate=pl.CostEstimate(flops=flops, bytes_accessed=nbytes, transcendentals=0),
        name=name,
    )(*[pltpu.with_memory_space_constraint(x, HBM) if space is HBM else x for space, x in inputs])
    return list(results)


def placed(space, arrays):
    return [(space, x) for x in arrays]


def pairwise(value, axis, step):
    count = lax.axis_size(axis)
    return lax.ppermute(value, axis, [(i, i ^ step) for i in range(count)])


def exchange_flat(flat, capacity):
    count = lax.axis_size("exp")
    rows = EXP_DEV * capacity
    blocks = [flat[s * rows : (s + 1) * rows] for s in range(count)]
    moved = [blocks[0]] + [pairwise(blocks[s], "exp", s) for s in range(1, count)]
    return jnp.concatenate(moved, axis=0)


def exchange(pieces, capacity, steps):
    if lax.axis_size("exp") != len(pieces):
        return [exchange_flat(pieces[0], capacity)]
    return [
        pairwise(piece, "exp", s) if s > 0 and s in steps else piece
        for s, piece in enumerate(pieces)
    ]


def doubled(value, axis, step):
    return value + pairwise(value, axis, step)


def sum_over(value, axis, first=1):
    step = first
    while step < lax.axis_size(axis):
        value = doubled(value, axis, step)
        step *= 2
    return value


def widened(act, value, axis, step):
    rows = value.shape[0]
    wide = jnp.pad(value, ((0, WIDE_LINES - rows), (0, 0)))
    return act(wide, axis, step)[:rows]


def shaped(shape, dtype):
    return jax.ShapeDtypeStruct(shape, dtype)


def per_device(
    queries,
    keys,
    values,
    resid,
    block_order,
    norm_gain,
    w_gate,
    w_down,
    routes,
    route_weight,
    d_out,
):
    query_rows = queries[0]
    resid_rows = resid[0]
    grad_rows = d_out[0]
    tokens = query_rows.shape[0]
    chosen = routes.reshape(1, tokens)
    gain = norm_gain.reshape(1, D)
    ctx_count = lax.axis_size("ctx")
    exp_count = lax.axis_size("exp")
    experts = EXP_DEV * exp_count
    capacity = 3 * tokens // (2 * experts)
    slots = experts * capacity
    rows = EXP_DEV * capacity
    piece_count = exp_count if rows % 16 == 0 else 1
    piece_shapes = [shaped((slots // piece_count, D), BF16)] * piece_count
    token_shape = shaped((tokens, D), BF16)
    kv_width = 2 * KEY_VALUE_HEADS * HEAD_SIZE
    attn_flops = 4 * tokens * ctx_count * tokens * QUERY_HEADS * HEAD_SIZE
    place_flops = 2 * slots * tokens * D
    expert_flops = 2 * slots * D * FFE * EXP_DEV

    own_keys, own_values = keys[0], values[0]
    near = [grad_rows, own_keys, own_values, gain, query_rows, resid_rows]
    grad_rows, own_keys, own_values, gain, query_rows, resid_rows, slot, pos, weight, *send_grad = run(
        functools.partial(dispatch_kernel, ctx_count, experts, capacity),
        "dispatch_grads",
        placed(HBM, near + [route_weight, chosen, block_order]),
        placed(
            VMEM,
            [shaped(x.shape, x.dtype) for x in near]
            + [
                shaped((1, tokens), jnp.int32),
                shaped((ctx_count, tokens), jnp.int32),
                shaped((1, tokens), F32),
            ]
            + piece_shapes,
        ),
        place_flops,
        scratch=[
            pltpu.SMEM(block_order.shape, jnp.int32),
            pltpu.VMEM((1, tokens), jnp.int32),
            pltpu.SemaphoreType.DMA((9,)),
        ],
    )
    all_keys = [own_keys] + [pairwise(own_keys, "ctx", s) for s in range(1, ctx_count)]
    all_values = [own_values] + [pairwise(own_values, "ctx", s) for s in range(1, ctx_count)]
    steps = range(piece_count)
    near = [s for s in steps if s & (s - 1) == 0]
    far = [s for s in steps if s & (s - 1) != 0]
    groups = [group for group in (far, near) if group]
    ordered = [s for group in groups for s in group]
    arrived_grad = exchange(send_grad, capacity, steps)

    hidden, *send_x = run(
        functools.partial(attention_kernel, ctx_count),
        "attention_forward",
        placed(VMEM, [pos, slot, gain, query_rows, resid_rows] + all_keys + all_values),
        placed(VMEM, [token_shape] + piece_shapes),
        attn_flops + place_flops,
    )
    probs, down_near, gate_near, place, weight_wide = run(
        functools.partial(probs_kernel, ctx_count),
        "probs_and_weights",
        placed(VMEM, [pos, slot, weight])
        + placed(HBM, [w_down, w_gate])
        + placed(VMEM, [query_rows] + all_keys),
        placed(
            VMEM,
            [
                shaped((QUERY_HEADS // 2, ctx_count * tokens, 2 * tokens), F32),
                shaped((EXP_DEV * FFE, D), BF16),
                shaped((D, EXP_DEV * FFE), BF16),
                shaped((tokens, slots), BF16),
                shaped((tokens, COLS), F32),
            ],
        ),
        attn_flops // 2,
        scratch=[pltpu.SemaphoreType.DMA((2 * EXP_DEV,))],
    )

    if far:
        arrived_x = exchange(send_x, capacity, far)
        after = [arrived_grad[s] for s in near]
        start, place, after = lax.optimization_barrier(([send_x[s] for s in near], place, after))
        for s, grad_piece, piece in zip(near, after, start):
            arrived_grad[s] = grad_piece
            arrived_x[s] = piece
        arrived_x = exchange(arrived_x, capacity, near)
    else:
        arrived_x = exchange(send_x, capacity, steps)

    (d_act,) = run(
        functools.partial(expert_grad_kernel, capacity),
        "act_grads",
        placed(VMEM, [down_near] + [arrived_grad[s] for s in ordered]),
        placed(VMEM, [shaped((slots, FFE), F32)]),
        expert_flops,
    )
    send_dn = [None] * piece_count
    acts = []
    done = 0
    for group in groups:
        group_rows = sum(piece_shapes[s].shape[0] for s in group)
        act, *parts = run(
            functools.partial(expert_back_kernel, capacity, len(group), done),
            "expert_backward",
            placed(VMEM, [gate_near, d_act] + [arrived_x[s] for s in group]),
            placed(
                VMEM,
                [shaped((group_rows, EXP_DEV * FFE), BF16)] + [piece_shapes[s] for s in group],
            ),
            2 * expert_flops * group_rows // slots,
        )
        acts.append(act)
        done += group_rows
        for s, part in zip(group, parts):
            send_dn[s] = part
    dn = exchange(send_dn, capacity, steps)
    terms, *outs = run(
        functools.partial(expert_out_kernel, piece_count, len(acts)),
        "expert_output",
        placed(VMEM, [down_near, gain] + acts)
        + placed(VMEM, [arrived_x[s] for s in ordered] + [send_dn[s] for s in ordered]),
        placed(VMEM, [shaped((GAIN_LINES, LANES), F32)] + piece_shapes),
        expert_flops,
    )
    send_y = [outs[ordered.index(s)] for s in steps]
    terms = doubled(sum_over(terms, "ctx"), "exp", 2)
    terms, send_y, dn = lax.optimization_barrier((terms, send_y, dn))
    y = exchange(send_y, capacity, steps)
    terms = widened(doubled, terms, "dp", 2)
    terms, place_back = lax.optimization_barrier((terms, place))
    terms = doubled(terms, "exp", 1)

    d_hidden, d_queries, kv_own, *kv_send = run(
        functools.partial(backward_kernel, ctx_count, piece_count),
        "residual_attention_backward",
        placed(VMEM, [place_back, gain, hidden, grad_rows, query_rows, probs])
        + placed(VMEM, dn + all_keys + all_values),
        placed(HBM, [token_shape] * 2)
        + placed(
            VMEM,
            [shaped((tokens, kv_width), F32)]
            + [shaped((tokens, kv_width), BF16)] * (ctx_count - 1),
        ),
        attn_flops + place_flops,
        scratch=[
            pltpu.VMEM((tokens, D), BF16),
            pltpu.VMEM((tokens, D), BF16),
            pltpu.VMEM((tokens, D), F32),
            pltpu.SemaphoreType.DMA((1 + KEY_VALUE_HEADS,)),
        ],
    )
    terms, kv_send = lax.optimization_barrier((terms, kv_send))
    terms = sum_over(sum_over(terms, "exp", first=4), "dp", first=4)
    terms = doubled(terms, "dp", 1)
    kv_arrived = [pairwise(part, "ctx", s) for s, part in enumerate(kv_send, 1)]

    kv_shape = shaped((tokens, kv_width // 2), BF16)
    final_shapes = [token_shape, kv_shape, kv_shape]
    final_shapes += [shaped((1, tokens), F32), shaped((GAIN_LINES, LANES), F32)]
    total_tokens = tokens * ctx_count * exp_count * lax.axis_size("dp")
    layer_out, d_keys, d_values, d_weight, d_gain = run(
        functools.partial(output_kernel, ctx_count, piece_count, total_tokens),
        "layer_output",
        placed(
            VMEM,
            [place, weight_wide, terms, hidden, grad_rows, kv_own]
            + kv_arrived
            + y,
        ),
        placed(HBM, final_shapes),
        place_flops,
        scratch=[pltpu.VMEM(x.shape, x.dtype) for x in final_shapes]
        + [pltpu.SemaphoreType.DMA((4 + D // COLS,))],
    )
    return (
        layer_out[None],
        d_hidden[None],
        d_queries[None],
        d_keys[None],
        d_values[None],
        d_weight,
        d_gain.reshape(D),
    )


def solution(mesh):
    in_specs = (
        P(("exp", "dp"), "ctx", None),
        P(("exp", "dp"), "ctx", None),
        P(("exp", "dp"), "ctx", None),
        P(("exp", "dp"), "ctx", None),
        P(),
        P(),
        P("exp", None, None),
        P("exp", None, None),
        P(("exp", "dp"), "ctx", None),
        P(("exp", "dp"), "ctx"),
        P(("exp", "dp"), "ctx", None),
    )
    out_specs = (
        P(("exp", "dp"), "ctx", None),
        P(("exp", "dp"), "ctx", None),
        P(("exp", "dp"), "ctx", None),
        P(("exp", "dp"), "ctx", None),
        P(("exp", "dp"), "ctx", None),
        P(("exp", "dp"), "ctx"),
        P(),
    )
    return jax.shard_map(
        per_device, mesh=mesh, in_specs=in_specs, out_specs=out_specs, check_vma=False
    )
```

```python
import functools

import jax
import jax.numpy as jnp
from jax import lax
from jax.experimental import pallas as pl
from jax.experimental.pallas import tpu as pltpu
from jax.sharding import PartitionSpec as P

D = 2048
HEAD_SIZE = 128
QUERY_HEADS = 16
KEY_VALUE_HEADS = 2
GROUP = QUERY_HEADS // KEY_VALUE_HEADS
FFE = 384
EXP_DEV = 2
COLS = 256
LANES = 128
GAIN_LINES = D // LANES
WIDE_LINES = 32
SCALE = HEAD_SIZE ** (-0.5)
EXP2_SCALE = SCALE * 1.4426950408889634
F32 = jnp.float32
BF16 = jnp.bfloat16
NN = (((1,), (0,)), ((), ()))
NT = (((1,), (1,)), ((), ()))
MIB = 1 << 20
VMEM, HBM = pltpu.VMEM, pltpu.HBM


def mm(a, b, dims=NN):
    return lax.dot_general(a, b, dims, preferred_element_type=F32)


def iota(shape, dim):
    return lax.broadcasted_iota(jnp.int32, shape, dim)


def row_to_col(row):
    n = row.shape[1]
    eye = iota((n, n), 0) == iota((n, n), 1)
    return jnp.sum(jnp.where(eye, row.astype(F32), 0.0), axis=1, keepdims=True)


def col_to_row(col):
    n = col.shape[0]
    eye = iota((n, n), 0) == iota((n, n), 1)
    return jnp.sum(jnp.where(eye, col, 0.0), axis=0, keepdims=True)


def block_positions(order_ref, ctx_index, tokens):
    span = tokens // 8
    index = iota((1, tokens), 1)
    which = index // span
    start = jnp.zeros((1, tokens), jnp.int32)
    for b in range(8):
        start = jnp.where(which == b, order_ref[ctx_index * 8 + b], start)
    return start * span + index % span


def stacked(refs, cols=slice(None)):
    parts = [r[:, cols] for r in refs]
    return parts[0] if len(parts) == 1 else jnp.concatenate(parts, axis=0)


def column_blocks(width=D, step=COLS):
    return [slice(c, c + step) for c in range(0, width, step)]


def store_pieces(refs, cols, rows_value):
    at = 0
    for r in refs:
        n = r.shape[0]
        r[:, cols] = rows_value[at : at + n]
        at += n


def pair_cols(pair):
    start = 2 * pair * HEAD_SIZE
    return slice(start, start + HEAD_SIZE), slice(start + HEAD_SIZE, start + 2 * HEAD_SIZE)


def head_pair(ref, pair):
    first, second = pair_cols(pair)
    return jnp.concatenate([ref[:, first], ref[:, second]], axis=0)


def placement_rows(slot_row, slots):
    tokens = slot_row.shape[1]
    return jnp.where(iota((slots, tokens), 0) == slot_row, 1.0, 0.0).astype(BF16)


def placement_cols(slot_row, slots):
    tokens = slot_row.shape[1]
    slot_col = row_to_col(slot_row)
    return jnp.where(iota((tokens, slots), 1).astype(F32) == slot_col, 1.0, 0.0).astype(BF16)


def dispatch_kernel(count, experts, capacity, *refs):
    sources, refs = refs[:9], refs[9:]
    targets, refs = refs[:6], refs[6:]
    grad_ref = targets[0]
    slot_ref, pos_ref, weight_ref = refs[:3]
    send_refs = refs[3:-3]
    order_ref, routes_ref, sems = refs[-3:]
    targets = targets + (weight_ref, routes_ref, order_ref)
    copies = [
        pltpu.make_async_copy(source, target, sems.at[i])
        for i, (source, target) in enumerate(zip(sources, targets))
    ]
    for copy in copies[6:] + copies[:6]:
        copy.start()
    for copy in copies[6:]:
        copy.wait()
    tokens = routes_ref.shape[1]
    chosen = routes_ref[...]
    lanes = max(experts, 16)
    hits = jnp.where(iota((lanes, tokens), 0) == chosen, 1.0, 0.0)
    before = jnp.where(iota((tokens, tokens), 0) < iota((tokens, tokens), 1), 1.0, 0.0)
    earlier = mm(hits.astype(BF16), before.astype(BF16))
    rank = jnp.sum(hits * earlier, axis=0, keepdims=True).astype(jnp.int32)
    target = (chosen // EXP_DEV) ^ lax.axis_index("exp")
    slot = (target * EXP_DEV + chosen % EXP_DEV) * capacity + rank
    slot_ref[...] = slot
    me = lax.axis_index("ctx")
    for s in range(count):
        pos_ref[s : s + 1, :] = block_positions(order_ref, me ^ s, tokens)
    place = placement_rows(slot, experts * capacity)
    weight = row_to_col(weight_ref[...])
    copies[0].wait()
    for cols in column_blocks():
        scaled = (weight * grad_ref[:, cols].astype(F32)).astype(BF16)
        store_pieces(send_refs, cols, mm(place, scaled).astype(BF16))
    for copy in copies[1:6]:
        copy.wait()


def kv_stacks(key_refs, value_refs, g):
    cols = slice(g * HEAD_SIZE, (g + 1) * HEAD_SIZE)
    return stacked(key_refs, cols), stacked(value_refs, cols)


def attention_kernel(
    count, pos_ref, slot_ref, gain_ref, query_ref, resid_ref, *refs
):
    key_refs, value_refs = refs[:count], refs[count : 2 * count]
    hidden_ref, send_refs = refs[2 * count], refs[2 * count + 1 :]
    tokens = query_ref.shape[0]
    query_pos = row_to_col(pos_ref[:1, :])
    bias = jnp.concatenate(
        [
            jnp.where(pos_ref[s : s + 1, :].astype(F32) <= query_pos, 0.0, -1e30)
            for s in range(count)
        ],
        axis=1,
    )
    length = count * tokens
    ones = jnp.ones((length, HEAD_SIZE), BF16)
    total = jnp.zeros((tokens, HEAD_SIZE), F32)
    for g in range(KEY_VALUE_HEADS):
        keys, values = kv_stacks(key_refs, value_refs, g)
        values = jnp.concatenate([values, ones], axis=1)
        for h in range(g * GROUP, (g + 1) * GROUP):
            cols = slice(h * HEAD_SIZE, (h + 1) * HEAD_SIZE)
            scores = mm(query_ref[:, cols], keys, NT) + bias
            peak = jnp.max(scores, axis=1, keepdims=True)
            weights = jnp.exp2((scores - peak) * EXP2_SCALE).astype(BF16)
            mixed = mm(weights, values)
            attended = mixed[:, :HEAD_SIZE] / mixed[:, HEAD_SIZE:]
            hidden = (resid_ref[:, cols].astype(F32) + attended).astype(BF16)
            hidden_ref[:, cols] = hidden
            wide = hidden.astype(F32)
            total = total + wide * wide
    inv_rms = lax.rsqrt(jnp.sum(total, axis=1, keepdims=True) * (1.0 / D) + 1e-06)
    slots = sum(r.shape[0] for r in send_refs)
    place = placement_rows(slot_ref[...], slots)
    for cols in column_blocks():
        normed = (hidden_ref[:, cols].astype(F32) * inv_rms * gain_ref[:, cols]).astype(BF16)
        store_pieces(send_refs, cols, mm(place, normed).astype(BF16))


def first_expert_rows(slots, capacity):
    return iota((slots, 1), 0) % (EXP_DEV * capacity) < capacity


def probs_kernel(count, pos_ref, slot_ref, weight_ref, down_hbm, gate_hbm, query_ref, *refs):
    key_refs = refs[:count]
    probs_ref, down_ref, gate_ref, place_ref, wide_ref, sems = refs[count:]
    spans = [slice(e * FFE, (e + 1) * FFE) for e in range(EXP_DEV)]
    down_copies = [
        pltpu.make_async_copy(down_hbm.at[e], down_ref.at[span, :], sems.at[e])
        for e, span in enumerate(spans)
    ]
    gate_copies = [
        pltpu.make_async_copy(gate_hbm.at[e], gate_ref.at[:, span], sems.at[EXP_DEV + e])
        for e, span in enumerate(spans)
    ]
    for copy in down_copies + gate_copies:
        copy.start()
    place_ref[...] = placement_cols(slot_ref[...], place_ref.shape[1])
    wide_ref[...] = jnp.broadcast_to(row_to_col(weight_ref[...]), wide_ref.shape)
    query_pos = pos_ref[:1, :].astype(F32)
    bias = jnp.concatenate(
        [
            jnp.where(row_to_col(pos_ref[s : s + 1, :]) <= query_pos, 0.0, -1e30)
            for s in range(count)
        ],
        axis=0,
    )
    bias = jnp.concatenate([bias, bias], axis=1)
    for g in range(KEY_VALUE_HEADS):
        keys = stacked(key_refs, slice(g * HEAD_SIZE, (g + 1) * HEAD_SIZE))
        for pair in range(g * GROUP // 2, (g + 1) * GROUP // 2):
            scores = mm(keys, head_pair(query_ref, pair), NT) + bias
            peak = jnp.max(scores, axis=0, keepdims=True)
            weights = jnp.exp2((scores - peak) * EXP2_SCALE)
            probs_ref[pair] = weights * (1.0 / jnp.sum(weights, axis=0, keepdims=True))
    for copy in down_copies + gate_copies:
        copy.wait()


def expert_grad_kernel(capacity, down_ref, *refs):
    grads = stacked(refs[:-1])
    first = first_expert_rows(grads.shape[0], capacity)
    both = mm(grads, down_ref[...], NT)
    refs[-1][...] = jnp.where(first, both[:, :FFE], both[:, FFE:])


def expert_back_kernel(capacity, pieces, gate_ref, d_act_ref, *refs):
    rows = stacked(refs[:pieces])
    act_ref, back_refs = refs[pieces], refs[pieces + 1 :]
    first = first_expert_rows(rows.shape[0], capacity)
    both = mm(rows, gate_ref[...])
    pre = jnp.where(first, both[:, :FFE], both[:, FFE:])
    gate = 1.0 / (1.0 + jnp.exp(-pre))
    act = pre * gate
    d_pre = d_act_ref[...] * gate * (1.0 + pre * (1.0 - gate))
    act, d_pre = [
        jnp.concatenate([jnp.where(first, x, 0.0), jnp.where(first, 0.0, x)], axis=1).astype(BF16)
        for x in (act, d_pre)
    ]
    act_ref[...] = act
    for cols in column_blocks():
        store_pieces(back_refs, cols, mm(d_pre, gate_ref[cols, :], NT).astype(BF16))


def expert_out_kernel(pieces, down_ref, gain_ref, act_ref, *refs):
    act = act_ref[...]
    row_refs, back_refs = refs[:pieces], refs[pieces : 2 * pieces]
    terms_ref, out_refs = refs[2 * pieces], refs[2 * pieces + 1 :]
    for cols in column_blocks():
        store_pieces(out_refs, cols, mm(act, down_ref[:, cols]).astype(BF16))
        products = stacked(row_refs, cols).astype(F32) * stacked(back_refs, cols).astype(F32)
        terms = jnp.sum(products, axis=0, keepdims=True) / gain_ref[:, cols]
        for at in range(0, COLS, LANES):
            line = (cols.start + at) // LANES
            part = jnp.broadcast_to(terms[:, at : at + LANES], (terms_ref.shape[0], LANES))
            terms_ref[:, line, :] = part


def backward_kernel(
    count, pieces, place_ref, gain_ref, hidden_ref, grad_ref, query_ref, probs_ref, *refs
):
    dn_refs = refs[:pieces]
    key_refs = refs[pieces : pieces + count]
    value_refs = refs[pieces + count : pieces + 2 * count]
    resid_hbm, dq_hbm, own_ref = refs[pieces + 2 * count : pieces + 2 * count + 3]
    other_refs = refs[pieces + 2 * count + 3 : -4]
    resid_ref, dq_ref, dn_scratch, sems = refs[-4:]
    tokens = hidden_ref.shape[0]
    place = place_ref[...]
    square = jnp.zeros((tokens, COLS), F32)
    mixing = jnp.zeros((tokens, COLS), F32)
    for cols in column_blocks():
        dn = mm(place, stacked(dn_refs, cols)) * gain_ref[:, cols]
        dn_scratch[:, cols] = dn
        hidden = hidden_ref[:, cols].astype(F32)
        square = square + hidden * hidden
        mixing = mixing + dn * hidden
    inv_rms = lax.rsqrt(jnp.sum(square, axis=1, keepdims=True) * (1.0 / D) + 1e-06)
    mean_mix = jnp.sum(mixing, axis=1, keepdims=True) * (1.0 / D)
    factor = inv_rms * inv_rms * inv_rms * mean_mix
    for cols in column_blocks():
        resid_ref[:, cols] = (
            grad_ref[:, cols].astype(F32)
            + dn_scratch[:, cols] * inv_rms
            - hidden_ref[:, cols].astype(F32) * factor
        ).astype(BF16)
    copies = [pltpu.make_async_copy(resid_ref, resid_hbm, sems.at[0])]
    copies[0].start()
    length = count * tokens
    group_width = GROUP * HEAD_SIZE
    for g in range(KEY_VALUE_HEADS):
        keys, values = kv_stacks(key_refs, value_refs, g)
        keys_t = jnp.transpose(keys.astype(F32)).astype(BF16)
        d_keys = jnp.zeros((length, HEAD_SIZE), F32)
        d_values = jnp.zeros((length, HEAD_SIZE), F32)
        for pair in range(g * GROUP // 2, (g + 1) * GROUP // 2):
            cols_a, cols_b = pair_cols(pair)
            d_out = head_pair(resid_ref, pair)
            probs = probs_ref[pair]
            d_probs = mm(values, d_out, NT)
            row_dot = jnp.sum(probs * d_probs, axis=0, keepdims=True)
            d_scores = (probs * (d_probs - row_dot)).astype(BF16)
            d_keys = d_keys + mm(d_scores, head_pair(query_ref, pair))
            d_values = d_values + mm(probs.astype(BF16), d_out)
            d_query_t = mm(keys_t, d_scores) * SCALE
            dq_ref[:, cols_a] = jnp.transpose(d_query_t[:, :tokens]).astype(BF16)
            dq_ref[:, cols_b] = jnp.transpose(d_query_t[:, tokens:]).astype(BF16)
        cols = slice(g * group_width, (g + 1) * group_width)
        copy = pltpu.make_async_copy(dq_ref.at[:, cols], dq_hbm.at[:, cols], sems.at[1 + g])
        copy.start()
        copies.append(copy)
        k_cols = slice(g * HEAD_SIZE, (g + 1) * HEAD_SIZE)
        v_cols = slice((KEY_VALUE_HEADS + g) * HEAD_SIZE, (KEY_VALUE_HEADS + g + 1) * HEAD_SIZE)
        d_keys = d_keys * SCALE
        own_ref[:, k_cols] = d_keys[:tokens]
        own_ref[:, v_cols] = d_values[:tokens]
        for s, ref in enumerate(other_refs, 1):
            ref[:, k_cols] = d_keys[s * tokens : (s + 1) * tokens].astype(BF16)
            ref[:, v_cols] = d_values[s * tokens : (s + 1) * tokens].astype(BF16)
    for copy in copies:
        copy.wait()


def output_kernel(
    count, pieces, tokens_in_all, place_ref, weight_ref, gain_ref, hidden_ref, grad_ref, *refs
):
    own_ref, refs = refs[0], refs[1:]
    arrived_refs = refs[: count - 1]
    y_refs = refs[count - 1 : count - 1 + pieces]
    out_hbm, dk_hbm, dv_hbm, d_weight_hbm, d_gain_hbm = refs[count - 1 + pieces : -6]
    out_ref, dk_ref, dv_ref, d_weight_ref, d_gain_ref, sems = refs[-6:]
    split = KEY_VALUE_HEADS * HEAD_SIZE
    d_kv = own_ref[...]
    for ref in arrived_refs:
        d_kv = d_kv + ref[...].astype(F32)
    dk_ref[...] = d_kv[:, :split].astype(BF16)
    dv_ref[...] = d_kv[:, split:].astype(BF16)
    d_gain_ref[...] = gain_ref[...] * (1.0 / tokens_in_all)
    copies = []

    def send(source, target):
        copy = pltpu.make_async_copy(source, target, sems.at[len(copies)])
        copy.start()
        copies.append(copy)

    send(dk_ref, dk_hbm)
    send(dv_ref, dv_hbm)
    send(d_gain_ref, d_gain_hbm)
    tokens = hidden_ref.shape[0]
    place = place_ref[...]
    weight = weight_ref[...]
    total = jnp.zeros((tokens, COLS), F32)
    for cols in column_blocks():
        y = mm(place, stacked(y_refs, cols))
        out_ref[:, cols] = (hidden_ref[:, cols].astype(F32) + weight * y).astype(BF16)
        send(out_ref.at[:, cols], out_hbm.at[:, cols])
        total = total + y * grad_ref[:, cols].astype(F32)
    d_weight_ref[...] = col_to_row(jnp.sum(total, axis=1, keepdims=True))
    send(d_weight_ref, d_weight_hbm)
    for copy in copies:
        copy.wait()


def run(kernel, name, inputs, outputs, flops, scratch=(), limit=20 * MIB):
    nbytes = sum(x.size * x.dtype.itemsize for _, x in inputs) + sum(
        x.size * x.dtype.itemsize for _, x in outputs
    )
    spec = {space: pl.BlockSpec(memory_space=space) for space in (VMEM, HBM)}
    results = pl.pallas_call(
        kernel,
        out_shape=[x for _, x in outputs],
        in_specs=[spec[space] for space, _ in inputs],
        out_specs=[spec[space] for space, _ in outputs],
        scratch_shapes=list(scratch),
        compiler_params=pltpu.CompilerParams(vmem_limit_bytes=limit),
        cost_estimate=pl.CostEstimate(flops=flops, bytes_accessed=nbytes, transcendentals=0),
        name=name,
    )(*[pltpu.with_memory_space_constraint(x, HBM) if space is HBM else x for space, x in inputs])
    return list(results)


def placed(space, arrays):
    return [(space, x) for x in arrays]


def pairwise(value, axis, step):
    count = lax.axis_size(axis)
    return lax.ppermute(value, axis, [(i, i ^ step) for i in range(count)])


def exchange_flat(flat, capacity):
    count = lax.axis_size("exp")
    rows = EXP_DEV * capacity
    blocks = [flat[s * rows : (s + 1) * rows] for s in range(count)]
    moved = [blocks[0]] + [pairwise(blocks[s], "exp", s) for s in range(1, count)]
    return jnp.concatenate(moved, axis=0)


def exchange(pieces, capacity):
    if lax.axis_size("exp") != len(pieces):
        return [exchange_flat(pieces[0], capacity)]
    return [pairwise(piece, "exp", s) if s > 0 else piece for s, piece in enumerate(pieces)]


def doubled(value, axis, step):
    return value + pairwise(value, axis, step)


def sum_over(value, axis, first=1):
    step = first
    while step < lax.axis_size(axis):
        value = doubled(value, axis, step)
        step *= 2
    return value


def widened(act, value, axis, step):
    rows = value.shape[0]
    wide = jnp.pad(value, ((0, WIDE_LINES - rows), (0, 0)))
    return act(wide, axis, step)[:rows]


def shaped(shape, dtype):
    return jax.ShapeDtypeStruct(shape, dtype)


def per_device(
    queries,
    keys,
    values,
    resid,
    block_order,
    norm_gain,
    w_gate,
    w_down,
    routes,
    route_weight,
    d_out,
):
    query_rows = queries[0]
    resid_rows = resid[0]
    grad_rows = d_out[0]
    tokens = query_rows.shape[0]
    chosen = routes.reshape(1, tokens)
    gain = norm_gain.reshape(1, D)
    ctx_count = lax.axis_size("ctx")
    exp_count = lax.axis_size("exp")
    experts = EXP_DEV * exp_count
    capacity = 3 * tokens // (2 * experts)
    slots = experts * capacity
    rows = EXP_DEV * capacity
    piece_count = exp_count if rows % 16 == 0 else 1
    piece_shapes = [shaped((slots // piece_count, D), BF16)] * piece_count
    token_shape = shaped((tokens, D), BF16)
    kv_width = 2 * KEY_VALUE_HEADS * HEAD_SIZE
    attn_flops = 4 * tokens * ctx_count * tokens * QUERY_HEADS * HEAD_SIZE
    place_flops = 2 * slots * tokens * D
    expert_flops = 2 * slots * D * FFE * EXP_DEV

    own_keys, own_values = keys[0], values[0]
    all_keys = [own_keys] + [pairwise(own_keys, "ctx", s) for s in range(1, ctx_count)]
    all_values = [own_values] + [pairwise(own_values, "ctx", s) for s in range(1, ctx_count)]

    near = [grad_rows, own_keys, own_values, gain, query_rows, resid_rows]
    grad_rows, own_keys, own_values, gain, query_rows, resid_rows, slot, pos, weight, *send_grad = run(
        functools.partial(dispatch_kernel, ctx_count, experts, capacity),
        "dispatch_grads",
        placed(HBM, near + [route_weight, chosen, block_order]),
        placed(
            VMEM,
            [shaped(x.shape, x.dtype) for x in near]
            + [
                shaped((1, tokens), jnp.int32),
                shaped((ctx_count, tokens), jnp.int32),
                shaped((1, tokens), F32),
            ]
            + piece_shapes,
        ),
        place_flops,
        scratch=[
            pltpu.SMEM(block_order.shape, jnp.int32),
            pltpu.VMEM((1, tokens), jnp.int32),
            pltpu.SemaphoreType.DMA((9,)),
        ],
    )
    all_keys[0], all_values[0] = own_keys, own_values
    arrived_grad = exchange(send_grad, capacity)

    hidden, *send_x = run(
        functools.partial(attention_kernel, ctx_count),
        "attention_forward",
        placed(VMEM, [pos, slot, gain, query_rows, resid_rows] + all_keys + all_values),
        placed(VMEM, [token_shape] + piece_shapes),
        attn_flops + place_flops,
    )
    arrived_x = exchange(send_x, capacity)

    probs, down_near, gate_near, place, weight_wide = run(
        functools.partial(probs_kernel, ctx_count),
        "probs_and_weights",
        placed(VMEM, [pos, slot, weight])
        + placed(HBM, [w_down, w_gate])
        + placed(VMEM, [query_rows] + all_keys),
        placed(
            VMEM,
            [
                shaped((QUERY_HEADS // 2, ctx_count * tokens, 2 * tokens), F32),
                shaped((EXP_DEV * FFE, D), BF16),
                shaped((D, EXP_DEV * FFE), BF16),
                shaped((tokens, slots), BF16),
                shaped((tokens, COLS), F32),
            ],
        ),
        attn_flops // 2,
        scratch=[pltpu.SemaphoreType.DMA((2 * EXP_DEV,))],
    )

    (d_act,) = run(
        functools.partial(expert_grad_kernel, capacity),
        "act_grads",
        placed(VMEM, [down_near] + arrived_grad),
        placed(VMEM, [shaped((slots, FFE), F32)]),
        expert_flops,
    )
    act, *send_dn = run(
        functools.partial(expert_back_kernel, capacity, piece_count),
        "expert_backward",
        placed(VMEM, [gate_near, d_act] + arrived_x),
        placed(VMEM, [shaped((slots, EXP_DEV * FFE), BF16)] + piece_shapes),
        2 * expert_flops,
    )
    dn = exchange(send_dn, capacity)
    group = exp_count * lax.axis_size("dp")
    terms, *send_y = run(
        functools.partial(expert_out_kernel, piece_count),
        "expert_output",
        placed(VMEM, [down_near, gain, act] + arrived_x + send_dn),
        placed(VMEM, [shaped((group, GAIN_LINES, LANES), F32)] + piece_shapes),
        expert_flops,
    )
    terms = lax.all_to_all(terms, ("exp", "dp"), split_axis=0, concat_axis=0, tiled=True)
    terms, send_y = lax.optimization_barrier((terms, send_y))
    y = exchange(send_y, capacity)

    d_hidden, d_queries, kv_own, *kv_send = run(
        functools.partial(backward_kernel, ctx_count, piece_count),
        "residual_attention_backward",
        placed(VMEM, [place, gain, hidden, grad_rows, query_rows, probs])
        + placed(VMEM, dn + all_keys + all_values),
        placed(HBM, [token_shape] * 2)
        + placed(
            VMEM,
            [shaped((tokens, kv_width), F32)]
            + [shaped((tokens, kv_width), BF16)] * (ctx_count - 1),
        ),
        attn_flops + place_flops,
        scratch=[
            pltpu.VMEM((tokens, D), BF16),
            pltpu.VMEM((tokens, D), BF16),
            pltpu.VMEM((tokens, D), F32),
            pltpu.SemaphoreType.DMA((1 + KEY_VALUE_HEADS,)),
        ],
    )
    terms, kv_own = lax.optimization_barrier((terms, kv_own))
    terms = sum_over(jnp.sum(terms, axis=0), "ctx")
    kv_arrived = [pairwise(part, "ctx", s) for s, part in enumerate(kv_send, 1)]

    kv_shape = shaped((tokens, kv_width // 2), BF16)
    final_shapes = [token_shape, kv_shape, kv_shape]
    final_shapes += [shaped((1, tokens), F32), shaped((GAIN_LINES, LANES), F32)]
    total_tokens = tokens * ctx_count * exp_count * lax.axis_size("dp")
    layer_out, d_keys, d_values, d_weight, d_gain = run(
        functools.partial(output_kernel, ctx_count, piece_count, total_tokens),
        "layer_output",
        placed(
            VMEM,
            [place, weight_wide, terms, hidden, grad_rows, kv_own]
            + kv_arrived
            + y,
        ),
        placed(HBM, final_shapes),
        place_flops,
        scratch=[pltpu.VMEM(x.shape, x.dtype) for x in final_shapes]
        + [pltpu.SemaphoreType.DMA((4 + D // COLS,))],
    )
    return (
        layer_out[None],
        d_hidden[None],
        d_queries[None],
        d_keys[None],
        d_values[None],
        d_weight,
        d_gain.reshape(D),
    )


def solution(mesh):
    in_specs = (
        P(("exp", "dp"), "ctx", None),
        P(("exp", "dp"), "ctx", None),
        P(("exp", "dp"), "ctx", None),
        P(("exp", "dp"), "ctx", None),
        P(),
        P(),
        P("exp", None, None),
        P("exp", None, None),
        P(("exp", "dp"), "ctx", None),
        P(("exp", "dp"), "ctx"),
        P(("exp", "dp"), "ctx", None),
    )
    out_specs = (
        P(("exp", "dp"), "ctx", None),
        P(("exp", "dp"), "ctx", None),
        P(("exp", "dp"), "ctx", None),
        P(("exp", "dp"), "ctx", None),
        P(("exp", "dp"), "ctx", None),
        P(("exp", "dp"), "ctx"),
        P(),
    )
    return jax.shard_map(
        per_device, mesh=mesh, in_specs=in_specs, out_specs=out_specs, check_vma=False
    )
```

```python
import functools

import jax
import jax.numpy as jnp
from jax import lax
from jax.experimental import pallas as pl
from jax.experimental.pallas import tpu as pltpu
from jax.sharding import PartitionSpec as P

D = 2048
HEAD_SIZE = 128
QUERY_HEADS = 16
KEY_VALUE_HEADS = 2
GROUP = QUERY_HEADS // KEY_VALUE_HEADS
FFE = 384
EXP_DEV = 2
COLS = 256
LANES = 128
GAIN_LINES = D // LANES
WIDE_LINES = 32
A_COST = 4000000000
B_COST = 0
SCALE = HEAD_SIZE ** (-0.5)
EXP2_SCALE = SCALE * 1.4426950408889634
F32 = jnp.float32
BF16 = jnp.bfloat16
NN = (((1,), (0,)), ((), ()))
NT = (((1,), (1,)), ((), ()))
MIB = 1 << 20
VMEM, HBM = pltpu.VMEM, pltpu.HBM


def mm(a, b, dims=NN):
    return lax.dot_general(a, b, dims, preferred_element_type=F32)


def iota(shape, dim):
    return lax.broadcasted_iota(jnp.int32, shape, dim)


def row_to_col(row):
    n = row.shape[1]
    eye = iota((n, n), 0) == iota((n, n), 1)
    return jnp.sum(jnp.where(eye, row.astype(F32), 0.0), axis=1, keepdims=True)


def col_to_row(col):
    n = col.shape[0]
    eye = iota((n, n), 0) == iota((n, n), 1)
    return jnp.sum(jnp.where(eye, col, 0.0), axis=0, keepdims=True)


def block_positions(order_ref, ctx_index, tokens):
    span = tokens // 8
    index = iota((1, tokens), 1)
    which = index // span
    start = jnp.zeros((1, tokens), jnp.int32)
    for b in range(8):
        start = jnp.where(which == b, order_ref[ctx_index * 8 + b], start)
    return start * span + index % span


def stacked(refs, cols=slice(None)):
    parts = [r[:, cols] for r in refs]
    return parts[0] if len(parts) == 1 else jnp.concatenate(parts, axis=0)


def column_blocks(width=D, step=COLS):
    return [slice(c, c + step) for c in range(0, width, step)]


def store_pieces(refs, cols, rows_value):
    at = 0
    for r in refs:
        n = r.shape[0]
        r[:, cols] = rows_value[at : at + n]
        at += n


def pair_cols(pair):
    start = 2 * pair * HEAD_SIZE
    return slice(start, start + HEAD_SIZE), slice(start + HEAD_SIZE, start + 2 * HEAD_SIZE)


def head_pair(ref, pair):
    first, second = pair_cols(pair)
    return jnp.concatenate([ref[:, first], ref[:, second]], axis=0)


def placement_rows(slot_row, slots):
    tokens = slot_row.shape[1]
    return jnp.where(iota((slots, tokens), 0) == slot_row, 1.0, 0.0).astype(BF16)


def placement_cols(slot_row, slots):
    tokens = slot_row.shape[1]
    slot_col = row_to_col(slot_row)
    return jnp.where(iota((tokens, slots), 1).astype(F32) == slot_col, 1.0, 0.0).astype(BF16)


def dispatch_kernel(count, experts, capacity, *refs):
    sources, refs = refs[:9], refs[9:]
    targets, refs = refs[:6], refs[6:]
    grad_ref = targets[0]
    slot_ref, pos_ref, weight_ref = refs[:3]
    send_refs = refs[3:-3]
    order_ref, routes_ref, sems = refs[-3:]
    targets = targets + (weight_ref, routes_ref, order_ref)
    copies = [
        pltpu.make_async_copy(source, target, sems.at[i])
        for i, (source, target) in enumerate(zip(sources, targets))
    ]
    for copy in copies[6:] + copies[:6]:
        copy.start()
    for copy in copies[6:]:
        copy.wait()
    tokens = routes_ref.shape[1]
    chosen = routes_ref[...]
    lanes = max(experts, 16)
    hits = jnp.where(iota((lanes, tokens), 0) == chosen, 1.0, 0.0)
    before = jnp.where(iota((tokens, tokens), 0) < iota((tokens, tokens), 1), 1.0, 0.0)
    earlier = mm(hits.astype(BF16), before.astype(BF16))
    rank = jnp.sum(hits * earlier, axis=0, keepdims=True).astype(jnp.int32)
    target = (chosen // EXP_DEV) ^ lax.axis_index("exp")
    slot = (target * EXP_DEV + chosen % EXP_DEV) * capacity + rank
    slot_ref[...] = slot
    me = lax.axis_index("ctx")
    for s in range(count):
        pos_ref[s : s + 1, :] = block_positions(order_ref, me ^ s, tokens)
    place = placement_rows(slot, experts * capacity)
    weight = row_to_col(weight_ref[...])
    copies[0].wait()
    for cols in column_blocks():
        scaled = (weight * grad_ref[:, cols].astype(F32)).astype(BF16)
        store_pieces(send_refs, cols, mm(place, scaled).astype(BF16))
    for copy in copies[1:6]:
        copy.wait()


def kv_stacks(key_refs, value_refs, g):
    cols = slice(g * HEAD_SIZE, (g + 1) * HEAD_SIZE)
    return stacked(key_refs, cols), stacked(value_refs, cols)


def attention_kernel(
    count, pos_ref, slot_ref, gain_ref, query_ref, resid_ref, *refs
):
    key_refs, value_refs = refs[:count], refs[count : 2 * count]
    hidden_ref, send_refs = refs[2 * count], refs[2 * count + 1 :]
    tokens = query_ref.shape[0]
    query_pos = row_to_col(pos_ref[:1, :])
    bias = jnp.concatenate(
        [
            jnp.where(pos_ref[s : s + 1, :].astype(F32) <= query_pos, 0.0, -1e30)
            for s in range(count)
        ],
        axis=1,
    )
    length = count * tokens
    ones = jnp.ones((length, HEAD_SIZE), BF16)
    total = jnp.zeros((tokens, HEAD_SIZE), F32)
    for g in range(KEY_VALUE_HEADS):
        keys, values = kv_stacks(key_refs, value_refs, g)
        values = jnp.concatenate([values, ones], axis=1)
        for h in range(g * GROUP, (g + 1) * GROUP):
            cols = slice(h * HEAD_SIZE, (h + 1) * HEAD_SIZE)
            scores = mm(query_ref[:, cols], keys, NT) + bias
            peak = jnp.max(scores, axis=1, keepdims=True)
            weights = jnp.exp2((scores - peak) * EXP2_SCALE).astype(BF16)
            mixed = mm(weights, values)
            attended = mixed[:, :HEAD_SIZE] / mixed[:, HEAD_SIZE:]
            hidden = (resid_ref[:, cols].astype(F32) + attended).astype(BF16)
            hidden_ref[:, cols] = hidden
            wide = hidden.astype(F32)
            total = total + wide * wide
    inv_rms = lax.rsqrt(jnp.sum(total, axis=1, keepdims=True) * (1.0 / D) + 1e-06)
    slots = sum(r.shape[0] for r in send_refs)
    place = placement_rows(slot_ref[...], slots)
    for cols in column_blocks():
        normed = (hidden_ref[:, cols].astype(F32) * inv_rms * gain_ref[:, cols]).astype(BF16)
        store_pieces(send_refs, cols, mm(place, normed).astype(BF16))


def first_expert_rows(slots, capacity):
    return iota((slots, 1), 0) % (EXP_DEV * capacity) < capacity


def probs_kernel(
    count,
    capacity,
    pieces,
    pos_ref,
    slot_ref,
    weight_ref,
    down_hbm,
    gate_hbm,
    query_ref,
    *refs,
):
    key_refs = refs[:count]
    grad_refs = refs[count : count + pieces]
    d_act_ref, probs_ref, down_ref, gate_ref, place_ref, wide_ref, sems = refs[count + pieces :]
    spans = [slice(e * FFE, (e + 1) * FFE) for e in range(EXP_DEV)]
    down_copies = [
        pltpu.make_async_copy(down_hbm.at[e], down_ref.at[span, :], sems.at[e])
        for e, span in enumerate(spans)
    ]
    gate_copies = [
        pltpu.make_async_copy(gate_hbm.at[e], gate_ref.at[:, span], sems.at[EXP_DEV + e])
        for e, span in enumerate(spans)
    ]
    for copy in down_copies + gate_copies:
        copy.start()
    place_ref[...] = placement_cols(slot_ref[...], place_ref.shape[1])
    wide_ref[...] = jnp.broadcast_to(row_to_col(weight_ref[...]), wide_ref.shape)
    query_pos = pos_ref[:1, :].astype(F32)
    bias = jnp.concatenate(
        [
            jnp.where(row_to_col(pos_ref[s : s + 1, :]) <= query_pos, 0.0, -1e30)
            for s in range(count)
        ],
        axis=0,
    )
    bias = jnp.concatenate([bias, bias], axis=1)
    for g in range(KEY_VALUE_HEADS):
        keys = stacked(key_refs, slice(g * HEAD_SIZE, (g + 1) * HEAD_SIZE))
        for pair in range(g * GROUP // 2, (g + 1) * GROUP // 2):
            scores = mm(keys, head_pair(query_ref, pair), NT) + bias
            peak = jnp.max(scores, axis=0, keepdims=True)
            weights = jnp.exp2((scores - peak) * EXP2_SCALE)
            probs_ref[pair] = weights * (1.0 / jnp.sum(weights, axis=0, keepdims=True))
    grads = stacked(grad_refs)
    first = first_expert_rows(grads.shape[0], capacity)
    for copy in down_copies:
        copy.wait()
    d_act = mm(grads, down_ref[...], NT)
    d_act_ref[...] = jnp.where(first, d_act[:, :FFE], d_act[:, FFE:])
    for copy in gate_copies:
        copy.wait()


def part_views(refs, rows, part):
    return [r if r.shape[0] != 2 * rows else r.at[part * rows : (part + 1) * rows] for r in refs]


def joined(step, pieces):
    return pieces > 1 and step > 0 and step & (step - 1) == 0


def split_parts(refs, pieces):
    back, out = [], []
    at = 0
    for s in range(pieces):
        back.append(refs[at])
        at += not joined(s, pieces)
        out.append(refs[at])
        at += 1
    return back, out


def expert_kernel(capacity, pieces, gate_ref, down_ref, d_act_ref, *refs):
    rows = stacked(refs[:pieces])
    back_refs, out_refs = split_parts(refs[pieces:], pieces)
    back_refs = part_views(back_refs, EXP_DEV * capacity, 0)
    out_refs = part_views(out_refs, EXP_DEV * capacity, 1)
    first = first_expert_rows(rows.shape[0], capacity)
    both = mm(rows, gate_ref[...])
    pre = jnp.where(first, both[:, :FFE], both[:, FFE:])
    gate = 1.0 / (1.0 + jnp.exp(-pre))
    act = pre * gate
    d_pre = d_act_ref[...] * gate * (1.0 + pre * (1.0 - gate))
    act, d_pre = [
        jnp.concatenate([jnp.where(first, x, 0.0), jnp.where(first, 0.0, x)], axis=1).astype(BF16)
        for x in (act, d_pre)
    ]
    for cols in column_blocks():
        store_pieces(back_refs, cols, mm(d_pre, gate_ref[cols, :], NT).astype(BF16))
        store_pieces(out_refs, cols, mm(act, down_ref[:, cols]).astype(BF16))


def gain_kernel(pieces, rows, gain_ref, *refs):
    row_refs = refs[:pieces]
    back_refs = part_views(refs[pieces:-1], rows, 0)
    terms_ref = refs[-1]
    for cols in column_blocks():
        products = stacked(row_refs, cols).astype(F32) * stacked(back_refs, cols).astype(F32)
        terms = jnp.sum(products, axis=0, keepdims=True) / gain_ref[:, cols]
        for at in range(0, COLS, LANES):
            line = (cols.start + at) // LANES
            terms_ref[line : line + 1, :] = terms[:, at : at + LANES]


def group_back(g, key_refs, value_refs, query_ref, probs_ref, d_resid, dq_ref, own_ref, shared):
    length = len(key_refs) * own_ref.shape[0]
    tokens = own_ref.shape[0]
    keys, values = kv_stacks(key_refs, value_refs, g)
    keys_t = jnp.transpose(keys.astype(F32)).astype(BF16)
    d_keys = jnp.zeros((length, HEAD_SIZE), F32)
    d_values = jnp.zeros((length, HEAD_SIZE), F32)
    for local in range(GROUP // 2):
        pair = g * GROUP // 2 + local
        cols_a, cols_b = pair_cols(local)
        d_out = head_pair(d_resid, local)
        probs = probs_ref[pair]
        d_probs = mm(values, d_out, NT)
        row_dot = jnp.sum(probs * d_probs, axis=0, keepdims=True)
        d_scores = (probs * (d_probs - row_dot)).astype(BF16)
        d_keys = d_keys + mm(d_scores, head_pair(query_ref, pair))
        d_values = d_values + mm(probs.astype(BF16), d_out)
        d_query_t = mm(keys_t, d_scores) * SCALE
        dq_ref[:, cols_a] = jnp.transpose(d_query_t[:, :tokens]).astype(BF16)
        dq_ref[:, cols_b] = jnp.transpose(d_query_t[:, tokens:]).astype(BF16)
    d_keys = d_keys * SCALE
    own_ref[:, :HEAD_SIZE] = d_keys[:tokens]
    own_ref[:, HEAD_SIZE:] = d_values[:tokens]
    start = 2 * g * HEAD_SIZE
    for s, ref in enumerate(shared, 1):
        span = slice(s * tokens, (s + 1) * tokens)
        ref[:, start : start + HEAD_SIZE] = d_keys[span].astype(BF16)
        ref[:, start + HEAD_SIZE : start + 2 * HEAD_SIZE] = d_values[span].astype(BF16)


def first_back_kernel(
    count, pieces, rows, place_ref, gain_ref, hidden_ref, grad_ref, query_ref, probs_ref, *refs
):
    key_refs, value_refs = refs[:count], refs[count : 2 * count]
    refs = refs[2 * count :]
    dn_refs = part_views(refs[:pieces], rows, 0)
    resid_hbm, dq_ref, rest_ref, own_ref = refs[pieces : pieces + 4]
    shared = refs[pieces + 4 : -3]
    resid_ref, dn_scratch, sem = refs[-3:]
    tokens = hidden_ref.shape[0]
    place = place_ref[...]
    square = jnp.zeros((tokens, COLS), F32)
    mixing = jnp.zeros((tokens, COLS), F32)
    for cols in column_blocks():
        dn = mm(place, stacked(dn_refs, cols)) * gain_ref[:, cols]
        dn_scratch[:, cols] = dn
        hidden = hidden_ref[:, cols].astype(F32)
        square = square + hidden * hidden
        mixing = mixing + dn * hidden
    inv_rms = lax.rsqrt(jnp.sum(square, axis=1, keepdims=True) * (1.0 / D) + 1e-06)
    mean_mix = jnp.sum(mixing, axis=1, keepdims=True) * (1.0 / D)
    factor = inv_rms * inv_rms * inv_rms * mean_mix
    half = GROUP * HEAD_SIZE
    for cols in column_blocks():
        part = (
            grad_ref[:, cols].astype(F32)
            + dn_scratch[:, cols] * inv_rms
            - hidden_ref[:, cols].astype(F32) * factor
        ).astype(BF16)
        resid_ref[:, cols] = part
        if cols.start >= half:
            rest_ref[:, cols.start - half : cols.stop - half] = part
    resid_copy = pltpu.make_async_copy(resid_ref, resid_hbm, sem)
    resid_copy.start()
    group_back(0, key_refs, value_refs, query_ref, probs_ref, resid_ref, dq_ref, own_ref, shared)
    resid_copy.wait()


def second_back_kernel(count, query_ref, probs_ref, rest_ref, *refs):
    key_refs, value_refs = refs[:count], refs[count : 2 * count]
    first_shared = refs[2 * count : 3 * count - 1]
    dq_ref, own_ref = refs[3 * count - 1 : 3 * count + 1]
    shared = refs[3 * count + 1 :]
    for source, target in zip(first_shared, shared):
        target[:, : 2 * HEAD_SIZE] = source[...]
    group_back(1, key_refs, value_refs, query_ref, probs_ref, rest_ref, dq_ref, own_ref, shared)


def output_kernel(
    count, pieces, rows, tokens_in_all, place_ref, weight_ref, gain_ref, hidden_ref, grad_ref, *refs
):
    own_refs, refs = refs[:KEY_VALUE_HEADS], refs[KEY_VALUE_HEADS:]
    dq_refs, refs = refs[:KEY_VALUE_HEADS], refs[KEY_VALUE_HEADS:]
    arrived_refs = refs[: count - 1]
    y_refs = part_views(refs[count - 1 : count - 1 + pieces], rows, 1)
    out_hbm, dq_hbm, dk_hbm, dv_hbm, d_weight_hbm, d_gain_hbm = refs[count - 1 + pieces : -6]
    out_ref, dk_ref, dv_ref, d_weight_ref, d_gain_ref, sems = refs[-6:]
    copies = []

    def send(source, target):
        copy = pltpu.make_async_copy(source, target, sems.at[len(copies)])
        copy.start()
        copies.append(copy)

    width = GROUP * HEAD_SIZE
    for g, dq_ref in enumerate(dq_refs):
        send(dq_ref, dq_hbm.at[:, g * width : (g + 1) * width])
    for g, own_ref in enumerate(own_refs):
        d_kv = own_ref[...]
        for ref in arrived_refs:
            d_kv = d_kv + ref[:, 2 * g * HEAD_SIZE : 2 * (g + 1) * HEAD_SIZE].astype(F32)
        cols = slice(g * HEAD_SIZE, (g + 1) * HEAD_SIZE)
        dk_ref[:, cols] = d_kv[:, :HEAD_SIZE].astype(BF16)
        dv_ref[:, cols] = d_kv[:, HEAD_SIZE:].astype(BF16)
    d_gain_ref[...] = gain_ref[...] * (1.0 / tokens_in_all)
    send(dk_ref, dk_hbm)
    send(dv_ref, dv_hbm)
    send(d_gain_ref, d_gain_hbm)
    tokens = hidden_ref.shape[0]
    place = place_ref[...]
    weight = weight_ref[...]
    total = jnp.zeros((tokens, COLS), F32)
    for cols in column_blocks():
        y = mm(place, stacked(y_refs, cols))
        out_ref[:, cols] = (hidden_ref[:, cols].astype(F32) + weight * y).astype(BF16)
        send(out_ref.at[:, cols], out_hbm.at[:, cols])
        total = total + y * grad_ref[:, cols].astype(F32)
    d_weight_ref[...] = col_to_row(jnp.sum(total, axis=1, keepdims=True))
    send(d_weight_ref, d_weight_hbm)
    for copy in copies:
        copy.wait()


def run(kernel, name, inputs, outputs, flops, scratch=(), limit=20 * MIB):
    nbytes = sum(x.size * x.dtype.itemsize for _, x in inputs + outputs) if flops else 0
    spec = {space: pl.BlockSpec(memory_space=space) for space in (VMEM, HBM)}
    results = pl.pallas_call(
        kernel,
        out_shape=[x for _, x in outputs],
        in_specs=[spec[space] for space, _ in inputs],
        out_specs=[spec[space] for space, _ in outputs],
        scratch_shapes=list(scratch),
        compiler_params=pltpu.CompilerParams(vmem_limit_bytes=limit),
        cost_estimate=pl.CostEstimate(flops=flops, bytes_accessed=nbytes, transcendentals=0),
        name=name,
    )(*[pltpu.with_memory_space_constraint(x, HBM) if space is HBM else x for space, x in inputs])
    return list(results)


def placed(space, arrays):
    return [(space, x) for x in arrays]


def pairwise(value, axis, step):
    count = lax.axis_size(axis)
    return lax.ppermute(value, axis, [(i, i ^ step) for i in range(count)])


def exchange_flat(flat, capacity):
    count = lax.axis_size("exp")
    rows = EXP_DEV * capacity
    blocks = [flat[s * rows : (s + 1) * rows] for s in range(count)]
    moved = [blocks[0]] + [pairwise(blocks[s], "exp", s) for s in range(1, count)]
    return jnp.concatenate(moved, axis=0)


def exchange(pieces, capacity):
    if lax.axis_size("exp") != len(pieces):
        return [exchange_flat(pieces[0], capacity)]
    return [pairwise(piece, "exp", s) if s > 0 else piece for s, piece in enumerate(pieces)]


def doubled(value, axis, step):
    return value + pairwise(value, axis, step)


def sum_over(value, axis, first=1):
    step = first
    while step < lax.axis_size(axis):
        value = doubled(value, axis, step)
        step *= 2
    return value


def widened(act, value, axis, step):
    rows = value.shape[0]
    wide = jnp.pad(value, ((0, WIDE_LINES - rows), (0, 0)))
    return act(wide, axis, step)[:rows]


def shaped(shape, dtype):
    return jax.ShapeDtypeStruct(shape, dtype)


def per_device(
    queries,
    keys,
    values,
    resid,
    block_order,
    norm_gain,
    w_gate,
    w_down,
    routes,
    route_weight,
    d_out,
):
    query_rows = queries[0]
    resid_rows = resid[0]
    grad_rows = d_out[0]
    tokens = query_rows.shape[0]
    chosen = routes.reshape(1, tokens)
    gain = norm_gain.reshape(1, D)
    ctx_count = lax.axis_size("ctx")
    exp_count = lax.axis_size("exp")
    experts = EXP_DEV * exp_count
    capacity = 3 * tokens // (2 * experts)
    slots = experts * capacity
    rows = EXP_DEV * capacity
    piece_count = exp_count if rows % 16 == 0 else 1
    piece_shapes = [shaped((slots // piece_count, D), BF16)] * piece_count
    token_shape = shaped((tokens, D), BF16)
    kv_width = 2 * KEY_VALUE_HEADS * HEAD_SIZE
    attn_flops = 4 * tokens * ctx_count * tokens * QUERY_HEADS * HEAD_SIZE
    place_flops = 2 * slots * tokens * D
    expert_flops = 2 * slots * D * FFE * EXP_DEV

    own_keys, own_values = keys[0], values[0]
    all_keys = [own_keys] + [pairwise(own_keys, "ctx", s) for s in range(1, ctx_count)]
    all_values = [own_values] + [pairwise(own_values, "ctx", s) for s in range(1, ctx_count)]

    near = [grad_rows, own_keys, own_values, gain, query_rows, resid_rows]
    grad_rows, own_keys, own_values, gain, query_rows, resid_rows, slot, pos, weight, *send_grad = run(
        functools.partial(dispatch_kernel, ctx_count, experts, capacity),
        "dispatch_grads",
        placed(HBM, near + [route_weight, chosen, block_order]),
        placed(
            VMEM,
            [shaped(x.shape, x.dtype) for x in near]
            + [
                shaped((1, tokens), jnp.int32),
                shaped((ctx_count, tokens), jnp.int32),
                shaped((1, tokens), F32),
            ]
            + piece_shapes,
        ),
        place_flops,
        scratch=[
            pltpu.SMEM(block_order.shape, jnp.int32),
            pltpu.VMEM((1, tokens), jnp.int32),
            pltpu.SemaphoreType.DMA((9,)),
        ],
    )
    all_keys[0], all_values[0] = own_keys, own_values
    arrived_grad = exchange(send_grad, capacity)

    hidden, *send_x = run(
        functools.partial(attention_kernel, ctx_count),
        "attention_forward",
        placed(VMEM, [pos, slot, gain, query_rows, resid_rows] + all_keys + all_values),
        placed(VMEM, [token_shape] + piece_shapes),
        attn_flops + place_flops,
    )
    arrived_x = exchange(send_x, capacity)

    d_act, probs, down_near, gate_near, place, weight_wide = run(
        functools.partial(probs_kernel, ctx_count, capacity, piece_count),
        "act_grads_and_probs",
        placed(VMEM, [pos, slot, weight])
        + placed(HBM, [w_down, w_gate])
        + placed(VMEM, [query_rows] + all_keys + arrived_grad),
        placed(
            VMEM,
            [
                shaped((slots, FFE), F32),
                shaped((QUERY_HEADS // 2, ctx_count * tokens, 2 * tokens), F32),
                shaped((EXP_DEV * FFE, D), BF16),
                shaped((D, EXP_DEV * FFE), BF16),
                shaped((tokens, slots), BF16),
                shaped((tokens, COLS), F32),
            ],
        ),
        expert_flops + attn_flops // 2,
        scratch=[pltpu.SemaphoreType.DMA((2 * EXP_DEV,))],
    )

    return_shapes = []
    for s in range(piece_count):
        if joined(s, piece_count):
            return_shapes.append(shaped((2 * rows, D), BF16))
        else:
            return_shapes.extend([piece_shapes[0]] * 2)
    sent = run(
        functools.partial(expert_kernel, capacity, piece_count),
        "experts",
        placed(VMEM, [gate_near, down_near, d_act] + arrived_x),
        placed(VMEM, return_shapes),
        3 * expert_flops,
    )
    send_dn, send_y = split_parts(sent, piece_count)
    dn = exchange(send_dn, capacity)
    far = [s for s in range(1, piece_count) if not joined(s, piece_count)]
    y = list(dn) if piece_count > 1 else [exchange_flat(send_y[0], capacity)]
    y[0] = send_y[0] if piece_count > 1 else y[0]
    (terms,) = run(
        functools.partial(gain_kernel, piece_count, rows),
        "gain_terms",
        placed(VMEM, [gain] + arrived_x + send_dn),
        placed(VMEM, [shaped((GAIN_LINES, LANES), F32)]),
        2 * slots * D,
    )
    terms = sum_over(sum_over(terms, "dp"), "ctx")
    send_far, terms, dn = lax.optimization_barrier(([send_y[s] for s in far], terms, dn))
    for s, piece in zip(far, send_far):
        y[s] = pairwise(piece, "exp", s)
    terms = doubled(terms, "exp", 1)

    half_shape = shaped((tokens, D // 2), BF16)
    own_shape = shaped((tokens, 2 * HEAD_SIZE), F32)
    d_hidden, dq_first, rest, own_first, *shared_first = run(
        functools.partial(first_back_kernel, ctx_count, piece_count, rows),
        "residual_and_first_group",
        placed(VMEM, [place, gain, hidden, grad_rows, query_rows, probs])
        + placed(VMEM, all_keys + all_values + dn),
        placed(HBM, [token_shape])
        + placed(
            VMEM,
            [half_shape, half_shape, own_shape]
            + [shaped((tokens, 2 * HEAD_SIZE), BF16)] * (ctx_count - 1),
        ),
        A_COST,
        scratch=[
            pltpu.VMEM((tokens, D), BF16),
            pltpu.VMEM((tokens, D), F32),
            pltpu.SemaphoreType.DMA(()),
        ],
    )
    arrived_far, terms, rest = lax.optimization_barrier(([y[s] for s in far], terms, rest))
    for s, piece in zip(far, arrived_far):
        y[s] = piece
    terms = widened(doubled, terms, "exp", 2)
    dq_second, own_second, *shared = run(
        functools.partial(second_back_kernel, ctx_count),
        "second_group",
        placed(VMEM, [query_rows, probs, rest] + all_keys + all_values + shared_first),
        placed(VMEM, [half_shape, own_shape])
        + placed(VMEM, [shaped((tokens, kv_width), BF16)] * (ctx_count - 1)),
        B_COST,
    )
    terms = sum_over(terms, "exp", first=4)
    kv_arrived = [pairwise(part, "ctx", s) for s, part in enumerate(shared, 1)]

    kv_shape = shaped((tokens, kv_width // 2), BF16)
    final_shapes = [token_shape, token_shape, kv_shape, kv_shape]
    final_shapes += [shaped((1, tokens), F32), shaped((GAIN_LINES, LANES), F32)]
    total_tokens = tokens * ctx_count * exp_count * lax.axis_size("dp")
    layer_out, d_queries, d_keys, d_values, d_weight, d_gain = run(
        functools.partial(output_kernel, ctx_count, piece_count, rows, total_tokens),
        "layer_output",
        placed(
            VMEM,
            [place, weight_wide, terms, hidden, grad_rows, own_first, own_second]
            + [dq_first, dq_second]
            + kv_arrived
            + y,
        ),
        placed(HBM, final_shapes),
        place_flops,
        scratch=[pltpu.VMEM(x.shape, x.dtype) for x in final_shapes[:1] + final_shapes[2:]]
        + [pltpu.SemaphoreType.DMA((4 + KEY_VALUE_HEADS + D // COLS,))],
    )
    return (
        layer_out[None],
        d_hidden[None],
        d_queries[None],
        d_keys[None],
        d_values[None],
        d_weight,
        d_gain.reshape(D),
    )


def solution(mesh):
    in_specs = (
        P(("exp", "dp"), "ctx", None),
        P(("exp", "dp"), "ctx", None),
        P(("exp", "dp"), "ctx", None),
        P(("exp", "dp"), "ctx", None),
        P(),
        P(),
        P("exp", None, None),
        P("exp", None, None),
        P(("exp", "dp"), "ctx", None),
        P(("exp", "dp"), "ctx"),
        P(("exp", "dp"), "ctx", None),
    )
    out_specs = (
        P(("exp", "dp"), "ctx", None),
        P(("exp", "dp"), "ctx", None),
        P(("exp", "dp"), "ctx", None),
        P(("exp", "dp"), "ctx", None),
        P(("exp", "dp"), "ctx", None),
        P(("exp", "dp"), "ctx"),
        P(),
    )
    return jax.shard_map(
        per_device, mesh=mesh, in_specs=in_specs, out_specs=out_specs, check_vma=False
    )
```

```python
import functools

import jax
import jax.numpy as jnp
from jax import lax
from jax.experimental import pallas as pl
from jax.experimental.pallas import tpu as pltpu
from jax.sharding import PartitionSpec as P

D = 2048
HEAD_SIZE = 128
QUERY_HEADS = 16
KEY_VALUE_HEADS = 2
GROUP = QUERY_HEADS // KEY_VALUE_HEADS
FFE = 384
EXP_DEV = 2
COLS = 256
LANES = 128
GAIN_LINES = D // LANES
SCALE = HEAD_SIZE ** (-0.5)
EXP2_SCALE = SCALE * 1.4426950408889634
F32 = jnp.float32
BF16 = jnp.bfloat16
NN = (((1,), (0,)), ((), ()))
NT = (((1,), (1,)), ((), ()))
MIB = 1 << 20
VMEM, HBM = pltpu.VMEM, pltpu.HBM


def mm(a, b, dims=NN):
    return lax.dot_general(a, b, dims, preferred_element_type=F32)


def iota(shape, dim):
    return lax.broadcasted_iota(jnp.int32, shape, dim)


def row_to_col(row):
    n = row.shape[1]
    eye = iota((n, n), 0) == iota((n, n), 1)
    return jnp.sum(jnp.where(eye, row.astype(F32), 0.0), axis=1, keepdims=True)


def col_to_row(col):
    n = col.shape[0]
    eye = iota((n, n), 0) == iota((n, n), 1)
    return jnp.sum(jnp.where(eye, col, 0.0), axis=0, keepdims=True)


def block_positions(order_ref, ctx_index, tokens):
    span = tokens // 8
    index = iota((1, tokens), 1)
    which = index // span
    start = jnp.zeros((1, tokens), jnp.int32)
    for b in range(8):
        start = jnp.where(which == b, order_ref[ctx_index * 8 + b], start)
    return start * span + index % span


def stacked(refs, cols=slice(None)):
    parts = [r[:, cols] for r in refs]
    return parts[0] if len(parts) == 1 else jnp.concatenate(parts, axis=0)


def column_blocks(width=D, step=COLS):
    return [slice(c, c + step) for c in range(0, width, step)]


def store_pieces(refs, cols, rows_value):
    at = 0
    for r in refs:
        n = r.shape[0]
        r[:, cols] = rows_value[at : at + n]
        at += n


def pair_cols(pair):
    start = 2 * pair * HEAD_SIZE
    return slice(start, start + HEAD_SIZE), slice(start + HEAD_SIZE, start + 2 * HEAD_SIZE)


def head_pair(ref, pair):
    first, second = pair_cols(pair)
    return jnp.concatenate([ref[:, first], ref[:, second]], axis=0)


def placement_rows(slot_row, slots):
    tokens = slot_row.shape[1]
    return jnp.where(iota((slots, tokens), 0) == slot_row, 1.0, 0.0).astype(BF16)


def placement_cols(slot_row, slots):
    tokens = slot_row.shape[1]
    slot_col = row_to_col(slot_row)
    return jnp.where(iota((tokens, slots), 1).astype(F32) == slot_col, 1.0, 0.0).astype(BF16)


def dispatch_kernel(count, experts, capacity, *refs):
    sources, refs = refs[:9], refs[9:]
    targets, refs = refs[:6], refs[6:]
    grad_ref = targets[0]
    slot_ref, pos_ref, weight_ref = refs[:3]
    send_refs = refs[3:-3]
    order_ref, routes_ref, sems = refs[-3:]
    targets = targets + (weight_ref, routes_ref, order_ref)
    copies = [
        pltpu.make_async_copy(source, target, sems.at[i])
        for i, (source, target) in enumerate(zip(sources, targets))
    ]
    for copy in copies[6:] + copies[:6]:
        copy.start()
    for copy in copies[6:]:
        copy.wait()
    tokens = routes_ref.shape[1]
    chosen = routes_ref[...]
    lanes = max(experts, 16)
    hits = jnp.where(iota((lanes, tokens), 0) == chosen, 1.0, 0.0)
    before = jnp.where(iota((tokens, tokens), 0) < iota((tokens, tokens), 1), 1.0, 0.0)
    earlier = mm(hits.astype(BF16), before.astype(BF16))
    rank = jnp.sum(hits * earlier, axis=0, keepdims=True).astype(jnp.int32)
    target = (chosen // EXP_DEV) ^ lax.axis_index("exp")
    slot = (target * EXP_DEV + chosen % EXP_DEV) * capacity + rank
    slot_ref[...] = slot
    me = lax.axis_index("ctx")
    for s in range(count):
        pos_ref[s : s + 1, :] = block_positions(order_ref, me ^ s, tokens)
    place = placement_rows(slot, experts * capacity)
    weight = row_to_col(weight_ref[...])
    copies[0].wait()
    for cols in column_blocks():
        scaled = (weight * grad_ref[:, cols].astype(F32)).astype(BF16)
        store_pieces(send_refs, cols, mm(place, scaled).astype(BF16))
    for copy in copies[1:6]:
        copy.wait()


def kv_stacks(key_refs, value_refs, g):
    cols = slice(g * HEAD_SIZE, (g + 1) * HEAD_SIZE)
    return stacked(key_refs, cols), stacked(value_refs, cols)


def attention_kernel(
    count, pos_ref, slot_ref, gain_ref, query_ref, resid_ref, *refs
):
    key_refs, value_refs = refs[:count], refs[count : 2 * count]
    hidden_ref, send_refs = refs[2 * count], refs[2 * count + 1 :]
    tokens = query_ref.shape[0]
    query_pos = row_to_col(pos_ref[:1, :])
    bias = jnp.concatenate(
        [
            jnp.where(pos_ref[s : s + 1, :].astype(F32) <= query_pos, 0.0, -1e30)
            for s in range(count)
        ],
        axis=1,
    )
    length = count * tokens
    ones = jnp.ones((length, HEAD_SIZE), BF16)
    total = jnp.zeros((tokens, HEAD_SIZE), F32)
    for g in range(KEY_VALUE_HEADS):
        keys, values = kv_stacks(key_refs, value_refs, g)
        values = jnp.concatenate([values, ones], axis=1)
        for h in range(g * GROUP, (g + 1) * GROUP):
            cols = slice(h * HEAD_SIZE, (h + 1) * HEAD_SIZE)
            scores = mm(query_ref[:, cols], keys, NT) + bias
            peak = jnp.max(scores, axis=1, keepdims=True)
            weights = jnp.exp2((scores - peak) * EXP2_SCALE).astype(BF16)
            mixed = mm(weights, values)
            attended = mixed[:, :HEAD_SIZE] / mixed[:, HEAD_SIZE:]
            hidden = (resid_ref[:, cols].astype(F32) + attended).astype(BF16)
            hidden_ref[:, cols] = hidden
            wide = hidden.astype(F32)
            total = total + wide * wide
    inv_rms = lax.rsqrt(jnp.sum(total, axis=1, keepdims=True) * (1.0 / D) + 1e-06)
    slots = sum(r.shape[0] for r in send_refs)
    place = placement_rows(slot_ref[...], slots)
    for cols in column_blocks():
        normed = (hidden_ref[:, cols].astype(F32) * inv_rms * gain_ref[:, cols]).astype(BF16)
        store_pieces(send_refs, cols, mm(place, normed).astype(BF16))


def first_expert_rows(slots, capacity):
    return iota((slots, 1), 0) % (EXP_DEV * capacity) < capacity


def probs_kernel(
    count,
    capacity,
    pieces,
    pos_ref,
    slot_ref,
    weight_ref,
    down_hbm,
    gate_hbm,
    query_ref,
    *refs,
):
    key_refs = refs[:count]
    grad_refs = refs[count : count + pieces]
    d_act_ref, probs_ref, down_ref, gate_ref, place_ref, wide_ref, sems = refs[count + pieces :]
    spans = [slice(e * FFE, (e + 1) * FFE) for e in range(EXP_DEV)]
    down_copies = [
        pltpu.make_async_copy(down_hbm.at[e], down_ref.at[span, :], sems.at[e])
        for e, span in enumerate(spans)
    ]
    gate_copies = [
        pltpu.make_async_copy(gate_hbm.at[e], gate_ref.at[:, span], sems.at[EXP_DEV + e])
        for e, span in enumerate(spans)
    ]
    for copy in down_copies + gate_copies:
        copy.start()
    place_ref[...] = placement_cols(slot_ref[...], place_ref.shape[1])
    wide_ref[...] = jnp.broadcast_to(row_to_col(weight_ref[...]), wide_ref.shape)
    query_pos = pos_ref[:1, :].astype(F32)
    bias = jnp.concatenate(
        [
            jnp.where(row_to_col(pos_ref[s : s + 1, :]) <= query_pos, 0.0, -1e30)
            for s in range(count)
        ],
        axis=0,
    )
    bias = jnp.concatenate([bias, bias], axis=1)
    for g in range(KEY_VALUE_HEADS):
        keys = stacked(key_refs, slice(g * HEAD_SIZE, (g + 1) * HEAD_SIZE))
        for pair in range(g * GROUP // 2, (g + 1) * GROUP // 2):
            scores = mm(keys, head_pair(query_ref, pair), NT) + bias
            peak = jnp.max(scores, axis=0, keepdims=True)
            weights = jnp.exp2((scores - peak) * EXP2_SCALE)
            probs_ref[pair] = weights * (1.0 / jnp.sum(weights, axis=0, keepdims=True))
    grads = stacked(grad_refs)
    first = first_expert_rows(grads.shape[0], capacity)
    for copy in down_copies:
        copy.wait()
    d_act = mm(grads, down_ref[...], NT)
    d_act_ref[...] = jnp.where(first, d_act[:, :FFE], d_act[:, FFE:])
    for copy in gate_copies:
        copy.wait()


def part_views(refs, rows, part):
    return [r if r.shape[0] != 2 * rows else r.at[part * rows : (part + 1) * rows] for r in refs]


def joined(step, pieces):
    return pieces > 1 and step > 0 and step & (step - 1) == 0


def split_parts(refs, pieces):
    back, out = [], []
    at = 0
    for s in range(pieces):
        back.append(refs[at])
        at += not joined(s, pieces)
        out.append(refs[at])
        at += 1
    return back, out


def expert_kernel(capacity, pieces, gate_ref, down_ref, d_act_ref, *refs):
    rows = stacked(refs[:pieces])
    back_refs, out_refs = split_parts(refs[pieces:], pieces)
    back_refs = part_views(back_refs, EXP_DEV * capacity, 0)
    out_refs = part_views(out_refs, EXP_DEV * capacity, 1)
    first = first_expert_rows(rows.shape[0], capacity)
    both = mm(rows, gate_ref[...])
    pre = jnp.where(first, both[:, :FFE], both[:, FFE:])
    gate = 1.0 / (1.0 + jnp.exp(-pre))
    act = pre * gate
    d_pre = d_act_ref[...] * gate * (1.0 + pre * (1.0 - gate))
    act, d_pre = [
        jnp.concatenate([jnp.where(first, x, 0.0), jnp.where(first, 0.0, x)], axis=1).astype(BF16)
        for x in (act, d_pre)
    ]
    for cols in column_blocks():
        store_pieces(back_refs, cols, mm(d_pre, gate_ref[cols, :], NT).astype(BF16))
        store_pieces(out_refs, cols, mm(act, down_ref[:, cols]).astype(BF16))


def gain_kernel(pieces, rows, gain_ref, *refs):
    row_refs = refs[:pieces]
    back_refs = part_views(refs[pieces:-1], rows, 0)
    terms_ref = refs[-1]
    for cols in column_blocks():
        products = stacked(row_refs, cols).astype(F32) * stacked(back_refs, cols).astype(F32)
        terms = jnp.sum(products, axis=0, keepdims=True) / gain_ref[:, cols]
        for at in range(0, COLS, LANES):
            line = (cols.start + at) // LANES
            terms_ref[line : line + 1, :] = terms[:, at : at + LANES]


def backward_kernel(
    count, pieces, rows, place_ref, gain_ref, hidden_ref, grad_ref, query_ref, probs_ref, *refs
):
    dn_refs = part_views(refs[:pieces], rows, 0)
    key_refs = refs[pieces : pieces + count]
    value_refs = refs[pieces + count : pieces + 2 * count]
    resid_hbm, dq_ref, own_ref = refs[pieces + 2 * count : pieces + 2 * count + 3]
    other_refs = refs[pieces + 2 * count + 3 : -3]
    resid_ref, dn_scratch, sem = refs[-3:]
    tokens = hidden_ref.shape[0]
    place = place_ref[...]
    square = jnp.zeros((tokens, COLS), F32)
    mixing = jnp.zeros((tokens, COLS), F32)
    for cols in column_blocks():
        dn = mm(place, stacked(dn_refs, cols)) * gain_ref[:, cols]
        dn_scratch[:, cols] = dn
        hidden = hidden_ref[:, cols].astype(F32)
        square = square + hidden * hidden
        mixing = mixing + dn * hidden
    inv_rms = lax.rsqrt(jnp.sum(square, axis=1, keepdims=True) * (1.0 / D) + 1e-06)
    mean_mix = jnp.sum(mixing, axis=1, keepdims=True) * (1.0 / D)
    factor = inv_rms * inv_rms * inv_rms * mean_mix
    for cols in column_blocks():
        resid_ref[:, cols] = (
            grad_ref[:, cols].astype(F32)
            + dn_scratch[:, cols] * inv_rms
            - hidden_ref[:, cols].astype(F32) * factor
        ).astype(BF16)
    resid_copy = pltpu.make_async_copy(resid_ref, resid_hbm, sem)
    resid_copy.start()
    length = count * tokens
    for g in range(KEY_VALUE_HEADS):
        keys, values = kv_stacks(key_refs, value_refs, g)
        keys_t = jnp.transpose(keys.astype(F32)).astype(BF16)
        d_keys = jnp.zeros((length, HEAD_SIZE), F32)
        d_values = jnp.zeros((length, HEAD_SIZE), F32)
        for pair in range(g * GROUP // 2, (g + 1) * GROUP // 2):
            cols_a, cols_b = pair_cols(pair)
            d_out = head_pair(resid_ref, pair)
            probs = probs_ref[pair]
            d_probs = mm(values, d_out, NT)
            row_dot = jnp.sum(probs * d_probs, axis=0, keepdims=True)
            d_scores = (probs * (d_probs - row_dot)).astype(BF16)
            d_keys = d_keys + mm(d_scores, head_pair(query_ref, pair))
            d_values = d_values + mm(probs.astype(BF16), d_out)
            d_query_t = mm(keys_t, d_scores) * SCALE
            dq_ref[:, cols_a] = jnp.transpose(d_query_t[:, :tokens]).astype(BF16)
            dq_ref[:, cols_b] = jnp.transpose(d_query_t[:, tokens:]).astype(BF16)
        k_cols = slice(g * HEAD_SIZE, (g + 1) * HEAD_SIZE)
        v_cols = slice((KEY_VALUE_HEADS + g) * HEAD_SIZE, (KEY_VALUE_HEADS + g + 1) * HEAD_SIZE)
        d_keys = d_keys * SCALE
        own_ref[:, k_cols] = d_keys[:tokens]
        own_ref[:, v_cols] = d_values[:tokens]
        for s, ref in enumerate(other_refs, 1):
            ref[:, k_cols] = d_keys[s * tokens : (s + 1) * tokens].astype(BF16)
            ref[:, v_cols] = d_values[s * tokens : (s + 1) * tokens].astype(BF16)
    resid_copy.wait()


def output_kernel(
    count, pieces, rows, tokens_in_all, place_ref, weight_ref, gain_ref, hidden_ref, grad_ref, *refs
):
    own_ref, dq_ref, refs = refs[0], refs[1], refs[2:]
    arrived_refs = refs[: count - 1]
    y_refs = part_views(refs[count - 1 : count - 1 + pieces], rows, 1)
    out_hbm, dq_hbm, dk_hbm, dv_hbm, d_weight_hbm, d_gain_hbm = refs[count - 1 + pieces : -6]
    out_ref, dk_ref, dv_ref, d_weight_ref, d_gain_ref, sems = refs[-6:]
    copies = []

    def send(source, target):
        copy = pltpu.make_async_copy(source, target, sems.at[len(copies)])
        copy.start()
        copies.append(copy)

    send(dq_ref, dq_hbm)
    split = KEY_VALUE_HEADS * HEAD_SIZE
    d_kv = own_ref[...]
    for ref in arrived_refs:
        d_kv = d_kv + ref[...].astype(F32)
    dk_ref[...] = d_kv[:, :split].astype(BF16)
    dv_ref[...] = d_kv[:, split:].astype(BF16)
    d_gain_ref[...] = gain_ref[...] * (1.0 / tokens_in_all)
    send(dk_ref, dk_hbm)
    send(dv_ref, dv_hbm)
    send(d_gain_ref, d_gain_hbm)
    tokens = hidden_ref.shape[0]
    place = place_ref[...]
    weight = weight_ref[...]
    total = jnp.zeros((tokens, COLS), F32)
    for cols in column_blocks():
        y = mm(place, stacked(y_refs, cols))
        out_ref[:, cols] = (hidden_ref[:, cols].astype(F32) + weight * y).astype(BF16)
        send(out_ref.at[:, cols], out_hbm.at[:, cols])
        total = total + y * grad_ref[:, cols].astype(F32)
    d_weight_ref[...] = col_to_row(jnp.sum(total, axis=1, keepdims=True))
    send(d_weight_ref, d_weight_hbm)
    for copy in copies:
        copy.wait()


def run(kernel, name, inputs, outputs, flops, scratch=(), limit=20 * MIB):
    nbytes = sum(x.size * x.dtype.itemsize for _, x in inputs + outputs)
    spec = {space: pl.BlockSpec(memory_space=space) for space in (VMEM, HBM)}
    results = pl.pallas_call(
        kernel,
        out_shape=[x for _, x in outputs],
        in_specs=[spec[space] for space, _ in inputs],
        out_specs=[spec[space] for space, _ in outputs],
        scratch_shapes=list(scratch),
        compiler_params=pltpu.CompilerParams(vmem_limit_bytes=limit),
        cost_estimate=pl.CostEstimate(flops=flops, bytes_accessed=nbytes, transcendentals=0),
        name=name,
    )(*[pltpu.with_memory_space_constraint(x, HBM) if space is HBM else x for space, x in inputs])
    return list(results)


def placed(space, arrays):
    return [(space, x) for x in arrays]


def pairwise(value, axis, step):
    count = lax.axis_size(axis)
    return lax.ppermute(value, axis, [(i, i ^ step) for i in range(count)])


def exchange_flat(flat, capacity):
    count = lax.axis_size("exp")
    rows = EXP_DEV * capacity
    blocks = [flat[s * rows : (s + 1) * rows] for s in range(count)]
    moved = [blocks[0]] + [pairwise(blocks[s], "exp", s) for s in range(1, count)]
    return jnp.concatenate(moved, axis=0)


def exchange(pieces, capacity):
    if lax.axis_size("exp") != len(pieces):
        return [exchange_flat(pieces[0], capacity)]
    return [pairwise(piece, "exp", s) if s > 0 else piece for s, piece in enumerate(pieces)]


def doubled(value, axis, step):
    return value + pairwise(value, axis, step)


def sum_over(value, axis, first=1):
    step = first
    while step < lax.axis_size(axis):
        value = doubled(value, axis, step)
        step *= 2
    return value


def shaped(shape, dtype):
    return jax.ShapeDtypeStruct(shape, dtype)


def per_device(
    queries,
    keys,
    values,
    resid,
    block_order,
    norm_gain,
    w_gate,
    w_down,
    routes,
    route_weight,
    d_out,
):
    query_rows = queries[0]
    resid_rows = resid[0]
    grad_rows = d_out[0]
    tokens = query_rows.shape[0]
    chosen = routes.reshape(1, tokens)
    gain = norm_gain.reshape(1, D)
    ctx_count = lax.axis_size("ctx")
    exp_count = lax.axis_size("exp")
    experts = EXP_DEV * exp_count
    capacity = 3 * tokens // (2 * experts)
    slots = experts * capacity
    rows = EXP_DEV * capacity
    piece_count = exp_count if rows % 16 == 0 else 1
    piece_shapes = [shaped((slots // piece_count, D), BF16)] * piece_count
    token_shape = shaped((tokens, D), BF16)
    kv_width = 2 * KEY_VALUE_HEADS * HEAD_SIZE
    attn_flops = 4 * tokens * ctx_count * tokens * QUERY_HEADS * HEAD_SIZE
    place_flops = 2 * slots * tokens * D
    expert_flops = 2 * slots * D * FFE * EXP_DEV

    own_keys, own_values = keys[0], values[0]
    all_keys = [own_keys] + [pairwise(own_keys, "ctx", s) for s in range(1, ctx_count)]
    all_values = [own_values] + [pairwise(own_values, "ctx", s) for s in range(1, ctx_count)]

    near = [grad_rows, own_keys, own_values, gain, query_rows, resid_rows]
    grad_rows, own_keys, own_values, gain, query_rows, resid_rows, slot, pos, weight, *send_grad = run(
        functools.partial(dispatch_kernel, ctx_count, experts, capacity),
        "dispatch_grads",
        placed(HBM, near + [route_weight, chosen, block_order]),
        placed(
            VMEM,
            [shaped(x.shape, x.dtype) for x in near]
            + [
                shaped((1, tokens), jnp.int32),
                shaped((ctx_count, tokens), jnp.int32),
                shaped((1, tokens), F32),
            ]
            + piece_shapes,
        ),
        place_flops,
        scratch=[
            pltpu.SMEM(block_order.shape, jnp.int32),
            pltpu.VMEM((1, tokens), jnp.int32),
            pltpu.SemaphoreType.DMA((9,)),
        ],
    )
    all_keys[0], all_values[0] = own_keys, own_values
    arrived_grad = exchange(send_grad, capacity)

    hidden, *send_x = run(
        functools.partial(attention_kernel, ctx_count),
        "attention_forward",
        placed(VMEM, [pos, slot, gain, query_rows, resid_rows] + all_keys + all_values),
        placed(VMEM, [token_shape] + piece_shapes),
        attn_flops + place_flops,
    )
    arrived_x = exchange(send_x, capacity)

    d_act, probs, down_near, gate_near, place, weight_wide = run(
        functools.partial(probs_kernel, ctx_count, capacity, piece_count),
        "act_grads_and_probs",
        placed(VMEM, [pos, slot, weight])
        + placed(HBM, [w_down, w_gate])
        + placed(VMEM, [query_rows] + all_keys + arrived_grad),
        placed(
            VMEM,
            [
                shaped((slots, FFE), F32),
                shaped((QUERY_HEADS // 2, ctx_count * tokens, 2 * tokens), F32),
                shaped((EXP_DEV * FFE, D), BF16),
                shaped((D, EXP_DEV * FFE), BF16),
                shaped((tokens, slots), BF16),
                shaped((tokens, COLS), F32),
            ],
        ),
        expert_flops + attn_flops // 2,
        scratch=[pltpu.SemaphoreType.DMA((2 * EXP_DEV,))],
    )

    return_shapes = []
    for s in range(piece_count):
        if joined(s, piece_count):
            return_shapes.append(shaped((2 * rows, D), BF16))
        else:
            return_shapes.extend([piece_shapes[0]] * 2)
    sent = run(
        functools.partial(expert_kernel, capacity, piece_count),
        "experts",
        placed(VMEM, [gate_near, down_near, d_act] + arrived_x),
        placed(VMEM, return_shapes),
        3 * expert_flops,
    )
    send_dn, send_y = split_parts(sent, piece_count)
    dn = exchange(send_dn, capacity)
    far = [s for s in range(1, piece_count) if not joined(s, piece_count)]
    y = list(dn) if piece_count > 1 else [exchange_flat(send_y[0], capacity)]
    y[0] = send_y[0] if piece_count > 1 else y[0]
    (terms,) = run(
        functools.partial(gain_kernel, piece_count, rows),
        "gain_terms",
        placed(VMEM, [gain] + arrived_x + send_dn),
        placed(VMEM, [shaped((GAIN_LINES, LANES), F32)]),
        2 * slots * D,
    )
    terms = sum_over(sum_over(terms, "dp"), "ctx")
    send_far, terms = lax.optimization_barrier(([send_y[s] for s in far], terms))
    for s, piece in zip(far, send_far):
        y[s] = pairwise(piece, "exp", s)
    terms, dn = lax.optimization_barrier((terms, dn))
    terms = doubled(terms, "exp", 1)

    d_hidden, d_queries, kv_own, *kv_send = run(
        functools.partial(backward_kernel, ctx_count, piece_count, rows),
        "residual_attention_backward",
        placed(VMEM, [place, gain, hidden, grad_rows, query_rows, probs])
        + placed(VMEM, dn + all_keys + all_values),
        placed(HBM, [token_shape])
        + placed(
            VMEM,
            [token_shape, shaped((tokens, kv_width), F32)]
            + [shaped((tokens, kv_width), BF16)] * (ctx_count - 1),
        ),
        attn_flops + place_flops,
        scratch=[
            pltpu.VMEM((tokens, D), BF16),
            pltpu.VMEM((tokens, D), F32),
            pltpu.SemaphoreType.DMA(()),
        ],
    )
    terms, kv_send = lax.optimization_barrier((terms, kv_send))
    terms = sum_over(terms, "exp", first=2)
    kv_arrived = [pairwise(part, "ctx", s) for s, part in enumerate(kv_send, 1)]

    kv_shape = shaped((tokens, kv_width // 2), BF16)
    final_shapes = [token_shape, token_shape, kv_shape, kv_shape]
    final_shapes += [shaped((1, tokens), F32), shaped((GAIN_LINES, LANES), F32)]
    total_tokens = tokens * ctx_count * exp_count * lax.axis_size("dp")
    layer_out, d_queries, d_keys, d_values, d_weight, d_gain = run(
        functools.partial(output_kernel, ctx_count, piece_count, rows, total_tokens),
        "layer_output",
        placed(
            VMEM,
            [place, weight_wide, terms, hidden, grad_rows, kv_own, d_queries]
            + kv_arrived
            + y,
        ),
        placed(HBM, final_shapes),
        place_flops,
        scratch=[pltpu.VMEM(x.shape, x.dtype) for x in final_shapes[:1] + final_shapes[2:]]
        + [pltpu.SemaphoreType.DMA((5 + D // COLS,))],
    )
    return (
        layer_out[None],
        d_hidden[None],
        d_queries[None],
        d_keys[None],
        d_values[None],
        d_weight,
        d_gain.reshape(D),
    )


def solution(mesh):
    in_specs = (
        P(("exp", "dp"), "ctx", None),
        P(("exp", "dp"), "ctx", None),
        P(("exp", "dp"), "ctx", None),
        P(("exp", "dp"), "ctx", None),
        P(),
        P(),
        P("exp", None, None),
        P("exp", None, None),
        P(("exp", "dp"), "ctx", None),
        P(("exp", "dp"), "ctx"),
        P(("exp", "dp"), "ctx", None),
    )
    out_specs = (
        P(("exp", "dp"), "ctx", None),
        P(("exp", "dp"), "ctx", None),
        P(("exp", "dp"), "ctx", None),
        P(("exp", "dp"), "ctx", None),
        P(("exp", "dp"), "ctx", None),
        P(("exp", "dp"), "ctx"),
        P(),
    )
    return jax.shard_map(
        per_device, mesh=mesh, in_specs=in_specs, out_specs=out_specs, check_vma=False
    )
```

```python
import functools

import jax
import jax.numpy as jnp
from jax import lax
from jax.experimental import pallas as pl
from jax.experimental.pallas import tpu as pltpu
from jax.sharding import PartitionSpec as P

D = 2048
HEAD_SIZE = 128
QUERY_HEADS = 16
KEY_VALUE_HEADS = 2
GROUP = QUERY_HEADS // KEY_VALUE_HEADS
FFE = 384
EXP_DEV = 2
COLS = 256
LANES = 128
GAIN_LINES = D // LANES
WIDE_LINES = 32
FIRST = 2
A_COST = 4000000000
B_COST = 0
SCALE = HEAD_SIZE ** (-0.5)
EXP2_SCALE = SCALE * 1.4426950408889634
F32 = jnp.float32
BF16 = jnp.bfloat16
NN = (((1,), (0,)), ((), ()))
NT = (((1,), (1,)), ((), ()))
MIB = 1 << 20
VMEM, HBM = pltpu.VMEM, pltpu.HBM


def mm(a, b, dims=NN):
    return lax.dot_general(a, b, dims, preferred_element_type=F32)


def iota(shape, dim):
    return lax.broadcasted_iota(jnp.int32, shape, dim)


def row_to_col(row):
    n = row.shape[1]
    eye = iota((n, n), 0) == iota((n, n), 1)
    return jnp.sum(jnp.where(eye, row.astype(F32), 0.0), axis=1, keepdims=True)


def col_to_row(col):
    n = col.shape[0]
    eye = iota((n, n), 0) == iota((n, n), 1)
    return jnp.sum(jnp.where(eye, col, 0.0), axis=0, keepdims=True)


def block_positions(order_ref, ctx_index, tokens):
    span = tokens // 8
    index = iota((1, tokens), 1)
    which = index // span
    start = jnp.zeros((1, tokens), jnp.int32)
    for b in range(8):
        start = jnp.where(which == b, order_ref[ctx_index * 8 + b], start)
    return start * span + index % span


def stacked(refs, cols=slice(None)):
    parts = [r[:, cols] for r in refs]
    return parts[0] if len(parts) == 1 else jnp.concatenate(parts, axis=0)


def column_blocks(width=D, step=COLS):
    return [slice(c, c + step) for c in range(0, width, step)]


def store_pieces(refs, cols, rows_value):
    at = 0
    for r in refs:
        n = r.shape[0]
        r[:, cols] = rows_value[at : at + n]
        at += n


def pair_cols(pair):
    start = 2 * pair * HEAD_SIZE
    return slice(start, start + HEAD_SIZE), slice(start + HEAD_SIZE, start + 2 * HEAD_SIZE)


def head_pair(ref, pair):
    first, second = pair_cols(pair)
    return jnp.concatenate([ref[:, first], ref[:, second]], axis=0)


def placement_rows(slot_row, slots):
    tokens = slot_row.shape[1]
    return jnp.where(iota((slots, tokens), 0) == slot_row, 1.0, 0.0).astype(BF16)


def placement_cols(slot_row, slots):
    tokens = slot_row.shape[1]
    slot_col = row_to_col(slot_row)
    return jnp.where(iota((tokens, slots), 1).astype(F32) == slot_col, 1.0, 0.0).astype(BF16)


def dispatch_kernel(count, experts, capacity, *refs):
    sources, refs = refs[:9], refs[9:]
    targets, refs = refs[:6], refs[6:]
    grad_ref = targets[0]
    slot_ref, pos_ref, weight_ref = refs[:3]
    send_refs = refs[3:-3]
    order_ref, routes_ref, sems = refs[-3:]
    targets = targets + (weight_ref, routes_ref, order_ref)
    copies = [
        pltpu.make_async_copy(source, target, sems.at[i])
        for i, (source, target) in enumerate(zip(sources, targets))
    ]
    for copy in copies[6:] + copies[:6]:
        copy.start()
    for copy in copies[6:]:
        copy.wait()
    tokens = routes_ref.shape[1]
    chosen = routes_ref[...]
    lanes = max(experts, 16)
    hits = jnp.where(iota((lanes, tokens), 0) == chosen, 1.0, 0.0)
    before = jnp.where(iota((tokens, tokens), 0) < iota((tokens, tokens), 1), 1.0, 0.0)
    earlier = mm(hits.astype(BF16), before.astype(BF16))
    rank = jnp.sum(hits * earlier, axis=0, keepdims=True).astype(jnp.int32)
    target = (chosen // EXP_DEV) ^ lax.axis_index("exp")
    slot = (target * EXP_DEV + chosen % EXP_DEV) * capacity + rank
    slot_ref[...] = slot
    me = lax.axis_index("ctx")
    for s in range(count):
        pos_ref[s : s + 1, :] = block_positions(order_ref, me ^ s, tokens)
    place = placement_rows(slot, experts * capacity)
    weight = row_to_col(weight_ref[...])
    copies[0].wait()
    for cols in column_blocks():
        scaled = (weight * grad_ref[:, cols].astype(F32)).astype(BF16)
        store_pieces(send_refs, cols, mm(place, scaled).astype(BF16))
    for copy in copies[1:6]:
        copy.wait()


def kv_stacks(key_refs, value_refs, g):
    cols = slice(g * HEAD_SIZE, (g + 1) * HEAD_SIZE)
    return stacked(key_refs, cols), stacked(value_refs, cols)


def attention_kernel(
    count, pos_ref, slot_ref, gain_ref, query_ref, resid_ref, *refs
):
    key_refs, value_refs = refs[:count], refs[count : 2 * count]
    hidden_ref, send_refs = refs[2 * count], refs[2 * count + 1 :]
    tokens = query_ref.shape[0]
    query_pos = row_to_col(pos_ref[:1, :])
    bias = jnp.concatenate(
        [
            jnp.where(pos_ref[s : s + 1, :].astype(F32) <= query_pos, 0.0, -1e30)
            for s in range(count)
        ],
        axis=1,
    )
    length = count * tokens
    ones = jnp.ones((length, HEAD_SIZE), BF16)
    total = jnp.zeros((tokens, HEAD_SIZE), F32)
    for g in range(KEY_VALUE_HEADS):
        keys, values = kv_stacks(key_refs, value_refs, g)
        values = jnp.concatenate([values, ones], axis=1)
        for h in range(g * GROUP, (g + 1) * GROUP):
            cols = slice(h * HEAD_SIZE, (h + 1) * HEAD_SIZE)
            scores = mm(query_ref[:, cols], keys, NT) + bias
            peak = jnp.max(scores, axis=1, keepdims=True)
            weights = jnp.exp2((scores - peak) * EXP2_SCALE).astype(BF16)
            mixed = mm(weights, values)
            attended = mixed[:, :HEAD_SIZE] / mixed[:, HEAD_SIZE:]
            hidden = (resid_ref[:, cols].astype(F32) + attended).astype(BF16)
            hidden_ref[:, cols] = hidden
            wide = hidden.astype(F32)
            total = total + wide * wide
    inv_rms = lax.rsqrt(jnp.sum(total, axis=1, keepdims=True) * (1.0 / D) + 1e-06)
    slots = sum(r.shape[0] for r in send_refs)
    place = placement_rows(slot_ref[...], slots)
    for cols in column_blocks():
        normed = (hidden_ref[:, cols].astype(F32) * inv_rms * gain_ref[:, cols]).astype(BF16)
        store_pieces(send_refs, cols, mm(place, normed).astype(BF16))


def first_expert_rows(slots, capacity):
    return iota((slots, 1), 0) % (EXP_DEV * capacity) < capacity


def probs_kernel(
    count,
    capacity,
    pieces,
    pos_ref,
    slot_ref,
    weight_ref,
    down_hbm,
    gate_hbm,
    query_ref,
    *refs,
):
    key_refs = refs[:count]
    grad_refs = refs[count : count + pieces]
    d_act_ref, probs_ref, down_ref, gate_ref, place_ref, wide_ref, sems = refs[count + pieces :]
    spans = [slice(e * FFE, (e + 1) * FFE) for e in range(EXP_DEV)]
    down_copies = [
        pltpu.make_async_copy(down_hbm.at[e], down_ref.at[span, :], sems.at[e])
        for e, span in enumerate(spans)
    ]
    gate_copies = [
        pltpu.make_async_copy(gate_hbm.at[e], gate_ref.at[:, span], sems.at[EXP_DEV + e])
        for e, span in enumerate(spans)
    ]
    for copy in down_copies + gate_copies:
        copy.start()
    place_ref[...] = placement_cols(slot_ref[...], place_ref.shape[1])
    wide_ref[...] = jnp.broadcast_to(row_to_col(weight_ref[...]), wide_ref.shape)
    query_pos = pos_ref[:1, :].astype(F32)
    bias = jnp.concatenate(
        [
            jnp.where(row_to_col(pos_ref[s : s + 1, :]) <= query_pos, 0.0, -1e30)
            for s in range(count)
        ],
        axis=0,
    )
    bias = jnp.concatenate([bias, bias], axis=1)
    for g in range(KEY_VALUE_HEADS):
        keys = stacked(key_refs, slice(g * HEAD_SIZE, (g + 1) * HEAD_SIZE))
        for pair in range(g * GROUP // 2, (g + 1) * GROUP // 2):
            scores = mm(keys, head_pair(query_ref, pair), NT) + bias
            peak = jnp.max(scores, axis=0, keepdims=True)
            weights = jnp.exp2((scores - peak) * EXP2_SCALE)
            probs_ref[pair] = weights * (1.0 / jnp.sum(weights, axis=0, keepdims=True))
    grads = stacked(grad_refs)
    first = first_expert_rows(grads.shape[0], capacity)
    for copy in down_copies:
        copy.wait()
    d_act = mm(grads, down_ref[...], NT)
    d_act_ref[...] = jnp.where(first, d_act[:, :FFE], d_act[:, FFE:])
    for copy in gate_copies:
        copy.wait()


def part_views(refs, rows, part):
    return [r if r.shape[0] != 2 * rows else r.at[part * rows : (part + 1) * rows] for r in refs]


def joined(step, pieces):
    return pieces > 1 and step > 0 and step & (step - 1) == 0


def split_parts(refs, pieces):
    back, out = [], []
    at = 0
    for s in range(pieces):
        back.append(refs[at])
        at += not joined(s, pieces)
        out.append(refs[at])
        at += 1
    return back, out


def expert_kernel(capacity, pieces, gate_ref, down_ref, d_act_ref, *refs):
    rows = stacked(refs[:pieces])
    back_refs, out_refs = split_parts(refs[pieces:], pieces)
    back_refs = part_views(back_refs, EXP_DEV * capacity, 0)
    out_refs = part_views(out_refs, EXP_DEV * capacity, 1)
    first = first_expert_rows(rows.shape[0], capacity)
    both = mm(rows, gate_ref[...])
    pre = jnp.where(first, both[:, :FFE], both[:, FFE:])
    gate = 1.0 / (1.0 + jnp.exp(-pre))
    act = pre * gate
    d_pre = d_act_ref[...] * gate * (1.0 + pre * (1.0 - gate))
    act, d_pre = [
        jnp.concatenate([jnp.where(first, x, 0.0), jnp.where(first, 0.0, x)], axis=1).astype(BF16)
        for x in (act, d_pre)
    ]
    for cols in column_blocks():
        store_pieces(back_refs, cols, mm(d_pre, gate_ref[cols, :], NT).astype(BF16))
        store_pieces(out_refs, cols, mm(act, down_ref[:, cols]).astype(BF16))


def gain_kernel(pieces, rows, gain_ref, *refs):
    row_refs = refs[:pieces]
    back_refs = part_views(refs[pieces:-1], rows, 0)
    terms_ref = refs[-1]
    for cols in column_blocks():
        products = stacked(row_refs, cols).astype(F32) * stacked(back_refs, cols).astype(F32)
        terms = jnp.sum(products, axis=0, keepdims=True) / gain_ref[:, cols]
        for at in range(0, COLS, LANES):
            line = (cols.start + at) // LANES
            terms_ref[line : line + 1, :] = terms[:, at : at + LANES]


def group_back(g, key_refs, value_refs, query_ref, probs_ref, d_resid, dq_ref, own_ref, shared):
    length = len(key_refs) * own_ref.shape[0]
    tokens = own_ref.shape[0]
    keys, values = kv_stacks(key_refs, value_refs, g)
    keys_t = jnp.transpose(keys.astype(F32)).astype(BF16)
    d_keys = jnp.zeros((length, HEAD_SIZE), F32)
    d_values = jnp.zeros((length, HEAD_SIZE), F32)
    for local in range(GROUP // 2):
        pair = g * GROUP // 2 + local
        cols_a, cols_b = pair_cols(local)
        d_out = head_pair(d_resid, local)
        probs = probs_ref[pair]
        d_probs = mm(values, d_out, NT)
        row_dot = jnp.sum(probs * d_probs, axis=0, keepdims=True)
        d_scores = (probs * (d_probs - row_dot)).astype(BF16)
        d_keys = d_keys + mm(d_scores, head_pair(query_ref, pair))
        d_values = d_values + mm(probs.astype(BF16), d_out)
        d_query_t = mm(keys_t, d_scores) * SCALE
        dq_ref[:, cols_a] = jnp.transpose(d_query_t[:, :tokens]).astype(BF16)
        dq_ref[:, cols_b] = jnp.transpose(d_query_t[:, tokens:]).astype(BF16)
    d_keys = d_keys * SCALE
    own_ref[:, :HEAD_SIZE] = d_keys[:tokens]
    own_ref[:, HEAD_SIZE:] = d_values[:tokens]
    start = 2 * g * HEAD_SIZE
    for s, ref in enumerate(shared, 1):
        span = slice(s * tokens, (s + 1) * tokens)
        ref[:, start : start + HEAD_SIZE] = d_keys[span].astype(BF16)
        ref[:, start + HEAD_SIZE : start + 2 * HEAD_SIZE] = d_values[span].astype(BF16)


def first_back_kernel(
    count, pieces, rows, place_ref, gain_ref, hidden_ref, grad_ref, query_ref, probs_ref, *refs
):
    key_refs, value_refs = refs[:count], refs[count : 2 * count]
    refs = refs[2 * count :]
    dn_refs = part_views(refs[:pieces], rows, 0)
    resid_hbm, dq_ref, rest_ref, own_ref = refs[pieces : pieces + 4]
    shared = refs[pieces + 4 : -3]
    resid_ref, dn_scratch, sem = refs[-3:]
    tokens = hidden_ref.shape[0]
    place = place_ref[...]
    square = jnp.zeros((tokens, COLS), F32)
    mixing = jnp.zeros((tokens, COLS), F32)
    for cols in column_blocks():
        dn = mm(place, stacked(dn_refs, cols)) * gain_ref[:, cols]
        dn_scratch[:, cols] = dn
        hidden = hidden_ref[:, cols].astype(F32)
        square = square + hidden * hidden
        mixing = mixing + dn * hidden
    inv_rms = lax.rsqrt(jnp.sum(square, axis=1, keepdims=True) * (1.0 / D) + 1e-06)
    mean_mix = jnp.sum(mixing, axis=1, keepdims=True) * (1.0 / D)
    factor = inv_rms * inv_rms * inv_rms * mean_mix
    half = GROUP * HEAD_SIZE
    for cols in column_blocks():
        part = (
            grad_ref[:, cols].astype(F32)
            + dn_scratch[:, cols] * inv_rms
            - hidden_ref[:, cols].astype(F32) * factor
        ).astype(BF16)
        resid_ref[:, cols] = part
        if cols.start >= half:
            rest_ref[:, cols.start - half : cols.stop - half] = part
    resid_copy = pltpu.make_async_copy(resid_ref, resid_hbm, sem)
    resid_copy.start()
    group_back(0, key_refs, value_refs, query_ref, probs_ref, resid_ref, dq_ref, own_ref, shared)
    resid_copy.wait()


def second_back_kernel(count, query_ref, probs_ref, rest_ref, *refs):
    key_refs, value_refs = refs[:count], refs[count : 2 * count]
    first_shared = refs[2 * count : 3 * count - 1]
    dq_ref, own_ref = refs[3 * count - 1 : 3 * count + 1]
    shared = refs[3 * count + 1 :]
    for source, target in zip(first_shared, shared):
        target[:, : 2 * HEAD_SIZE] = source[...]
    group_back(1, key_refs, value_refs, query_ref, probs_ref, rest_ref, dq_ref, own_ref, shared)


def output_kernel(
    count, pieces, rows, tokens_in_all, place_ref, weight_ref, gain_ref, hidden_ref, grad_ref, *refs
):
    own_refs, refs = refs[:KEY_VALUE_HEADS], refs[KEY_VALUE_HEADS:]
    dq_refs, refs = refs[:KEY_VALUE_HEADS], refs[KEY_VALUE_HEADS:]
    arrived_refs = refs[: count - 1]
    y_refs = part_views(refs[count - 1 : count - 1 + pieces], rows, 1)
    out_hbm, dq_hbm, dk_hbm, dv_hbm, d_weight_hbm, d_gain_hbm = refs[count - 1 + pieces : -6]
    out_ref, dk_ref, dv_ref, d_weight_ref, d_gain_ref, sems = refs[-6:]
    copies = []

    def send(source, target):
        copy = pltpu.make_async_copy(source, target, sems.at[len(copies)])
        copy.start()
        copies.append(copy)

    width = GROUP * HEAD_SIZE
    for g, dq_ref in enumerate(dq_refs):
        send(dq_ref, dq_hbm.at[:, g * width : (g + 1) * width])
    for g, own_ref in enumerate(own_refs):
        d_kv = own_ref[...]
        for ref in arrived_refs:
            d_kv = d_kv + ref[:, 2 * g * HEAD_SIZE : 2 * (g + 1) * HEAD_SIZE].astype(F32)
        cols = slice(g * HEAD_SIZE, (g + 1) * HEAD_SIZE)
        dk_ref[:, cols] = d_kv[:, :HEAD_SIZE].astype(BF16)
        dv_ref[:, cols] = d_kv[:, HEAD_SIZE:].astype(BF16)
    d_gain_ref[...] = gain_ref[...] * (1.0 / tokens_in_all)
    send(dk_ref, dk_hbm)
    send(dv_ref, dv_hbm)
    send(d_gain_ref, d_gain_hbm)
    tokens = hidden_ref.shape[0]
    place = place_ref[...]
    weight = weight_ref[...]
    total = jnp.zeros((tokens, COLS), F32)
    for cols in column_blocks():
        y = mm(place, stacked(y_refs, cols))
        out_ref[:, cols] = (hidden_ref[:, cols].astype(F32) + weight * y).astype(BF16)
        send(out_ref.at[:, cols], out_hbm.at[:, cols])
        total = total + y * grad_ref[:, cols].astype(F32)
    d_weight_ref[...] = col_to_row(jnp.sum(total, axis=1, keepdims=True))
    send(d_weight_ref, d_weight_hbm)
    for copy in copies:
        copy.wait()


def run(kernel, name, inputs, outputs, flops, scratch=(), limit=20 * MIB):
    nbytes = sum(x.size * x.dtype.itemsize for _, x in inputs + outputs) if flops else 0
    spec = {space: pl.BlockSpec(memory_space=space) for space in (VMEM, HBM)}
    results = pl.pallas_call(
        kernel,
        out_shape=[x for _, x in outputs],
        in_specs=[spec[space] for space, _ in inputs],
        out_specs=[spec[space] for space, _ in outputs],
        scratch_shapes=list(scratch),
        compiler_params=pltpu.CompilerParams(vmem_limit_bytes=limit),
        cost_estimate=pl.CostEstimate(flops=flops, bytes_accessed=nbytes, transcendentals=0),
        name=name,
    )(*[pltpu.with_memory_space_constraint(x, HBM) if space is HBM else x for space, x in inputs])
    return list(results)


def placed(space, arrays):
    return [(space, x) for x in arrays]


def pairwise(value, axis, step):
    count = lax.axis_size(axis)
    return lax.ppermute(value, axis, [(i, i ^ step) for i in range(count)])


def exchange_flat(flat, capacity):
    count = lax.axis_size("exp")
    rows = EXP_DEV * capacity
    blocks = [flat[s * rows : (s + 1) * rows] for s in range(count)]
    moved = [blocks[0]] + [pairwise(blocks[s], "exp", s) for s in range(1, count)]
    return jnp.concatenate(moved, axis=0)


def exchange(pieces, capacity):
    if lax.axis_size("exp") != len(pieces):
        return [exchange_flat(pieces[0], capacity)]
    return [pairwise(piece, "exp", s) if s > 0 else piece for s, piece in enumerate(pieces)]


def doubled(value, axis, step):
    return value + pairwise(value, axis, step)


def sum_over(value, axis, first=1):
    step = first
    while step < lax.axis_size(axis):
        value = doubled(value, axis, step)
        step *= 2
    return value


def widened(act, value, axis, step):
    rows = value.shape[0]
    wide = jnp.pad(value, ((0, WIDE_LINES - rows), (0, 0)))
    return act(wide, axis, step)[:rows]


def shaped(shape, dtype):
    return jax.ShapeDtypeStruct(shape, dtype)


def per_device(
    queries,
    keys,
    values,
    resid,
    block_order,
    norm_gain,
    w_gate,
    w_down,
    routes,
    route_weight,
    d_out,
):
    query_rows = queries[0]
    resid_rows = resid[0]
    grad_rows = d_out[0]
    tokens = query_rows.shape[0]
    chosen = routes.reshape(1, tokens)
    gain = norm_gain.reshape(1, D)
    ctx_count = lax.axis_size("ctx")
    exp_count = lax.axis_size("exp")
    experts = EXP_DEV * exp_count
    capacity = 3 * tokens // (2 * experts)
    slots = experts * capacity
    rows = EXP_DEV * capacity
    piece_count = exp_count if rows % 16 == 0 else 1
    piece_shapes = [shaped((slots // piece_count, D), BF16)] * piece_count
    token_shape = shaped((tokens, D), BF16)
    kv_width = 2 * KEY_VALUE_HEADS * HEAD_SIZE
    attn_flops = 4 * tokens * ctx_count * tokens * QUERY_HEADS * HEAD_SIZE
    place_flops = 2 * slots * tokens * D
    expert_flops = 2 * slots * D * FFE * EXP_DEV

    own_keys, own_values = keys[0], values[0]
    all_keys = [own_keys] + [pairwise(own_keys, "ctx", s) for s in range(1, ctx_count)]
    all_values = [own_values] + [pairwise(own_values, "ctx", s) for s in range(1, ctx_count)]

    near = [grad_rows, own_keys, own_values, gain, query_rows, resid_rows]
    grad_rows, own_keys, own_values, gain, query_rows, resid_rows, slot, pos, weight, *send_grad = run(
        functools.partial(dispatch_kernel, ctx_count, experts, capacity),
        "dispatch_grads",
        placed(HBM, near + [route_weight, chosen, block_order]),
        placed(
            VMEM,
            [shaped(x.shape, x.dtype) for x in near]
            + [
                shaped((1, tokens), jnp.int32),
                shaped((ctx_count, tokens), jnp.int32),
                shaped((1, tokens), F32),
            ]
            + piece_shapes,
        ),
        place_flops,
        scratch=[
            pltpu.SMEM(block_order.shape, jnp.int32),
            pltpu.VMEM((1, tokens), jnp.int32),
            pltpu.SemaphoreType.DMA((9,)),
        ],
    )
    all_keys[0], all_values[0] = own_keys, own_values
    arrived_grad = exchange(send_grad, capacity)

    hidden, *send_x = run(
        functools.partial(attention_kernel, ctx_count),
        "attention_forward",
        placed(VMEM, [pos, slot, gain, query_rows, resid_rows] + all_keys + all_values),
        placed(VMEM, [token_shape] + piece_shapes),
        attn_flops + place_flops,
    )
    arrived_x = exchange(send_x, capacity)

    d_act, probs, down_near, gate_near, place, weight_wide = run(
        functools.partial(probs_kernel, ctx_count, capacity, piece_count),
        "act_grads_and_probs",
        placed(VMEM, [pos, slot, weight])
        + placed(HBM, [w_down, w_gate])
        + placed(VMEM, [query_rows] + all_keys + arrived_grad),
        placed(
            VMEM,
            [
                shaped((slots, FFE), F32),
                shaped((QUERY_HEADS // 2, ctx_count * tokens, 2 * tokens), F32),
                shaped((EXP_DEV * FFE, D), BF16),
                shaped((D, EXP_DEV * FFE), BF16),
                shaped((tokens, slots), BF16),
                shaped((tokens, COLS), F32),
            ],
        ),
        expert_flops + attn_flops // 2,
        scratch=[pltpu.SemaphoreType.DMA((2 * EXP_DEV,))],
    )

    return_shapes = []
    for s in range(piece_count):
        if joined(s, piece_count):
            return_shapes.append(shaped((2 * rows, D), BF16))
        else:
            return_shapes.extend([piece_shapes[0]] * 2)
    sent = run(
        functools.partial(expert_kernel, capacity, piece_count),
        "experts",
        placed(VMEM, [gate_near, down_near, d_act] + arrived_x),
        placed(VMEM, return_shapes),
        3 * expert_flops,
    )
    send_dn, send_y = split_parts(sent, piece_count)
    dn = exchange(send_dn, capacity)
    far = [s for s in range(1, piece_count) if not joined(s, piece_count)]
    y = list(dn) if piece_count > 1 else [exchange_flat(send_y[0], capacity)]
    y[0] = send_y[0] if piece_count > 1 else y[0]
    (terms,) = run(
        functools.partial(gain_kernel, piece_count, rows),
        "gain_terms",
        placed(VMEM, [gain] + arrived_x + send_dn),
        placed(VMEM, [shaped((GAIN_LINES, LANES), F32)]),
        2 * slots * D,
    )
    terms = sum_over(sum_over(terms, "dp"), "ctx")
    send_far, terms = lax.optimization_barrier(([send_y[s] for s in far], terms))
    for s, piece in zip(far, send_far):
        y[s] = pairwise(piece, "exp", s)
    beside = pairwise(terms, "exp", FIRST)

    half_shape = shaped((tokens, D // 2), BF16)
    own_shape = shaped((tokens, 2 * HEAD_SIZE), F32)
    d_hidden, dq_first, rest, own_first, *shared_first = run(
        functools.partial(first_back_kernel, ctx_count, piece_count, rows),
        "residual_and_first_group",
        placed(VMEM, [place, gain, hidden, grad_rows, query_rows, probs])
        + placed(VMEM, all_keys + all_values + dn),
        placed(HBM, [token_shape])
        + placed(
            VMEM,
            [half_shape, half_shape, own_shape]
            + [shaped((tokens, 2 * HEAD_SIZE), BF16)] * (ctx_count - 1),
        ),
        A_COST,
        scratch=[
            pltpu.VMEM((tokens, D), BF16),
            pltpu.VMEM((tokens, D), F32),
            pltpu.SemaphoreType.DMA(()),
        ],
    )
    terms, rest = lax.optimization_barrier((terms, rest))
    terms = terms + beside
    terms = widened(doubled, terms, "exp", 3 - FIRST)
    dq_second, own_second, *shared = run(
        functools.partial(second_back_kernel, ctx_count),
        "second_group",
        placed(VMEM, [query_rows, probs, rest] + all_keys + all_values + shared_first),
        placed(VMEM, [half_shape, own_shape])
        + placed(VMEM, [shaped((tokens, kv_width), BF16)] * (ctx_count - 1)),
        B_COST,
    )
    terms = sum_over(terms, "exp", first=4)
    arrived_far, shared = lax.optimization_barrier(([y[s] for s in far], shared))
    for s, piece in zip(far, arrived_far):
        y[s] = piece
    kv_arrived = [pairwise(part, "ctx", s) for s, part in enumerate(shared, 1)]

    kv_shape = shaped((tokens, kv_width // 2), BF16)
    final_shapes = [token_shape, token_shape, kv_shape, kv_shape]
    final_shapes += [shaped((1, tokens), F32), shaped((GAIN_LINES, LANES), F32)]
    total_tokens = tokens * ctx_count * exp_count * lax.axis_size("dp")
    layer_out, d_queries, d_keys, d_values, d_weight, d_gain = run(
        functools.partial(output_kernel, ctx_count, piece_count, rows, total_tokens),
        "layer_output",
        placed(
            VMEM,
            [place, weight_wide, terms, hidden, grad_rows, own_first, own_second]
            + [dq_first, dq_second]
            + kv_arrived
            + y,
        ),
        placed(HBM, final_shapes),
        place_flops,
        scratch=[pltpu.VMEM(x.shape, x.dtype) for x in final_shapes[:1] + final_shapes[2:]]
        + [pltpu.SemaphoreType.DMA((4 + KEY_VALUE_HEADS + D // COLS,))],
    )
    return (
        layer_out[None],
        d_hidden[None],
        d_queries[None],
        d_keys[None],
        d_values[None],
        d_weight,
        d_gain.reshape(D),
    )


def solution(mesh):
    in_specs = (
        P(("exp", "dp"), "ctx", None),
        P(("exp", "dp"), "ctx", None),
        P(("exp", "dp"), "ctx", None),
        P(("exp", "dp"), "ctx", None),
        P(),
        P(),
        P("exp", None, None),
        P("exp", None, None),
        P(("exp", "dp"), "ctx", None),
        P(("exp", "dp"), "ctx"),
        P(("exp", "dp"), "ctx", None),
    )
    out_specs = (
        P(("exp", "dp"), "ctx", None),
        P(("exp", "dp"), "ctx", None),
        P(("exp", "dp"), "ctx", None),
        P(("exp", "dp"), "ctx", None),
        P(("exp", "dp"), "ctx", None),
        P(("exp", "dp"), "ctx"),
        P(),
    )
    return jax.shard_map(
        per_device, mesh=mesh, in_specs=in_specs, out_specs=out_specs, check_vma=False
    )
```

```python
import functools

import jax
import jax.numpy as jnp
from jax import lax
from jax.experimental import pallas as pl
from jax.experimental.pallas import tpu as pltpu
from jax.sharding import PartitionSpec as P

D = 2048
HEAD_SIZE = 128
QUERY_HEADS = 16
KEY_VALUE_HEADS = 2
GROUP = QUERY_HEADS // KEY_VALUE_HEADS
FFE = 384
EXP_DEV = 2
COLS = 256
LANES = 128
GAIN_LINES = D // LANES
WIDE_LINES = 32
FIRST = 2
A_COST = 4000000000
B_COST = 0
SCALE = HEAD_SIZE ** (-0.5)
EXP2_SCALE = SCALE * 1.4426950408889634
F32 = jnp.float32
BF16 = jnp.bfloat16
NN = (((1,), (0,)), ((), ()))
NT = (((1,), (1,)), ((), ()))
MIB = 1 << 20
VMEM, HBM = pltpu.VMEM, pltpu.HBM


def mm(a, b, dims=NN):
    return lax.dot_general(a, b, dims, preferred_element_type=F32)


def iota(shape, dim):
    return lax.broadcasted_iota(jnp.int32, shape, dim)


def row_to_col(row):
    n = row.shape[1]
    eye = iota((n, n), 0) == iota((n, n), 1)
    return jnp.sum(jnp.where(eye, row.astype(F32), 0.0), axis=1, keepdims=True)


def col_to_row(col):
    n = col.shape[0]
    eye = iota((n, n), 0) == iota((n, n), 1)
    return jnp.sum(jnp.where(eye, col, 0.0), axis=0, keepdims=True)


def block_positions(order_ref, ctx_index, tokens):
    span = tokens // 8
    index = iota((1, tokens), 1)
    which = index // span
    start = jnp.zeros((1, tokens), jnp.int32)
    for b in range(8):
        start = jnp.where(which == b, order_ref[ctx_index * 8 + b], start)
    return start * span + index % span


def stacked(refs, cols=slice(None)):
    parts = [r[:, cols] for r in refs]
    return parts[0] if len(parts) == 1 else jnp.concatenate(parts, axis=0)


def column_blocks(width=D, step=COLS):
    return [slice(c, c + step) for c in range(0, width, step)]


def store_pieces(refs, cols, rows_value):
    at = 0
    for r in refs:
        n = r.shape[0]
        r[:, cols] = rows_value[at : at + n]
        at += n


def pair_cols(pair):
    start = 2 * pair * HEAD_SIZE
    return slice(start, start + HEAD_SIZE), slice(start + HEAD_SIZE, start + 2 * HEAD_SIZE)


def head_pair(ref, pair):
    first, second = pair_cols(pair)
    return jnp.concatenate([ref[:, first], ref[:, second]], axis=0)


def placement_rows(slot_row, slots):
    tokens = slot_row.shape[1]
    return jnp.where(iota((slots, tokens), 0) == slot_row, 1.0, 0.0).astype(BF16)


def placement_cols(slot_row, slots):
    tokens = slot_row.shape[1]
    slot_col = row_to_col(slot_row)
    return jnp.where(iota((tokens, slots), 1).astype(F32) == slot_col, 1.0, 0.0).astype(BF16)


def dispatch_kernel(count, experts, capacity, *refs):
    sources, refs = refs[:9], refs[9:]
    targets, refs = refs[:6], refs[6:]
    grad_ref = targets[0]
    slot_ref, pos_ref, weight_ref = refs[:3]
    send_refs = refs[3:-3]
    order_ref, routes_ref, sems = refs[-3:]
    targets = targets + (weight_ref, routes_ref, order_ref)
    copies = [
        pltpu.make_async_copy(source, target, sems.at[i])
        for i, (source, target) in enumerate(zip(sources, targets))
    ]
    for copy in copies[6:] + copies[:6]:
        copy.start()
    for copy in copies[6:]:
        copy.wait()
    tokens = routes_ref.shape[1]
    chosen = routes_ref[...]
    lanes = max(experts, 16)
    hits = jnp.where(iota((lanes, tokens), 0) == chosen, 1.0, 0.0)
    before = jnp.where(iota((tokens, tokens), 0) < iota((tokens, tokens), 1), 1.0, 0.0)
    earlier = mm(hits.astype(BF16), before.astype(BF16))
    rank = jnp.sum(hits * earlier, axis=0, keepdims=True).astype(jnp.int32)
    target = (chosen // EXP_DEV) ^ lax.axis_index("exp")
    slot = (target * EXP_DEV + chosen % EXP_DEV) * capacity + rank
    slot_ref[...] = slot
    me = lax.axis_index("ctx")
    for s in range(count):
        pos_ref[s : s + 1, :] = block_positions(order_ref, me ^ s, tokens)
    place = placement_rows(slot, experts * capacity)
    weight = row_to_col(weight_ref[...])
    copies[0].wait()
    for cols in column_blocks():
        scaled = (weight * grad_ref[:, cols].astype(F32)).astype(BF16)
        store_pieces(send_refs, cols, mm(place, scaled).astype(BF16))
    for copy in copies[1:6]:
        copy.wait()


def kv_stacks(key_refs, value_refs, g):
    cols = slice(g * HEAD_SIZE, (g + 1) * HEAD_SIZE)
    return stacked(key_refs, cols), stacked(value_refs, cols)


def attention_kernel(
    count, pos_ref, slot_ref, gain_ref, query_ref, resid_ref, *refs
):
    key_refs, value_refs = refs[:count], refs[count : 2 * count]
    hidden_ref, send_refs = refs[2 * count], refs[2 * count + 1 :]
    tokens = query_ref.shape[0]
    query_pos = row_to_col(pos_ref[:1, :])
    bias = jnp.concatenate(
        [
            jnp.where(pos_ref[s : s + 1, :].astype(F32) <= query_pos, 0.0, -1e30)
            for s in range(count)
        ],
        axis=1,
    )
    length = count * tokens
    ones = jnp.ones((length, HEAD_SIZE), BF16)
    total = jnp.zeros((tokens, HEAD_SIZE), F32)
    for g in range(KEY_VALUE_HEADS):
        keys, values = kv_stacks(key_refs, value_refs, g)
        values = jnp.concatenate([values, ones], axis=1)
        for h in range(g * GROUP, (g + 1) * GROUP):
            cols = slice(h * HEAD_SIZE, (h + 1) * HEAD_SIZE)
            scores = mm(query_ref[:, cols], keys, NT) + bias
            peak = jnp.max(scores, axis=1, keepdims=True)
            weights = jnp.exp2((scores - peak) * EXP2_SCALE).astype(BF16)
            mixed = mm(weights, values)
            attended = mixed[:, :HEAD_SIZE] / mixed[:, HEAD_SIZE:]
            hidden = (resid_ref[:, cols].astype(F32) + attended).astype(BF16)
            hidden_ref[:, cols] = hidden
            wide = hidden.astype(F32)
            total = total + wide * wide
    inv_rms = lax.rsqrt(jnp.sum(total, axis=1, keepdims=True) * (1.0 / D) + 1e-06)
    slots = sum(r.shape[0] for r in send_refs)
    place = placement_rows(slot_ref[...], slots)
    for cols in column_blocks():
        normed = (hidden_ref[:, cols].astype(F32) * inv_rms * gain_ref[:, cols]).astype(BF16)
        store_pieces(send_refs, cols, mm(place, normed).astype(BF16))


def first_expert_rows(slots, capacity):
    return iota((slots, 1), 0) % (EXP_DEV * capacity) < capacity


def probs_kernel(
    count,
    capacity,
    pieces,
    pos_ref,
    slot_ref,
    weight_ref,
    down_hbm,
    gate_hbm,
    query_ref,
    *refs,
):
    key_refs = refs[:count]
    grad_refs = refs[count : count + pieces]
    d_act_ref, probs_ref, down_ref, gate_ref, place_ref, wide_ref, sems = refs[count + pieces :]
    spans = [slice(e * FFE, (e + 1) * FFE) for e in range(EXP_DEV)]
    down_copies = [
        pltpu.make_async_copy(down_hbm.at[e], down_ref.at[span, :], sems.at[e])
        for e, span in enumerate(spans)
    ]
    gate_copies = [
        pltpu.make_async_copy(gate_hbm.at[e], gate_ref.at[:, span], sems.at[EXP_DEV + e])
        for e, span in enumerate(spans)
    ]
    for copy in down_copies + gate_copies:
        copy.start()
    place_ref[...] = placement_cols(slot_ref[...], place_ref.shape[1])
    wide_ref[...] = jnp.broadcast_to(row_to_col(weight_ref[...]), wide_ref.shape)
    query_pos = pos_ref[:1, :].astype(F32)
    bias = jnp.concatenate(
        [
            jnp.where(row_to_col(pos_ref[s : s + 1, :]) <= query_pos, 0.0, -1e30)
            for s in range(count)
        ],
        axis=0,
    )
    bias = jnp.concatenate([bias, bias], axis=1)
    for g in range(KEY_VALUE_HEADS):
        keys = stacked(key_refs, slice(g * HEAD_SIZE, (g + 1) * HEAD_SIZE))
        for pair in range(g * GROUP // 2, (g + 1) * GROUP // 2):
            scores = mm(keys, head_pair(query_ref, pair), NT) + bias
            peak = jnp.max(scores, axis=0, keepdims=True)
            weights = jnp.exp2((scores - peak) * EXP2_SCALE)
            probs_ref[pair] = weights * (1.0 / jnp.sum(weights, axis=0, keepdims=True))
    grads = stacked(grad_refs)
    first = first_expert_rows(grads.shape[0], capacity)
    for copy in down_copies:
        copy.wait()
    d_act = mm(grads, down_ref[...], NT)
    d_act_ref[...] = jnp.where(first, d_act[:, :FFE], d_act[:, FFE:])
    for copy in gate_copies:
        copy.wait()


def part_views(refs, rows, part):
    return [r if r.shape[0] != 2 * rows else r.at[part * rows : (part + 1) * rows] for r in refs]


def joined(step, pieces):
    return pieces > 1 and step > 0 and step & (step - 1) == 0


def split_parts(refs, pieces):
    back, out = [], []
    at = 0
    for s in range(pieces):
        back.append(refs[at])
        at += not joined(s, pieces)
        out.append(refs[at])
        at += 1
    return back, out


def expert_kernel(capacity, pieces, gate_ref, down_ref, d_act_ref, *refs):
    rows = stacked(refs[:pieces])
    back_refs, out_refs = split_parts(refs[pieces:], pieces)
    back_refs = part_views(back_refs, EXP_DEV * capacity, 0)
    out_refs = part_views(out_refs, EXP_DEV * capacity, 1)
    first = first_expert_rows(rows.shape[0], capacity)
    both = mm(rows, gate_ref[...])
    pre = jnp.where(first, both[:, :FFE], both[:, FFE:])
    gate = 1.0 / (1.0 + jnp.exp(-pre))
    act = pre * gate
    d_pre = d_act_ref[...] * gate * (1.0 + pre * (1.0 - gate))
    act, d_pre = [
        jnp.concatenate([jnp.where(first, x, 0.0), jnp.where(first, 0.0, x)], axis=1).astype(BF16)
        for x in (act, d_pre)
    ]
    for cols in column_blocks():
        store_pieces(back_refs, cols, mm(d_pre, gate_ref[cols, :], NT).astype(BF16))
        store_pieces(out_refs, cols, mm(act, down_ref[:, cols]).astype(BF16))


def gain_kernel(pieces, rows, gain_ref, *refs):
    row_refs = refs[:pieces]
    back_refs = part_views(refs[pieces:-1], rows, 0)
    terms_ref = refs[-1]
    for cols in column_blocks():
        products = stacked(row_refs, cols).astype(F32) * stacked(back_refs, cols).astype(F32)
        terms = jnp.sum(products, axis=0, keepdims=True) / gain_ref[:, cols]
        for at in range(0, COLS, LANES):
            line = (cols.start + at) // LANES
            terms_ref[line : line + 1, :] = terms[:, at : at + LANES]


def group_back(g, key_refs, value_refs, query_ref, probs_ref, d_resid, dq_ref, own_ref, shared):
    length = len(key_refs) * own_ref.shape[0]
    tokens = own_ref.shape[0]
    keys, values = kv_stacks(key_refs, value_refs, g)
    keys_t = jnp.transpose(keys.astype(F32)).astype(BF16)
    d_keys = jnp.zeros((length, HEAD_SIZE), F32)
    d_values = jnp.zeros((length, HEAD_SIZE), F32)
    for local in range(GROUP // 2):
        pair = g * GROUP // 2 + local
        cols_a, cols_b = pair_cols(local)
        d_out = head_pair(d_resid, local)
        probs = probs_ref[pair]
        d_probs = mm(values, d_out, NT)
        row_dot = jnp.sum(probs * d_probs, axis=0, keepdims=True)
        d_scores = (probs * (d_probs - row_dot)).astype(BF16)
        d_keys = d_keys + mm(d_scores, head_pair(query_ref, pair))
        d_values = d_values + mm(probs.astype(BF16), d_out)
        d_query_t = mm(keys_t, d_scores) * SCALE
        dq_ref[:, cols_a] = jnp.transpose(d_query_t[:, :tokens]).astype(BF16)
        dq_ref[:, cols_b] = jnp.transpose(d_query_t[:, tokens:]).astype(BF16)
    d_keys = d_keys * SCALE
    own_ref[:, :HEAD_SIZE] = d_keys[:tokens]
    own_ref[:, HEAD_SIZE:] = d_values[:tokens]
    start = 2 * g * HEAD_SIZE
    for s, ref in enumerate(shared, 1):
        span = slice(s * tokens, (s + 1) * tokens)
        ref[:, start : start + HEAD_SIZE] = d_keys[span].astype(BF16)
        ref[:, start + HEAD_SIZE : start + 2 * HEAD_SIZE] = d_values[span].astype(BF16)


def first_back_kernel(
    count, pieces, rows, place_ref, gain_ref, hidden_ref, grad_ref, query_ref, probs_ref, *refs
):
    key_refs, value_refs = refs[:count], refs[count : 2 * count]
    refs = refs[2 * count :]
    dn_refs = part_views(refs[:pieces], rows, 0)
    resid_hbm, dq_ref, rest_ref, own_ref = refs[pieces : pieces + 4]
    shared = refs[pieces + 4 : -3]
    resid_ref, dn_scratch, sem = refs[-3:]
    tokens = hidden_ref.shape[0]
    place = place_ref[...]
    square = jnp.zeros((tokens, COLS), F32)
    mixing = jnp.zeros((tokens, COLS), F32)
    for cols in column_blocks():
        dn = mm(place, stacked(dn_refs, cols)) * gain_ref[:, cols]
        dn_scratch[:, cols] = dn
        hidden = hidden_ref[:, cols].astype(F32)
        square = square + hidden * hidden
        mixing = mixing + dn * hidden
    inv_rms = lax.rsqrt(jnp.sum(square, axis=1, keepdims=True) * (1.0 / D) + 1e-06)
    mean_mix = jnp.sum(mixing, axis=1, keepdims=True) * (1.0 / D)
    factor = inv_rms * inv_rms * inv_rms * mean_mix
    half = GROUP * HEAD_SIZE
    for cols in column_blocks():
        part = (
            grad_ref[:, cols].astype(F32)
            + dn_scratch[:, cols] * inv_rms
            - hidden_ref[:, cols].astype(F32) * factor
        ).astype(BF16)
        resid_ref[:, cols] = part
        if cols.start >= half:
            rest_ref[:, cols.start - half : cols.stop - half] = part
    resid_copy = pltpu.make_async_copy(resid_ref, resid_hbm, sem)
    resid_copy.start()
    group_back(0, key_refs, value_refs, query_ref, probs_ref, resid_ref, dq_ref, own_ref, shared)
    resid_copy.wait()


def second_back_kernel(count, query_ref, probs_ref, rest_ref, *refs):
    key_refs, value_refs = refs[:count], refs[count : 2 * count]
    first_shared = refs[2 * count : 3 * count - 1]
    dq_ref, own_ref = refs[3 * count - 1 : 3 * count + 1]
    shared = refs[3 * count + 1 :]
    for source, target in zip(first_shared, shared):
        target[:, : 2 * HEAD_SIZE] = source[...]
    group_back(1, key_refs, value_refs, query_ref, probs_ref, rest_ref, dq_ref, own_ref, shared)


def output_kernel(
    count, pieces, rows, tokens_in_all, place_ref, weight_ref, gain_ref, hidden_ref, grad_ref, *refs
):
    own_refs, refs = refs[:KEY_VALUE_HEADS], refs[KEY_VALUE_HEADS:]
    dq_refs, refs = refs[:KEY_VALUE_HEADS], refs[KEY_VALUE_HEADS:]
    arrived_refs = refs[: count - 1]
    y_refs = part_views(refs[count - 1 : count - 1 + pieces], rows, 1)
    out_hbm, dq_hbm, dk_hbm, dv_hbm, d_weight_hbm, d_gain_hbm = refs[count - 1 + pieces : -6]
    out_ref, dk_ref, dv_ref, d_weight_ref, d_gain_ref, sems = refs[-6:]
    copies = []

    def send(source, target):
        copy = pltpu.make_async_copy(source, target, sems.at[len(copies)])
        copy.start()
        copies.append(copy)

    width = GROUP * HEAD_SIZE
    for g, dq_ref in enumerate(dq_refs):
        send(dq_ref, dq_hbm.at[:, g * width : (g + 1) * width])
    for g, own_ref in enumerate(own_refs):
        d_kv = own_ref[...]
        for ref in arrived_refs:
            d_kv = d_kv + ref[:, 2 * g * HEAD_SIZE : 2 * (g + 1) * HEAD_SIZE].astype(F32)
        cols = slice(g * HEAD_SIZE, (g + 1) * HEAD_SIZE)
        dk_ref[:, cols] = d_kv[:, :HEAD_SIZE].astype(BF16)
        dv_ref[:, cols] = d_kv[:, HEAD_SIZE:].astype(BF16)
    d_gain_ref[...] = gain_ref[...] * (1.0 / tokens_in_all)
    send(dk_ref, dk_hbm)
    send(dv_ref, dv_hbm)
    send(d_gain_ref, d_gain_hbm)
    tokens = hidden_ref.shape[0]
    place = place_ref[...]
    weight = weight_ref[...]
    total = jnp.zeros((tokens, COLS), F32)
    for cols in column_blocks():
        y = mm(place, stacked(y_refs, cols))
        out_ref[:, cols] = (hidden_ref[:, cols].astype(F32) + weight * y).astype(BF16)
        send(out_ref.at[:, cols], out_hbm.at[:, cols])
        total = total + y * grad_ref[:, cols].astype(F32)
    d_weight_ref[...] = col_to_row(jnp.sum(total, axis=1, keepdims=True))
    send(d_weight_ref, d_weight_hbm)
    for copy in copies:
        copy.wait()


def run(kernel, name, inputs, outputs, flops, scratch=(), limit=20 * MIB):
    nbytes = sum(x.size * x.dtype.itemsize for _, x in inputs + outputs) if flops else 0
    spec = {space: pl.BlockSpec(memory_space=space) for space in (VMEM, HBM)}
    results = pl.pallas_call(
        kernel,
        out_shape=[x for _, x in outputs],
        in_specs=[spec[space] for space, _ in inputs],
        out_specs=[spec[space] for space, _ in outputs],
        scratch_shapes=list(scratch),
        compiler_params=pltpu.CompilerParams(vmem_limit_bytes=limit),
        cost_estimate=pl.CostEstimate(flops=flops, bytes_accessed=nbytes, transcendentals=0),
        name=name,
    )(*[pltpu.with_memory_space_constraint(x, HBM) if space is HBM else x for space, x in inputs])
    return list(results)


def placed(space, arrays):
    return [(space, x) for x in arrays]


def pairwise(value, axis, step):
    count = lax.axis_size(axis)
    return lax.ppermute(value, axis, [(i, i ^ step) for i in range(count)])


def exchange_flat(flat, capacity):
    count = lax.axis_size("exp")
    rows = EXP_DEV * capacity
    blocks = [flat[s * rows : (s + 1) * rows] for s in range(count)]
    moved = [blocks[0]] + [pairwise(blocks[s], "exp", s) for s in range(1, count)]
    return jnp.concatenate(moved, axis=0)


def exchange(pieces, capacity):
    if lax.axis_size("exp") != len(pieces):
        return [exchange_flat(pieces[0], capacity)]
    return [pairwise(piece, "exp", s) if s > 0 else piece for s, piece in enumerate(pieces)]


def doubled(value, axis, step):
    return value + pairwise(value, axis, step)


def sum_over(value, axis, first=1):
    step = first
    while step < lax.axis_size(axis):
        value = doubled(value, axis, step)
        step *= 2
    return value


def widened(act, value, axis, step):
    rows = value.shape[0]
    wide = jnp.pad(value, ((0, WIDE_LINES - rows), (0, 0)))
    return act(wide, axis, step)[:rows]


def shaped(shape, dtype):
    return jax.ShapeDtypeStruct(shape, dtype)


def per_device(
    queries,
    keys,
    values,
    resid,
    block_order,
    norm_gain,
    w_gate,
    w_down,
    routes,
    route_weight,
    d_out,
):
    query_rows = queries[0]
    resid_rows = resid[0]
    grad_rows = d_out[0]
    tokens = query_rows.shape[0]
    chosen = routes.reshape(1, tokens)
    gain = norm_gain.reshape(1, D)
    ctx_count = lax.axis_size("ctx")
    exp_count = lax.axis_size("exp")
    experts = EXP_DEV * exp_count
    capacity = 3 * tokens // (2 * experts)
    slots = experts * capacity
    rows = EXP_DEV * capacity
    piece_count = exp_count if rows % 16 == 0 else 1
    piece_shapes = [shaped((slots // piece_count, D), BF16)] * piece_count
    token_shape = shaped((tokens, D), BF16)
    kv_width = 2 * KEY_VALUE_HEADS * HEAD_SIZE
    attn_flops = 4 * tokens * ctx_count * tokens * QUERY_HEADS * HEAD_SIZE
    place_flops = 2 * slots * tokens * D
    expert_flops = 2 * slots * D * FFE * EXP_DEV

    own_keys, own_values = keys[0], values[0]
    all_keys = [own_keys] + [pairwise(own_keys, "ctx", s) for s in range(1, ctx_count)]
    all_values = [own_values] + [pairwise(own_values, "ctx", s) for s in range(1, ctx_count)]

    near = [grad_rows, own_keys, own_values, gain, query_rows, resid_rows]
    grad_rows, own_keys, own_values, gain, query_rows, resid_rows, slot, pos, weight, *send_grad = run(
        functools.partial(dispatch_kernel, ctx_count, experts, capacity),
        "dispatch_grads",
        placed(HBM, near + [route_weight, chosen, block_order]),
        placed(
            VMEM,
            [shaped(x.shape, x.dtype) for x in near]
            + [
                shaped((1, tokens), jnp.int32),
                shaped((ctx_count, tokens), jnp.int32),
                shaped((1, tokens), F32),
            ]
            + piece_shapes,
        ),
        place_flops,
        scratch=[
            pltpu.SMEM(block_order.shape, jnp.int32),
            pltpu.VMEM((1, tokens), jnp.int32),
            pltpu.SemaphoreType.DMA((9,)),
        ],
    )
    all_keys[0], all_values[0] = own_keys, own_values
    arrived_grad = exchange(send_grad, capacity)

    hidden, *send_x = run(
        functools.partial(attention_kernel, ctx_count),
        "attention_forward",
        placed(VMEM, [pos, slot, gain, query_rows, resid_rows] + all_keys + all_values),
        placed(VMEM, [token_shape] + piece_shapes),
        attn_flops + place_flops,
    )
    arrived_x = exchange(send_x, capacity)

    d_act, probs, down_near, gate_near, place, weight_wide = run(
        functools.partial(probs_kernel, ctx_count, capacity, piece_count),
        "act_grads_and_probs",
        placed(VMEM, [pos, slot, weight])
        + placed(HBM, [w_down, w_gate])
        + placed(VMEM, [query_rows] + all_keys + arrived_grad),
        placed(
            VMEM,
            [
                shaped((slots, FFE), F32),
                shaped((QUERY_HEADS // 2, ctx_count * tokens, 2 * tokens), F32),
                shaped((EXP_DEV * FFE, D), BF16),
                shaped((D, EXP_DEV * FFE), BF16),
                shaped((tokens, slots), BF16),
                shaped((tokens, COLS), F32),
            ],
        ),
        expert_flops + attn_flops // 2,
        scratch=[pltpu.SemaphoreType.DMA((2 * EXP_DEV,))],
    )

    return_shapes = []
    for s in range(piece_count):
        if joined(s, piece_count):
            return_shapes.append(shaped((2 * rows, D), BF16))
        else:
            return_shapes.extend([piece_shapes[0]] * 2)
    sent = run(
        functools.partial(expert_kernel, capacity, piece_count),
        "experts",
        placed(VMEM, [gate_near, down_near, d_act] + arrived_x),
        placed(VMEM, return_shapes),
        3 * expert_flops,
    )
    send_dn, send_y = split_parts(sent, piece_count)
    dn = exchange(send_dn, capacity)
    far = [s for s in range(1, piece_count) if not joined(s, piece_count)]
    y = list(dn) if piece_count > 1 else [exchange_flat(send_y[0], capacity)]
    y[0] = send_y[0] if piece_count > 1 else y[0]
    (terms,) = run(
        functools.partial(gain_kernel, piece_count, rows),
        "gain_terms",
        placed(VMEM, [gain] + arrived_x + send_dn),
        placed(VMEM, [shaped((GAIN_LINES, LANES), F32)]),
        2 * slots * D,
    )
    terms = sum_over(terms, "dp")
    send_far, terms = lax.optimization_barrier(([send_y[s] for s in far], terms))
    for s, piece in zip(far, send_far):
        y[s] = pairwise(piece, "exp", s)
    terms = sum_over(terms, "ctx")
    beside = pairwise(terms, "exp", FIRST)

    half_shape = shaped((tokens, D // 2), BF16)
    own_shape = shaped((tokens, 2 * HEAD_SIZE), F32)
    d_hidden, dq_first, rest, own_first, *shared_first = run(
        functools.partial(first_back_kernel, ctx_count, piece_count, rows),
        "residual_and_first_group",
        placed(VMEM, [place, gain, hidden, grad_rows, query_rows, probs])
        + placed(VMEM, all_keys + all_values + dn),
        placed(HBM, [token_shape])
        + placed(
            VMEM,
            [half_shape, half_shape, own_shape]
            + [shaped((tokens, 2 * HEAD_SIZE), BF16)] * (ctx_count - 1),
        ),
        A_COST,
        scratch=[
            pltpu.VMEM((tokens, D), BF16),
            pltpu.VMEM((tokens, D), F32),
            pltpu.SemaphoreType.DMA(()),
        ],
    )
    terms, rest = lax.optimization_barrier((terms, rest))
    terms = terms + beside
    terms = widened(doubled, terms, "exp", 3 - FIRST)
    dq_second, own_second, *shared = run(
        functools.partial(second_back_kernel, ctx_count),
        "second_group",
        placed(VMEM, [query_rows, probs, rest] + all_keys + all_values + shared_first),
        placed(VMEM, [half_shape, own_shape])
        + placed(VMEM, [shaped((tokens, kv_width), BF16)] * (ctx_count - 1)),
        B_COST,
    )
    terms = sum_over(terms, "exp", first=4)
    arrived_far, shared = lax.optimization_barrier(([y[s] for s in far], shared))
    for s, piece in zip(far, arrived_far):
        y[s] = piece
    kv_arrived = [pairwise(part, "ctx", s) for s, part in enumerate(shared, 1)]

    kv_shape = shaped((tokens, kv_width // 2), BF16)
    final_shapes = [token_shape, token_shape, kv_shape, kv_shape]
    final_shapes += [shaped((1, tokens), F32), shaped((GAIN_LINES, LANES), F32)]
    total_tokens = tokens * ctx_count * exp_count * lax.axis_size("dp")
    layer_out, d_queries, d_keys, d_values, d_weight, d_gain = run(
        functools.partial(output_kernel, ctx_count, piece_count, rows, total_tokens),
        "layer_output",
        placed(
            VMEM,
            [place, weight_wide, terms, hidden, grad_rows, own_first, own_second]
            + [dq_first, dq_second]
            + kv_arrived
            + y,
        ),
        placed(HBM, final_shapes),
        place_flops,
        scratch=[pltpu.VMEM(x.shape, x.dtype) for x in final_shapes[:1] + final_shapes[2:]]
        + [pltpu.SemaphoreType.DMA((4 + KEY_VALUE_HEADS + D // COLS,))],
    )
    return (
        layer_out[None],
        d_hidden[None],
        d_queries[None],
        d_keys[None],
        d_values[None],
        d_weight,
        d_gain.reshape(D),
    )


def solution(mesh):
    in_specs = (
        P(("exp", "dp"), "ctx", None),
        P(("exp", "dp"), "ctx", None),
        P(("exp", "dp"), "ctx", None),
        P(("exp", "dp"), "ctx", None),
        P(),
        P(),
        P("exp", None, None),
        P("exp", None, None),
        P(("exp", "dp"), "ctx", None),
        P(("exp", "dp"), "ctx"),
        P(("exp", "dp"), "ctx", None),
    )
    out_specs = (
        P(("exp", "dp"), "ctx", None),
        P(("exp", "dp"), "ctx", None),
        P(("exp", "dp"), "ctx", None),
        P(("exp", "dp"), "ctx", None),
        P(("exp", "dp"), "ctx", None),
        P(("exp", "dp"), "ctx"),
        P(),
    )
    return jax.shard_map(
        per_device, mesh=mesh, in_specs=in_specs, out_specs=out_specs, check_vma=False
    )
```

```python
import functools

import jax
import jax.numpy as jnp
from jax import lax
from jax.experimental import pallas as pl
from jax.experimental.pallas import tpu as pltpu
from jax.sharding import PartitionSpec as P

D = 2048
HEAD_SIZE = 128
QUERY_HEADS = 16
KEY_VALUE_HEADS = 2
GROUP = QUERY_HEADS // KEY_VALUE_HEADS
FFE = 384
EXP_DEV = 2
COLS = 256
LANES = 128
GAIN_LINES = D // LANES
WIDE_LINES = 32
FIRST = 1
A_COST = 4000000000
B_COST = 0
SCALE = HEAD_SIZE ** (-0.5)
EXP2_SCALE = SCALE * 1.4426950408889634
F32 = jnp.float32
BF16 = jnp.bfloat16
NN = (((1,), (0,)), ((), ()))
NT = (((1,), (1,)), ((), ()))
MIB = 1 << 20
VMEM, HBM = pltpu.VMEM, pltpu.HBM


def mm(a, b, dims=NN):
    return lax.dot_general(a, b, dims, preferred_element_type=F32)


def iota(shape, dim):
    return lax.broadcasted_iota(jnp.int32, shape, dim)


def row_to_col(row):
    n = row.shape[1]
    eye = iota((n, n), 0) == iota((n, n), 1)
    return jnp.sum(jnp.where(eye, row.astype(F32), 0.0), axis=1, keepdims=True)


def col_to_row(col):
    n = col.shape[0]
    eye = iota((n, n), 0) == iota((n, n), 1)
    return jnp.sum(jnp.where(eye, col, 0.0), axis=0, keepdims=True)


def block_positions(order_ref, ctx_index, tokens):
    span = tokens // 8
    index = iota((1, tokens), 1)
    which = index // span
    start = jnp.zeros((1, tokens), jnp.int32)
    for b in range(8):
        start = jnp.where(which == b, order_ref[ctx_index * 8 + b], start)
    return start * span + index % span


def stacked(refs, cols=slice(None)):
    parts = [r[:, cols] for r in refs]
    return parts[0] if len(parts) == 1 else jnp.concatenate(parts, axis=0)


def column_blocks(width=D, step=COLS):
    return [slice(c, c + step) for c in range(0, width, step)]


def store_pieces(refs, cols, rows_value):
    at = 0
    for r in refs:
        n = r.shape[0]
        r[:, cols] = rows_value[at : at + n]
        at += n


def pair_cols(pair):
    start = 2 * pair * HEAD_SIZE
    return slice(start, start + HEAD_SIZE), slice(start + HEAD_SIZE, start + 2 * HEAD_SIZE)


def head_pair(ref, pair):
    first, second = pair_cols(pair)
    return jnp.concatenate([ref[:, first], ref[:, second]], axis=0)


def placement_rows(slot_row, slots):
    tokens = slot_row.shape[1]
    return jnp.where(iota((slots, tokens), 0) == slot_row, 1.0, 0.0).astype(BF16)


def placement_cols(slot_row, slots):
    tokens = slot_row.shape[1]
    slot_col = row_to_col(slot_row)
    return jnp.where(iota((tokens, slots), 1).astype(F32) == slot_col, 1.0, 0.0).astype(BF16)


def dispatch_kernel(count, experts, capacity, *refs):
    sources, refs = refs[:9], refs[9:]
    targets, refs = refs[:6], refs[6:]
    grad_ref = targets[0]
    slot_ref, pos_ref, weight_ref = refs[:3]
    send_refs = refs[3:-3]
    order_ref, routes_ref, sems = refs[-3:]
    targets = targets + (weight_ref, routes_ref, order_ref)
    copies = [
        pltpu.make_async_copy(source, target, sems.at[i])
        for i, (source, target) in enumerate(zip(sources, targets))
    ]
    for copy in copies[6:] + copies[:6]:
        copy.start()
    for copy in copies[6:]:
        copy.wait()
    tokens = routes_ref.shape[1]
    chosen = routes_ref[...]
    lanes = max(experts, 16)
    hits = jnp.where(iota((lanes, tokens), 0) == chosen, 1.0, 0.0)
    before = jnp.where(iota((tokens, tokens), 0) < iota((tokens, tokens), 1), 1.0, 0.0)
    earlier = mm(hits.astype(BF16), before.astype(BF16))
    rank = jnp.sum(hits * earlier, axis=0, keepdims=True).astype(jnp.int32)
    target = (chosen // EXP_DEV) ^ lax.axis_index("exp")
    slot = (target * EXP_DEV + chosen % EXP_DEV) * capacity + rank
    slot_ref[...] = slot
    me = lax.axis_index("ctx")
    for s in range(count):
        pos_ref[s : s + 1, :] = block_positions(order_ref, me ^ s, tokens)
    place = placement_rows(slot, experts * capacity)
    weight = row_to_col(weight_ref[...])
    copies[0].wait()
    for cols in column_blocks():
        scaled = (weight * grad_ref[:, cols].astype(F32)).astype(BF16)
        store_pieces(send_refs, cols, mm(place, scaled).astype(BF16))
    for copy in copies[1:6]:
        copy.wait()


def kv_stacks(key_refs, value_refs, g):
    cols = slice(g * HEAD_SIZE, (g + 1) * HEAD_SIZE)
    return stacked(key_refs, cols), stacked(value_refs, cols)


def attention_kernel(
    count, pos_ref, slot_ref, gain_ref, query_ref, resid_ref, *refs
):
    key_refs, value_refs = refs[:count], refs[count : 2 * count]
    hidden_ref, send_refs = refs[2 * count], refs[2 * count + 1 :]
    tokens = query_ref.shape[0]
    query_pos = row_to_col(pos_ref[:1, :])
    bias = jnp.concatenate(
        [
            jnp.where(pos_ref[s : s + 1, :].astype(F32) <= query_pos, 0.0, -1e30)
            for s in range(count)
        ],
        axis=1,
    )
    length = count * tokens
    ones = jnp.ones((length, HEAD_SIZE), BF16)
    total = jnp.zeros((tokens, HEAD_SIZE), F32)
    for g in range(KEY_VALUE_HEADS):
        keys, values = kv_stacks(key_refs, value_refs, g)
        values = jnp.concatenate([values, ones], axis=1)
        for h in range(g * GROUP, (g + 1) * GROUP):
            cols = slice(h * HEAD_SIZE, (h + 1) * HEAD_SIZE)
            scores = mm(query_ref[:, cols], keys, NT) + bias
            peak = jnp.max(scores, axis=1, keepdims=True)
            weights = jnp.exp2((scores - peak) * EXP2_SCALE).astype(BF16)
            mixed = mm(weights, values)
            attended = mixed[:, :HEAD_SIZE] / mixed[:, HEAD_SIZE:]
            hidden = (resid_ref[:, cols].astype(F32) + attended).astype(BF16)
            hidden_ref[:, cols] = hidden
            wide = hidden.astype(F32)
            total = total + wide * wide
    inv_rms = lax.rsqrt(jnp.sum(total, axis=1, keepdims=True) * (1.0 / D) + 1e-06)
    slots = sum(r.shape[0] for r in send_refs)
    place = placement_rows(slot_ref[...], slots)
    for cols in column_blocks():
        normed = (hidden_ref[:, cols].astype(F32) * inv_rms * gain_ref[:, cols]).astype(BF16)
        store_pieces(send_refs, cols, mm(place, normed).astype(BF16))


def first_expert_rows(slots, capacity):
    return iota((slots, 1), 0) % (EXP_DEV * capacity) < capacity


def probs_kernel(
    count,
    capacity,
    pieces,
    pos_ref,
    slot_ref,
    weight_ref,
    down_hbm,
    gate_hbm,
    query_ref,
    *refs,
):
    key_refs = refs[:count]
    grad_refs = refs[count : count + pieces]
    d_act_ref, probs_ref, down_ref, gate_ref, place_ref, wide_ref, sems = refs[count + pieces :]
    spans = [slice(e * FFE, (e + 1) * FFE) for e in range(EXP_DEV)]
    down_copies = [
        pltpu.make_async_copy(down_hbm.at[e], down_ref.at[span, :], sems.at[e])
        for e, span in enumerate(spans)
    ]
    gate_copies = [
        pltpu.make_async_copy(gate_hbm.at[e], gate_ref.at[:, span], sems.at[EXP_DEV + e])
        for e, span in enumerate(spans)
    ]
    for copy in down_copies + gate_copies:
        copy.start()
    place_ref[...] = placement_cols(slot_ref[...], place_ref.shape[1])
    wide_ref[...] = jnp.broadcast_to(row_to_col(weight_ref[...]), wide_ref.shape)
    query_pos = pos_ref[:1, :].astype(F32)
    bias = jnp.concatenate(
        [
            jnp.where(row_to_col(pos_ref[s : s + 1, :]) <= query_pos, 0.0, -1e30)
            for s in range(count)
        ],
        axis=0,
    )
    bias = jnp.concatenate([bias, bias], axis=1)
    for g in range(KEY_VALUE_HEADS):
        keys = stacked(key_refs, slice(g * HEAD_SIZE, (g + 1) * HEAD_SIZE))
        for pair in range(g * GROUP // 2, (g + 1) * GROUP // 2):
            scores = mm(keys, head_pair(query_ref, pair), NT) + bias
            peak = jnp.max(scores, axis=0, keepdims=True)
            weights = jnp.exp2((scores - peak) * EXP2_SCALE)
            probs_ref[pair] = weights * (1.0 / jnp.sum(weights, axis=0, keepdims=True))
    grads = stacked(grad_refs)
    first = first_expert_rows(grads.shape[0], capacity)
    for copy in down_copies:
        copy.wait()
    d_act = mm(grads, down_ref[...], NT)
    d_act_ref[...] = jnp.where(first, d_act[:, :FFE], d_act[:, FFE:])
    for copy in gate_copies:
        copy.wait()


def part_views(refs, rows, part):
    return [r if r.shape[0] != 2 * rows else r.at[part * rows : (part + 1) * rows] for r in refs]


def joined(step, pieces):
    return pieces > 1 and step > 0 and step & (step - 1) == 0


def split_parts(refs, pieces):
    back, out = [], []
    at = 0
    for s in range(pieces):
        back.append(refs[at])
        at += not joined(s, pieces)
        out.append(refs[at])
        at += 1
    return back, out


def expert_kernel(capacity, pieces, gate_ref, down_ref, d_act_ref, *refs):
    rows = stacked(refs[:pieces])
    back_refs, out_refs = split_parts(refs[pieces:], pieces)
    back_refs = part_views(back_refs, EXP_DEV * capacity, 0)
    out_refs = part_views(out_refs, EXP_DEV * capacity, 1)
    first = first_expert_rows(rows.shape[0], capacity)
    both = mm(rows, gate_ref[...])
    pre = jnp.where(first, both[:, :FFE], both[:, FFE:])
    gate = 1.0 / (1.0 + jnp.exp(-pre))
    act = pre * gate
    d_pre = d_act_ref[...] * gate * (1.0 + pre * (1.0 - gate))
    act, d_pre = [
        jnp.concatenate([jnp.where(first, x, 0.0), jnp.where(first, 0.0, x)], axis=1).astype(BF16)
        for x in (act, d_pre)
    ]
    for cols in column_blocks():
        store_pieces(back_refs, cols, mm(d_pre, gate_ref[cols, :], NT).astype(BF16))
        store_pieces(out_refs, cols, mm(act, down_ref[:, cols]).astype(BF16))


def gain_kernel(pieces, rows, gain_ref, *refs):
    row_refs = refs[:pieces]
    back_refs = part_views(refs[pieces:-1], rows, 0)
    terms_ref = refs[-1]
    for cols in column_blocks():
        products = stacked(row_refs, cols).astype(F32) * stacked(back_refs, cols).astype(F32)
        terms = jnp.sum(products, axis=0, keepdims=True) / gain_ref[:, cols]
        for at in range(0, COLS, LANES):
            line = (cols.start + at) // LANES
            terms_ref[line : line + 1, :] = terms[:, at : at + LANES]


def group_back(g, key_refs, value_refs, query_ref, probs_ref, d_resid, dq_ref, own_ref, shared):
    length = len(key_refs) * own_ref.shape[0]
    tokens = own_ref.shape[0]
    keys, values = kv_stacks(key_refs, value_refs, g)
    keys_t = jnp.transpose(keys.astype(F32)).astype(BF16)
    d_keys = jnp.zeros((length, HEAD_SIZE), F32)
    d_values = jnp.zeros((length, HEAD_SIZE), F32)
    for local in range(GROUP // 2):
        pair = g * GROUP // 2 + local
        cols_a, cols_b = pair_cols(local)
        d_out = head_pair(d_resid, local)
        probs = probs_ref[pair]
        d_probs = mm(values, d_out, NT)
        row_dot = jnp.sum(probs * d_probs, axis=0, keepdims=True)
        d_scores = (probs * (d_probs - row_dot)).astype(BF16)
        d_keys = d_keys + mm(d_scores, head_pair(query_ref, pair))
        d_values = d_values + mm(probs.astype(BF16), d_out)
        d_query_t = mm(keys_t, d_scores) * SCALE
        dq_ref[:, cols_a] = jnp.transpose(d_query_t[:, :tokens]).astype(BF16)
        dq_ref[:, cols_b] = jnp.transpose(d_query_t[:, tokens:]).astype(BF16)
    d_keys = d_keys * SCALE
    own_ref[:, :HEAD_SIZE] = d_keys[:tokens]
    own_ref[:, HEAD_SIZE:] = d_values[:tokens]
    start = 2 * g * HEAD_SIZE
    for s, ref in enumerate(shared, 1):
        span = slice(s * tokens, (s + 1) * tokens)
        ref[:, start : start + HEAD_SIZE] = d_keys[span].astype(BF16)
        ref[:, start + HEAD_SIZE : start + 2 * HEAD_SIZE] = d_values[span].astype(BF16)


def first_back_kernel(
    count, pieces, rows, place_ref, gain_ref, hidden_ref, grad_ref, query_ref, probs_ref, *refs
):
    key_refs, value_refs = refs[:count], refs[count : 2 * count]
    refs = refs[2 * count :]
    dn_refs = part_views(refs[:pieces], rows, 0)
    resid_hbm, dq_ref, rest_ref, own_ref = refs[pieces : pieces + 4]
    shared = refs[pieces + 4 : -3]
    resid_ref, dn_scratch, sem = refs[-3:]
    tokens = hidden_ref.shape[0]
    place = place_ref[...]
    square = jnp.zeros((tokens, COLS), F32)
    mixing = jnp.zeros((tokens, COLS), F32)
    for cols in column_blocks():
        dn = mm(place, stacked(dn_refs, cols)) * gain_ref[:, cols]
        dn_scratch[:, cols] = dn
        hidden = hidden_ref[:, cols].astype(F32)
        square = square + hidden * hidden
        mixing = mixing + dn * hidden
    inv_rms = lax.rsqrt(jnp.sum(square, axis=1, keepdims=True) * (1.0 / D) + 1e-06)
    mean_mix = jnp.sum(mixing, axis=1, keepdims=True) * (1.0 / D)
    factor = inv_rms * inv_rms * inv_rms * mean_mix
    half = GROUP * HEAD_SIZE
    for cols in column_blocks():
        part = (
            grad_ref[:, cols].astype(F32)
            + dn_scratch[:, cols] * inv_rms
            - hidden_ref[:, cols].astype(F32) * factor
        ).astype(BF16)
        resid_ref[:, cols] = part
        if cols.start >= half:
            rest_ref[:, cols.start - half : cols.stop - half] = part
    resid_copy = pltpu.make_async_copy(resid_ref, resid_hbm, sem)
    resid_copy.start()
    group_back(0, key_refs, value_refs, query_ref, probs_ref, resid_ref, dq_ref, own_ref, shared)
    resid_copy.wait()


def second_back_kernel(count, query_ref, probs_ref, rest_ref, *refs):
    key_refs, value_refs = refs[:count], refs[count : 2 * count]
    first_shared = refs[2 * count : 3 * count - 1]
    dq_ref, own_ref = refs[3 * count - 1 : 3 * count + 1]
    shared = refs[3 * count + 1 :]
    for source, target in zip(first_shared, shared):
        target[:, : 2 * HEAD_SIZE] = source[...]
    group_back(1, key_refs, value_refs, query_ref, probs_ref, rest_ref, dq_ref, own_ref, shared)


def output_kernel(
    count, pieces, rows, tokens_in_all, place_ref, weight_ref, gain_ref, hidden_ref, grad_ref, *refs
):
    own_refs, refs = refs[:KEY_VALUE_HEADS], refs[KEY_VALUE_HEADS:]
    dq_refs, refs = refs[:KEY_VALUE_HEADS], refs[KEY_VALUE_HEADS:]
    arrived_refs = refs[: count - 1]
    y_refs = part_views(refs[count - 1 : count - 1 + pieces], rows, 1)
    out_hbm, dq_hbm, dk_hbm, dv_hbm, d_weight_hbm, d_gain_hbm = refs[count - 1 + pieces : -6]
    out_ref, dk_ref, dv_ref, d_weight_ref, d_gain_ref, sems = refs[-6:]
    copies = []

    def send(source, target):
        copy = pltpu.make_async_copy(source, target, sems.at[len(copies)])
        copy.start()
        copies.append(copy)

    width = GROUP * HEAD_SIZE
    for g, dq_ref in enumerate(dq_refs):
        send(dq_ref, dq_hbm.at[:, g * width : (g + 1) * width])
    for g, own_ref in enumerate(own_refs):
        d_kv = own_ref[...]
        for ref in arrived_refs:
            d_kv = d_kv + ref[:, 2 * g * HEAD_SIZE : 2 * (g + 1) * HEAD_SIZE].astype(F32)
        cols = slice(g * HEAD_SIZE, (g + 1) * HEAD_SIZE)
        dk_ref[:, cols] = d_kv[:, :HEAD_SIZE].astype(BF16)
        dv_ref[:, cols] = d_kv[:, HEAD_SIZE:].astype(BF16)
    d_gain_ref[...] = gain_ref[...] * (1.0 / tokens_in_all)
    send(dk_ref, dk_hbm)
    send(dv_ref, dv_hbm)
    send(d_gain_ref, d_gain_hbm)
    tokens = hidden_ref.shape[0]
    place = place_ref[...]
    weight = weight_ref[...]
    total = jnp.zeros((tokens, COLS), F32)
    for cols in column_blocks():
        y = mm(place, stacked(y_refs, cols))
        out_ref[:, cols] = (hidden_ref[:, cols].astype(F32) + weight * y).astype(BF16)
        send(out_ref.at[:, cols], out_hbm.at[:, cols])
        total = total + y * grad_ref[:, cols].astype(F32)
    d_weight_ref[...] = col_to_row(jnp.sum(total, axis=1, keepdims=True))
    send(d_weight_ref, d_weight_hbm)
    for copy in copies:
        copy.wait()


def run(kernel, name, inputs, outputs, flops, scratch=(), limit=20 * MIB):
    nbytes = sum(x.size * x.dtype.itemsize for _, x in inputs + outputs) if flops else 0
    spec = {space: pl.BlockSpec(memory_space=space) for space in (VMEM, HBM)}
    results = pl.pallas_call(
        kernel,
        out_shape=[x for _, x in outputs],
        in_specs=[spec[space] for space, _ in inputs],
        out_specs=[spec[space] for space, _ in outputs],
        scratch_shapes=list(scratch),
        compiler_params=pltpu.CompilerParams(vmem_limit_bytes=limit),
        cost_estimate=pl.CostEstimate(flops=flops, bytes_accessed=nbytes, transcendentals=0),
        name=name,
    )(*[pltpu.with_memory_space_constraint(x, HBM) if space is HBM else x for space, x in inputs])
    return list(results)


def placed(space, arrays):
    return [(space, x) for x in arrays]


def pairwise(value, axis, step):
    count = lax.axis_size(axis)
    return lax.ppermute(value, axis, [(i, i ^ step) for i in range(count)])


def exchange_flat(flat, capacity):
    count = lax.axis_size("exp")
    rows = EXP_DEV * capacity
    blocks = [flat[s * rows : (s + 1) * rows] for s in range(count)]
    moved = [blocks[0]] + [pairwise(blocks[s], "exp", s) for s in range(1, count)]
    return jnp.concatenate(moved, axis=0)


def exchange(pieces, capacity):
    if lax.axis_size("exp") != len(pieces):
        return [exchange_flat(pieces[0], capacity)]
    return [pairwise(piece, "exp", s) if s > 0 else piece for s, piece in enumerate(pieces)]


def doubled(value, axis, step):
    return value + pairwise(value, axis, step)


def sum_over(value, axis, first=1):
    step = first
    while step < lax.axis_size(axis):
        value = doubled(value, axis, step)
        step *= 2
    return value


def widened(act, value, axis, step):
    rows = value.shape[0]
    wide = jnp.pad(value, ((0, WIDE_LINES - rows), (0, 0)))
    return act(wide, axis, step)[:rows]


def shaped(shape, dtype):
    return jax.ShapeDtypeStruct(shape, dtype)


def per_device(
    queries,
    keys,
    values,
    resid,
    block_order,
    norm_gain,
    w_gate,
    w_down,
    routes,
    route_weight,
    d_out,
):
    query_rows = queries[0]
    resid_rows = resid[0]
    grad_rows = d_out[0]
    tokens = query_rows.shape[0]
    chosen = routes.reshape(1, tokens)
    gain = norm_gain.reshape(1, D)
    ctx_count = lax.axis_size("ctx")
    exp_count = lax.axis_size("exp")
    experts = EXP_DEV * exp_count
    capacity = 3 * tokens // (2 * experts)
    slots = experts * capacity
    rows = EXP_DEV * capacity
    piece_count = exp_count if rows % 16 == 0 else 1
    piece_shapes = [shaped((slots // piece_count, D), BF16)] * piece_count
    token_shape = shaped((tokens, D), BF16)
    kv_width = 2 * KEY_VALUE_HEADS * HEAD_SIZE
    attn_flops = 4 * tokens * ctx_count * tokens * QUERY_HEADS * HEAD_SIZE
    place_flops = 2 * slots * tokens * D
    expert_flops = 2 * slots * D * FFE * EXP_DEV

    own_keys, own_values = keys[0], values[0]
    all_keys = [own_keys] + [pairwise(own_keys, "ctx", s) for s in range(1, ctx_count)]
    all_values = [own_values] + [pairwise(own_values, "ctx", s) for s in range(1, ctx_count)]

    near = [grad_rows, own_keys, own_values, gain, query_rows, resid_rows]
    grad_rows, own_keys, own_values, gain, query_rows, resid_rows, slot, pos, weight, *send_grad = run(
        functools.partial(dispatch_kernel, ctx_count, experts, capacity),
        "dispatch_grads",
        placed(HBM, near + [route_weight, chosen, block_order]),
        placed(
            VMEM,
            [shaped(x.shape, x.dtype) for x in near]
            + [
                shaped((1, tokens), jnp.int32),
                shaped((ctx_count, tokens), jnp.int32),
                shaped((1, tokens), F32),
            ]
            + piece_shapes,
        ),
        place_flops,
        scratch=[
            pltpu.SMEM(block_order.shape, jnp.int32),
            pltpu.VMEM((1, tokens), jnp.int32),
            pltpu.SemaphoreType.DMA((9,)),
        ],
    )
    all_keys[0], all_values[0] = own_keys, own_values
    arrived_grad = exchange(send_grad, capacity)

    hidden, *send_x = run(
        functools.partial(attention_kernel, ctx_count),
        "attention_forward",
        placed(VMEM, [pos, slot, gain, query_rows, resid_rows] + all_keys + all_values),
        placed(VMEM, [token_shape] + piece_shapes),
        attn_flops + place_flops,
    )
    arrived_x = exchange(send_x, capacity)

    d_act, probs, down_near, gate_near, place, weight_wide = run(
        functools.partial(probs_kernel, ctx_count, capacity, piece_count),
        "act_grads_and_probs",
        placed(VMEM, [pos, slot, weight])
        + placed(HBM, [w_down, w_gate])
        + placed(VMEM, [query_rows] + all_keys + arrived_grad),
        placed(
            VMEM,
            [
                shaped((slots, FFE), F32),
                shaped((QUERY_HEADS // 2, ctx_count * tokens, 2 * tokens), F32),
                shaped((EXP_DEV * FFE, D), BF16),
                shaped((D, EXP_DEV * FFE), BF16),
                shaped((tokens, slots), BF16),
                shaped((tokens, COLS), F32),
            ],
        ),
        expert_flops + attn_flops // 2,
        scratch=[pltpu.SemaphoreType.DMA((2 * EXP_DEV,))],
    )

    return_shapes = []
    for s in range(piece_count):
        if joined(s, piece_count):
            return_shapes.append(shaped((2 * rows, D), BF16))
        else:
            return_shapes.extend([piece_shapes[0]] * 2)
    sent = run(
        functools.partial(expert_kernel, capacity, piece_count),
        "experts",
        placed(VMEM, [gate_near, down_near, d_act] + arrived_x),
        placed(VMEM, return_shapes),
        3 * expert_flops,
    )
    send_dn, send_y = split_parts(sent, piece_count)
    dn = exchange(send_dn, capacity)
    far = [s for s in range(1, piece_count) if not joined(s, piece_count)]
    y = list(dn) if piece_count > 1 else [exchange_flat(send_y[0], capacity)]
    y[0] = send_y[0] if piece_count > 1 else y[0]
    (terms,) = run(
        functools.partial(gain_kernel, piece_count, rows),
        "gain_terms",
        placed(VMEM, [gain] + arrived_x + send_dn),
        placed(VMEM, [shaped((GAIN_LINES, LANES), F32)]),
        2 * slots * D,
    )
    terms = sum_over(sum_over(terms, "dp"), "ctx")
    send_far, terms = lax.optimization_barrier(([send_y[s] for s in far], terms))
    for s, piece in zip(far, send_far):
        y[s] = pairwise(piece, "exp", s)
    beside = pairwise(terms, "exp", FIRST)

    half_shape = shaped((tokens, D // 2), BF16)
    own_shape = shaped((tokens, 2 * HEAD_SIZE), F32)
    d_hidden, dq_first, rest, own_first, *shared_first = run(
        functools.partial(first_back_kernel, ctx_count, piece_count, rows),
        "residual_and_first_group",
        placed(VMEM, [place, gain, hidden, grad_rows, query_rows, probs])
        + placed(VMEM, all_keys + all_values + dn),
        placed(HBM, [token_shape])
        + placed(
            VMEM,
            [half_shape, half_shape, own_shape]
            + [shaped((tokens, 2 * HEAD_SIZE), BF16)] * (ctx_count - 1),
        ),
        A_COST,
        scratch=[
            pltpu.VMEM((tokens, D), BF16),
            pltpu.VMEM((tokens, D), F32),
            pltpu.SemaphoreType.DMA(()),
        ],
    )
    terms, rest = lax.optimization_barrier((terms, rest))
    terms = terms + beside
    terms = widened(doubled, terms, "exp", 3 - FIRST)
    dq_second, own_second, *shared = run(
        functools.partial(second_back_kernel, ctx_count),
        "second_group",
        placed(VMEM, [query_rows, probs, rest] + all_keys + all_values + shared_first),
        placed(VMEM, [half_shape, own_shape])
        + placed(VMEM, [shaped((tokens, kv_width), BF16)] * (ctx_count - 1)),
        B_COST,
    )
    terms = sum_over(terms, "exp", first=4)
    arrived_far, shared = lax.optimization_barrier(([y[s] for s in far], shared))
    for s, piece in zip(far, arrived_far):
        y[s] = piece
    kv_arrived = [pairwise(part, "ctx", s) for s, part in enumerate(shared, 1)]

    kv_shape = shaped((tokens, kv_width // 2), BF16)
    final_shapes = [token_shape, token_shape, kv_shape, kv_shape]
    final_shapes += [shaped((1, tokens), F32), shaped((GAIN_LINES, LANES), F32)]
    total_tokens = tokens * ctx_count * exp_count * lax.axis_size("dp")
    layer_out, d_queries, d_keys, d_values, d_weight, d_gain = run(
        functools.partial(output_kernel, ctx_count, piece_count, rows, total_tokens),
        "layer_output",
        placed(
            VMEM,
            [place, weight_wide, terms, hidden, grad_rows, own_first, own_second]
            + [dq_first, dq_second]
            + kv_arrived
            + y,
        ),
        placed(HBM, final_shapes),
        place_flops,
        scratch=[pltpu.VMEM(x.shape, x.dtype) for x in final_shapes[:1] + final_shapes[2:]]
        + [pltpu.SemaphoreType.DMA((4 + KEY_VALUE_HEADS + D // COLS,))],
    )
    return (
        layer_out[None],
        d_hidden[None],
        d_queries[None],
        d_keys[None],
        d_values[None],
        d_weight,
        d_gain.reshape(D),
    )


def solution(mesh):
    in_specs = (
        P(("exp", "dp"), "ctx", None),
        P(("exp", "dp"), "ctx", None),
        P(("exp", "dp"), "ctx", None),
        P(("exp", "dp"), "ctx", None),
        P(),
        P(),
        P("exp", None, None),
        P("exp", None, None),
        P(("exp", "dp"), "ctx", None),
        P(("exp", "dp"), "ctx"),
        P(("exp", "dp"), "ctx", None),
    )
    out_specs = (
        P(("exp", "dp"), "ctx", None),
        P(("exp", "dp"), "ctx", None),
        P(("exp", "dp"), "ctx", None),
        P(("exp", "dp"), "ctx", None),
        P(("exp", "dp"), "ctx", None),
        P(("exp", "dp"), "ctx"),
        P(),
    )
    return jax.shard_map(
        per_device, mesh=mesh, in_specs=in_specs, out_specs=out_specs, check_vma=False
    )
```

```python
import functools

import jax
import jax.numpy as jnp
from jax import lax
from jax.experimental import pallas as pl
from jax.experimental.pallas import tpu as pltpu
from jax.sharding import PartitionSpec as P

D = 2048
HEAD_SIZE = 128
QUERY_HEADS = 16
KEY_VALUE_HEADS = 2
GROUP = QUERY_HEADS // KEY_VALUE_HEADS
FFE = 384
EXP_DEV = 2
COLS = 256
LANES = 128
GAIN_LINES = D // LANES
WIDE_LINES = 32
FIRST = 1
A_COST = 4000000000
B_COST = 0
SCALE = HEAD_SIZE ** (-0.5)
EXP2_SCALE = SCALE * 1.4426950408889634
F32 = jnp.float32
BF16 = jnp.bfloat16
NN = (((1,), (0,)), ((), ()))
NT = (((1,), (1,)), ((), ()))
MIB = 1 << 20
VMEM, HBM = pltpu.VMEM, pltpu.HBM


def mm(a, b, dims=NN):
    return lax.dot_general(a, b, dims, preferred_element_type=F32)


def iota(shape, dim):
    return lax.broadcasted_iota(jnp.int32, shape, dim)


def row_to_col(row):
    n = row.shape[1]
    eye = iota((n, n), 0) == iota((n, n), 1)
    return jnp.sum(jnp.where(eye, row.astype(F32), 0.0), axis=1, keepdims=True)


def col_to_row(col):
    n = col.shape[0]
    eye = iota((n, n), 0) == iota((n, n), 1)
    return jnp.sum(jnp.where(eye, col, 0.0), axis=0, keepdims=True)


def block_positions(order_ref, ctx_index, tokens):
    span = tokens // 8
    index = iota((1, tokens), 1)
    which = index // span
    start = jnp.zeros((1, tokens), jnp.int32)
    for b in range(8):
        start = jnp.where(which == b, order_ref[ctx_index * 8 + b], start)
    return start * span + index % span


def stacked(refs, cols=slice(None)):
    parts = [r[:, cols] for r in refs]
    return parts[0] if len(parts) == 1 else jnp.concatenate(parts, axis=0)


def column_blocks(width=D, step=COLS):
    return [slice(c, c + step) for c in range(0, width, step)]


def store_pieces(refs, cols, rows_value):
    at = 0
    for r in refs:
        n = r.shape[0]
        r[:, cols] = rows_value[at : at + n]
        at += n


def pair_cols(pair):
    start = 2 * pair * HEAD_SIZE
    return slice(start, start + HEAD_SIZE), slice(start + HEAD_SIZE, start + 2 * HEAD_SIZE)


def head_pair(ref, pair):
    first, second = pair_cols(pair)
    return jnp.concatenate([ref[:, first], ref[:, second]], axis=0)


def placement_rows(slot_row, slots):
    tokens = slot_row.shape[1]
    return jnp.where(iota((slots, tokens), 0) == slot_row, 1.0, 0.0).astype(BF16)


def placement_cols(slot_row, slots):
    tokens = slot_row.shape[1]
    slot_col = row_to_col(slot_row)
    return jnp.where(iota((tokens, slots), 1).astype(F32) == slot_col, 1.0, 0.0).astype(BF16)


def dispatch_kernel(count, experts, capacity, *refs):
    sources, refs = refs[:9], refs[9:]
    targets, refs = refs[:6], refs[6:]
    grad_ref = targets[0]
    slot_ref, pos_ref, weight_ref = refs[:3]
    send_refs = refs[3:-3]
    order_ref, routes_ref, sems = refs[-3:]
    targets = targets + (weight_ref, routes_ref, order_ref)
    copies = [
        pltpu.make_async_copy(source, target, sems.at[i])
        for i, (source, target) in enumerate(zip(sources, targets))
    ]
    for copy in copies[6:] + copies[:6]:
        copy.start()
    for copy in copies[6:]:
        copy.wait()
    tokens = routes_ref.shape[1]
    chosen = routes_ref[...]
    lanes = max(experts, 16)
    hits = jnp.where(iota((lanes, tokens), 0) == chosen, 1.0, 0.0)
    before = jnp.where(iota((tokens, tokens), 0) < iota((tokens, tokens), 1), 1.0, 0.0)
    earlier = mm(hits.astype(BF16), before.astype(BF16))
    rank = jnp.sum(hits * earlier, axis=0, keepdims=True).astype(jnp.int32)
    target = (chosen // EXP_DEV) ^ lax.axis_index("exp")
    slot = (target * EXP_DEV + chosen % EXP_DEV) * capacity + rank
    slot_ref[...] = slot
    me = lax.axis_index("ctx")
    for s in range(count):
        pos_ref[s : s + 1, :] = block_positions(order_ref, me ^ s, tokens)
    place = placement_rows(slot, experts * capacity)
    weight = row_to_col(weight_ref[...])
    copies[0].wait()
    for cols in column_blocks():
        scaled = (weight * grad_ref[:, cols].astype(F32)).astype(BF16)
        store_pieces(send_refs, cols, mm(place, scaled).astype(BF16))
    for copy in copies[1:6]:
        copy.wait()


def kv_stacks(key_refs, value_refs, g):
    cols = slice(g * HEAD_SIZE, (g + 1) * HEAD_SIZE)
    return stacked(key_refs, cols), stacked(value_refs, cols)


def attention_kernel(
    count, pos_ref, slot_ref, gain_ref, query_ref, resid_ref, *refs
):
    key_refs, value_refs = refs[:count], refs[count : 2 * count]
    hidden_ref, send_refs = refs[2 * count], refs[2 * count + 1 :]
    tokens = query_ref.shape[0]
    query_pos = row_to_col(pos_ref[:1, :])
    bias = jnp.concatenate(
        [
            jnp.where(pos_ref[s : s + 1, :].astype(F32) <= query_pos, 0.0, -1e30)
            for s in range(count)
        ],
        axis=1,
    )
    length = count * tokens
    ones = jnp.ones((length, HEAD_SIZE), BF16)
    total = jnp.zeros((tokens, HEAD_SIZE), F32)
    for g in range(KEY_VALUE_HEADS):
        keys, values = kv_stacks(key_refs, value_refs, g)
        values = jnp.concatenate([values, ones], axis=1)
        for h in range(g * GROUP, (g + 1) * GROUP):
            cols = slice(h * HEAD_SIZE, (h + 1) * HEAD_SIZE)
            scores = mm(query_ref[:, cols], keys, NT) + bias
            peak = jnp.max(scores, axis=1, keepdims=True)
            weights = jnp.exp2((scores - peak) * EXP2_SCALE).astype(BF16)
            mixed = mm(weights, values)
            attended = mixed[:, :HEAD_SIZE] / mixed[:, HEAD_SIZE:]
            hidden = (resid_ref[:, cols].astype(F32) + attended).astype(BF16)
            hidden_ref[:, cols] = hidden
            wide = hidden.astype(F32)
            total = total + wide * wide
    inv_rms = lax.rsqrt(jnp.sum(total, axis=1, keepdims=True) * (1.0 / D) + 1e-06)
    slots = sum(r.shape[0] for r in send_refs)
    place = placement_rows(slot_ref[...], slots)
    for cols in column_blocks():
        normed = (hidden_ref[:, cols].astype(F32) * inv_rms * gain_ref[:, cols]).astype(BF16)
        store_pieces(send_refs, cols, mm(place, normed).astype(BF16))


def first_expert_rows(slots, capacity):
    return iota((slots, 1), 0) % (EXP_DEV * capacity) < capacity


def probs_kernel(
    count,
    capacity,
    pieces,
    pos_ref,
    slot_ref,
    weight_ref,
    down_hbm,
    gate_hbm,
    query_ref,
    *refs,
):
    key_refs = refs[:count]
    grad_refs = refs[count : count + pieces]
    d_act_ref, probs_ref, down_ref, gate_ref, place_ref, wide_ref, sems = refs[count + pieces :]
    spans = [slice(e * FFE, (e + 1) * FFE) for e in range(EXP_DEV)]
    down_copies = [
        pltpu.make_async_copy(down_hbm.at[e], down_ref.at[span, :], sems.at[e])
        for e, span in enumerate(spans)
    ]
    gate_copies = [
        pltpu.make_async_copy(gate_hbm.at[e], gate_ref.at[:, span], sems.at[EXP_DEV + e])
        for e, span in enumerate(spans)
    ]
    for copy in down_copies + gate_copies:
        copy.start()
    place_ref[...] = placement_cols(slot_ref[...], place_ref.shape[1])
    wide_ref[...] = jnp.broadcast_to(row_to_col(weight_ref[...]), wide_ref.shape)
    query_pos = pos_ref[:1, :].astype(F32)
    bias = jnp.concatenate(
        [
            jnp.where(row_to_col(pos_ref[s : s + 1, :]) <= query_pos, 0.0, -1e30)
            for s in range(count)
        ],
        axis=0,
    )
    bias = jnp.concatenate([bias, bias], axis=1)
    for g in range(KEY_VALUE_HEADS):
        keys = stacked(key_refs, slice(g * HEAD_SIZE, (g + 1) * HEAD_SIZE))
        for pair in range(g * GROUP // 2, (g + 1) * GROUP // 2):
            scores = mm(keys, head_pair(query_ref, pair), NT) + bias
            peak = jnp.max(scores, axis=0, keepdims=True)
            weights = jnp.exp2((scores - peak) * EXP2_SCALE)
            probs_ref[pair] = weights * (1.0 / jnp.sum(weights, axis=0, keepdims=True))
    grads = stacked(grad_refs)
    first = first_expert_rows(grads.shape[0], capacity)
    for copy in down_copies:
        copy.wait()
    d_act = mm(grads, down_ref[...], NT)
    d_act_ref[...] = jnp.where(first, d_act[:, :FFE], d_act[:, FFE:])
    for copy in gate_copies:
        copy.wait()


def part_views(refs, rows, part):
    return [r if r.shape[0] != 2 * rows else r.at[part * rows : (part + 1) * rows] for r in refs]


def joined(step, pieces):
    return pieces > 1 and step > 0 and step & (step - 1) == 0


def split_parts(refs, pieces):
    back, out = [], []
    at = 0
    for s in range(pieces):
        back.append(refs[at])
        at += not joined(s, pieces)
        out.append(refs[at])
        at += 1
    return back, out


def expert_kernel(capacity, pieces, gate_ref, down_ref, d_act_ref, *refs):
    rows = stacked(refs[:pieces])
    back_refs, out_refs = split_parts(refs[pieces:], pieces)
    back_refs = part_views(back_refs, EXP_DEV * capacity, 0)
    out_refs = part_views(out_refs, EXP_DEV * capacity, 1)
    first = first_expert_rows(rows.shape[0], capacity)
    both = mm(rows, gate_ref[...])
    pre = jnp.where(first, both[:, :FFE], both[:, FFE:])
    gate = 1.0 / (1.0 + jnp.exp(-pre))
    act = pre * gate
    d_pre = d_act_ref[...] * gate * (1.0 + pre * (1.0 - gate))
    act, d_pre = [
        jnp.concatenate([jnp.where(first, x, 0.0), jnp.where(first, 0.0, x)], axis=1).astype(BF16)
        for x in (act, d_pre)
    ]
    for cols in column_blocks():
        store_pieces(back_refs, cols, mm(d_pre, gate_ref[cols, :], NT).astype(BF16))
        store_pieces(out_refs, cols, mm(act, down_ref[:, cols]).astype(BF16))


def gain_kernel(pieces, rows, gain_ref, *refs):
    row_refs = refs[:pieces]
    back_refs = part_views(refs[pieces:-1], rows, 0)
    terms_ref = refs[-1]
    for cols in column_blocks():
        products = stacked(row_refs, cols).astype(F32) * stacked(back_refs, cols).astype(F32)
        terms = jnp.sum(products, axis=0, keepdims=True) / gain_ref[:, cols]
        for at in range(0, COLS, LANES):
            line = (cols.start + at) // LANES
            terms_ref[line : line + 1, :] = terms[:, at : at + LANES]


def group_back(g, key_refs, value_refs, query_ref, probs_ref, d_resid, dq_ref, own_ref, shared):
    length = len(key_refs) * own_ref.shape[0]
    tokens = own_ref.shape[0]
    keys, values = kv_stacks(key_refs, value_refs, g)
    keys_t = jnp.transpose(keys.astype(F32)).astype(BF16)
    d_keys = jnp.zeros((length, HEAD_SIZE), F32)
    d_values = jnp.zeros((length, HEAD_SIZE), F32)
    for local in range(GROUP // 2):
        pair = g * GROUP // 2 + local
        cols_a, cols_b = pair_cols(local)
        d_out = head_pair(d_resid, local)
        probs = probs_ref[pair]
        d_probs = mm(values, d_out, NT)
        row_dot = jnp.sum(probs * d_probs, axis=0, keepdims=True)
        d_scores = (probs * (d_probs - row_dot)).astype(BF16)
        d_keys = d_keys + mm(d_scores, head_pair(query_ref, pair))
        d_values = d_values + mm(probs.astype(BF16), d_out)
        d_query_t = mm(keys_t, d_scores) * SCALE
        dq_ref[:, cols_a] = jnp.transpose(d_query_t[:, :tokens]).astype(BF16)
        dq_ref[:, cols_b] = jnp.transpose(d_query_t[:, tokens:]).astype(BF16)
    d_keys = d_keys * SCALE
    own_ref[:, :HEAD_SIZE] = d_keys[:tokens]
    own_ref[:, HEAD_SIZE:] = d_values[:tokens]
    start = 2 * g * HEAD_SIZE
    for s, ref in enumerate(shared, 1):
        span = slice(s * tokens, (s + 1) * tokens)
        ref[:, start : start + HEAD_SIZE] = d_keys[span].astype(BF16)
        ref[:, start + HEAD_SIZE : start + 2 * HEAD_SIZE] = d_values[span].astype(BF16)


def first_back_kernel(
    count, pieces, rows, place_ref, gain_ref, hidden_ref, grad_ref, query_ref, probs_ref, *refs
):
    key_refs, value_refs = refs[:count], refs[count : 2 * count]
    refs = refs[2 * count :]
    dn_refs = part_views(refs[:pieces], rows, 0)
    resid_hbm, dq_ref, rest_ref, own_ref = refs[pieces : pieces + 4]
    shared = refs[pieces + 4 : -3]
    resid_ref, dn_scratch, sem = refs[-3:]
    tokens = hidden_ref.shape[0]
    place = place_ref[...]
    square = jnp.zeros((tokens, COLS), F32)
    mixing = jnp.zeros((tokens, COLS), F32)
    for cols in column_blocks():
        dn = mm(place, stacked(dn_refs, cols)) * gain_ref[:, cols]
        dn_scratch[:, cols] = dn
        hidden = hidden_ref[:, cols].astype(F32)
        square = square + hidden * hidden
        mixing = mixing + dn * hidden
    inv_rms = lax.rsqrt(jnp.sum(square, axis=1, keepdims=True) * (1.0 / D) + 1e-06)
    mean_mix = jnp.sum(mixing, axis=1, keepdims=True) * (1.0 / D)
    factor = inv_rms * inv_rms * inv_rms * mean_mix
    half = GROUP * HEAD_SIZE
    for cols in column_blocks():
        part = (
            grad_ref[:, cols].astype(F32)
            + dn_scratch[:, cols] * inv_rms
            - hidden_ref[:, cols].astype(F32) * factor
        ).astype(BF16)
        resid_ref[:, cols] = part
        if cols.start >= half:
            rest_ref[:, cols.start - half : cols.stop - half] = part
    resid_copy = pltpu.make_async_copy(resid_ref, resid_hbm, sem)
    resid_copy.start()
    group_back(0, key_refs, value_refs, query_ref, probs_ref, resid_ref, dq_ref, own_ref, shared)
    resid_copy.wait()


def second_back_kernel(count, query_ref, probs_ref, rest_ref, *refs):
    key_refs, value_refs = refs[:count], refs[count : 2 * count]
    first_shared = refs[2 * count : 3 * count - 1]
    dq_ref, own_ref = refs[3 * count - 1 : 3 * count + 1]
    shared = refs[3 * count + 1 :]
    for source, target in zip(first_shared, shared):
        target[:, : 2 * HEAD_SIZE] = source[...]
    group_back(1, key_refs, value_refs, query_ref, probs_ref, rest_ref, dq_ref, own_ref, shared)


def output_kernel(
    count, pieces, rows, tokens_in_all, place_ref, weight_ref, gain_ref, hidden_ref, grad_ref, *refs
):
    own_refs, refs = refs[:KEY_VALUE_HEADS], refs[KEY_VALUE_HEADS:]
    dq_refs, refs = refs[:KEY_VALUE_HEADS], refs[KEY_VALUE_HEADS:]
    arrived_refs = refs[: count - 1]
    y_refs = part_views(refs[count - 1 : count - 1 + pieces], rows, 1)
    out_hbm, dq_hbm, dk_hbm, dv_hbm, d_weight_hbm, d_gain_hbm = refs[count - 1 + pieces : -6]
    out_ref, dk_ref, dv_ref, d_weight_ref, d_gain_ref, sems = refs[-6:]
    copies = []

    def send(source, target):
        copy = pltpu.make_async_copy(source, target, sems.at[len(copies)])
        copy.start()
        copies.append(copy)

    width = GROUP * HEAD_SIZE
    for g, dq_ref in enumerate(dq_refs):
        send(dq_ref, dq_hbm.at[:, g * width : (g + 1) * width])
    for g, own_ref in enumerate(own_refs):
        d_kv = own_ref[...]
        for ref in arrived_refs:
            d_kv = d_kv + ref[:, 2 * g * HEAD_SIZE : 2 * (g + 1) * HEAD_SIZE].astype(F32)
        cols = slice(g * HEAD_SIZE, (g + 1) * HEAD_SIZE)
        dk_ref[:, cols] = d_kv[:, :HEAD_SIZE].astype(BF16)
        dv_ref[:, cols] = d_kv[:, HEAD_SIZE:].astype(BF16)
    d_gain_ref[...] = gain_ref[...] * (1.0 / tokens_in_all)
    send(dk_ref, dk_hbm)
    send(dv_ref, dv_hbm)
    send(d_gain_ref, d_gain_hbm)
    tokens = hidden_ref.shape[0]
    place = place_ref[...]
    weight = weight_ref[...]
    total = jnp.zeros((tokens, COLS), F32)
    for cols in column_blocks():
        y = mm(place, stacked(y_refs, cols))
        out_ref[:, cols] = (hidden_ref[:, cols].astype(F32) + weight * y).astype(BF16)
        send(out_ref.at[:, cols], out_hbm.at[:, cols])
        total = total + y * grad_ref[:, cols].astype(F32)
    d_weight_ref[...] = col_to_row(jnp.sum(total, axis=1, keepdims=True))
    send(d_weight_ref, d_weight_hbm)
    for copy in copies:
        copy.wait()


def run(kernel, name, inputs, outputs, flops, scratch=(), limit=20 * MIB):
    nbytes = sum(x.size * x.dtype.itemsize for _, x in inputs + outputs) if flops else 0
    spec = {space: pl.BlockSpec(memory_space=space) for space in (VMEM, HBM)}
    results = pl.pallas_call(
        kernel,
        out_shape=[x for _, x in outputs],
        in_specs=[spec[space] for space, _ in inputs],
        out_specs=[spec[space] for space, _ in outputs],
        scratch_shapes=list(scratch),
        compiler_params=pltpu.CompilerParams(vmem_limit_bytes=limit),
        cost_estimate=pl.CostEstimate(flops=flops, bytes_accessed=nbytes, transcendentals=0),
        name=name,
    )(*[pltpu.with_memory_space_constraint(x, HBM) if space is HBM else x for space, x in inputs])
    return list(results)


def placed(space, arrays):
    return [(space, x) for x in arrays]


def pairwise(value, axis, step):
    count = lax.axis_size(axis)
    return lax.ppermute(value, axis, [(i, i ^ step) for i in range(count)])


def exchange_flat(flat, capacity):
    count = lax.axis_size("exp")
    rows = EXP_DEV * capacity
    blocks = [flat[s * rows : (s + 1) * rows] for s in range(count)]
    moved = [blocks[0]] + [pairwise(blocks[s], "exp", s) for s in range(1, count)]
    return jnp.concatenate(moved, axis=0)


def exchange(pieces, capacity):
    if lax.axis_size("exp") != len(pieces):
        return [exchange_flat(pieces[0], capacity)]
    return [pairwise(piece, "exp", s) if s > 0 else piece for s, piece in enumerate(pieces)]


def doubled(value, axis, step):
    return value + pairwise(value, axis, step)


def sum_over(value, axis, first=1):
    step = first
    while step < lax.axis_size(axis):
        value = doubled(value, axis, step)
        step *= 2
    return value


def widened(act, value, axis, step):
    rows = value.shape[0]
    wide = jnp.pad(value, ((0, WIDE_LINES - rows), (0, 0)))
    return act(wide, axis, step)[:rows]


def shaped(shape, dtype):
    return jax.ShapeDtypeStruct(shape, dtype)


def per_device(
    queries,
    keys,
    values,
    resid,
    block_order,
    norm_gain,
    w_gate,
    w_down,
    routes,
    route_weight,
    d_out,
):
    query_rows = queries[0]
    resid_rows = resid[0]
    grad_rows = d_out[0]
    tokens = query_rows.shape[0]
    chosen = routes.reshape(1, tokens)
    gain = norm_gain.reshape(1, D)
    ctx_count = lax.axis_size("ctx")
    exp_count = lax.axis_size("exp")
    experts = EXP_DEV * exp_count
    capacity = 3 * tokens // (2 * experts)
    slots = experts * capacity
    rows = EXP_DEV * capacity
    piece_count = exp_count if rows % 16 == 0 else 1
    piece_shapes = [shaped((slots // piece_count, D), BF16)] * piece_count
    token_shape = shaped((tokens, D), BF16)
    kv_width = 2 * KEY_VALUE_HEADS * HEAD_SIZE
    attn_flops = 4 * tokens * ctx_count * tokens * QUERY_HEADS * HEAD_SIZE
    place_flops = 2 * slots * tokens * D
    expert_flops = 2 * slots * D * FFE * EXP_DEV

    own_keys, own_values = keys[0], values[0]
    all_keys = [own_keys] + [pairwise(own_keys, "ctx", s) for s in range(1, ctx_count)]
    all_values = [own_values] + [pairwise(own_values, "ctx", s) for s in range(1, ctx_count)]

    near = [grad_rows, own_keys, own_values, gain, query_rows, resid_rows]
    grad_rows, own_keys, own_values, gain, query_rows, resid_rows, slot, pos, weight, *send_grad = run(
        functools.partial(dispatch_kernel, ctx_count, experts, capacity),
        "dispatch_grads",
        placed(HBM, near + [route_weight, chosen, block_order]),
        placed(
            VMEM,
            [shaped(x.shape, x.dtype) for x in near]
            + [
                shaped((1, tokens), jnp.int32),
                shaped((ctx_count, tokens), jnp.int32),
                shaped((1, tokens), F32),
            ]
            + piece_shapes,
        ),
        place_flops,
        scratch=[
            pltpu.SMEM(block_order.shape, jnp.int32),
            pltpu.VMEM((1, tokens), jnp.int32),
            pltpu.SemaphoreType.DMA((9,)),
        ],
    )
    all_keys[0], all_values[0] = own_keys, own_values
    arrived_grad = exchange(send_grad, capacity)

    hidden, *send_x = run(
        functools.partial(attention_kernel, ctx_count),
        "attention_forward",
        placed(VMEM, [pos, slot, gain, query_rows, resid_rows] + all_keys + all_values),
        placed(VMEM, [token_shape] + piece_shapes),
        attn_flops + place_flops,
    )
    arrived_x = exchange(send_x, capacity)

    d_act, probs, down_near, gate_near, place, weight_wide = run(
        functools.partial(probs_kernel, ctx_count, capacity, piece_count),
        "act_grads_and_probs",
        placed(VMEM, [pos, slot, weight])
        + placed(HBM, [w_down, w_gate])
        + placed(VMEM, [query_rows] + all_keys + arrived_grad),
        placed(
            VMEM,
            [
                shaped((slots, FFE), F32),
                shaped((QUERY_HEADS // 2, ctx_count * tokens, 2 * tokens), F32),
                shaped((EXP_DEV * FFE, D), BF16),
                shaped((D, EXP_DEV * FFE), BF16),
                shaped((tokens, slots), BF16),
                shaped((tokens, COLS), F32),
            ],
        ),
        expert_flops + attn_flops // 2,
        scratch=[pltpu.SemaphoreType.DMA((2 * EXP_DEV,))],
    )

    return_shapes = []
    for s in range(piece_count):
        if joined(s, piece_count):
            return_shapes.append(shaped((2 * rows, D), BF16))
        else:
            return_shapes.extend([piece_shapes[0]] * 2)
    sent = run(
        functools.partial(expert_kernel, capacity, piece_count),
        "experts",
        placed(VMEM, [gate_near, down_near, d_act] + arrived_x),
        placed(VMEM, return_shapes),
        3 * expert_flops,
    )
    send_dn, send_y = split_parts(sent, piece_count)
    dn = exchange(send_dn, capacity)
    far = [s for s in range(1, piece_count) if not joined(s, piece_count)]
    y = list(dn) if piece_count > 1 else [exchange_flat(send_y[0], capacity)]
    y[0] = send_y[0] if piece_count > 1 else y[0]
    (terms,) = run(
        functools.partial(gain_kernel, piece_count, rows),
        "gain_terms",
        placed(VMEM, [gain] + arrived_x + send_dn),
        placed(VMEM, [shaped((GAIN_LINES, LANES), F32)]),
        2 * slots * D,
    )
    terms = sum_over(terms, "dp")
    send_far, terms = lax.optimization_barrier(([send_y[s] for s in far], terms))
    for s, piece in zip(far, send_far):
        y[s] = pairwise(piece, "exp", s)
    beside = pairwise(terms, "exp", FIRST)

    half_shape = shaped((tokens, D // 2), BF16)
    own_shape = shaped((tokens, 2 * HEAD_SIZE), F32)
    d_hidden, dq_first, rest, own_first, *shared_first = run(
        functools.partial(first_back_kernel, ctx_count, piece_count, rows),
        "residual_and_first_group",
        placed(VMEM, [place, gain, hidden, grad_rows, query_rows, probs])
        + placed(VMEM, all_keys + all_values + dn),
        placed(HBM, [token_shape])
        + placed(
            VMEM,
            [half_shape, half_shape, own_shape]
            + [shaped((tokens, 2 * HEAD_SIZE), BF16)] * (ctx_count - 1),
        ),
        A_COST,
        scratch=[
            pltpu.VMEM((tokens, D), BF16),
            pltpu.VMEM((tokens, D), F32),
            pltpu.SemaphoreType.DMA(()),
        ],
    )
    terms, rest = lax.optimization_barrier((terms, rest))
    terms = terms + beside
    terms = widened(doubled, terms, "exp", 3 - FIRST)
    dq_second, own_second, *shared = run(
        functools.partial(second_back_kernel, ctx_count),
        "second_group",
        placed(VMEM, [query_rows, probs, rest] + all_keys + all_values + shared_first),
        placed(VMEM, [half_shape, own_shape])
        + placed(VMEM, [shaped((tokens, kv_width), BF16)] * (ctx_count - 1)),
        B_COST,
    )
    terms = sum_over(sum_over(terms, "exp", first=4), "ctx")
    arrived_far, shared = lax.optimization_barrier(([y[s] for s in far], shared))
    for s, piece in zip(far, arrived_far):
        y[s] = piece
    kv_arrived = [pairwise(part, "ctx", s) for s, part in enumerate(shared, 1)]

    kv_shape = shaped((tokens, kv_width // 2), BF16)
    final_shapes = [token_shape, token_shape, kv_shape, kv_shape]
    final_shapes += [shaped((1, tokens), F32), shaped((GAIN_LINES, LANES), F32)]
    total_tokens = tokens * ctx_count * exp_count * lax.axis_size("dp")
    layer_out, d_queries, d_keys, d_values, d_weight, d_gain = run(
        functools.partial(output_kernel, ctx_count, piece_count, rows, total_tokens),
        "layer_output",
        placed(
            VMEM,
            [place, weight_wide, terms, hidden, grad_rows, own_first, own_second]
            + [dq_first, dq_second]
            + kv_arrived
            + y,
        ),
        placed(HBM, final_shapes),
        place_flops,
        scratch=[pltpu.VMEM(x.shape, x.dtype) for x in final_shapes[:1] + final_shapes[2:]]
        + [pltpu.SemaphoreType.DMA((4 + KEY_VALUE_HEADS + D // COLS,))],
    )
    return (
        layer_out[None],
        d_hidden[None],
        d_queries[None],
        d_keys[None],
        d_values[None],
        d_weight,
        d_gain.reshape(D),
    )


def solution(mesh):
    in_specs = (
        P(("exp", "dp"), "ctx", None),
        P(("exp", "dp"), "ctx", None),
        P(("exp", "dp"), "ctx", None),
        P(("exp", "dp"), "ctx", None),
        P(),
        P(),
        P("exp", None, None),
        P("exp", None, None),
        P(("exp", "dp"), "ctx", None),
        P(("exp", "dp"), "ctx"),
        P(("exp", "dp"), "ctx", None),
    )
    out_specs = (
        P(("exp", "dp"), "ctx", None),
        P(("exp", "dp"), "ctx", None),
        P(("exp", "dp"), "ctx", None),
        P(("exp", "dp"), "ctx", None),
        P(("exp", "dp"), "ctx", None),
        P(("exp", "dp"), "ctx"),
        P(),
    )
    return jax.shard_map(
        per_device, mesh=mesh, in_specs=in_specs, out_specs=out_specs, check_vma=False
    )
```

```python
import functools

import jax
import jax.numpy as jnp
from jax import lax
from jax.experimental import pallas as pl
from jax.experimental.pallas import tpu as pltpu
from jax.sharding import PartitionSpec as P

D = 2048
HEAD_SIZE = 128
QUERY_HEADS = 16
KEY_VALUE_HEADS = 2
GROUP = QUERY_HEADS // KEY_VALUE_HEADS
FFE = 384
EXP_DEV = 2
COLS = 256
LANES = 128
GAIN_LINES = D // LANES
WIDE_LINES = 32
FIRST = 1
A_COST = 4000000000
B_COST = 0
SCALE = HEAD_SIZE ** (-0.5)
EXP2_SCALE = SCALE * 1.4426950408889634
F32 = jnp.float32
BF16 = jnp.bfloat16
NN = (((1,), (0,)), ((), ()))
NT = (((1,), (1,)), ((), ()))
MIB = 1 << 20
VMEM, HBM = pltpu.VMEM, pltpu.HBM


def mm(a, b, dims=NN):
    return lax.dot_general(a, b, dims, preferred_element_type=F32)


def iota(shape, dim):
    return lax.broadcasted_iota(jnp.int32, shape, dim)


def row_to_col(row):
    n = row.shape[1]
    eye = iota((n, n), 0) == iota((n, n), 1)
    return jnp.sum(jnp.where(eye, row.astype(F32), 0.0), axis=1, keepdims=True)


def col_to_row(col):
    n = col.shape[0]
    eye = iota((n, n), 0) == iota((n, n), 1)
    return jnp.sum(jnp.where(eye, col, 0.0), axis=0, keepdims=True)


def block_positions(order_ref, ctx_index, tokens):
    span = tokens // 8
    index = iota((1, tokens), 1)
    which = index // span
    start = jnp.zeros((1, tokens), jnp.int32)
    for b in range(8):
        start = jnp.where(which == b, order_ref[ctx_index * 8 + b], start)
    return start * span + index % span


def stacked(refs, cols=slice(None)):
    parts = [r[:, cols] for r in refs]
    return parts[0] if len(parts) == 1 else jnp.concatenate(parts, axis=0)


def column_blocks(width=D, step=COLS):
    return [slice(c, c + step) for c in range(0, width, step)]


def store_pieces(refs, cols, rows_value):
    at = 0
    for r in refs:
        n = r.shape[0]
        r[:, cols] = rows_value[at : at + n]
        at += n


def pair_cols(pair):
    start = 2 * pair * HEAD_SIZE
    return slice(start, start + HEAD_SIZE), slice(start + HEAD_SIZE, start + 2 * HEAD_SIZE)


def head_pair(ref, pair):
    first, second = pair_cols(pair)
    return jnp.concatenate([ref[:, first], ref[:, second]], axis=0)


def placement_rows(slot_row, slots):
    tokens = slot_row.shape[1]
    return jnp.where(iota((slots, tokens), 0) == slot_row, 1.0, 0.0).astype(BF16)


def placement_cols(slot_row, slots):
    tokens = slot_row.shape[1]
    slot_col = row_to_col(slot_row)
    return jnp.where(iota((tokens, slots), 1).astype(F32) == slot_col, 1.0, 0.0).astype(BF16)


def dispatch_kernel(count, experts, capacity, *refs):
    sources, refs = refs[:9], refs[9:]
    targets, refs = refs[:6], refs[6:]
    grad_ref = targets[0]
    slot_ref, pos_ref, weight_ref = refs[:3]
    send_refs = refs[3:-3]
    order_ref, routes_ref, sems = refs[-3:]
    targets = targets + (weight_ref, routes_ref, order_ref)
    copies = [
        pltpu.make_async_copy(source, target, sems.at[i])
        for i, (source, target) in enumerate(zip(sources, targets))
    ]
    for copy in copies[6:] + copies[:6]:
        copy.start()
    for copy in copies[6:]:
        copy.wait()
    tokens = routes_ref.shape[1]
    chosen = routes_ref[...]
    lanes = max(experts, 16)
    hits = jnp.where(iota((lanes, tokens), 0) == chosen, 1.0, 0.0)
    before = jnp.where(iota((tokens, tokens), 0) < iota((tokens, tokens), 1), 1.0, 0.0)
    earlier = mm(hits.astype(BF16), before.astype(BF16))
    rank = jnp.sum(hits * earlier, axis=0, keepdims=True).astype(jnp.int32)
    target = (chosen // EXP_DEV) ^ lax.axis_index("exp")
    slot = (target * EXP_DEV + chosen % EXP_DEV) * capacity + rank
    slot_ref[...] = slot
    me = lax.axis_index("ctx")
    for s in range(count):
        pos_ref[s : s + 1, :] = block_positions(order_ref, me ^ s, tokens)
    place = placement_rows(slot, experts * capacity)
    weight = row_to_col(weight_ref[...])
    copies[0].wait()
    for cols in column_blocks():
        scaled = (weight * grad_ref[:, cols].astype(F32)).astype(BF16)
        store_pieces(send_refs, cols, mm(place, scaled).astype(BF16))
    for copy in copies[1:6]:
        copy.wait()


def kv_stacks(key_refs, value_refs, g):
    cols = slice(g * HEAD_SIZE, (g + 1) * HEAD_SIZE)
    return stacked(key_refs, cols), stacked(value_refs, cols)


def attention_kernel(
    count, pos_ref, slot_ref, gain_ref, query_ref, resid_ref, *refs
):
    key_refs, value_refs = refs[:count], refs[count : 2 * count]
    hidden_ref, send_refs = refs[2 * count], refs[2 * count + 1 :]
    tokens = query_ref.shape[0]
    query_pos = row_to_col(pos_ref[:1, :])
    bias = jnp.concatenate(
        [
            jnp.where(pos_ref[s : s + 1, :].astype(F32) <= query_pos, 0.0, -1e30)
            for s in range(count)
        ],
        axis=1,
    )
    length = count * tokens
    ones = jnp.ones((length, HEAD_SIZE), BF16)
    total = jnp.zeros((tokens, HEAD_SIZE), F32)
    for g in range(KEY_VALUE_HEADS):
        keys, values = kv_stacks(key_refs, value_refs, g)
        values = jnp.concatenate([values, ones], axis=1)
        for h in range(g * GROUP, (g + 1) * GROUP):
            cols = slice(h * HEAD_SIZE, (h + 1) * HEAD_SIZE)
            scores = mm(query_ref[:, cols], keys, NT) + bias
            peak = jnp.max(scores, axis=1, keepdims=True)
            weights = jnp.exp2((scores - peak) * EXP2_SCALE).astype(BF16)
            mixed = mm(weights, values)
            attended = mixed[:, :HEAD_SIZE] / mixed[:, HEAD_SIZE:]
            hidden = (resid_ref[:, cols].astype(F32) + attended).astype(BF16)
            hidden_ref[:, cols] = hidden
            wide = hidden.astype(F32)
            total = total + wide * wide
    inv_rms = lax.rsqrt(jnp.sum(total, axis=1, keepdims=True) * (1.0 / D) + 1e-06)
    slots = sum(r.shape[0] for r in send_refs)
    place = placement_rows(slot_ref[...], slots)
    for cols in column_blocks():
        normed = (hidden_ref[:, cols].astype(F32) * inv_rms * gain_ref[:, cols]).astype(BF16)
        store_pieces(send_refs, cols, mm(place, normed).astype(BF16))


def first_expert_rows(slots, capacity):
    return iota((slots, 1), 0) % (EXP_DEV * capacity) < capacity


def probs_kernel(
    count,
    capacity,
    pieces,
    pos_ref,
    slot_ref,
    weight_ref,
    down_hbm,
    gate_hbm,
    query_ref,
    *refs,
):
    key_refs = refs[:count]
    grad_refs = refs[count : count + pieces]
    d_act_ref, probs_ref, down_ref, gate_ref, place_ref, wide_ref, sems = refs[count + pieces :]
    spans = [slice(e * FFE, (e + 1) * FFE) for e in range(EXP_DEV)]
    down_copies = [
        pltpu.make_async_copy(down_hbm.at[e], down_ref.at[span, :], sems.at[e])
        for e, span in enumerate(spans)
    ]
    gate_copies = [
        pltpu.make_async_copy(gate_hbm.at[e], gate_ref.at[:, span], sems.at[EXP_DEV + e])
        for e, span in enumerate(spans)
    ]
    for copy in down_copies + gate_copies:
        copy.start()
    place_ref[...] = placement_cols(slot_ref[...], place_ref.shape[1])
    wide_ref[...] = jnp.broadcast_to(row_to_col(weight_ref[...]), wide_ref.shape)
    query_pos = pos_ref[:1, :].astype(F32)
    bias = jnp.concatenate(
        [
            jnp.where(row_to_col(pos_ref[s : s + 1, :]) <= query_pos, 0.0, -1e30)
            for s in range(count)
        ],
        axis=0,
    )
    bias = jnp.concatenate([bias, bias], axis=1)
    for g in range(KEY_VALUE_HEADS):
        keys = stacked(key_refs, slice(g * HEAD_SIZE, (g + 1) * HEAD_SIZE))
        for pair in range(g * GROUP // 2, (g + 1) * GROUP // 2):
            scores = mm(keys, head_pair(query_ref, pair), NT) + bias
            peak = jnp.max(scores, axis=0, keepdims=True)
            weights = jnp.exp2((scores - peak) * EXP2_SCALE)
            probs_ref[pair] = weights * (1.0 / jnp.sum(weights, axis=0, keepdims=True))
    grads = stacked(grad_refs)
    first = first_expert_rows(grads.shape[0], capacity)
    for copy in down_copies:
        copy.wait()
    d_act = mm(grads, down_ref[...], NT)
    d_act_ref[...] = jnp.where(first, d_act[:, :FFE], d_act[:, FFE:])
    for copy in gate_copies:
        copy.wait()


def part_views(refs, rows, part):
    return [r if r.shape[0] != 2 * rows else r.at[part * rows : (part + 1) * rows] for r in refs]


def joined(step, pieces):
    return pieces > 1 and step > 0 and step & (step - 1) == 0


def expert_kernel(capacity, pieces, gate_ref, down_ref, d_act_ref, *refs):
    rows = stacked(refs[:pieces])
    act_ref, piece_refs = refs[pieces], refs[pieces + 1 :]
    span = EXP_DEV * capacity
    back_refs = part_views(piece_refs, span, 0)
    near = [s for s in range(pieces) if joined(s, pieces)]
    out_refs = part_views([piece_refs[s] for s in near], span, 1)
    first = first_expert_rows(rows.shape[0], capacity)
    both = mm(rows, gate_ref[...])
    pre = jnp.where(first, both[:, :FFE], both[:, FFE:])
    gate = 1.0 / (1.0 + jnp.exp(-pre))
    act = pre * gate
    d_pre = d_act_ref[...] * gate * (1.0 + pre * (1.0 - gate))
    act, d_pre = [
        jnp.concatenate([jnp.where(first, x, 0.0), jnp.where(first, 0.0, x)], axis=1).astype(BF16)
        for x in (act, d_pre)
    ]
    act_ref[...] = act
    near_act = [act[s * span : (s + 1) * span] for s in near]
    near_act = jnp.concatenate(near_act, axis=0) if near else None
    for cols in column_blocks():
        store_pieces(back_refs, cols, mm(d_pre, gate_ref[cols, :], NT).astype(BF16))
        if near:
            store_pieces(out_refs, cols, mm(near_act, down_ref[:, cols]).astype(BF16))


def gain_kernel(pieces, rows, gain_ref, down_ref, act_ref, *refs):
    row_refs = refs[:pieces]
    back_refs = part_views(refs[pieces : 2 * pieces], rows, 0)
    terms_ref, out_refs = refs[2 * pieces], refs[2 * pieces + 1 :]
    act = [act_ref[...]]
    if pieces > 1:
        act = [
            act_ref[s * rows : (s + 1) * rows, :] for s in range(pieces) if not joined(s, pieces)
        ]
    act = jnp.concatenate(act, axis=0)
    for cols in column_blocks():
        store_pieces(out_refs, cols, mm(act, down_ref[:, cols]).astype(BF16))
    for cols in column_blocks():
        products = stacked(row_refs, cols).astype(F32) * stacked(back_refs, cols).astype(F32)
        terms = jnp.sum(products, axis=0, keepdims=True) / gain_ref[:, cols]
        for at in range(0, COLS, LANES):
            line = (cols.start + at) // LANES
            terms_ref[line : line + 1, :] = terms[:, at : at + LANES]


def group_back(g, key_refs, value_refs, query_ref, probs_ref, d_resid, dq_ref, own_ref, shared):
    length = len(key_refs) * own_ref.shape[0]
    tokens = own_ref.shape[0]
    keys, values = kv_stacks(key_refs, value_refs, g)
    keys_t = jnp.transpose(keys.astype(F32)).astype(BF16)
    d_keys = jnp.zeros((length, HEAD_SIZE), F32)
    d_values = jnp.zeros((length, HEAD_SIZE), F32)
    for local in range(GROUP // 2):
        pair = g * GROUP // 2 + local
        cols_a, cols_b = pair_cols(local)
        d_out = head_pair(d_resid, local)
        probs = probs_ref[pair]
        d_probs = mm(values, d_out, NT)
        row_dot = jnp.sum(probs * d_probs, axis=0, keepdims=True)
        d_scores = (probs * (d_probs - row_dot)).astype(BF16)
        d_keys = d_keys + mm(d_scores, head_pair(query_ref, pair))
        d_values = d_values + mm(probs.astype(BF16), d_out)
        d_query_t = mm(keys_t, d_scores) * SCALE
        dq_ref[:, cols_a] = jnp.transpose(d_query_t[:, :tokens]).astype(BF16)
        dq_ref[:, cols_b] = jnp.transpose(d_query_t[:, tokens:]).astype(BF16)
    d_keys = d_keys * SCALE
    own_ref[:, :HEAD_SIZE] = d_keys[:tokens]
    own_ref[:, HEAD_SIZE:] = d_values[:tokens]
    start = 2 * g * HEAD_SIZE
    for s, ref in enumerate(shared, 1):
        span = slice(s * tokens, (s + 1) * tokens)
        ref[:, start : start + HEAD_SIZE] = d_keys[span].astype(BF16)
        ref[:, start + HEAD_SIZE : start + 2 * HEAD_SIZE] = d_values[span].astype(BF16)


def first_back_kernel(
    count, pieces, rows, place_ref, gain_ref, hidden_ref, grad_ref, query_ref, probs_ref, *refs
):
    key_refs, value_refs = refs[:count], refs[count : 2 * count]
    refs = refs[2 * count :]
    dn_refs = part_views(refs[:pieces], rows, 0)
    resid_hbm, dq_ref, rest_ref, own_ref = refs[pieces : pieces + 4]
    shared = refs[pieces + 4 : -3]
    resid_ref, dn_scratch, sem = refs[-3:]
    tokens = hidden_ref.shape[0]
    place = place_ref[...]
    square = jnp.zeros((tokens, COLS), F32)
    mixing = jnp.zeros((tokens, COLS), F32)
    for cols in column_blocks():
        dn = mm(place, stacked(dn_refs, cols)) * gain_ref[:, cols]
        dn_scratch[:, cols] = dn
        hidden = hidden_ref[:, cols].astype(F32)
        square = square + hidden * hidden
        mixing = mixing + dn * hidden
    inv_rms = lax.rsqrt(jnp.sum(square, axis=1, keepdims=True) * (1.0 / D) + 1e-06)
    mean_mix = jnp.sum(mixing, axis=1, keepdims=True) * (1.0 / D)
    factor = inv_rms * inv_rms * inv_rms * mean_mix
    half = GROUP * HEAD_SIZE
    for cols in column_blocks():
        part = (
            grad_ref[:, cols].astype(F32)
            + dn_scratch[:, cols] * inv_rms
            - hidden_ref[:, cols].astype(F32) * factor
        ).astype(BF16)
        resid_ref[:, cols] = part
        if cols.start >= half:
            rest_ref[:, cols.start - half : cols.stop - half] = part
    resid_copy = pltpu.make_async_copy(resid_ref, resid_hbm, sem)
    resid_copy.start()
    group_back(0, key_refs, value_refs, query_ref, probs_ref, resid_ref, dq_ref, own_ref, shared)
    resid_copy.wait()


def second_back_kernel(count, query_ref, probs_ref, rest_ref, *refs):
    key_refs, value_refs = refs[:count], refs[count : 2 * count]
    first_shared = refs[2 * count : 3 * count - 1]
    dq_ref, own_ref = refs[3 * count - 1 : 3 * count + 1]
    shared = refs[3 * count + 1 :]
    for source, target in zip(first_shared, shared):
        target[:, : 2 * HEAD_SIZE] = source[...]
    group_back(1, key_refs, value_refs, query_ref, probs_ref, rest_ref, dq_ref, own_ref, shared)


def output_kernel(
    count, pieces, rows, tokens_in_all, place_ref, weight_ref, gain_ref, hidden_ref, grad_ref, *refs
):
    own_refs, refs = refs[:KEY_VALUE_HEADS], refs[KEY_VALUE_HEADS:]
    dq_refs, refs = refs[:KEY_VALUE_HEADS], refs[KEY_VALUE_HEADS:]
    arrived_refs = refs[: count - 1]
    y_refs = part_views(refs[count - 1 : count - 1 + pieces], rows, 1)
    out_hbm, dq_hbm, dk_hbm, dv_hbm, d_weight_hbm, d_gain_hbm = refs[count - 1 + pieces : -6]
    out_ref, dk_ref, dv_ref, d_weight_ref, d_gain_ref, sems = refs[-6:]
    copies = []

    def send(source, target):
        copy = pltpu.make_async_copy(source, target, sems.at[len(copies)])
        copy.start()
        copies.append(copy)

    width = GROUP * HEAD_SIZE
    for g, dq_ref in enumerate(dq_refs):
        send(dq_ref, dq_hbm.at[:, g * width : (g + 1) * width])
    for g, own_ref in enumerate(own_refs):
        d_kv = own_ref[...]
        for ref in arrived_refs:
            d_kv = d_kv + ref[:, 2 * g * HEAD_SIZE : 2 * (g + 1) * HEAD_SIZE].astype(F32)
        cols = slice(g * HEAD_SIZE, (g + 1) * HEAD_SIZE)
        dk_ref[:, cols] = d_kv[:, :HEAD_SIZE].astype(BF16)
        dv_ref[:, cols] = d_kv[:, HEAD_SIZE:].astype(BF16)
    d_gain_ref[...] = gain_ref[...] * (1.0 / tokens_in_all)
    send(dk_ref, dk_hbm)
    send(dv_ref, dv_hbm)
    send(d_gain_ref, d_gain_hbm)
    tokens = hidden_ref.shape[0]
    place = place_ref[...]
    weight = weight_ref[...]
    total = jnp.zeros((tokens, COLS), F32)
    for cols in column_blocks():
        y = mm(place, stacked(y_refs, cols))
        out_ref[:, cols] = (hidden_ref[:, cols].astype(F32) + weight * y).astype(BF16)
        send(out_ref.at[:, cols], out_hbm.at[:, cols])
        total = total + y * grad_ref[:, cols].astype(F32)
    d_weight_ref[...] = col_to_row(jnp.sum(total, axis=1, keepdims=True))
    send(d_weight_ref, d_weight_hbm)
    for copy in copies:
        copy.wait()


def run(kernel, name, inputs, outputs, flops, scratch=(), limit=20 * MIB):
    nbytes = sum(x.size * x.dtype.itemsize for _, x in inputs + outputs) if flops else 0
    spec = {space: pl.BlockSpec(memory_space=space) for space in (VMEM, HBM)}
    results = pl.pallas_call(
        kernel,
        out_shape=[x for _, x in outputs],
        in_specs=[spec[space] for space, _ in inputs],
        out_specs=[spec[space] for space, _ in outputs],
        scratch_shapes=list(scratch),
        compiler_params=pltpu.CompilerParams(vmem_limit_bytes=limit),
        cost_estimate=pl.CostEstimate(flops=flops, bytes_accessed=nbytes, transcendentals=0),
        name=name,
    )(*[pltpu.with_memory_space_constraint(x, HBM) if space is HBM else x for space, x in inputs])
    return list(results)


def placed(space, arrays):
    return [(space, x) for x in arrays]


def pairwise(value, axis, step):
    count = lax.axis_size(axis)
    return lax.ppermute(value, axis, [(i, i ^ step) for i in range(count)])


def exchange_flat(flat, capacity):
    count = lax.axis_size("exp")
    rows = EXP_DEV * capacity
    blocks = [flat[s * rows : (s + 1) * rows] for s in range(count)]
    moved = [blocks[0]] + [pairwise(blocks[s], "exp", s) for s in range(1, count)]
    return jnp.concatenate(moved, axis=0)


def exchange(pieces, capacity):
    if lax.axis_size("exp") != len(pieces):
        return [exchange_flat(pieces[0], capacity)]
    return [pairwise(piece, "exp", s) if s > 0 else piece for s, piece in enumerate(pieces)]


def doubled(value, axis, step):
    return value + pairwise(value, axis, step)


def sum_over(value, axis, first=1):
    step = first
    while step < lax.axis_size(axis):
        value = doubled(value, axis, step)
        step *= 2
    return value


def widened(act, value, axis, step):
    rows = value.shape[0]
    wide = jnp.pad(value, ((0, WIDE_LINES - rows), (0, 0)))
    return act(wide, axis, step)[:rows]


def shaped(shape, dtype):
    return jax.ShapeDtypeStruct(shape, dtype)


def per_device(
    queries,
    keys,
    values,
    resid,
    block_order,
    norm_gain,
    w_gate,
    w_down,
    routes,
    route_weight,
    d_out,
):
    query_rows = queries[0]
    resid_rows = resid[0]
    grad_rows = d_out[0]
    tokens = query_rows.shape[0]
    chosen = routes.reshape(1, tokens)
    gain = norm_gain.reshape(1, D)
    ctx_count = lax.axis_size("ctx")
    exp_count = lax.axis_size("exp")
    experts = EXP_DEV * exp_count
    capacity = 3 * tokens // (2 * experts)
    slots = experts * capacity
    rows = EXP_DEV * capacity
    piece_count = exp_count if rows % 16 == 0 else 1
    piece_shapes = [shaped((slots // piece_count, D), BF16)] * piece_count
    token_shape = shaped((tokens, D), BF16)
    kv_width = 2 * KEY_VALUE_HEADS * HEAD_SIZE
    attn_flops = 4 * tokens * ctx_count * tokens * QUERY_HEADS * HEAD_SIZE
    place_flops = 2 * slots * tokens * D
    expert_flops = 2 * slots * D * FFE * EXP_DEV

    own_keys, own_values = keys[0], values[0]
    all_keys = [own_keys] + [pairwise(own_keys, "ctx", s) for s in range(1, ctx_count)]
    all_values = [own_values] + [pairwise(own_values, "ctx", s) for s in range(1, ctx_count)]

    near = [grad_rows, own_keys, own_values, gain, query_rows, resid_rows]
    grad_rows, own_keys, own_values, gain, query_rows, resid_rows, slot, pos, weight, *send_grad = run(
        functools.partial(dispatch_kernel, ctx_count, experts, capacity),
        "dispatch_grads",
        placed(HBM, near + [route_weight, chosen, block_order]),
        placed(
            VMEM,
            [shaped(x.shape, x.dtype) for x in near]
            + [
                shaped((1, tokens), jnp.int32),
                shaped((ctx_count, tokens), jnp.int32),
                shaped((1, tokens), F32),
            ]
            + piece_shapes,
        ),
        place_flops,
        scratch=[
            pltpu.SMEM(block_order.shape, jnp.int32),
            pltpu.VMEM((1, tokens), jnp.int32),
            pltpu.SemaphoreType.DMA((9,)),
        ],
    )
    all_keys[0], all_values[0] = own_keys, own_values
    arrived_grad = exchange(send_grad, capacity)

    hidden, *send_x = run(
        functools.partial(attention_kernel, ctx_count),
        "attention_forward",
        placed(VMEM, [pos, slot, gain, query_rows, resid_rows] + all_keys + all_values),
        placed(VMEM, [token_shape] + piece_shapes),
        attn_flops + place_flops,
    )
    arrived_x = exchange(send_x, capacity)

    d_act, probs, down_near, gate_near, place, weight_wide = run(
        functools.partial(probs_kernel, ctx_count, capacity, piece_count),
        "act_grads_and_probs",
        placed(VMEM, [pos, slot, weight])
        + placed(HBM, [w_down, w_gate])
        + placed(VMEM, [query_rows] + all_keys + arrived_grad),
        placed(
            VMEM,
            [
                shaped((slots, FFE), F32),
                shaped((QUERY_HEADS // 2, ctx_count * tokens, 2 * tokens), F32),
                shaped((EXP_DEV * FFE, D), BF16),
                shaped((D, EXP_DEV * FFE), BF16),
                shaped((tokens, slots), BF16),
                shaped((tokens, COLS), F32),
            ],
        ),
        expert_flops + attn_flops // 2,
        scratch=[pltpu.SemaphoreType.DMA((2 * EXP_DEV,))],
    )

    steps = range(piece_count)
    apart = [s for s in steps if not joined(s, piece_count)]
    far = [s for s in apart if s > 0]
    return_shapes = [
        piece_shapes[s] if s in apart else shaped((2 * rows, D), BF16) for s in steps
    ]
    act, *send_dn = run(
        functools.partial(expert_kernel, capacity, piece_count),
        "experts",
        placed(VMEM, [gate_near, down_near, d_act] + arrived_x),
        placed(VMEM, [shaped((slots, EXP_DEV * FFE), BF16)] + return_shapes),
        5 * expert_flops // 2,
    )
    dn = exchange(send_dn, capacity)
    terms, *outs = run(
        functools.partial(gain_kernel, piece_count, rows),
        "gain_terms",
        placed(VMEM, [gain, down_near, act] + arrived_x + send_dn),
        placed(VMEM, [shaped((GAIN_LINES, LANES), F32)] + [piece_shapes[s] for s in apart]),
        expert_flops // 2,
    )
    send_y = dict(zip(apart, outs))
    y = list(dn) if piece_count > 1 else [exchange_flat(send_y[0], capacity)]
    y[0] = send_y[0] if piece_count > 1 else y[0]
    terms = sum_over(sum_over(terms, "dp"), "ctx")
    send_far, terms = lax.optimization_barrier(([send_y[s] for s in far], terms))
    for s, piece in zip(far, send_far):
        y[s] = pairwise(piece, "exp", s)
    beside = pairwise(terms, "exp", FIRST)

    half_shape = shaped((tokens, D // 2), BF16)
    own_shape = shaped((tokens, 2 * HEAD_SIZE), F32)
    d_hidden, dq_first, rest, own_first, *shared_first = run(
        functools.partial(first_back_kernel, ctx_count, piece_count, rows),
        "residual_and_first_group",
        placed(VMEM, [place, gain, hidden, grad_rows, query_rows, probs])
        + placed(VMEM, all_keys + all_values + dn),
        placed(HBM, [token_shape])
        + placed(
            VMEM,
            [half_shape, half_shape, own_shape]
            + [shaped((tokens, 2 * HEAD_SIZE), BF16)] * (ctx_count - 1),
        ),
        A_COST,
        scratch=[
            pltpu.VMEM((tokens, D), BF16),
            pltpu.VMEM((tokens, D), F32),
            pltpu.SemaphoreType.DMA(()),
        ],
    )
    terms, rest = lax.optimization_barrier((terms, rest))
    terms = terms + beside
    terms = widened(doubled, terms, "exp", 3 - FIRST)
    dq_second, own_second, *shared = run(
        functools.partial(second_back_kernel, ctx_count),
        "second_group",
        placed(VMEM, [query_rows, probs, rest] + all_keys + all_values + shared_first),
        placed(VMEM, [half_shape, own_shape])
        + placed(VMEM, [shaped((tokens, kv_width), BF16)] * (ctx_count - 1)),
        B_COST,
    )
    terms = sum_over(terms, "exp", first=4)
    arrived_far, shared = lax.optimization_barrier(([y[s] for s in far], shared))
    for s, piece in zip(far, arrived_far):
        y[s] = piece
    kv_arrived = [pairwise(part, "ctx", s) for s, part in enumerate(shared, 1)]

    kv_shape = shaped((tokens, kv_width // 2), BF16)
    final_shapes = [token_shape, token_shape, kv_shape, kv_shape]
    final_shapes += [shaped((1, tokens), F32), shaped((GAIN_LINES, LANES), F32)]
    total_tokens = tokens * ctx_count * exp_count * lax.axis_size("dp")
    layer_out, d_queries, d_keys, d_values, d_weight, d_gain = run(
        functools.partial(output_kernel, ctx_count, piece_count, rows, total_tokens),
        "layer_output",
        placed(
            VMEM,
            [place, weight_wide, terms, hidden, grad_rows, own_first, own_second]
            + [dq_first, dq_second]
            + kv_arrived
            + y,
        ),
        placed(HBM, final_shapes),
        place_flops,
        scratch=[pltpu.VMEM(x.shape, x.dtype) for x in final_shapes[:1] + final_shapes[2:]]
        + [pltpu.SemaphoreType.DMA((4 + KEY_VALUE_HEADS + D // COLS,))],
    )
    return (
        layer_out[None],
        d_hidden[None],
        d_queries[None],
        d_keys[None],
        d_values[None],
        d_weight,
        d_gain.reshape(D),
    )


def solution(mesh):
    in_specs = (
        P(("exp", "dp"), "ctx", None),
        P(("exp", "dp"), "ctx", None),
        P(("exp", "dp"), "ctx", None),
        P(("exp", "dp"), "ctx", None),
        P(),
        P(),
        P("exp", None, None),
        P("exp", None, None),
        P(("exp", "dp"), "ctx", None),
        P(("exp", "dp"), "ctx"),
        P(("exp", "dp"), "ctx", None),
    )
    out_specs = (
        P(("exp", "dp"), "ctx", None),
        P(("exp", "dp"), "ctx", None),
        P(("exp", "dp"), "ctx", None),
        P(("exp", "dp"), "ctx", None),
        P(("exp", "dp"), "ctx", None),
        P(("exp", "dp"), "ctx"),
        P(),
    )
    return jax.shard_map(
        per_device, mesh=mesh, in_specs=in_specs, out_specs=out_specs, check_vma=False
    )
```

```python
import functools

import jax
import jax.numpy as jnp
from jax import lax
from jax.experimental import pallas as pl
from jax.experimental.pallas import tpu as pltpu
from jax.sharding import PartitionSpec as P

D = 2048
HEAD_SIZE = 128
QUERY_HEADS = 16
KEY_VALUE_HEADS = 2
GROUP = QUERY_HEADS // KEY_VALUE_HEADS
FFE = 384
EXP_DEV = 2
COLS = 512
LANES = 128
GAIN_LINES = D // LANES
WIDE_LINES = 32
FIRST = 1
A_COST = 4000000000
B_COST = 0
SCALE = HEAD_SIZE ** (-0.5)
EXP2_SCALE = SCALE * 1.4426950408889634
F32 = jnp.float32
BF16 = jnp.bfloat16
NN = (((1,), (0,)), ((), ()))
NT = (((1,), (1,)), ((), ()))
MIB = 1 << 20
VMEM, HBM = pltpu.VMEM, pltpu.HBM


def mm(a, b, dims=NN):
    return lax.dot_general(a, b, dims, preferred_element_type=F32)


def iota(shape, dim):
    return lax.broadcasted_iota(jnp.int32, shape, dim)


def row_to_col(row):
    n = row.shape[1]
    eye = iota((n, n), 0) == iota((n, n), 1)
    return jnp.sum(jnp.where(eye, row.astype(F32), 0.0), axis=1, keepdims=True)


def col_to_row(col):
    n = col.shape[0]
    eye = iota((n, n), 0) == iota((n, n), 1)
    return jnp.sum(jnp.where(eye, col, 0.0), axis=0, keepdims=True)


def block_positions(order_ref, ctx_index, tokens):
    span = tokens // 8
    index = iota((1, tokens), 1)
    which = index // span
    start = jnp.zeros((1, tokens), jnp.int32)
    for b in range(8):
        start = jnp.where(which == b, order_ref[ctx_index * 8 + b], start)
    return start * span + index % span


def stacked(refs, cols=slice(None)):
    parts = [r[:, cols] for r in refs]
    return parts[0] if len(parts) == 1 else jnp.concatenate(parts, axis=0)


def column_blocks(width=D, step=COLS):
    return [slice(c, c + step) for c in range(0, width, step)]


def store_pieces(refs, cols, rows_value):
    at = 0
    for r in refs:
        n = r.shape[0]
        r[:, cols] = rows_value[at : at + n]
        at += n


def pair_cols(pair):
    start = 2 * pair * HEAD_SIZE
    return slice(start, start + HEAD_SIZE), slice(start + HEAD_SIZE, start + 2 * HEAD_SIZE)


def head_pair(ref, pair):
    first, second = pair_cols(pair)
    return jnp.concatenate([ref[:, first], ref[:, second]], axis=0)


def placement_rows(slot_row, slots):
    tokens = slot_row.shape[1]
    return jnp.where(iota((slots, tokens), 0) == slot_row, 1.0, 0.0).astype(BF16)


def placement_cols(slot_row, slots):
    tokens = slot_row.shape[1]
    slot_col = row_to_col(slot_row)
    return jnp.where(iota((tokens, slots), 1).astype(F32) == slot_col, 1.0, 0.0).astype(BF16)


def dispatch_kernel(count, experts, capacity, *refs):
    sources, refs = refs[:9], refs[9:]
    targets, refs = refs[:6], refs[6:]
    grad_ref = targets[0]
    slot_ref, pos_ref, weight_ref = refs[:3]
    send_refs = refs[3:-3]
    order_ref, routes_ref, sems = refs[-3:]
    targets = targets + (weight_ref, routes_ref, order_ref)
    copies = [
        pltpu.make_async_copy(source, target, sems.at[i])
        for i, (source, target) in enumerate(zip(sources, targets))
    ]
    for copy in copies[6:] + copies[:6]:
        copy.start()
    for copy in copies[6:]:
        copy.wait()
    tokens = routes_ref.shape[1]
    chosen = routes_ref[...]
    lanes = max(experts, 16)
    hits = jnp.where(iota((lanes, tokens), 0) == chosen, 1.0, 0.0)
    before = jnp.where(iota((tokens, tokens), 0) < iota((tokens, tokens), 1), 1.0, 0.0)
    earlier = mm(hits.astype(BF16), before.astype(BF16))
    rank = jnp.sum(hits * earlier, axis=0, keepdims=True).astype(jnp.int32)
    target = (chosen // EXP_DEV) ^ lax.axis_index("exp")
    slot = (target * EXP_DEV + chosen % EXP_DEV) * capacity + rank
    slot_ref[...] = slot
    me = lax.axis_index("ctx")
    for s in range(count):
        pos_ref[s : s + 1, :] = block_positions(order_ref, me ^ s, tokens)
    place = placement_rows(slot, experts * capacity)
    weight = row_to_col(weight_ref[...])
    copies[0].wait()
    for cols in column_blocks():
        scaled = (weight * grad_ref[:, cols].astype(F32)).astype(BF16)
        store_pieces(send_refs, cols, mm(place, scaled).astype(BF16))
    for copy in copies[1:6]:
        copy.wait()


def kv_stacks(key_refs, value_refs, g):
    cols = slice(g * HEAD_SIZE, (g + 1) * HEAD_SIZE)
    return stacked(key_refs, cols), stacked(value_refs, cols)


def attention_kernel(
    count, pos_ref, slot_ref, gain_ref, query_ref, resid_ref, *refs
):
    key_refs, value_refs = refs[:count], refs[count : 2 * count]
    hidden_ref, send_refs = refs[2 * count], refs[2 * count + 1 :]
    tokens = query_ref.shape[0]
    query_pos = row_to_col(pos_ref[:1, :])
    bias = jnp.concatenate(
        [
            jnp.where(pos_ref[s : s + 1, :].astype(F32) <= query_pos, 0.0, -1e30)
            for s in range(count)
        ],
        axis=1,
    )
    length = count * tokens
    ones = jnp.ones((length, HEAD_SIZE), BF16)
    total = jnp.zeros((tokens, HEAD_SIZE), F32)
    for g in range(KEY_VALUE_HEADS):
        keys, values = kv_stacks(key_refs, value_refs, g)
        values = jnp.concatenate([values, ones], axis=1)
        for h in range(g * GROUP, (g + 1) * GROUP):
            cols = slice(h * HEAD_SIZE, (h + 1) * HEAD_SIZE)
            scores = mm(query_ref[:, cols], keys, NT) + bias
            peak = jnp.max(scores, axis=1, keepdims=True)
            weights = jnp.exp2((scores - peak) * EXP2_SCALE).astype(BF16)
            mixed = mm(weights, values)
            attended = mixed[:, :HEAD_SIZE] / mixed[:, HEAD_SIZE:]
            hidden = (resid_ref[:, cols].astype(F32) + attended).astype(BF16)
            hidden_ref[:, cols] = hidden
            wide = hidden.astype(F32)
            total = total + wide * wide
    inv_rms = lax.rsqrt(jnp.sum(total, axis=1, keepdims=True) * (1.0 / D) + 1e-06)
    slots = sum(r.shape[0] for r in send_refs)
    place = placement_rows(slot_ref[...], slots)
    for cols in column_blocks():
        normed = (hidden_ref[:, cols].astype(F32) * inv_rms * gain_ref[:, cols]).astype(BF16)
        store_pieces(send_refs, cols, mm(place, normed).astype(BF16))


def first_expert_rows(slots, capacity):
    return iota((slots, 1), 0) % (EXP_DEV * capacity) < capacity


def probs_kernel(
    count,
    capacity,
    pieces,
    pos_ref,
    slot_ref,
    weight_ref,
    down_hbm,
    gate_hbm,
    query_ref,
    *refs,
):
    key_refs = refs[:count]
    grad_refs = refs[count : count + pieces]
    d_act_ref, probs_ref, down_ref, gate_ref, place_ref, wide_ref, sems = refs[count + pieces :]
    spans = [slice(e * FFE, (e + 1) * FFE) for e in range(EXP_DEV)]
    down_copies = [
        pltpu.make_async_copy(down_hbm.at[e], down_ref.at[span, :], sems.at[e])
        for e, span in enumerate(spans)
    ]
    gate_copies = [
        pltpu.make_async_copy(gate_hbm.at[e], gate_ref.at[:, span], sems.at[EXP_DEV + e])
        for e, span in enumerate(spans)
    ]
    for copy in down_copies + gate_copies:
        copy.start()
    place_ref[...] = placement_cols(slot_ref[...], place_ref.shape[1])
    wide_ref[...] = jnp.broadcast_to(row_to_col(weight_ref[...]), wide_ref.shape)
    query_pos = pos_ref[:1, :].astype(F32)
    bias = jnp.concatenate(
        [
            jnp.where(row_to_col(pos_ref[s : s + 1, :]) <= query_pos, 0.0, -1e30)
            for s in range(count)
        ],
        axis=0,
    )
    bias = jnp.concatenate([bias, bias], axis=1)
    for g in range(KEY_VALUE_HEADS):
        keys = stacked(key_refs, slice(g * HEAD_SIZE, (g + 1) * HEAD_SIZE))
        for pair in range(g * GROUP // 2, (g + 1) * GROUP // 2):
            scores = mm(keys, head_pair(query_ref, pair), NT) + bias
            peak = jnp.max(scores, axis=0, keepdims=True)
            weights = jnp.exp2((scores - peak) * EXP2_SCALE)
            probs_ref[pair] = weights * (1.0 / jnp.sum(weights, axis=0, keepdims=True))
    grads = stacked(grad_refs)
    first = first_expert_rows(grads.shape[0], capacity)
    for copy in down_copies:
        copy.wait()
    d_act = mm(grads, down_ref[...], NT)
    d_act_ref[...] = jnp.where(first, d_act[:, :FFE], d_act[:, FFE:])
    for copy in gate_copies:
        copy.wait()


def part_views(refs, rows, part):
    return [r if r.shape[0] != 2 * rows else r.at[part * rows : (part + 1) * rows] for r in refs]


def joined(step, pieces):
    return pieces > 1 and step > 0 and step & (step - 1) == 0


def split_parts(refs, pieces):
    back, out = [], []
    at = 0
    for s in range(pieces):
        back.append(refs[at])
        at += not joined(s, pieces)
        out.append(refs[at])
        at += 1
    return back, out


def expert_kernel(capacity, pieces, gate_ref, down_ref, d_act_ref, *refs):
    rows = stacked(refs[:pieces])
    back_refs, out_refs = split_parts(refs[pieces:], pieces)
    back_refs = part_views(back_refs, EXP_DEV * capacity, 0)
    out_refs = part_views(out_refs, EXP_DEV * capacity, 1)
    first = first_expert_rows(rows.shape[0], capacity)
    both = mm(rows, gate_ref[...])
    pre = jnp.where(first, both[:, :FFE], both[:, FFE:])
    gate = 1.0 / (1.0 + jnp.exp(-pre))
    act = pre * gate
    d_pre = d_act_ref[...] * gate * (1.0 + pre * (1.0 - gate))
    act, d_pre = [
        jnp.concatenate([jnp.where(first, x, 0.0), jnp.where(first, 0.0, x)], axis=1).astype(BF16)
        for x in (act, d_pre)
    ]
    for cols in column_blocks():
        store_pieces(back_refs, cols, mm(d_pre, gate_ref[cols, :], NT).astype(BF16))
        store_pieces(out_refs, cols, mm(act, down_ref[:, cols]).astype(BF16))


def gain_kernel(pieces, rows, gain_ref, *refs):
    row_refs = refs[:pieces]
    back_refs = part_views(refs[pieces:-1], rows, 0)
    terms_ref = refs[-1]
    for cols in column_blocks():
        products = stacked(row_refs, cols).astype(F32) * stacked(back_refs, cols).astype(F32)
        terms = jnp.sum(products, axis=0, keepdims=True) / gain_ref[:, cols]
        for at in range(0, COLS, LANES):
            line = (cols.start + at) // LANES
            terms_ref[line : line + 1, :] = terms[:, at : at + LANES]


def group_back(g, key_refs, value_refs, query_ref, probs_ref, d_resid, dq_ref, own_ref, shared):
    length = len(key_refs) * own_ref.shape[0]
    tokens = own_ref.shape[0]
    keys, values = kv_stacks(key_refs, value_refs, g)
    keys_t = jnp.transpose(keys.astype(F32)).astype(BF16)
    d_keys = jnp.zeros((length, HEAD_SIZE), F32)
    d_values = jnp.zeros((length, HEAD_SIZE), F32)
    for local in range(GROUP // 2):
        pair = g * GROUP // 2 + local
        cols_a, cols_b = pair_cols(local)
        d_out = head_pair(d_resid, local)
        probs = probs_ref[pair]
        d_probs = mm(values, d_out, NT)
        row_dot = jnp.sum(probs * d_probs, axis=0, keepdims=True)
        d_scores = (probs * (d_probs - row_dot)).astype(BF16)
        d_keys = d_keys + mm(d_scores, head_pair(query_ref, pair))
        d_values = d_values + mm(probs.astype(BF16), d_out)
        d_query_t = mm(keys_t, d_scores) * SCALE
        dq_ref[:, cols_a] = jnp.transpose(d_query_t[:, :tokens]).astype(BF16)
        dq_ref[:, cols_b] = jnp.transpose(d_query_t[:, tokens:]).astype(BF16)
    d_keys = d_keys * SCALE
    own_ref[:, :HEAD_SIZE] = d_keys[:tokens]
    own_ref[:, HEAD_SIZE:] = d_values[:tokens]
    start = 2 * g * HEAD_SIZE
    for s, ref in enumerate(shared, 1):
        span = slice(s * tokens, (s + 1) * tokens)
        ref[:, start : start + HEAD_SIZE] = d_keys[span].astype(BF16)
        ref[:, start + HEAD_SIZE : start + 2 * HEAD_SIZE] = d_values[span].astype(BF16)


def first_back_kernel(
    count, pieces, rows, place_ref, gain_ref, hidden_ref, grad_ref, query_ref, probs_ref, *refs
):
    key_refs, value_refs = refs[:count], refs[count : 2 * count]
    refs = refs[2 * count :]
    dn_refs = part_views(refs[:pieces], rows, 0)
    resid_hbm, dq_ref, rest_ref, own_ref = refs[pieces : pieces + 4]
    shared = refs[pieces + 4 : -3]
    resid_ref, dn_scratch, sem = refs[-3:]
    tokens = hidden_ref.shape[0]
    place = place_ref[...]
    square = jnp.zeros((tokens, COLS), F32)
    mixing = jnp.zeros((tokens, COLS), F32)
    for cols in column_blocks():
        dn = mm(place, stacked(dn_refs, cols)) * gain_ref[:, cols]
        dn_scratch[:, cols] = dn
        hidden = hidden_ref[:, cols].astype(F32)
        square = square + hidden * hidden
        mixing = mixing + dn * hidden
    inv_rms = lax.rsqrt(jnp.sum(square, axis=1, keepdims=True) * (1.0 / D) + 1e-06)
    mean_mix = jnp.sum(mixing, axis=1, keepdims=True) * (1.0 / D)
    factor = inv_rms * inv_rms * inv_rms * mean_mix
    half = GROUP * HEAD_SIZE
    for cols in column_blocks():
        part = (
            grad_ref[:, cols].astype(F32)
            + dn_scratch[:, cols] * inv_rms
            - hidden_ref[:, cols].astype(F32) * factor
        ).astype(BF16)
        resid_ref[:, cols] = part
        if cols.start >= half:
            rest_ref[:, cols.start - half : cols.stop - half] = part
    resid_copy = pltpu.make_async_copy(resid_ref, resid_hbm, sem)
    resid_copy.start()
    group_back(0, key_refs, value_refs, query_ref, probs_ref, resid_ref, dq_ref, own_ref, shared)
    resid_copy.wait()


def second_back_kernel(count, query_ref, probs_ref, rest_ref, *refs):
    key_refs, value_refs = refs[:count], refs[count : 2 * count]
    first_shared = refs[2 * count : 3 * count - 1]
    dq_ref, own_ref = refs[3 * count - 1 : 3 * count + 1]
    shared = refs[3 * count + 1 :]
    for source, target in zip(first_shared, shared):
        target[:, : 2 * HEAD_SIZE] = source[...]
    group_back(1, key_refs, value_refs, query_ref, probs_ref, rest_ref, dq_ref, own_ref, shared)


def output_kernel(
    count, pieces, rows, tokens_in_all, place_ref, weight_ref, gain_ref, hidden_ref, grad_ref, *refs
):
    own_refs, refs = refs[:KEY_VALUE_HEADS], refs[KEY_VALUE_HEADS:]
    dq_refs, refs = refs[:KEY_VALUE_HEADS], refs[KEY_VALUE_HEADS:]
    arrived_refs = refs[: count - 1]
    y_refs = part_views(refs[count - 1 : count - 1 + pieces], rows, 1)
    out_hbm, dq_hbm, dk_hbm, dv_hbm, d_weight_hbm, d_gain_hbm = refs[count - 1 + pieces : -6]
    out_ref, dk_ref, dv_ref, d_weight_ref, d_gain_ref, sems = refs[-6:]
    copies = []

    def send(source, target):
        copy = pltpu.make_async_copy(source, target, sems.at[len(copies)])
        copy.start()
        copies.append(copy)

    width = GROUP * HEAD_SIZE
    for g, dq_ref in enumerate(dq_refs):
        send(dq_ref, dq_hbm.at[:, g * width : (g + 1) * width])
    for g, own_ref in enumerate(own_refs):
        d_kv = own_ref[...]
        for ref in arrived_refs:
            d_kv = d_kv + ref[:, 2 * g * HEAD_SIZE : 2 * (g + 1) * HEAD_SIZE].astype(F32)
        cols = slice(g * HEAD_SIZE, (g + 1) * HEAD_SIZE)
        dk_ref[:, cols] = d_kv[:, :HEAD_SIZE].astype(BF16)
        dv_ref[:, cols] = d_kv[:, HEAD_SIZE:].astype(BF16)
    d_gain_ref[...] = gain_ref[...] * (1.0 / tokens_in_all)
    send(dk_ref, dk_hbm)
    send(dv_ref, dv_hbm)
    send(d_gain_ref, d_gain_hbm)
    tokens = hidden_ref.shape[0]
    place = place_ref[...]
    weight = weight_ref[...]
    total = jnp.zeros((tokens, COLS), F32)
    for cols in column_blocks():
        y = mm(place, stacked(y_refs, cols))
        out_ref[:, cols] = (hidden_ref[:, cols].astype(F32) + weight * y).astype(BF16)
        send(out_ref.at[:, cols], out_hbm.at[:, cols])
        total = total + y * grad_ref[:, cols].astype(F32)
    d_weight_ref[...] = col_to_row(jnp.sum(total, axis=1, keepdims=True))
    send(d_weight_ref, d_weight_hbm)
    for copy in copies:
        copy.wait()


def run(kernel, name, inputs, outputs, flops, scratch=(), limit=20 * MIB):
    nbytes = sum(x.size * x.dtype.itemsize for _, x in inputs + outputs) if flops else 0
    spec = {space: pl.BlockSpec(memory_space=space) for space in (VMEM, HBM)}
    results = pl.pallas_call(
        kernel,
        out_shape=[x for _, x in outputs],
        in_specs=[spec[space] for space, _ in inputs],
        out_specs=[spec[space] for space, _ in outputs],
        scratch_shapes=list(scratch),
        compiler_params=pltpu.CompilerParams(vmem_limit_bytes=limit),
        cost_estimate=pl.CostEstimate(flops=flops, bytes_accessed=nbytes, transcendentals=0),
        name=name,
    )(*[pltpu.with_memory_space_constraint(x, HBM) if space is HBM else x for space, x in inputs])
    return list(results)


def placed(space, arrays):
    return [(space, x) for x in arrays]


def pairwise(value, axis, step):
    count = lax.axis_size(axis)
    return lax.ppermute(value, axis, [(i, i ^ step) for i in range(count)])


def exchange_flat(flat, capacity):
    count = lax.axis_size("exp")
    rows = EXP_DEV * capacity
    blocks = [flat[s * rows : (s + 1) * rows] for s in range(count)]
    moved = [blocks[0]] + [pairwise(blocks[s], "exp", s) for s in range(1, count)]
    return jnp.concatenate(moved, axis=0)


def exchange(pieces, capacity):
    if lax.axis_size("exp") != len(pieces):
        return [exchange_flat(pieces[0], capacity)]
    return [pairwise(piece, "exp", s) if s > 0 else piece for s, piece in enumerate(pieces)]


def doubled(value, axis, step):
    return value + pairwise(value, axis, step)


def sum_over(value, axis, first=1):
    step = first
    while step < lax.axis_size(axis):
        value = doubled(value, axis, step)
        step *= 2
    return value


def widened(act, value, axis, step):
    rows = value.shape[0]
    wide = jnp.pad(value, ((0, WIDE_LINES - rows), (0, 0)))
    return act(wide, axis, step)[:rows]


def shaped(shape, dtype):
    return jax.ShapeDtypeStruct(shape, dtype)


def per_device(
    queries,
    keys,
    values,
    resid,
    block_order,
    norm_gain,
    w_gate,
    w_down,
    routes,
    route_weight,
    d_out,
):
    query_rows = queries[0]
    resid_rows = resid[0]
    grad_rows = d_out[0]
    tokens = query_rows.shape[0]
    chosen = routes.reshape(1, tokens)
    gain = norm_gain.reshape(1, D)
    ctx_count = lax.axis_size("ctx")
    exp_count = lax.axis_size("exp")
    experts = EXP_DEV * exp_count
    capacity = 3 * tokens // (2 * experts)
    slots = experts * capacity
    rows = EXP_DEV * capacity
    piece_count = exp_count if rows % 16 == 0 else 1
    piece_shapes = [shaped((slots // piece_count, D), BF16)] * piece_count
    token_shape = shaped((tokens, D), BF16)
    kv_width = 2 * KEY_VALUE_HEADS * HEAD_SIZE
    attn_flops = 4 * tokens * ctx_count * tokens * QUERY_HEADS * HEAD_SIZE
    place_flops = 2 * slots * tokens * D
    expert_flops = 2 * slots * D * FFE * EXP_DEV

    own_keys, own_values = keys[0], values[0]
    all_keys = [own_keys] + [pairwise(own_keys, "ctx", s) for s in range(1, ctx_count)]
    all_values = [own_values] + [pairwise(own_values, "ctx", s) for s in range(1, ctx_count)]

    near = [grad_rows, own_keys, own_values, gain, query_rows, resid_rows]
    grad_rows, own_keys, own_values, gain, query_rows, resid_rows, slot, pos, weight, *send_grad = run(
        functools.partial(dispatch_kernel, ctx_count, experts, capacity),
        "dispatch_grads",
        placed(HBM, near + [route_weight, chosen, block_order]),
        placed(
            VMEM,
            [shaped(x.shape, x.dtype) for x in near]
            + [
                shaped((1, tokens), jnp.int32),
                shaped((ctx_count, tokens), jnp.int32),
                shaped((1, tokens), F32),
            ]
            + piece_shapes,
        ),
        place_flops,
        scratch=[
            pltpu.SMEM(block_order.shape, jnp.int32),
            pltpu.VMEM((1, tokens), jnp.int32),
            pltpu.SemaphoreType.DMA((9,)),
        ],
    )
    all_keys[0], all_values[0] = own_keys, own_values
    arrived_grad = exchange(send_grad, capacity)

    hidden, *send_x = run(
        functools.partial(attention_kernel, ctx_count),
        "attention_forward",
        placed(VMEM, [pos, slot, gain, query_rows, resid_rows] + all_keys + all_values),
        placed(VMEM, [token_shape] + piece_shapes),
        attn_flops + place_flops,
    )
    arrived_x = exchange(send_x, capacity)

    d_act, probs, down_near, gate_near, place, weight_wide = run(
        functools.partial(probs_kernel, ctx_count, capacity, piece_count),
        "act_grads_and_probs",
        placed(VMEM, [pos, slot, weight])
        + placed(HBM, [w_down, w_gate])
        + placed(VMEM, [query_rows] + all_keys + arrived_grad),
        placed(
            VMEM,
            [
                shaped((slots, FFE), F32),
                shaped((QUERY_HEADS // 2, ctx_count * tokens, 2 * tokens), F32),
                shaped((EXP_DEV * FFE, D), BF16),
                shaped((D, EXP_DEV * FFE), BF16),
                shaped((tokens, slots), BF16),
                shaped((tokens, COLS), F32),
            ],
        ),
        expert_flops + attn_flops // 2,
        scratch=[pltpu.SemaphoreType.DMA((2 * EXP_DEV,))],
    )

    return_shapes = []
    for s in range(piece_count):
        if joined(s, piece_count):
            return_shapes.append(shaped((2 * rows, D), BF16))
        else:
            return_shapes.extend([piece_shapes[0]] * 2)
    sent = run(
        functools.partial(expert_kernel, capacity, piece_count),
        "experts",
        placed(VMEM, [gate_near, down_near, d_act] + arrived_x),
        placed(VMEM, return_shapes),
        3 * expert_flops,
    )
    send_dn, send_y = split_parts(sent, piece_count)
    dn = exchange(send_dn, capacity)
    far = [s for s in range(1, piece_count) if not joined(s, piece_count)]
    y = list(dn) if piece_count > 1 else [exchange_flat(send_y[0], capacity)]
    y[0] = send_y[0] if piece_count > 1 else y[0]
    (terms,) = run(
        functools.partial(gain_kernel, piece_count, rows),
        "gain_terms",
        placed(VMEM, [gain] + arrived_x + send_dn),
        placed(VMEM, [shaped((GAIN_LINES, LANES), F32)]),
        2 * slots * D,
    )
    terms = sum_over(sum_over(terms, "dp"), "ctx")
    send_far, terms = lax.optimization_barrier(([send_y[s] for s in far], terms))
    for s, piece in zip(far, send_far):
        y[s] = pairwise(piece, "exp", s)
    beside = pairwise(terms, "exp", FIRST)

    half_shape = shaped((tokens, D // 2), BF16)
    own_shape = shaped((tokens, 2 * HEAD_SIZE), F32)
    d_hidden, dq_first, rest, own_first, *shared_first = run(
        functools.partial(first_back_kernel, ctx_count, piece_count, rows),
        "residual_and_first_group",
        placed(VMEM, [place, gain, hidden, grad_rows, query_rows, probs])
        + placed(VMEM, all_keys + all_values + dn),
        placed(HBM, [token_shape])
        + placed(
            VMEM,
            [half_shape, half_shape, own_shape]
            + [shaped((tokens, 2 * HEAD_SIZE), BF16)] * (ctx_count - 1),
        ),
        A_COST,
        scratch=[
            pltpu.VMEM((tokens, D), BF16),
            pltpu.VMEM((tokens, D), F32),
            pltpu.SemaphoreType.DMA(()),
        ],
    )
    terms, rest = lax.optimization_barrier((terms, rest))
    terms = terms + beside
    terms = widened(doubled, terms, "exp", 3 - FIRST)
    dq_second, own_second, *shared = run(
        functools.partial(second_back_kernel, ctx_count),
        "second_group",
        placed(VMEM, [query_rows, probs, rest] + all_keys + all_values + shared_first),
        placed(VMEM, [half_shape, own_shape])
        + placed(VMEM, [shaped((tokens, kv_width), BF16)] * (ctx_count - 1)),
        B_COST,
    )
    terms = sum_over(terms, "exp", first=4)
    arrived_far, shared = lax.optimization_barrier(([y[s] for s in far], shared))
    for s, piece in zip(far, arrived_far):
        y[s] = piece
    kv_arrived = [pairwise(part, "ctx", s) for s, part in enumerate(shared, 1)]

    kv_shape = shaped((tokens, kv_width // 2), BF16)
    final_shapes = [token_shape, token_shape, kv_shape, kv_shape]
    final_shapes += [shaped((1, tokens), F32), shaped((GAIN_LINES, LANES), F32)]
    total_tokens = tokens * ctx_count * exp_count * lax.axis_size("dp")
    layer_out, d_queries, d_keys, d_values, d_weight, d_gain = run(
        functools.partial(output_kernel, ctx_count, piece_count, rows, total_tokens),
        "layer_output",
        placed(
            VMEM,
            [place, weight_wide, terms, hidden, grad_rows, own_first, own_second]
            + [dq_first, dq_second]
            + kv_arrived
            + y,
        ),
        placed(HBM, final_shapes),
        place_flops,
        scratch=[pltpu.VMEM(x.shape, x.dtype) for x in final_shapes[:1] + final_shapes[2:]]
        + [pltpu.SemaphoreType.DMA((4 + KEY_VALUE_HEADS + D // COLS,))],
    )
    return (
        layer_out[None],
        d_hidden[None],
        d_queries[None],
        d_keys[None],
        d_values[None],
        d_weight,
        d_gain.reshape(D),
    )


def solution(mesh):
    in_specs = (
        P(("exp", "dp"), "ctx", None),
        P(("exp", "dp"), "ctx", None),
        P(("exp", "dp"), "ctx", None),
        P(("exp", "dp"), "ctx", None),
        P(),
        P(),
        P("exp", None, None),
        P("exp", None, None),
        P(("exp", "dp"), "ctx", None),
        P(("exp", "dp"), "ctx"),
        P(("exp", "dp"), "ctx", None),
    )
    out_specs = (
        P(("exp", "dp"), "ctx", None),
        P(("exp", "dp"), "ctx", None),
        P(("exp", "dp"), "ctx", None),
        P(("exp", "dp"), "ctx", None),
        P(("exp", "dp"), "ctx", None),
        P(("exp", "dp"), "ctx"),
        P(),
    )
    return jax.shard_map(
        per_device, mesh=mesh, in_specs=in_specs, out_specs=out_specs, check_vma=False
    )
```
